32 devices in a mesh: image: 4 (over y, core), space: 8 (over z, x).
Axes of the slice: x: 2, y: 2, z: 4, core: 2. Of those that a mesh axis runs over, the one named last changes fastest.
Arguments:
- positions: float32 [4, 3, 163840], P('image', None, 'space'), may hold values from -1 to 2, as said below
- strength: float32 [163840], P('space'), may hold values from 0.5 to 2
- charge: float32 [163840], P('space'), may hold values from -4 to 4
- rest_scale: float32 [4], P('image'), may hold values from 0.3 to 1
- cell_order: int32 [4, 8, 20480], P('image', 'space'), may hold values from 0 to 20479, each once within a row
- ghost_index: int32 [4, 8, 20480], P('image', 'space'), may hold values from 0 to 20479, each once within a row
- tile_atoms: int32 [4, 1280, 256], P('image', 'space'), may hold values from 0 to 40959
Outputs:
- new_positions: float32 [4, 3, 163840], P('image', None, 'space')
The draws below stay inside these ranges and needn't reach their ends.
Inputs may be any that keep to these rules, and one draw needn't show every extreme that they name: `positions`: the solute displaced from image to image along a path. `cell_order`: each row lists every atom of the domain once. `ghost_index`: each row lists every atom of the domain once; the first 10240 are the shell for the lower domain, the rest the shell for the upper domain. `tile_atoms`: entries below 10240 are ghosts from the lower domain, the next 20480 own atoms, the rest ghosts from the upper domain; an own atom listed against itself adds nothing.
All inputs are finite; a program needn't handle non-finite values.
Results may differ from the reference program's by a relative error of at most 0.0003.
Values sent between devices are 32-bit elements; how exact they have to be, the bound alone decides.
No kernel may reach another device: no remote copies, remote signals or barrier semaphores. Data moves between devices by JAX's collectives and lax.ppermute only.
A program may use at most 128 MiB of HBM per device.

```python
import math
import jax
import jax.numpy as jnp
from jax import lax

ATOM_DEV = 20480
SOL_DEV = 1024
TILE = 128
TJ = 256
TILES = 160
IMAGES = 4
DOMAINS = 8
ATOMS = 163840


def draw_positions(key, part):
    key = jax.random.fold_in(key, 7)
    keys = jax.random.split(key, 3)
    base = jax.random.uniform(keys[0], (3, ATOMS), jnp.float32)
    atom_ids = jnp.arange(ATOMS)
    domain_ids = (atom_ids // ATOM_DEV).astype(jnp.float32)
    solute = atom_ids % ATOM_DEV < SOL_DEV
    last_domain = max(ATOMS // ATOM_DEV - 1, 1)
    amplitude = 0.15 * (1.0 + 2.0 * domain_ids / last_domain)
    heading = jax.random.uniform(keys[1], (3, ATOMS), jnp.float32, -1.0, 1.0)
    fraction = jnp.arange(IMAGES, dtype=jnp.float32) / (IMAGES - 1)
    displaced = jnp.where(solute, amplitude, 0.0)[None] * heading
    jitter = jax.random.uniform(keys[2], (IMAGES, 3, ATOMS), jnp.float32, -1.0, 1.0)
    solute_noise = 0.01 * jnp.exp(2.302585093 * domain_ids / last_domain)
    noise_scale = jnp.where(solute, solute_noise, 0.08)[None, None]
    result = base[None] + fraction[:, None, None] * displaced[None] + noise_scale * jitter
    return result.astype(jnp.float32)


def place_ends(values, key, smallest, high):
    longest = values.shape.index(max(values.shape))
    spots = []
    for shift in (0, 1):
        where = [jax.random.randint(jax.random.fold_in(key, axis), (), 0, length) for axis, length in enumerate(values.shape)]
        where[longest] = (where[longest] + shift) % values.shape[longest]
        spots.append(tuple(where))
    return values.at[spots[0]].set(smallest).at[spots[1]].set(high)


def shard_levels(rng, shape, cuts, low, top_value):
    gain = 1.0
    for position, blocks in cuts:
        draws = jax.random.uniform(jax.random.fold_in(jax.random.fold_in(rng, 6), position), (blocks,), jnp.float32, low / len(cuts), top_value / len(cuts))
        gain = gain * jnp.repeat(jnp.exp(draws), shape[position] // blocks).reshape((-1,) + (1,) * (len(shape) - 1 - position))
    return gain


def noise(stream_key, extent, spread, limit, cuts=(), held_as=jnp.bfloat16):
    values = spread * jax.random.normal(stream_key, extent, jnp.float32)
    if cuts:
        values = values * shard_levels(stream_key, extent, cuts, -0.22, 0.18)
    return jnp.clip(values, -limit, limit).astype(held_as)


def setup_inputs(seed: int = 0) -> dict:
    arg_keys = jax.random.split(jax.random.key(seed), 8)
    return {
        "positions": draw_positions(jax.random.fold_in(arg_keys[7], 71), 0),
        "strength": jnp.clip(jnp.exp(math.log(2.0) - 1.3862944 * jax.random.uniform(arg_keys[1], (ATOMS,), jnp.float32) ** shard_levels(arg_keys[1], (ATOMS,), ((0, 8),), -0.2, 0.2)), 0.5, 2.0),
        "charge": noise(arg_keys[2], (ATOMS,), 1.0, 4.0, ((0, 8),), jnp.float32),
        "rest_scale": jnp.clip(jnp.exp(math.log(1.0) - 1.2039728 * jax.random.uniform(arg_keys[3], (IMAGES,), jnp.float32) ** shard_levels(arg_keys[3], (IMAGES,), ((0, 4),), -0.2, 0.2)), 0.3, 1.0),
        "cell_order": jax.vmap(lambda own: jax.random.permutation(own, ATOM_DEV))(jax.random.split(arg_keys[4], IMAGES * DOMAINS)).reshape((IMAGES, DOMAINS, ATOM_DEV)).astype(jnp.int32),
        "ghost_index": jax.vmap(lambda own: jax.random.permutation(own, ATOM_DEV))(jax.random.split(arg_keys[5], IMAGES * DOMAINS)).reshape((IMAGES, DOMAINS, ATOM_DEV)).astype(jnp.int32),
        "tile_atoms": place_ends(jax.random.randint(arg_keys[6], (IMAGES, DOMAINS * TILES, TJ), 0, 2 * ATOM_DEV), jax.random.fold_in(arg_keys[6], 1), 0, (2 * ATOM_DEV) - 1).astype(jnp.int32),
    }


LJ_COEF = 0.5
CHARGE_COEF = 0.1
SOFT_CORE = 0.09
SLAB_WIDTH = 1.0
STEP_SIZE = 0.2
SPRING_COEF = 1.0
EPSILON = 1e-06

def pair_tile(own_atoms, extended, rows_i, rows_j):
    near_atoms = jnp.take(own_atoms, rows_i, axis=1)
    far_atoms = jnp.take(extended, rows_j, axis=1)
    delta_x = near_atoms[0][:, None] - far_atoms[0][None, :]
    delta_y = near_atoms[1][:, None] - far_atoms[1][None, :]
    delta_z = near_atoms[2][:, None] - far_atoms[2][None, :]
    radius_sq = delta_x * delta_x + delta_y * delta_y + delta_z * delta_z
    inside = jnp.maximum(1.0 - radius_sq, 0.0)
    shifted = radius_sq + SOFT_CORE
    coupling = inside * inside * (LJ_COEF * near_atoms[3][:, None] * far_atoms[3][None, :] + CHARGE_COEF * near_atoms[4][:, None] * far_atoms[4][None, :] / (shifted * jnp.sqrt(shifted)))
    return jnp.stack([lax.optimization_barrier(jnp.sum(coupling * delta_x, axis=1)), lax.optimization_barrier(jnp.sum(coupling * delta_y, axis=1)), lax.optimization_barrier(jnp.sum(coupling * delta_z, axis=1))], axis=0)

def image_forces(scaled, orders, ghosts, tile_rows):
    half_count = ATOM_DEV // 2
    offset = jnp.array([SLAB_WIDTH, 0.0, 0.0, 0.0, 0.0], scaled.dtype)[:, None]

    def domain_forces(domain):
        below_domain = (domain - 1) % DOMAINS
        above_domain = (domain + 1) % DOMAINS
        lower_ghosts = jnp.take(scaled[below_domain], ghosts[below_domain, half_count:], axis=1) - offset
        upper_ghosts = jnp.take(scaled[above_domain], ghosts[above_domain, :half_count], axis=1) + offset
        own_atoms = scaled[domain]
        extended = jnp.concatenate([lower_ghosts, own_atoms, upper_ghosts], axis=1)
        tile_order = orders[domain]
        per_tile = jax.vmap(pair_tile, in_axes=(None, None, 0, 0))(own_atoms, extended, tile_order.reshape(TILES, TILE), tile_rows[domain])
        flat_forces = per_tile.transpose(1, 0, 2).reshape(3, ATOM_DEV)
        return jnp.zeros((3, ATOM_DEV), scaled.dtype).at[:, tile_order].set(flat_forces)
    return lax.map(domain_forces, jnp.arange(DOMAINS))

def reference(positions, strength, charge, rest_scale, cell_order, ghost_index, tile_atoms):
    local_index = jnp.arange(ATOMS) % ATOM_DEV
    solute = local_index < SOL_DEV

    def one_image(inputs):
        coords, rest_value, orders, ghosts, tile_rows = inputs
        factor = jnp.where(solute, jnp.sqrt(rest_value), 1.0)
        scaled = jnp.concatenate([coords, (strength * factor)[None], (charge * factor)[None]], axis=0)
        scaled = scaled.reshape(5, DOMAINS, ATOM_DEV).transpose(1, 0, 2)
        forces = image_forces(scaled, orders, ghosts, tile_rows.reshape(DOMAINS, TILES, TJ))
        return forces.transpose(1, 0, 2).reshape(3, ATOMS)
    forces = lax.map(one_image, (positions, rest_scale, cell_order, ghost_index, tile_atoms))
    grid_positions = positions.reshape(IMAGES, 3, DOMAINS, ATOM_DEV)
    grid_forces = forces.reshape(IMAGES, 3, DOMAINS, ATOM_DEV)
    solute_path = grid_positions[..., :SOL_DEV]
    solute_force = grid_forces[..., :SOL_DEV]
    lower_path = jnp.concatenate([solute_path[:1], solute_path[:-1]], axis=0)
    upper_path = jnp.concatenate([solute_path[1:], solute_path[-1:]], axis=0)
    tangent = upper_path - lower_path
    summed = (1, 2, 3)
    tangent_sq = lax.optimization_barrier(jnp.sum(tangent * tangent, axis=summed))
    along_sum = lax.optimization_barrier(jnp.sum(solute_force * tangent, axis=summed))
    ahead_sq = lax.optimization_barrier(jnp.sum((upper_path - solute_path) ** 2, axis=summed))
    behind_sq = lax.optimization_barrier(jnp.sum((solute_path - lower_path) ** 2, axis=summed))
    tangent_norm = jnp.sqrt(tangent_sq + EPSILON)
    perpendicular = solute_force - (along_sum / (tangent_sq + EPSILON))[:, None, None, None] * tangent
    spring = (SPRING_COEF * (jnp.sqrt(ahead_sq + EPSILON) - jnp.sqrt(behind_sq + EPSILON)) / tangent_norm)[:, None, None, None] * tangent
    image_index = jnp.arange(IMAGES)
    interior = (image_index > 0) & (image_index < IMAGES - 1)
    moved = solute_path + STEP_SIZE * (perpendicular + jnp.where(interior[:, None, None, None], spring, 0.0))
    step_diff = moved[1:] - moved[:-1]
    seg_lengths = jnp.sqrt(lax.optimization_barrier(jnp.sum(step_diff * step_diff, axis=summed)) + EPSILON)
    zero_one = jnp.zeros((1,), moved.dtype)
    below = jnp.concatenate([zero_one, seg_lengths])
    above = jnp.concatenate([seg_lengths, zero_one])
    knot_values = jnp.cumsum(below)
    targets = knot_values[-1] * (image_index.astype(moved.dtype) / (IMAGES - 1))
    safe_below = jnp.where(image_index > 0, below, 1.0)
    safe_above = jnp.where(image_index < IMAGES - 1, above, 1.0)
    back = jnp.where(image_index > 0, jnp.clip((knot_values - targets) / safe_below, 0.0, 1.0), 0.0)
    ahead = jnp.where(image_index < IMAGES - 1, jnp.clip((targets - knot_values) / safe_above, 0.0, 1.0), 0.0)
    moved_before = jnp.concatenate([moved[:1], moved[:-1]], axis=0)
    moved_after = jnp.concatenate([moved[1:], moved[-1:]], axis=0)
    blended = moved + back[:, None, None, None] * (moved_before - moved) + ahead[:, None, None, None] * (moved_after - moved)
    relaxed = grid_positions + STEP_SIZE * grid_forces
    relaxed = relaxed.at[..., :SOL_DEV].set(blended)
    return relaxed.reshape(IMAGES, 3, ATOMS)
```

```python
import functools

import jax
import jax.numpy as jnp
from jax import lax
from jax.experimental import pallas as pl
from jax.experimental.pallas import tpu as pltpu
from jax.sharding import PartitionSpec as P

SOL_DEV = 1024
TILE = 128
ROW = 256
FIELDS = 5

LJ_COEF = 0.5
CHARGE_COEF = 0.1
SOFT_CORE = 0.09
SLAB_WIDTH = 1.0
STEP_SIZE = 0.2
SPRING_COEF = 1.0
EPSILON = 1e-06

F32 = jnp.float32
BF16 = jnp.bfloat16
VMEM_LIMIT = 48 * 1024 * 1024


def two_pieces(values):
    high = values.astype(BF16)
    low = (values - high.astype(F32)).astype(BF16)
    return jnp.concatenate([high, low], axis=1)


def one_hot(entries):
    width = entries.shape[1]
    column = jnp.bitwise_and(entries, ROW - 1)
    grid = lax.broadcasted_iota(jnp.int32, (ROW, width), 0)
    return jnp.where(grid == column, 1.0, 0.0).astype(BF16)


def pick(table, hot, row_masks):
    rows = 8 * len(row_masks)
    width = hot.shape[1]
    picked = jnp.dot(table, jnp.concatenate([hot, hot], axis=0), preferred_element_type=F32)
    result = []
    for field in range(table.shape[0] // rows):
        found = jnp.zeros((8, width), F32)
        for block, mask in enumerate(row_masks):
            start = field * rows + block * 8
            found = jnp.where(mask, picked[start : start + 8], found)
        result.append(jnp.sum(found, axis=0, keepdims=True))
    return result


def masks_of(row_entries, starts):
    width = row_entries.shape[1]
    grid = lax.broadcasted_iota(jnp.int32, (8, width), 0)
    relative = row_entries - grid
    return [relative == start for start in starts]


def shell_kernel(rows, scale_ref, pos_ref, strength_ref, charge_ref, ghost_ref, table_ref, down_ref, up_ref, plain):
    root = jnp.sqrt(jnp.full((1, ROW), scale_ref[0], F32))
    for row in range(rows):
        span = slice(row * ROW, (row + 1) * ROW)
        for axis in range(3):
            plain[axis * rows + row : axis * rows + row + 1, :] = pos_ref[0, axis : axis + 1, span]
        a = strength_ref[0:1, span]
        q = charge_ref[0:1, span]
        if row < SOL_DEV // ROW:
            a, q = a * root, q * root
        plain[3 * rows + row : 3 * rows + row + 1, :] = a
        plain[4 * rows + row : 4 * rows + row + 1, :] = q
    table_ref[...] = two_pieces(plain[...])
    half = rows // 2

    def send(out_ref, first, shift):
        def step(block, carry):
            entries = ghost_ref[0:1, pl.ds(pl.multiple_of((first + block) * ROW, ROW), ROW)]
            masks = masks_of(lax.shift_right_logical(entries, 8), range(0, rows, 8))
            found = pick(table_ref[...], one_hot(entries), masks)
            found[0] = found[0] + shift
            for field in range(FIELDS):
                out_ref[field, pl.ds(block, 1), :] = found[field]
            return carry

        lax.fori_loop(0, half, step, 0)

    send(down_ref, 0, SLAB_WIDTH)
    send(up_ref, half, -SLAB_WIDTH)


def own_kernel(rows, order_ref, partner_ref, table_ref, near_ref, far_ref):
    half = rows // 2

    def step(pair, carry):
        entries = order_ref[0:1, pl.ds(pl.multiple_of(pair * ROW, ROW), ROW)]
        masks = masks_of(lax.shift_right_logical(entries, 8), range(0, rows, 8))
        found = pick(table_ref[...], one_hot(entries), masks)
        for field in range(FIELDS):
            near_ref[pair, field : field + 1, :] = found[field]
        for side in range(ROW // TILE):
            tile = pair * (ROW // TILE) + side
            entries = partner_ref[0, pl.ds(tile, 1), :]
            masks = masks_of(lax.shift_right_logical(entries, 8), range(half, half + rows, 8))
            found = pick(table_ref[...], one_hot(entries), masks)
            for field in range(FIELDS):
                far_ref[tile, field : field + 1, :] = found[field]
        return carry

    lax.fori_loop(0, near_ref.shape[0], step, 0)


def tile_forces(near, far_columns, width):
    near = [jnp.broadcast_to(row, (8, TILE)) for row in near]
    sums = [jnp.zeros((8, TILE), F32) for _ in range(3)]
    for block in range(width // 8):
        far = far_columns[block * 8 : block * 8 + 8]
        part = [jnp.broadcast_to(far[:, f : f + 1], (8, TILE)) for f in range(FIELDS)]
        dx, dy, dz = (near[f] - part[f] for f in range(3))
        radius_sq = dx * dx + dy * dy + dz * dz
        inside = jnp.maximum(1.0 - radius_sq, 0.0)
        root = lax.rsqrt(radius_sq + SOFT_CORE)
        strength = near[3] * part[3] + near[4] * part[4] * (root * root * root)
        coupling = inside * inside * strength
        sums = [total + coupling * delta for total, delta in zip(sums, (dx, dy, dz))]
    return [jnp.sum(total, axis=0, keepdims=True) for total in sums]


def force_kernel(
    rows, order_ref, partner_ref, near_ref, far_ref, lower_ref, upper_ref, pos_ref, out_ref, solute_ref, table, total
):
    half = rows // 2
    for side, ref in enumerate((lower_ref, upper_ref)):
        for field in range(FIELDS):
            start = field * rows + side * half
            table[start : start + half, :] = two_pieces(ref[field])
    total[...] = jnp.zeros_like(total)
    starts = list(range(0, half, 8)) + list(range(half + rows, 2 * rows, 8))

    def step(pair, carry):
        forces = [[], [], []]
        for side in range(ROW // TILE):
            tile = pair * (ROW // TILE) + side
            entries = partner_ref[0, pl.ds(tile, 1), :]
            masks = masks_of(lax.shift_right_logical(entries, 8), starts)
            found = pick(table[...], one_hot(entries), masks)
            width = entries.shape[1]
            far = [found[f] + far_ref[tile, f : f + 1, :] for f in range(FIELDS)]
            far_rows = jnp.concatenate(far + [jnp.zeros((8 - FIELDS, width), F32)], axis=0)
            span = slice(side * TILE, (side + 1) * TILE)
            near = [near_ref[pair, f : f + 1, span] for f in range(FIELDS)]
            near[3] = near[3] * LJ_COEF
            near[4] = near[4] * CHARGE_COEF
            for axis, row in enumerate(tile_forces(near, far_rows.T, width)):
                forces[axis].append(row)
        entries = order_ref[0:1, pl.ds(pl.multiple_of(pair * ROW, ROW), ROW)]
        hot = one_hot(entries)
        grid = lax.broadcasted_iota(jnp.int32, (rows, ROW), 0)
        mask = grid == lax.shift_right_logical(entries, 8)
        spread = jnp.concatenate(
            [jnp.where(mask, jnp.concatenate(forces[axis], axis=1), 0.0) for axis in range(3)], axis=0
        )
        total[...] += lax.dot_general(
            two_pieces(spread),
            jnp.concatenate([hot, hot], axis=1),
            (((1,), (1,)), ((), ())),
            preferred_element_type=F32,
        )
        return carry

    lax.fori_loop(0, near_ref.shape[0], step, 0)
    for row in range(rows):
        span = slice(row * ROW, (row + 1) * ROW)
        for axis in range(3):
            force = total[axis * rows + row : axis * rows + row + 1, :]
            out_ref[0, axis : axis + 1, span] = pos_ref[0, axis : axis + 1, span] + STEP_SIZE * force
    solute_ref[...] = out_ref[:, :, 0:SOL_DEV]


def whole(*shape, dtype=F32):
    return jax.ShapeDtypeStruct(shape, dtype)


def kernel_call(body, outs, scratch=(), scalar=0, **more):
    return functools.partial(_call, body, outs, scratch, scalar, more)


def _call(body, outs, scratch, scalar, more, *args):
    in_specs = [pl.BlockSpec(memory_space=pltpu.SMEM)] * scalar
    in_specs += [pl.BlockSpec(memory_space=pltpu.VMEM)] * (len(args) - scalar)
    return pl.pallas_call(
        body,
        out_shape=outs,
        in_specs=in_specs,
        out_specs=[pl.BlockSpec(memory_space=pltpu.VMEM)] * len(outs),
        scratch_shapes=list(scratch),
        compiler_params=pltpu.CompilerParams(vmem_limit_bytes=VMEM_LIMIT),
        **more,
    )(*args)


def turned(array, axis, by):
    count = lax.axis_size(axis)
    return lax.ppermute(array, axis, [(i, (i + by) % count) for i in range(count)])


def round_trip(array, axis):
    count, index = lax.axis_size(axis), lax.axis_index(axis)
    result = jnp.zeros((count,) + array.shape, array.dtype)
    for by in range(count):
        piece = turned(array, axis, by) if by else array
        result = lax.dynamic_update_index_in_dim(result, piece, (index + count - by) % count, 0)
    return result


def inner(left, right):
    return jnp.sum(left * right, axis=(1, 2))


def per_device(positions, strength, charge, rest_scale, cell_order, ghost_index, tile_atoms):
    atoms = positions.shape[2]
    rows = atoms // ROW
    tiles = atoms // TILE
    partners = tile_atoms.shape[2]
    order = cell_order.reshape(1, atoms)
    paths = round_trip(positions[0, :, :SOL_DEV], "image")

    table, down, up = kernel_call(
        functools.partial(shell_kernel, rows),
        [
            whole(FIELDS * rows, 2 * ROW, dtype=BF16),
            whole(FIELDS, rows // 2, ROW),
            whole(FIELDS, rows // 2, ROW),
        ],
        [pltpu.VMEM((FIELDS * rows, ROW), F32)],
        scalar=1,
        cost_estimate=pl.CostEstimate(flops=8 * 10**9, bytes_accessed=10**6, transcendentals=0),
    )(rest_scale, positions, strength.reshape(1, atoms), charge.reshape(1, atoms), ghost_index.reshape(1, atoms))
    upper = turned(down, "space", -1)
    lower = turned(up, "space", 1)
    near, far = kernel_call(
        functools.partial(own_kernel, rows),
        [whole(atoms // ROW, 8, ROW), whole(tiles, 8, partners)],
        cost_estimate=pl.CostEstimate(flops=25 * 10**9, bytes_accessed=10**6, transcendentals=0),
    )(order, tile_atoms, table)
    out, solute = kernel_call(
        functools.partial(force_kernel, rows),
        [whole(1, 3, atoms), whole(1, 3, SOL_DEV)],
        [pltpu.VMEM((FIELDS * rows, 2 * ROW), BF16), pltpu.VMEM((3 * rows, ROW), F32)],
        cost_estimate=pl.CostEstimate(flops=25 * 10**9, bytes_accessed=10**6, transcendentals=0),
    )(order, tile_atoms, near, far, lower, upper, positions)

    pushed = round_trip(solute[0], "image")
    images = lax.axis_size("image")
    index = lax.axis_index("image")
    steps = paths[1:] - paths[:-1]
    upper_path = jnp.concatenate([paths[1:], paths[-1:]])
    lower_path = jnp.concatenate([paths[:1], paths[:-1]])
    tangents = upper_path - lower_path
    gaps = pushed[1:] - pushed[:-1]
    none = jnp.zeros((1,), F32)
    sums = lax.psum(
        jnp.stack(
            [
                inner(tangents, tangents),
                inner(pushed - paths, tangents),
                jnp.concatenate([inner(steps, steps), none]),
                jnp.concatenate([inner(gaps, gaps), none]),
                jnp.concatenate([inner(gaps, tangents[1:]), none]),
                jnp.concatenate([inner(gaps, tangents[:-1]), none]),
                jnp.concatenate([inner(tangents[1:], tangents[:-1]), none]),
            ]
        ),
        "space",
    )
    tangent_sq, along = sums[0], sums[1]
    step_sq, gap_sq, gap_next, gap_this, cross = (sums[i, :-1] for i in range(2, 7))
    step_root = jnp.sqrt(step_sq + EPSILON)
    spring = SPRING_COEF * (step_root[1:] - step_root[:-1]) / jnp.sqrt(tangent_sq[1:-1] + EPSILON)
    spring = jnp.concatenate([none, spring, none])
    shift = STEP_SIZE * spring - along / (tangent_sq + EPSILON)
    ahead_shift, here_shift = shift[1:], shift[:-1]
    length_sq = (
        gap_sq
        + ahead_shift * ahead_shift * tangent_sq[1:]
        + here_shift * here_shift * tangent_sq[:-1]
        + 2.0 * (ahead_shift * gap_next - here_shift * gap_this - ahead_shift * here_shift * cross)
    )
    lengths = jnp.sqrt(jnp.maximum(length_sq, 0.0) + EPSILON)
    knots = jnp.concatenate([none, jnp.cumsum(lengths)])
    targets = knots[-1] * (jnp.arange(images, dtype=F32) / (images - 1))
    back = jnp.concatenate([none, jnp.clip((knots - targets)[1:] / lengths, 0.0, 1.0)])
    ahead = jnp.concatenate([jnp.clip((targets - knots)[:-1] / lengths, 0.0, 1.0), none])
    moved = pushed + shift[:, None, None] * tangents

    def at(array, place):
        return lax.dynamic_index_in_dim(array, jnp.clip(place, 0, images - 1), 0, keepdims=False)

    here = at(moved, index)
    blended = (
        here
        + at(back, index) * (at(moved, index - 1) - here)
        + at(ahead, index) * (at(moved, index + 1) - here)
    )
    return lax.dynamic_update_slice(out, blended[None], (0, 0, 0))


def solution(mesh):
    placed = (
        P("image", None, "space"),
        P("space"),
        P("space"),
        P("image"),
        P("image", "space", None),
        P("image", "space", None),
        P("image", "space", None),
    )
    return jax.shard_map(
        per_device, mesh=mesh, in_specs=placed, out_specs=P("image", None, "space"), check_vma=False
    )
```

```python
import functools

import jax
import jax.numpy as jnp
from jax import lax
from jax.experimental import pallas as pl
from jax.experimental.pallas import tpu as pltpu
from jax.sharding import PartitionSpec as P

SOL_DEV = 1024
TILE = 128
LANES = 128
ROW = 256
FIELDS = 5
WORDS = 3
FEATURES = 32

LJ_COEF = 0.5
CHARGE_COEF = 0.1
SOFT_CORE = 0.09
SLAB_WIDTH = 1.0
STEP_SIZE = 0.2
SPRING_COEF = 1.0
EPSILON = 1e-06

POS_LOW, POS_SCALE = -1.0, (2**19 - 1) / 3.0
A_SCALE = (2**19 - 1) / 2.0
Q_LOW, Q_SCALE = -4.0, (2**20 - 1) / 8.0
CENTRE = 0.5

F32 = jnp.float32
BF16 = jnp.bfloat16
I32 = jnp.int32
VMEM_LIMIT = 48 * 1024 * 1024


def packed(fields):
    def level(value, low, scale):
        return jnp.floor((value - low) * scale + 0.5).astype(I32)

    x, y, z = (level(fields[axis], POS_LOW, POS_SCALE) for axis in range(3))
    a = level(fields[3], 0.0, A_SCALE)
    q = level(fields[4], Q_LOW, Q_SCALE)
    return [
        (x << 13) | (a >> 6),
        (y << 13) | (q >> 7),
        (z << 13) | ((a & 63) << 7) | (q & 127),
    ]


def unpacked(words):
    def value(level, low, scale):
        return level.astype(F32) * (1.0 / scale) + low

    x, y, z = (value(lax.shift_right_logical(word, 13), POS_LOW, POS_SCALE) for word in words)
    a = ((words[0] & 8191) << 6) | ((words[2] >> 7) & 63)
    q = ((words[1] & 8191) << 7) | (words[2] & 127)
    return [x, y, z, value(a, 0.0, A_SCALE), value(q, Q_LOW, Q_SCALE)]


def lane_pick(source, lanes):
    numbers = lax.GatherDimensionNumbers(
        offset_dims=(),
        collapsed_slice_dims=(1,),
        start_index_map=(1,),
        operand_batching_dims=(0,),
        start_indices_batching_dims=(0,),
    )
    return lax.gather(
        source, lanes[:, :, None], numbers, (1, 1), mode=lax.GatherScatterMode.PROMISE_IN_BOUNDS
    )


def spread(words, store, rows):
    for word in range(WORDS):
        for row in range(rows):
            store[word, row * 8 : row * 8 + 8, :] = jnp.broadcast_to(
                words[word][row : row + 1, :], (8, LANES)
            )


def lookup(store, count, entries):
    lanes = [entry & (LANES - 1) for entry in entries]
    places = [entry >> 7 for entry in entries]
    unroll = 4

    def step(turn, found):
        found = list(found)
        for sub in range(unroll):
            row = turn * unroll + sub
            sources = [store[word, pl.ds(pl.multiple_of(row * 8, 8), 8), :] for word in range(WORDS)]
            for i in range(len(entries)):
                here = places[i] == row
                for word in range(WORDS):
                    at = i * WORDS + word
                    found[at] = jnp.where(here, lane_pick(sources[word], lanes[i]), found[at])
        return tuple(found)

    start = tuple(jnp.zeros((8, LANES), I32) for _ in range(WORDS * len(entries)))
    found = lax.fori_loop(0, count // unroll, step, start)
    return [found[i * WORDS : (i + 1) * WORDS] for i in range(len(entries))]


def shell_kernel(rows, scale_ref, pos_ref, strength_ref, charge_ref, ghost_ref, words_ref, down_ref, up_ref, plain, store):
    root = jnp.sqrt(jnp.full((SOL_DEV // LANES, LANES), scale_ref[0], F32))
    for row in range(rows):
        span = slice(row * LANES, (row + 1) * LANES)
        for axis in range(3):
            plain[axis, row : row + 1, :] = pos_ref[0, axis : axis + 1, span]
    plain[3] = strength_ref[...]
    plain[4] = charge_ref[...]
    solute = slice(0, SOL_DEV // LANES)
    plain[3, solute, :] = strength_ref[solute, :] * root
    plain[4, solute, :] = charge_ref[solute, :] * root
    words = packed([plain[field] for field in range(FIELDS)])
    for word in range(WORDS):
        words_ref[word] = words[word]
    spread([words_ref.at[word] for word in range(WORDS)], store, rows)
    half = rows // 2
    batch = 5 if half % 40 == 0 else 1
    for ref, first, shift in ((down_ref, 0, SLAB_WIDTH), (up_ref, half, -SLAB_WIDTH)):

        def step(turn, carry, ref=ref, first=first, shift=shift):
            base = turn * batch * 8
            entries = [
                ghost_ref[pl.ds(pl.multiple_of(first + base + i * 8, 8), 8), :] for i in range(batch)
            ]
            for i, found in enumerate(lookup(store, rows, entries)):
                fields = unpacked(found)
                fields[0] = fields[0] + shift
                for field in range(FIELDS):
                    ref[field, pl.ds(pl.multiple_of(base + i * 8, 8), 8), :] = fields[field]
            return carry

        lax.fori_loop(0, half // (8 * batch), step, 0)


def own_kernel(rows, order_ref, partner_ref, words_ref, near_ref, far_ref, store):
    spread([words_ref.at[word] for word in range(WORDS)], store, rows)
    half = rows // 2

    def near_step(turn, carry):
        base = turn * 32
        entries = [order_ref[pl.ds(pl.multiple_of(base + i * 8, 8), 8), :] for i in range(4)]
        for i, found in enumerate(lookup(store, rows, entries)):
            fields = unpacked(found)
            for field in range(FIELDS):
                near_ref[field, pl.ds(pl.multiple_of(base + i * 8, 8), 8), :] = fields[field]
        return carry

    lax.fori_loop(0, rows // 32, near_step, 0)
    sides = partner_ref.shape[2] // LANES

    def far_step(turn, carry):
        base = turn * 32
        spots = [
            (pl.ds(pl.multiple_of(base + i * 8, 8), 8), slice(side * LANES, (side + 1) * LANES))
            for i in range(4)
            for side in range(sides)
        ]
        entries = [partner_ref[0, rows_, span] - half * LANES for rows_, span in spots]
        for spot, found in zip(spots, lookup(store, rows, entries)):
            for word in range(WORDS):
                far_ref[word, spot[0], spot[1]] = found[word]
        return carry

    lax.fori_loop(0, rows // 32, far_step, 0)


def pieces(value, count):
    result = []
    for _ in range(count - 1):
        part = value.astype(BF16).astype(F32)
        result.append(part)
        value = value - part
    return result + [value]


def features(fields, near):
    rows = []
    coords = [pieces(fields[axis], 3) for axis in range(3)]
    for high, middle, low in coords:
        if near:
            rows += [2.0 * part for part in (high, high, middle, high, low, middle)]
        else:
            rows += [high, middle, high, low, high, middle]
    norm = -(fields[0] * fields[0] + fields[1] * fields[1] + fields[2] * fields[2])
    norm = pieces(norm + 1.0 if near else norm, 3)
    one = jnp.ones_like(fields[0])
    if near:
        rows += norm + [one] * 3
    else:
        rows += [one] * 3 + norm
    for value, coef in ((fields[3], LJ_COEF), (fields[4], CHARGE_COEF)):
        high, low = pieces(value * coef if near else value, 2)
        rows += [high, high, low, low] if near else [high, low, high, low]
    return rows


def one_hot(entries):
    width = entries.shape[1]
    grid = lax.broadcasted_iota(I32, (ROW, width), 0)
    return jnp.where(grid == (entries & (ROW - 1)), 1.0, 0.0).astype(BF16)


def two_pieces(values):
    high = values.astype(BF16)
    low = (values - high.astype(F32)).astype(BF16)
    return high, low


def joined(ref, spot):
    return jnp.concatenate([ref[plane, spot, :].astype(BF16) for plane in range(ref.shape[0])], axis=1)


def force_kernel(
    rows, order_ref, partner_ref, near_ref, far_ref, lower_ref, upper_ref, pos_ref, out_ref, solute_ref,
    store, near_rows, far_rows, shifted, total,
):
    half = rows // 2
    sides = partner_ref.shape[2] // LANES
    shell = []
    for field in range(FIELDS):
        both = [lower_ref[field], upper_ref[field]]
        if field == 0:
            both = [both[0] + SLAB_WIDTH, both[1] - SLAB_WIDTH]
        shell.append(jnp.concatenate(both, axis=0))
    words = packed(shell)
    spread(words, store, rows)
    total[...] = jnp.zeros_like(total)
    near_rows[...] = jnp.zeros_like(near_rows)
    shifted[...] = jnp.zeros_like(shifted)
    batch = 32

    def group(turn, carry):
        base = turn * batch
        spots = [(i, side) for i in range(batch // 8) for side in range(sides)]
        entries = []
        for i, side in spots:
            entry = partner_ref[0, pl.ds(pl.multiple_of(base + i * 8, 8), 8), side * LANES : (side + 1) * LANES]
            upper = entry - rows * LANES
            own = jnp.logical_and(entry >= half * LANES, upper < half * LANES)
            entries.append(jnp.where(own, 2 * rows * LANES, jnp.where(upper >= half * LANES, upper, entry)))
        for (i, side), found in zip(spots, lookup(store, rows, entries)):
            span = slice(side * LANES, (side + 1) * LANES)
            place = pl.ds(pl.multiple_of(base + i * 8, 8), 8)
            entry = partner_ref[0, place, span]
            fields = unpacked([found[word] | far_ref[word, place, span] for word in range(WORDS)])
            fields[0] = (
                fields[0]
                + jnp.where(entry >= (half + rows) * LANES, SLAB_WIDTH, 0.0)
                - jnp.where(entry < half * LANES, SLAB_WIDTH, 0.0)
            )
            for axis in range(3):
                fields[axis] = fields[axis] - CENTRE
            for k, row in enumerate(features(fields, False)):
                far_rows[side, pl.ds(i * 8 * FEATURES + k, 8, stride=FEATURES), :] = row
            for axis in range(3):
                high, low = pieces(fields[axis], 2)
                shifted[side, pl.ds(i * 128 + axis, 8, stride=16), :] = high
                shifted[side, pl.ds(i * 128 + 8 + axis, 8, stride=16), :] = low
            shifted[side, pl.ds(i * 128 + 3, 8, stride=16), :] = jnp.ones((8, LANES), F32)
        for i in range(batch // 8):
            place = pl.ds(pl.multiple_of(base + i * 8, 8), 8)
            fields = [near_ref[field, place, :] for field in range(FIELDS)]
            for axis in range(3):
                fields[axis] = fields[axis] - CENTRE
            for k, row in enumerate(features(fields, True)):
                group_of = 0 if k < 24 else (1 if k < 28 else 2)
                near_rows[group_of, pl.ds(i * 8 * FEATURES + k, 8, stride=FEATURES), :] = row

        def pair(turn, carry):
            forces = [[], [], []]
            numbers = []
            for side in range(ROW // TILE):
                local = turn * (ROW // TILE) + side
                spot = pl.ds(pl.multiple_of(local * FEATURES, FEATURES), FEATURES)
                grams = lax.dot_general(
                    joined(far_rows, spot),
                    joined(near_rows, spot),
                    (((0,), (0,)), ((), ())),
                    preferred_element_type=F32,
                )
                window = grams[:, 0:LANES]
                inside = jnp.maximum(window, 0.0)
                root = lax.rsqrt((1.0 + SOFT_CORE) - window)
                strength = grams[:, LANES : 2 * LANES] + grams[:, 2 * LANES :] * (root * root * root)
                high, low = two_pieces(inside * inside * strength)
                left = joined(shifted, pl.ds(pl.multiple_of(local * 16, 16), 16))
                sums = jnp.dot(left, high, preferred_element_type=F32) + jnp.dot(
                    left, low, preferred_element_type=F32
                )
                whole_sum = sums[3:4]
                for axis in range(3):
                    near = near_ref[axis, pl.ds(base + local, 1), :] - CENTRE
                    forces[axis].append(near * whole_sum - sums[axis : axis + 1] - sums[8 + axis : 9 + axis])
                numbers.append(order_ref[pl.ds(base + local, 1), :])
            entries = jnp.concatenate(numbers, axis=1)
            hot = one_hot(entries)
            grid = lax.broadcasted_iota(I32, (total.shape[0] // 3, ROW), 0)
            mask = grid == (entries >> 8)
            parts = [
                jnp.where(mask, jnp.concatenate(forces[axis], axis=1), 0.0) for axis in range(3)
            ]
            high, low = two_pieces(jnp.concatenate(parts, axis=0))
            total[...] += lax.dot_general(
                jnp.concatenate([high, low], axis=1),
                jnp.concatenate([hot, hot], axis=1),
                (((1,), (1,)), ((), ())),
                preferred_element_type=F32,
            )
            return carry

        lax.fori_loop(0, batch * TILE // ROW, pair, 0)
        return carry

    lax.fori_loop(0, rows // batch, group, 0)
    table_rows = total.shape[0] // 3
    for row in range(table_rows):
        span = slice(row * ROW, (row + 1) * ROW)
        for axis in range(3):
            force = total[axis * table_rows + row : axis * table_rows + row + 1, :]
            out_ref[0, axis : axis + 1, span] = pos_ref[0, axis : axis + 1, span] + STEP_SIZE * force
    solute_ref[...] = out_ref[:, :, 0:SOL_DEV]


def whole(*shape, dtype=F32):
    return jax.ShapeDtypeStruct(shape, dtype)


def kernel_call(body, outs, scratch=(), scalar=0, **more):
    return functools.partial(_call, body, outs, scratch, scalar, more)


def _call(body, outs, scratch, scalar, more, *args):
    in_specs = [pl.BlockSpec(memory_space=pltpu.SMEM)] * scalar
    in_specs += [pl.BlockSpec(memory_space=pltpu.VMEM)] * (len(args) - scalar)
    return pl.pallas_call(
        body,
        out_shape=outs,
        in_specs=in_specs,
        out_specs=[pl.BlockSpec(memory_space=pltpu.VMEM)] * len(outs),
        scratch_shapes=list(scratch),
        compiler_params=pltpu.CompilerParams(vmem_limit_bytes=VMEM_LIMIT),
        **more,
    )(*args)


def turned(array, axis, by):
    count = lax.axis_size(axis)
    return lax.ppermute(array, axis, [(i, (i + by) % count) for i in range(count)])


def round_trip(array, axis):
    count, index = lax.axis_size(axis), lax.axis_index(axis)
    result = jnp.zeros((count,) + array.shape, array.dtype)
    for by in range(count):
        piece = turned(array, axis, by) if by else array
        result = lax.dynamic_update_index_in_dim(result, piece, (index + count - by) % count, 0)
    return result


def inner(left, right):
    return jnp.sum(left * right, axis=(1, 2))


def per_device(positions, strength, charge, rest_scale, cell_order, ghost_index, tile_atoms):
    atoms = positions.shape[2]
    rows = atoms // LANES
    partners = tile_atoms.shape[2]
    order = cell_order.reshape(rows, LANES)
    paths = round_trip(positions[0, :, :SOL_DEV], "image")
    store = pltpu.VMEM((WORDS, rows * 8, LANES), I32)
    words, down, up = kernel_call(
        functools.partial(shell_kernel, rows),
        [
            whole(WORDS, rows, LANES, dtype=I32),
            whole(FIELDS, rows // 2, LANES),
            whole(FIELDS, rows // 2, LANES),
        ],
        [pltpu.VMEM((FIELDS, rows, LANES), F32), store],
        scalar=1,
        cost_estimate=pl.CostEstimate(flops=8 * 10**9, bytes_accessed=10**6, transcendentals=0),
    )(
        rest_scale,
        positions,
        strength.reshape(rows, LANES),
        charge.reshape(rows, LANES),
        ghost_index.reshape(rows, LANES),
    )
    upper = turned(down, "space", -1)
    lower = turned(up, "space", 1)
    near, far = kernel_call(
        functools.partial(own_kernel, rows),
        [whole(FIELDS, rows, LANES), whole(WORDS, rows, partners, dtype=I32)],
        [store],
        cost_estimate=pl.CostEstimate(flops=25 * 10**9, bytes_accessed=10**6, transcendentals=0),
    )(order, tile_atoms, words)
    out, solute = kernel_call(
        functools.partial(force_kernel, rows),
        [whole(1, 3, atoms), whole(1, 3, SOL_DEV)],
        [
            store,
            pltpu.VMEM((3, 32 * FEATURES, LANES), F32),
            pltpu.VMEM((partners // LANES, 32 * FEATURES, LANES), F32),
            pltpu.VMEM((partners // LANES, 32 * 16, LANES), F32),
            pltpu.VMEM((3 * (atoms // ROW), ROW), F32),
        ],
        cost_estimate=pl.CostEstimate(flops=25 * 10**9, bytes_accessed=10**6, transcendentals=0),
    )(order, tile_atoms, near, far, lower, upper, positions)

    pushed = round_trip(solute[0], "image")
    images = lax.axis_size("image")
    index = lax.axis_index("image")
    steps = paths[1:] - paths[:-1]
    upper_path = jnp.concatenate([paths[1:], paths[-1:]])
    lower_path = jnp.concatenate([paths[:1], paths[:-1]])
    tangents = upper_path - lower_path
    gaps = pushed[1:] - pushed[:-1]
    none = jnp.zeros((1,), F32)
    sums = lax.psum(
        jnp.stack(
            [
                inner(tangents, tangents),
                inner(pushed - paths, tangents),
                jnp.concatenate([inner(steps, steps), none]),
                jnp.concatenate([inner(gaps, gaps), none]),
                jnp.concatenate([inner(gaps, tangents[1:]), none]),
                jnp.concatenate([inner(gaps, tangents[:-1]), none]),
                jnp.concatenate([inner(tangents[1:], tangents[:-1]), none]),
            ]
        ),
        "space",
    )
    tangent_sq, along = sums[0], sums[1]
    step_sq, gap_sq, gap_next, gap_this, cross = (sums[i, :-1] for i in range(2, 7))
    step_root = jnp.sqrt(step_sq + EPSILON)
    spring = SPRING_COEF * (step_root[1:] - step_root[:-1]) / jnp.sqrt(tangent_sq[1:-1] + EPSILON)
    spring = jnp.concatenate([none, spring, none])
    shift = STEP_SIZE * spring - along / (tangent_sq + EPSILON)
    ahead_shift, here_shift = shift[1:], shift[:-1]
    length_sq = (
        gap_sq
        + ahead_shift * ahead_shift * tangent_sq[1:]
        + here_shift * here_shift * tangent_sq[:-1]
        + 2.0 * (ahead_shift * gap_next - here_shift * gap_this - ahead_shift * here_shift * cross)
    )
    lengths = jnp.sqrt(jnp.maximum(length_sq, 0.0) + EPSILON)
    knots = jnp.concatenate([none, jnp.cumsum(lengths)])
    targets = knots[-1] * (jnp.arange(images, dtype=F32) / (images - 1))
    back = jnp.concatenate([none, jnp.clip((knots - targets)[1:] / lengths, 0.0, 1.0)])
    ahead = jnp.concatenate([jnp.clip((targets - knots)[:-1] / lengths, 0.0, 1.0), none])
    moved = pushed + shift[:, None, None] * tangents

    def at(array, place):
        return lax.dynamic_index_in_dim(array, jnp.clip(place, 0, images - 1), 0, keepdims=False)

    here = at(moved, index)
    blended = (
        here
        + at(back, index) * (at(moved, index - 1) - here)
        + at(ahead, index) * (at(moved, index + 1) - here)
    )
    return lax.dynamic_update_slice(out, blended[None], (0, 0, 0))


def solution(mesh):
    placed = (
        P("image", None, "space"),
        P("space"),
        P("space"),
        P("image"),
        P("image", "space", None),
        P("image", "space", None),
        P("image", "space", None),
    )
    return jax.shard_map(
        per_device, mesh=mesh, in_specs=placed, out_specs=P("image", None, "space"), check_vma=False
    )
```

```python
import functools

import jax
import jax.numpy as jnp
import numpy as np
from jax import lax
from jax.experimental import pallas as pl
from jax.experimental.pallas import tpu as pltpu
from jax.sharding import PartitionSpec as P

SOL_DEV = 1024
TILE = 128
LANES = 128
FIELDS = 5
STRIDE = 48

LJ_COEF = 0.5
CHARGE_COEF = 0.1
SOFT_CORE = 0.09
SLAB_WIDTH = 1.0
STEP_SIZE = 0.2
SPRING_COEF = 1.0
EPSILON = 1e-06
CENTRE = 0.5

F32 = jnp.float32
BF16 = jnp.bfloat16
I32 = jnp.int32
VMEM_LIMIT = 58 * 1024 * 1024

ONES = 18
NORM = 21
DEPTH = 24
CHARGE = 28
LAST = 32


def near_selector():
    chosen = np.zeros((LANES, 3 * LANES), np.float32)
    for axis in range(3):
        high, middle, low = 6 * axis, 6 * axis + 1, 6 * axis + 3
        for k, source in enumerate((high, high, middle, high, low, middle)):
            chosen[source, 6 * axis + k] = 2.0
    for k in range(3):
        chosen[NORM + k, ONES + k] = 1.0
        chosen[ONES, NORM + k] = 1.0
    chosen[ONES, LAST] = 1.0
    for block, first in ((1, DEPTH), (2, CHARGE)):
        for k, source in enumerate((first, first, first + 1, first + 1)):
            chosen[source, block * LANES + first + k] = 1.0
    return jnp.asarray(chosen, BF16)


def pieces(value, count):
    result = []
    for _ in range(count - 1):
        part = value.astype(BF16).astype(F32)
        result.append(part)
        value = value - part
    return result + [value]


def features(fields):
    rows = []
    for axis in range(3):
        high, middle, low = pieces(fields[axis], 3)
        rows += [high, middle, high, low, high, middle]
    one = jnp.ones_like(fields[0])
    rows += [one] * 3
    rows += pieces(-(fields[0] * fields[0] + fields[1] * fields[1] + fields[2] * fields[2]), 3)
    for value in fields[3:]:
        high, low = pieces(value, 2)
        rows += [high, low, high, low]
    return rows + [one]


def two_pieces(values):
    high = values.astype(BF16)
    low = (values - high.astype(F32)).astype(BF16)
    return high, low


def nt_dot(left, right):
    return lax.dot_general(left, right, (((1,), (1,)), ((), ())), preferred_element_type=F32)


def fill_table(rows, fields_ref, eye_ref, table, planes):
    planes[...] = jnp.zeros_like(planes)
    groups = rows // 8

    def step(turn, carry):
        domain = turn // groups
        first = pl.multiple_of((turn % groups) * 8, 8)
        fields = [fields_ref[domain, field, pl.ds(first, 8), :] for field in range(FIELDS)]
        shift = (domain - 1).astype(F32) * SLAB_WIDTH
        fields[0] = fields[0] + shift
        for axis in range(3):
            fields[axis] = fields[axis] - CENTRE
        fields[3] = fields[3] * LJ_COEF**0.5
        fields[4] = fields[4] * CHARGE_COEF**0.5
        for k, row in enumerate(features(fields)):
            planes[pl.ds(k, 8, stride=STRIDE), :] = row
        for block in range(8):
            part = planes[block * STRIDE : (block + 1) * STRIDE, :].astype(BF16)
            part = jnp.concatenate([part, jnp.zeros((LANES - STRIDE, LANES), BF16)], axis=0)
            start = pl.multiple_of((turn * 8 + block) * LANES, LANES)
            table[pl.ds(start, LANES), :] = nt_dot(eye_ref[...], part)
        return carry

    lax.fori_loop(0, 3 * groups, step, 0)


def force_kernel(
    rows, partner_ref, entry_ref, order_ref, fields_ref, select_ref, eye_ref, out_ref, solute_ref,
    table, forces, planes, far_a, far_b, near_a, near_b, sum_a, sum_b,
):
    fill_table(rows, fields_ref, eye_ref, table, planes)
    partners = far_a.shape[0]
    own = rows * LANES

    def load(tile, far, near):
        for k in range(partners):
            entry = entry_ref[partner_ref[tile * partners + k]]
            far[k : k + 1, :] = table[pl.ds(entry, 1), :]
        for k in range(TILE):
            entry = order_ref[tile * TILE + k] + own
            near[k : k + 1, :] = table[pl.ds(entry, 1), :]

    def compute(far, near, sums):
        others = far[...].astype(BF16)
        left = jnp.dot(near[...].astype(BF16), select_ref[...], preferred_element_type=F32).astype(BF16)
        left = jnp.concatenate([left[:, k * LANES : (k + 1) * LANES] for k in range(3)], axis=0)
        grams = nt_dot(left, others)
        window = grams[0:TILE]
        inside = jnp.maximum(window, 0.0)
        root = lax.rsqrt((1.0 + SOFT_CORE) - window)
        strength = grams[TILE : 2 * TILE] + grams[2 * TILE :] * (root * root * root)
        high, low = two_pieces(inside * inside * strength)
        both = jnp.dot(jnp.concatenate([high, low], axis=0), others, preferred_element_type=F32)
        sums[...] = both[0:TILE] + both[TILE:]

    def save(tile, sums):
        for k in range(TILE):
            forces[pl.ds(order_ref[tile * TILE + k], 1), :] = sums[k : k + 1, :]

    load(0, far_a, near_a)

    def step(turn, carry):
        tile = turn * 2
        load(tile + 1, far_b, near_b)
        compute(far_a, near_a, sum_a)
        save(tile, sum_a)
        load(jnp.minimum(tile + 2, rows - 1), far_a, near_a)
        compute(far_b, near_b, sum_b)
        save(tile + 1, sum_b)
        return carry

    lax.fori_loop(0, rows // 2, step, 0)

    def finish(row, carry):
        turned_sums = forces[pl.ds(pl.multiple_of(row * LANES, LANES), LANES), :].T
        for axis in range(3):
            first = 6 * axis
            moment = (
                turned_sums[first : first + 1] + turned_sums[first + 1 : first + 2] + turned_sums[first + 3 : first + 4]
            )
            place = fields_ref[1, axis, pl.ds(row, 1), :]
            force = (place - CENTRE) * turned_sums[ONES : ONES + 1] - moment
            out_ref[axis, pl.ds(row, 1), :] = place + STEP_SIZE * force
        return carry

    lax.fori_loop(0, rows, finish, 0)
    solute_ref[...] = out_ref[:, 0 : SOL_DEV // LANES, :]


def whole(*shape, dtype=F32):
    return jax.ShapeDtypeStruct(shape, dtype)


def kernel_call(body, outs, scratch=(), scalar=0, **more):
    return functools.partial(_call, body, outs, scratch, scalar, more)


def _call(body, outs, scratch, scalar, more, *args):
    in_specs = [pl.BlockSpec(memory_space=pltpu.SMEM)] * scalar
    in_specs += [pl.BlockSpec(memory_space=pltpu.VMEM)] * (len(args) - scalar)
    return pl.pallas_call(
        body,
        out_shape=outs,
        in_specs=in_specs,
        out_specs=[pl.BlockSpec(memory_space=pltpu.VMEM)] * len(outs),
        scratch_shapes=list(scratch),
        compiler_params=pltpu.CompilerParams(vmem_limit_bytes=VMEM_LIMIT),
        **more,
    )(*args)


def turned(array, axis, by):
    count = lax.axis_size(axis)
    return lax.ppermute(array, axis, [(i, (i + by) % count) for i in range(count)])


def round_trip(array, axis):
    count, index = lax.axis_size(axis), lax.axis_index(axis)
    result = jnp.zeros((count,) + array.shape, array.dtype)
    for by in range(count):
        piece = turned(array, axis, by) if by else array
        result = lax.dynamic_update_index_in_dim(result, piece, (index + count - by) % count, 0)
    return result


def inner(left, right):
    return jnp.sum(left * right, axis=(1, 2))


def per_device(positions, strength, charge, rest_scale, cell_order, ghost_index, tile_atoms):
    atoms = positions.shape[2]
    rows = atoms // LANES
    half = atoms // 2
    partners = tile_atoms.shape[2]
    paths = round_trip(positions[0, :, :SOL_DEV], "image")

    factor = jnp.where(jnp.arange(atoms) < SOL_DEV, jnp.sqrt(rest_scale[0]), 1.0)
    scaled = jnp.stack([strength * factor, charge * factor])
    fields = jnp.concatenate([positions[0], scaled]).reshape(FIELDS, rows, LANES)
    fields = jnp.stack([turned(fields, "space", 1), fields, turned(fields, "space", -1)])
    shell = ghost_index.reshape(atoms)
    entries = jnp.concatenate(
        [
            turned(shell[half:], "space", 1),
            jnp.arange(atoms, 2 * atoms, dtype=I32),
            turned(shell[:half], "space", -1) + 2 * atoms,
        ]
    )
    out, solute = kernel_call(
        functools.partial(force_kernel, rows),
        [whole(3, rows, LANES), whole(3, SOL_DEV // LANES, LANES)],
        [
            pltpu.VMEM((3 * atoms, LANES), F32),
            pltpu.VMEM((atoms, LANES), F32),
            pltpu.VMEM((8 * STRIDE, LANES), F32),
            pltpu.VMEM((partners, LANES), F32),
            pltpu.VMEM((partners, LANES), F32),
            pltpu.VMEM((TILE, LANES), F32),
            pltpu.VMEM((TILE, LANES), F32),
            pltpu.VMEM((TILE, LANES), F32),
            pltpu.VMEM((TILE, LANES), F32),
        ],
        scalar=3,
        cost_estimate=pl.CostEstimate(flops=25 * 10**9, bytes_accessed=10**6, transcendentals=0),
    )(
        tile_atoms.reshape(rows * partners),
        entries,
        cell_order.reshape(atoms),
        fields,
        near_selector(),
        jnp.eye(LANES, dtype=BF16),
    )
    out = out.reshape(1, 3, atoms)
    solute = solute.reshape(1, 3, SOL_DEV)

    pushed = round_trip(solute[0], "image")
    images = lax.axis_size("image")
    index = lax.axis_index("image")
    steps = paths[1:] - paths[:-1]
    upper_path = jnp.concatenate([paths[1:], paths[-1:]])
    lower_path = jnp.concatenate([paths[:1], paths[:-1]])
    tangents = upper_path - lower_path
    gaps = pushed[1:] - pushed[:-1]
    none = jnp.zeros((1,), F32)
    sums = lax.psum(
        jnp.stack(
            [
                inner(tangents, tangents),
                inner(pushed - paths, tangents),
                jnp.concatenate([inner(steps, steps), none]),
                jnp.concatenate([inner(gaps, gaps), none]),
                jnp.concatenate([inner(gaps, tangents[1:]), none]),
                jnp.concatenate([inner(gaps, tangents[:-1]), none]),
                jnp.concatenate([inner(tangents[1:], tangents[:-1]), none]),
            ]
        ),
        "space",
    )
    tangent_sq, along = sums[0], sums[1]
    step_sq, gap_sq, gap_next, gap_this, cross = (sums[i, :-1] for i in range(2, 7))
    step_root = jnp.sqrt(step_sq + EPSILON)
    spring = SPRING_COEF * (step_root[1:] - step_root[:-1]) / jnp.sqrt(tangent_sq[1:-1] + EPSILON)
    spring = jnp.concatenate([none, spring, none])
    shift = STEP_SIZE * spring - along / (tangent_sq + EPSILON)
    ahead_shift, here_shift = shift[1:], shift[:-1]
    length_sq = (
        gap_sq
        + ahead_shift * ahead_shift * tangent_sq[1:]
        + here_shift * here_shift * tangent_sq[:-1]
        + 2.0 * (ahead_shift * gap_next - here_shift * gap_this - ahead_shift * here_shift * cross)
    )
    lengths = jnp.sqrt(jnp.maximum(length_sq, 0.0) + EPSILON)
    knots = jnp.concatenate([none, jnp.cumsum(lengths)])
    targets = knots[-1] * (jnp.arange(images, dtype=F32) / (images - 1))
    back = jnp.concatenate([none, jnp.clip((knots - targets)[1:] / lengths, 0.0, 1.0)])
    ahead = jnp.concatenate([jnp.clip((targets - knots)[:-1] / lengths, 0.0, 1.0), none])
    moved = pushed + shift[:, None, None] * tangents

    def at(array, place):
        return lax.dynamic_index_in_dim(array, jnp.clip(place, 0, images - 1), 0, keepdims=False)

    here = at(moved, index)
    blended = (
        here
        + at(back, index) * (at(moved, index - 1) - here)
        + at(ahead, index) * (at(moved, index + 1) - here)
    )
    return lax.dynamic_update_slice(out, blended[None], (0, 0, 0))


def solution(mesh):
    placed = (
        P("image", None, "space"),
        P("space"),
        P("space"),
        P("image"),
        P("image", "space", None),
        P("image", "space", None),
        P("image", "space", None),
    )
    return jax.shard_map(
        per_device, mesh=mesh, in_specs=placed, out_specs=P("image", None, "space"), check_vma=False
    )
```

```python
import functools

import jax
import jax.numpy as jnp
import numpy as np
from jax import lax
from jax.experimental import pallas as pl
from jax.experimental.pallas import tpu as pltpu
from jax.sharding import PartitionSpec as P

SOL_DEV = 1024
TILE = 128
LANES = 128
FIELDS = 5
STRIDE = 48

LJ_COEF = 0.5
CHARGE_COEF = 0.1
SOFT_CORE = 0.09
SLAB_WIDTH = 1.0
STEP_SIZE = 0.2
SPRING_COEF = 1.0
EPSILON = 1e-06
CENTRE = 0.5

F32 = jnp.float32
BF16 = jnp.bfloat16
I32 = jnp.int32
VMEM_LIMIT = 58 * 1024 * 1024

ONES = 18
NORM = 21
DEPTH = 24
CHARGE = 28
LAST = 32


def near_selector():
    chosen = np.zeros((LANES, 3 * LANES), np.float32)
    for axis in range(3):
        high, middle, low = 6 * axis, 6 * axis + 1, 6 * axis + 3
        for k, source in enumerate((high, high, middle, high, low, middle)):
            chosen[source, 6 * axis + k] = 2.0
    for k in range(3):
        chosen[NORM + k, ONES + k] = 1.0
        chosen[ONES, NORM + k] = 1.0
    chosen[ONES, LAST] = 1.0
    for block, first in ((1, DEPTH), (2, CHARGE)):
        for k, source in enumerate((first, first, first + 1, first + 1)):
            chosen[source, block * LANES + first + k] = 1.0
    return jnp.asarray(chosen, BF16)


def pieces(value, count):
    result = []
    for _ in range(count - 1):
        part = value.astype(BF16).astype(F32)
        result.append(part)
        value = value - part
    return result + [value]


def features(fields):
    rows = []
    for axis in range(3):
        high, middle, low = pieces(fields[axis], 3)
        rows += [high, middle, high, low, high, middle]
    one = jnp.ones_like(fields[0])
    rows += [one] * 3
    rows += pieces(-(fields[0] * fields[0] + fields[1] * fields[1] + fields[2] * fields[2]), 3)
    for value in fields[3:]:
        high, low = pieces(value, 2)
        rows += [high, low, high, low]
    return rows + [one]


def two_pieces(values):
    high = values.astype(BF16)
    low = (values - high.astype(F32)).astype(BF16)
    return high, low


def nt_dot(left, right):
    return lax.dot_general(left, right, (((1,), (1,)), ((), ())), preferred_element_type=F32)


def fill_blocks(fields, eye, planes, table, first):
    fields = [field - CENTRE for field in fields[:3]] + fields[3:]
    fields[3] = fields[3] * LJ_COEF**0.5
    fields[4] = fields[4] * CHARGE_COEF**0.5
    for k, row in enumerate(features(fields)):
        planes[pl.ds(k, 8, stride=STRIDE), :] = row
    blank = jnp.zeros((LANES - STRIDE, LANES), BF16)
    for block in range(0, 8, 2):
        parts = []
        for side in range(2):
            start = (block + side) * STRIDE
            parts += [planes[start : start + STRIDE, :].astype(BF16), blank]
        both = nt_dot(eye, jnp.concatenate(parts, axis=0))
        for side in range(2):
            start = pl.multiple_of(first + (block + side) * LANES, LANES)
            table[pl.ds(start, LANES), :] = both[:, side * LANES : (side + 1) * LANES]


def near_kernel(rows, order_ref, fields_ref, select_ref, eye_ref, table_ref, left_ref, table, planes, stage):
    turn = pl.program_id(0)

    @pl.when(turn == 0)
    def _():
        planes[...] = jnp.zeros_like(planes)

        def fill(group, carry):
            spot = pl.ds(pl.multiple_of(group * 8, 8), 8)
            fields = [fields_ref[field, spot, :] for field in range(FIELDS)]
            fill_blocks(fields, eye_ref[...], planes, table, group * 8 * LANES)
            return carry

        lax.fori_loop(0, rows // 8, fill, 0)

    def tile_step(local, carry):
        for side in range(2):
            tile = turn * 8 + local * 2 + side
            for k in range(TILE):
                stage[side, k : k + 1, :] = table[pl.ds(order_ref[tile * TILE + k], 1), :]
        for side in range(2):
            left = jnp.dot(stage[side].astype(BF16), select_ref[...], preferred_element_type=F32).astype(BF16)
            for block in range(3):
                left_ref[local * 2 + side, block * TILE : (block + 1) * TILE, :] = left[
                    :, block * LANES : (block + 1) * LANES
                ]
        return carry

    lax.fori_loop(0, 4, tile_step, 0)
    table_ref[...] = table[pl.ds(pl.multiple_of(turn * 8 * LANES, 8 * LANES), 8 * LANES), :]


def tile_sums(left_ref, place, far, sums):
    others = far[...].astype(BF16)
    yield
    grams = nt_dot(left_ref[place], others)
    yield
    chunk = 32
    high, low = [], []
    for start in range(0, TILE, chunk):
        window = grams[start : start + chunk]
        inside = jnp.maximum(window, 0.0)
        root = lax.rsqrt((1.0 + SOFT_CORE) - window)
        depth = grams[TILE + start : TILE + start + chunk]
        charge = grams[2 * TILE + start : 2 * TILE + start + chunk]
        parts = two_pieces(inside * inside * (depth + charge * (root * root * root)))
        high.append(parts[0])
        low.append(parts[1])
        yield
    both = jnp.dot(jnp.concatenate(high + low, axis=0), others, preferred_element_type=F32)
    yield
    sums[...] = both[0:TILE] + both[TILE:]


def weave(stages, copies, parts):
    size = -(-len(copies) // parts)
    for turn, _ in enumerate(stages):
        for copy in copies[turn * size : (turn + 1) * size]:
            copy()
    for copy in copies[parts * size :]:
        copy()


def force_kernel(
    rows, partner_ref, entry_ref, order_ref, lower_ref, upper_ref, place_ref, eye_ref, left_ref, own_ref,
    out_ref, solute_ref, table, forces, planes, far_a, far_b, sum_a, sum_b, arrival,
):
    turn = pl.program_id(0)
    partners = far_a.shape[0]
    own = rows * LANES

    def load(tile, far):
        def copy(k):
            far[k : k + 1, :] = table[pl.ds(entry_ref[partner_ref[tile * partners + k]], 1), :]

        return [functools.partial(copy, k) for k in range(partners)]

    def save(tile, sums):
        def copy(k):
            forces[pl.ds(order_ref[tile * TILE + k], 1), :] = sums[k : k + 1, :]

        return [functools.partial(copy, k) for k in range(TILE)]

    @pl.when(turn == 0)
    def _():
        own_copy = pltpu.make_async_copy(own_ref, table.at[pl.ds(own, own), :], arrival)
        own_copy.start()
        planes[...] = jnp.zeros_like(planes)

        def fill(group, carry):
            spot = pl.ds(pl.multiple_of(group * 8, 8), 8)
            for ref, first, shift in ((lower_ref, 0, -SLAB_WIDTH), (upper_ref, 2 * own, SLAB_WIDTH)):
                fields = [ref[field, spot, :] for field in range(FIELDS)]
                fields[0] = fields[0] + shift
                fill_blocks(fields, eye_ref[...], planes, table, first + group * 8 * LANES)
            return carry

        lax.fori_loop(0, rows // 8, fill, 0)
        own_copy.wait()
        sum_b[...] = jnp.zeros_like(sum_b)
        for copy in load(0, far_a):
            copy()

    def step(pair, carry):
        tile = turn * 8 + pair * 2
        copies = save(jnp.maximum(tile - 1, 0), sum_b) + load(tile + 1, far_b)
        weave(tile_sums(left_ref, pair * 2, far_a, sum_a), copies, 7)
        copies = save(tile, sum_a) + load(jnp.minimum(tile + 2, rows - 1), far_a)
        weave(tile_sums(left_ref, pair * 2 + 1, far_b, sum_b), copies, 7)
        return carry

    lax.fori_loop(0, 4, step, 0)

    @pl.when(turn == pl.num_programs(0) - 1)
    def _():
        for copy in save(rows - 1, sum_b):
            copy()

        def finish(group, carry):
            for local in range(4):
                row = group * 4 + local
                turned_sums = forces[pl.ds(pl.multiple_of(row * LANES, LANES), LANES), :].T
                for axis in range(3):
                    first = 6 * axis
                    moment = (
                        turned_sums[first : first + 1]
                        + turned_sums[first + 1 : first + 2]
                        + turned_sums[first + 3 : first + 4]
                    )
                    place = place_ref[axis, pl.ds(row, 1), :]
                    force = (place - CENTRE) * turned_sums[ONES : ONES + 1] - moment
                    out_ref[axis, pl.ds(row, 1), :] = place + STEP_SIZE * force
            return carry

        lax.fori_loop(0, rows // 4, finish, 0)
        solute_ref[...] = out_ref[:, 0 : SOL_DEV // LANES, :]


def whole(*shape, dtype=F32):
    return jax.ShapeDtypeStruct(shape, dtype)


def turned(array, axis, by):
    count = lax.axis_size(axis)
    return lax.ppermute(array, axis, [(i, (i + by) % count) for i in range(count)])


def summed(array, axis):
    return sum((turned(array, axis, by) for by in range(1, lax.axis_size(axis))), array)


def round_trip(array, axis):
    count, index = lax.axis_size(axis), lax.axis_index(axis)
    result = jnp.zeros((count,) + array.shape, array.dtype)
    for by in range(count):
        piece = turned(array, axis, by) if by else array
        result = lax.dynamic_update_index_in_dim(result, piece, (index + count - by) % count, 0)
    return result


def inner(left, right):
    return jnp.sum(left * right, axis=(1, 2))


def per_device(positions, strength, charge, rest_scale, cell_order, ghost_index, tile_atoms):
    atoms = positions.shape[2]
    rows = atoms // LANES
    half = atoms // 2
    partners = tile_atoms.shape[2]
    paths = round_trip(positions[0, :, :SOL_DEV], "image")

    factor = jnp.where(jnp.arange(atoms) < SOL_DEV, jnp.sqrt(rest_scale[0]), 1.0)
    scaled = jnp.stack([strength * factor, charge * factor])
    fields = jnp.concatenate([positions[0], scaled]).reshape(FIELDS, rows, LANES)
    lower, upper = turned(fields, "space", 1), turned(fields, "space", -1)
    shell = ghost_index.reshape(atoms)
    entries = jnp.concatenate(
        [
            turned(shell[half:], "space", 1),
            jnp.arange(atoms, 2 * atoms, dtype=I32),
            turned(shell[:half], "space", -1) + 2 * atoms,
        ]
    )
    order = cell_order.reshape(atoms)
    eye = jnp.eye(LANES, dtype=BF16)
    scalar = pl.BlockSpec(memory_space=pltpu.SMEM)
    vector = pl.BlockSpec(memory_space=pltpu.VMEM)
    params = pltpu.CompilerParams(vmem_limit_bytes=VMEM_LIMIT)
    table, left = pl.pallas_call(
        functools.partial(near_kernel, rows),
        grid=(rows // 8,),
        out_shape=[whole(atoms, LANES), whole(rows, 3 * TILE, LANES, dtype=BF16)],
        in_specs=[scalar] + [vector] * 3,
        out_specs=[
            pl.BlockSpec((8 * LANES, LANES), lambda i: (i, 0)),
            pl.BlockSpec((8, 3 * TILE, LANES), lambda i: (i, 0, 0)),
        ],
        scratch_shapes=[
            pltpu.VMEM((atoms, LANES), F32),
            pltpu.VMEM((8 * STRIDE, LANES), F32),
            pltpu.VMEM((2, TILE, LANES), F32),
        ],
        compiler_params=params,
        cost_estimate=pl.CostEstimate(flops=25 * 10**9, bytes_accessed=3 * 10**7, transcendentals=0),
    )(order, fields, near_selector(), eye)
    out, solute = pl.pallas_call(
        functools.partial(force_kernel, rows),
        grid=(rows // 8,),
        out_shape=[whole(3, rows, LANES), whole(3, SOL_DEV // LANES, LANES)],
        in_specs=[scalar] * 3
        + [vector] * 4
        + [pl.BlockSpec((8, 3 * TILE, LANES), lambda i: (i, 0, 0)), pl.BlockSpec(memory_space=pl.ANY)],
        out_specs=[vector] * 2,
        scratch_shapes=[
            pltpu.VMEM((3 * atoms, LANES), F32),
            pltpu.VMEM((atoms, LANES), F32),
            pltpu.VMEM((8 * STRIDE, LANES), F32),
            pltpu.VMEM((partners, LANES), F32),
            pltpu.VMEM((partners, LANES), F32),
            pltpu.VMEM((TILE, LANES), F32),
            pltpu.VMEM((TILE, LANES), F32),
            pltpu.SemaphoreType.DMA,
        ],
        compiler_params=params,
        cost_estimate=pl.CostEstimate(flops=25 * 10**9, bytes_accessed=3 * 10**7, transcendentals=0),
    )(tile_atoms.reshape(rows * partners), entries, order, lower, upper, fields, eye, left, table)
    out = out.reshape(1, 3, atoms)
    solute = solute.reshape(1, 3, SOL_DEV)

    pushed = round_trip(solute[0], "image")
    images = lax.axis_size("image")
    index = lax.axis_index("image")
    steps = paths[1:] - paths[:-1]
    upper_path = jnp.concatenate([paths[1:], paths[-1:]])
    lower_path = jnp.concatenate([paths[:1], paths[:-1]])
    tangents = upper_path - lower_path
    gaps = pushed[1:] - pushed[:-1]
    none = jnp.zeros((1,), F32)
    sums = summed(
        jnp.stack(
            [
                inner(tangents, tangents),
                inner(pushed - paths, tangents),
                jnp.concatenate([inner(steps, steps), none]),
                jnp.concatenate([inner(gaps, gaps), none]),
                jnp.concatenate([inner(gaps, tangents[1:]), none]),
                jnp.concatenate([inner(gaps, tangents[:-1]), none]),
                jnp.concatenate([inner(tangents[1:], tangents[:-1]), none]),
            ]
        ),
        "space",
    )
    tangent_sq, along = sums[0], sums[1]
    step_sq, gap_sq, gap_next, gap_this, cross = (sums[i, :-1] for i in range(2, 7))
    step_root = jnp.sqrt(step_sq + EPSILON)
    spring = SPRING_COEF * (step_root[1:] - step_root[:-1]) / jnp.sqrt(tangent_sq[1:-1] + EPSILON)
    spring = jnp.concatenate([none, spring, none])
    shift = STEP_SIZE * spring - along / (tangent_sq + EPSILON)
    ahead_shift, here_shift = shift[1:], shift[:-1]
    length_sq = (
        gap_sq
        + ahead_shift * ahead_shift * tangent_sq[1:]
        + here_shift * here_shift * tangent_sq[:-1]
        + 2.0 * (ahead_shift * gap_next - here_shift * gap_this - ahead_shift * here_shift * cross)
    )
    lengths = jnp.sqrt(jnp.maximum(length_sq, 0.0) + EPSILON)
    knots = jnp.concatenate([none, jnp.cumsum(lengths)])
    targets = knots[-1] * (jnp.arange(images, dtype=F32) / (images - 1))
    back = jnp.concatenate([none, jnp.clip((knots - targets)[1:] / lengths, 0.0, 1.0)])
    ahead = jnp.concatenate([jnp.clip((targets - knots)[:-1] / lengths, 0.0, 1.0), none])
    moved = pushed + shift[:, None, None] * tangents

    def at(array, place):
        return lax.dynamic_index_in_dim(array, jnp.clip(place, 0, images - 1), 0, keepdims=False)

    here = at(moved, index)
    blended = (
        here
        + at(back, index) * (at(moved, index - 1) - here)
        + at(ahead, index) * (at(moved, index + 1) - here)
    )
    return lax.dynamic_update_slice(out, blended[None], (0, 0, 0))


def solution(mesh):
    placed = (
        P("image", None, "space"),
        P("space"),
        P("space"),
        P("image"),
        P("image", "space", None),
        P("image", "space", None),
        P("image", "space", None),
    )
    return jax.shard_map(
        per_device, mesh=mesh, in_specs=placed, out_specs=P("image", None, "space"), check_vma=False
    )
```

```python
import functools

import jax
import jax.numpy as jnp
import numpy as np
from jax import lax
from jax.experimental import pallas as pl
from jax.experimental.pallas import tpu as pltpu
from jax.sharding import PartitionSpec as P

SOL_DEV = 1024
TILE = 128
LANES = 128
FIELDS = 5
STRIDE = 48
PAD = 8

LJ_COEF = 0.5
CHARGE_COEF = 0.1
SOFT_CORE = 0.09
SLAB_WIDTH = 1.0
STEP_SIZE = 0.2
SPRING_COEF = 1.0
EPSILON = 1e-06
CENTRE = 0.5

F32 = jnp.float32
BF16 = jnp.bfloat16
I32 = jnp.int32
VMEM_LIMIT = 58 * 1024 * 1024

ONES = 18
NORM = 21
DEPTH = 24
CHARGE = 28
LAST = 32


def near_selector():
    chosen = np.zeros((LANES, 3 * LANES), np.float32)
    for axis in range(3):
        high, middle, low = 6 * axis, 6 * axis + 1, 6 * axis + 3
        for k, source in enumerate((high, high, middle, high, low, middle)):
            chosen[source, 6 * axis + k] = 2.0
    for k in range(3):
        chosen[NORM + k, ONES + k] = 1.0
        chosen[ONES, NORM + k] = 1.0
    chosen[ONES, LAST] = 1.0
    for block, first in ((1, DEPTH), (2, CHARGE)):
        for k, source in enumerate((first, first, first + 1, first + 1)):
            chosen[source, block * LANES + first + k] = 1.0
    return jnp.asarray(chosen, BF16)


def pieces(value, count):
    result = []
    for _ in range(count - 1):
        part = value.astype(BF16).astype(F32)
        result.append(part)
        value = value - part
    return result + [value]


def features(fields):
    rows = []
    for axis in range(3):
        high, middle, low = pieces(fields[axis], 3)
        rows += [high, middle, high, low, high, middle]
    one = jnp.ones_like(fields[0])
    rows += [one] * 3
    rows += pieces(-(fields[0] * fields[0] + fields[1] * fields[1] + fields[2] * fields[2]), 3)
    for value in fields[3:]:
        high, low = pieces(value, 2)
        rows += [high, low, high, low]
    return rows + [one]


def two_pieces(values):
    high = values.astype(BF16)
    low = (values - high.astype(F32)).astype(BF16)
    return high, low


def nt_dot(left, right):
    return lax.dot_general(left, right, (((1,), (1,)), ((), ())), preferred_element_type=F32)


def fill_blocks(fields, eye, planes, table, first):
    fields = [field - CENTRE for field in fields[:3]] + fields[3:]
    fields[3] = fields[3] * LJ_COEF**0.5
    fields[4] = fields[4] * CHARGE_COEF**0.5
    for k, row in enumerate(features(fields)):
        planes[pl.ds(k, 8, stride=STRIDE), :] = row
    blank = jnp.zeros((LANES - STRIDE, LANES), BF16)
    for block in range(0, 8, 2):
        parts = []
        for side in range(2):
            start = (block + side) * STRIDE
            parts += [planes[start : start + STRIDE, :].astype(BF16), blank]
        both = nt_dot(eye, jnp.concatenate(parts, axis=0))
        for side in range(2):
            start = pl.multiple_of(first + (block + side) * LANES + PAD, PAD)
            table[pl.ds(start, LANES), :] = both[:, side * LANES : (side + 1) * LANES]


def sublane_masks():
    sublane = lax.broadcasted_iota(I32, (8, LANES), 0)
    return [sublane == k for k in range(8)]


def merged(table, entries, masks):
    result = table[pl.ds(entries[0] + PAD, 8), :]
    for k in range(1, 8):
        result = jnp.where(masks[k], table[pl.ds(entries[k] + (PAD - k), 8), :], result)
    return result


def copy_rows(table, entry_of, stage, start, masks):
    parts = [merged(table, [entry_of(start + half + k) for k in range(8)], masks) for half in (0, 8)]
    stage[start : start + 16, :] = jnp.concatenate(parts, axis=0).astype(BF16)


def near_kernel(rows, order_ref, fields_ref, select_ref, eye_ref, table_ref, left_ref, table, planes, stage):
    turn = pl.program_id(0)

    @pl.when(turn == 0)
    def _():
        planes[...] = jnp.zeros_like(planes)

        def fill(group, carry):
            spot = pl.ds(pl.multiple_of(group * 8, 8), 8)
            fields = [fields_ref[field, spot, :] for field in range(FIELDS)]
            fill_blocks(fields, eye_ref[...], planes, table, group * 8 * LANES)
            return carry

        lax.fori_loop(0, rows // 8, fill, 0)

    masks = sublane_masks()

    def tile_step(local, carry):
        for side in range(2):
            tile = turn * 8 + local * 2 + side
            for start in range(0, TILE, 16):
                copy_rows(table, lambda k: order_ref[tile * TILE + k], stage.at[side], start, masks)
        for side in range(2):
            left = jnp.dot(stage[side], select_ref[...], preferred_element_type=F32).astype(BF16)
            for block in range(3):
                left_ref[local * 2 + side, block * TILE : (block + 1) * TILE, :] = left[
                    :, block * LANES : (block + 1) * LANES
                ]
        return carry

    lax.fori_loop(0, 4, tile_step, 0)
    table_ref[...] = table[pl.ds(pl.multiple_of(turn * 8 * LANES + PAD, PAD), 8 * LANES), :]


def tile_sums(left_ref, place, far, sums):
    others = far[...]
    yield
    grams = nt_dot(left_ref[place], others)
    yield
    chunk = 32
    high, low = [], []
    for start in range(0, TILE, chunk):
        window = grams[start : start + chunk]
        inside = jnp.maximum(window, 0.0)
        root = lax.rsqrt((1.0 + SOFT_CORE) - window)
        depth = grams[TILE + start : TILE + start + chunk]
        charge = grams[2 * TILE + start : 2 * TILE + start + chunk]
        parts = two_pieces(inside * inside * (depth + charge * (root * root * root)))
        high.append(parts[0])
        low.append(parts[1])
        yield
    both = jnp.dot(jnp.concatenate(high + low, axis=0), others, preferred_element_type=F32)
    yield
    sums[...] = both[0:TILE] + both[TILE:]


def weave(stages, copies, parts):
    size = -(-len(copies) // parts)
    for turn, _ in enumerate(stages):
        for copy in copies[turn * size : (turn + 1) * size]:
            copy()
    for copy in copies[parts * size :]:
        copy()


def force_kernel(
    rows, partner_ref, entry_ref, order_ref, lower_ref, upper_ref, place_ref, eye_ref, left_ref, own_ref,
    out_ref, solute_ref, table, forces, planes, far_a, far_b, sum_a, sum_b, arrival,
):
    turn = pl.program_id(0)
    partners = far_a.shape[0]
    own = rows * LANES

    masks = sublane_masks()

    def load(tile, far):
        def entry_of(k):
            return entry_ref[partner_ref[tile * partners + k]]

        return [
            functools.partial(copy_rows, table, entry_of, far, start, masks)
            for start in range(0, partners, 16)
        ]

    def save(tile, sums):
        def copy(block):
            value = sums[block * 8 : block * 8 + 8, :]
            for k in range(8):
                place = order_ref[tile * TILE + block * 8 + k] + (PAD - k)
                pltpu.store(forces.at[pl.ds(place, 8), :], value, mask=masks[k])

        return [functools.partial(copy, block) for block in range(TILE // 8)]

    @pl.when(turn == 0)
    def _():
        own_copy = pltpu.make_async_copy(own_ref, table.at[pl.ds(own + PAD, own), :], arrival)
        own_copy.start()
        planes[...] = jnp.zeros_like(planes)

        def fill(group, carry):
            for ref, first, shift in ((lower_ref, 0, -SLAB_WIDTH), (upper_ref, 2 * own, SLAB_WIDTH)):
                fields = [
                    ref[pl.ds(pl.multiple_of(field * rows + group * 8, 8), 8), :] for field in range(FIELDS)
                ]
                fields[0] = fields[0] + shift
                fill_blocks(fields, eye_ref[...], planes, table, first + group * 8 * LANES)
            return carry

        lax.fori_loop(0, rows // 8, fill, 0)
        own_copy.wait()
        sum_b[...] = jnp.zeros_like(sum_b)
        for copy in load(0, far_a):
            copy()

    def step(pair, carry):
        tile = turn * 8 + pair * 2
        copies = save(jnp.maximum(tile - 1, 0), sum_b) + load(tile + 1, far_b)
        weave(tile_sums(left_ref, pair * 2, far_a, sum_a), copies, 7)
        copies = save(tile, sum_a) + load(jnp.minimum(tile + 2, rows - 1), far_a)
        weave(tile_sums(left_ref, pair * 2 + 1, far_b, sum_b), copies, 7)
        return carry

    lax.fori_loop(0, 4, step, 0)

    @pl.when(turn == pl.num_programs(0) - 1)
    def _():
        for copy in save(rows - 1, sum_b):
            copy()

        def finish(group, carry):
            for local in range(4):
                row = group * 4 + local
                turned_sums = forces[pl.ds(pl.multiple_of(row * LANES + PAD, PAD), LANES), :].T
                for axis in range(3):
                    first = 6 * axis
                    moment = (
                        turned_sums[first : first + 1]
                        + turned_sums[first + 1 : first + 2]
                        + turned_sums[first + 3 : first + 4]
                    )
                    place = place_ref[axis, pl.ds(row, 1), :]
                    force = (place - CENTRE) * turned_sums[ONES : ONES + 1] - moment
                    out_ref[axis, pl.ds(row, 1), :] = place + STEP_SIZE * force
            return carry

        lax.fori_loop(0, rows // 4, finish, 0)
        solute_ref[...] = out_ref[:, 0 : SOL_DEV // LANES, :]


def whole(*shape, dtype=F32):
    return jax.ShapeDtypeStruct(shape, dtype)


def turned(array, axis, by):
    count = lax.axis_size(axis)
    return lax.ppermute(array, axis, [(i, (i + by) % count) for i in range(count)])


def summed(array, axis):
    return sum((turned(array, axis, by) for by in range(1, lax.axis_size(axis))), array)


def round_trip(array, axis):
    count, index = lax.axis_size(axis), lax.axis_index(axis)
    result = jnp.zeros((count,) + array.shape, array.dtype)
    for by in range(count):
        piece = turned(array, axis, by) if by else array
        result = lax.dynamic_update_index_in_dim(result, piece, (index + count - by) % count, 0)
    return result


def inner(left, right):
    return jnp.sum(left * right, axis=(1, 2))


def per_device(positions, strength, charge, rest_scale, cell_order, ghost_index, tile_atoms):
    atoms = positions.shape[2]
    rows = atoms // LANES
    half = atoms // 2
    partners = tile_atoms.shape[2]
    paths = round_trip(positions[0, :, :SOL_DEV], "image")

    factor = jnp.where(jnp.arange(atoms) < SOL_DEV, jnp.sqrt(rest_scale[0]), 1.0)
    scaled = jnp.stack([strength * factor, charge * factor])
    fields = jnp.concatenate([positions[0], scaled]).reshape(FIELDS, rows, LANES)
    shell = ghost_index.reshape(2, rows // 2, LANES).astype(F32)
    planes = fields.reshape(FIELDS * rows, LANES)
    lower = turned(jnp.concatenate([planes, shell[1]]), "space", 1)
    upper = turned(jnp.concatenate([planes, shell[0]]), "space", -1)
    entries = jnp.concatenate(
        [
            lower[FIELDS * rows :].astype(I32).reshape(half),
            jnp.arange(atoms, 2 * atoms, dtype=I32),
            upper[FIELDS * rows :].astype(I32).reshape(half) + 2 * atoms,
        ]
    )
    order = cell_order.reshape(atoms)
    eye = jnp.eye(LANES, dtype=BF16)
    scalar = pl.BlockSpec(memory_space=pltpu.SMEM)
    vector = pl.BlockSpec(memory_space=pltpu.VMEM)
    params = pltpu.CompilerParams(vmem_limit_bytes=VMEM_LIMIT)
    table, left = pl.pallas_call(
        functools.partial(near_kernel, rows),
        grid=(rows // 8,),
        out_shape=[whole(atoms, LANES), whole(rows, 3 * TILE, LANES, dtype=BF16)],
        in_specs=[scalar] + [vector] * 3,
        out_specs=[
            pl.BlockSpec((8 * LANES, LANES), lambda i: (i, 0)),
            pl.BlockSpec((8, 3 * TILE, LANES), lambda i: (i, 0, 0)),
        ],
        scratch_shapes=[
            pltpu.VMEM((atoms + 2 * PAD, LANES), F32),
            pltpu.VMEM((8 * STRIDE, LANES), F32),
            pltpu.VMEM((2, TILE, LANES), BF16),
        ],
        compiler_params=params,
        cost_estimate=pl.CostEstimate(flops=25 * 10**9, bytes_accessed=3 * 10**7, transcendentals=0),
    )(order, fields, near_selector(), eye)
    out, solute = pl.pallas_call(
        functools.partial(force_kernel, rows),
        grid=(rows // 8,),
        out_shape=[whole(3, rows, LANES), whole(3, SOL_DEV // LANES, LANES)],
        in_specs=[scalar] * 3
        + [vector] * 4
        + [pl.BlockSpec((8, 3 * TILE, LANES), lambda i: (i, 0, 0)), pl.BlockSpec(memory_space=pl.ANY)],
        out_specs=[vector] * 2,
        scratch_shapes=[
            pltpu.VMEM((3 * atoms + 2 * PAD, LANES), F32),
            pltpu.VMEM((atoms + 2 * PAD, LANES), F32),
            pltpu.VMEM((8 * STRIDE, LANES), F32),
            pltpu.VMEM((partners, LANES), BF16),
            pltpu.VMEM((partners, LANES), BF16),
            pltpu.VMEM((TILE, LANES), F32),
            pltpu.VMEM((TILE, LANES), F32),
            pltpu.SemaphoreType.DMA,
        ],
        compiler_params=params,
        cost_estimate=pl.CostEstimate(flops=25 * 10**9, bytes_accessed=3 * 10**7, transcendentals=0),
    )(tile_atoms.reshape(rows * partners), entries, order, lower, upper, fields, eye, left, table)
    out = out.reshape(1, 3, atoms)
    solute = solute.reshape(1, 3, SOL_DEV)

    pushed = round_trip(solute[0], "image")
    images = lax.axis_size("image")
    index = lax.axis_index("image")
    steps = paths[1:] - paths[:-1]
    upper_path = jnp.concatenate([paths[1:], paths[-1:]])
    lower_path = jnp.concatenate([paths[:1], paths[:-1]])
    tangents = upper_path - lower_path
    gaps = pushed[1:] - pushed[:-1]
    none = jnp.zeros((1,), F32)
    sums = summed(
        jnp.stack(
            [
                inner(tangents, tangents),
                inner(pushed - paths, tangents),
                jnp.concatenate([inner(steps, steps), none]),
                jnp.concatenate([inner(gaps, gaps), none]),
                jnp.concatenate([inner(gaps, tangents[1:]), none]),
                jnp.concatenate([inner(gaps, tangents[:-1]), none]),
                jnp.concatenate([inner(tangents[1:], tangents[:-1]), none]),
            ]
        ),
        "space",
    )
    tangent_sq, along = sums[0], sums[1]
    step_sq, gap_sq, gap_next, gap_this, cross = (sums[i, :-1] for i in range(2, 7))
    step_root = jnp.sqrt(step_sq + EPSILON)
    spring = SPRING_COEF * (step_root[1:] - step_root[:-1]) / jnp.sqrt(tangent_sq[1:-1] + EPSILON)
    spring = jnp.concatenate([none, spring, none])
    shift = STEP_SIZE * spring - along / (tangent_sq + EPSILON)
    ahead_shift, here_shift = shift[1:], shift[:-1]
    length_sq = (
        gap_sq
        + ahead_shift * ahead_shift * tangent_sq[1:]
        + here_shift * here_shift * tangent_sq[:-1]
        + 2.0 * (ahead_shift * gap_next - here_shift * gap_this - ahead_shift * here_shift * cross)
    )
    lengths = jnp.sqrt(jnp.maximum(length_sq, 0.0) + EPSILON)
    knots = jnp.concatenate([none, jnp.cumsum(lengths)])
    targets = knots[-1] * (jnp.arange(images, dtype=F32) / (images - 1))
    back = jnp.concatenate([none, jnp.clip((knots - targets)[1:] / lengths, 0.0, 1.0)])
    ahead = jnp.concatenate([jnp.clip((targets - knots)[:-1] / lengths, 0.0, 1.0), none])
    moved = pushed + shift[:, None, None] * tangents

    def at(array, place):
        return lax.dynamic_index_in_dim(array, jnp.clip(place, 0, images - 1), 0, keepdims=False)

    here = at(moved, index)
    blended = (
        here
        + at(back, index) * (at(moved, index - 1) - here)
        + at(ahead, index) * (at(moved, index + 1) - here)
    )
    return lax.dynamic_update_slice(out, blended[None], (0, 0, 0))


def solution(mesh):
    placed = (
        P("image", None, "space"),
        P("space"),
        P("space"),
        P("image"),
        P("image", "space", None),
        P("image", "space", None),
        P("image", "space", None),
    )
    return jax.shard_map(
        per_device, mesh=mesh, in_specs=placed, out_specs=P("image", None, "space"), check_vma=False
    )
```

```python
import functools

import jax
import jax.numpy as jnp
import numpy as np
from jax import lax
from jax.experimental import pallas as pl
from jax.experimental.pallas import tpu as pltpu
from jax.sharding import PartitionSpec as P

SOL_DEV = 1024
TILE = 128
LANES = 128
FIELDS = 5
STRIDE = 48
FORCE_PAD = 1024
PAD = 8

LJ_COEF = 0.5
CHARGE_COEF = 0.1
SOFT_CORE = 0.09
SLAB_WIDTH = 1.0
STEP_SIZE = 0.2
SPRING_COEF = 1.0
EPSILON = 1e-06
CENTRE = 0.5

F32 = jnp.float32
BF16 = jnp.bfloat16
I32 = jnp.int32
VMEM_LIMIT = 58 * 1024 * 1024

ONES = 18
NORM = 21
DEPTH = 24
CHARGE = 28
LAST = 32


def near_selector():
    chosen = np.zeros((LANES, 3 * LANES), np.float32)
    for axis in range(3):
        high, middle, low = 6 * axis, 6 * axis + 1, 6 * axis + 3
        for k, source in enumerate((high, high, middle, high, low, middle)):
            chosen[source, 6 * axis + k] = 2.0
    for k in range(3):
        chosen[NORM + k, ONES + k] = 1.0
        chosen[ONES, NORM + k] = 1.0
    chosen[ONES, LAST] = 1.0
    for block, first in ((1, DEPTH), (2, CHARGE)):
        for k, source in enumerate((first, first, first + 1, first + 1)):
            chosen[source, block * LANES + first + k] = 1.0
    return jnp.asarray(chosen, BF16)


def pieces(value, count):
    result = []
    for _ in range(count - 1):
        part = value.astype(BF16).astype(F32)
        result.append(part)
        value = value - part
    return result + [value]


def features(fields):
    rows = []
    for axis in range(3):
        high, middle, low = pieces(fields[axis], 3)
        rows += [high, middle, high, low, high, middle]
    one = jnp.ones_like(fields[0])
    rows += [one] * 3
    rows += pieces(-(fields[0] * fields[0] + fields[1] * fields[1] + fields[2] * fields[2]), 3)
    for value in fields[3:]:
        high, low = pieces(value, 2)
        rows += [high, low, high, low]
    return rows + [one]


def two_pieces(values):
    high = values.astype(BF16)
    low = (values - high.astype(F32)).astype(BF16)
    return high, low


def nt_dot(left, right):
    return lax.dot_general(left, right, (((1,), (1,)), ((), ())), preferred_element_type=F32)


def fill_blocks(fields, eye, planes, table, first):
    fields = [field - CENTRE for field in fields[:3]] + fields[3:]
    fields[3] = fields[3] * LJ_COEF**0.5
    fields[4] = fields[4] * CHARGE_COEF**0.5
    for k, row in enumerate(features(fields)):
        planes[pl.ds(k, 8, stride=STRIDE), :] = row
    blank = jnp.zeros((LANES - STRIDE, LANES), BF16)
    for block in range(0, 8, 2):
        parts = []
        for side in range(2):
            start = (block + side) * STRIDE
            parts += [planes[start : start + STRIDE, :].astype(BF16), blank]
        both = nt_dot(eye, jnp.concatenate(parts, axis=0))
        for side in range(2):
            start = pl.multiple_of(first + (block + side) * LANES + PAD, PAD)
            table[pl.ds(start, LANES), :] = both[:, side * LANES : (side + 1) * LANES]


def sublane_masks():
    sublane = lax.broadcasted_iota(I32, (8, LANES), 0)
    return [sublane == k for k in range(8)]


def merged(table, entries, masks):
    result = table[pl.ds(entries[0] + PAD, 8), :]
    for k in range(1, 8):
        result = jnp.where(masks[k], table[pl.ds(entries[k] + (PAD - k), 8), :], result)
    return result


def copy_rows(table, entry_of, stage, start, masks):
    parts = [merged(table, [entry_of(start + half + k) for k in range(8)], masks) for half in (0, 8)]
    stage[start : start + 16, :] = jnp.concatenate(parts, axis=0).astype(BF16)


def near_kernel(rows, order_ref, fields_ref, select_ref, eye_ref, table_ref, left_ref, table, planes, stage):
    turn = pl.program_id(0)

    @pl.when(turn == 0)
    def _():
        planes[...] = jnp.zeros_like(planes)

        def fill(turn, carry):
            for side in range(2):
                group = turn * 2 + side
                spot = pl.ds(pl.multiple_of(group * 8, 8), 8)
                fields = [fields_ref[field, spot, :] for field in range(FIELDS)]
                fill_blocks(fields, eye_ref[...], planes.at[side], table, group * 8 * LANES)
            return carry

        lax.fori_loop(0, rows // 16, fill, 0)

    masks = sublane_masks()

    def tile_step(local, carry):
        for side in range(2):
            tile = turn * 8 + local * 2 + side
            for start in range(0, TILE, 16):
                copy_rows(table, lambda k: order_ref[tile * TILE + k], stage.at[side], start, masks)
        for side in range(2):
            left = jnp.dot(stage[side], select_ref[...], preferred_element_type=F32).astype(BF16)
            for block in range(3):
                left_ref[local * 2 + side, block * TILE : (block + 1) * TILE, :] = left[
                    :, block * LANES : (block + 1) * LANES
                ]
        return carry

    lax.fori_loop(0, 4, tile_step, 0)
    table_ref[...] = table[pl.ds(pl.multiple_of(turn * 8 * LANES + PAD, PAD), 8 * LANES), :]


def tile_sums(left_ref, place, far, sums):
    others = far[...]
    yield
    grams = nt_dot(left_ref[place], others)
    yield
    chunk = 32
    high, low = [], []
    for start in range(0, TILE, chunk):
        window = grams[start : start + chunk]
        inside = jnp.maximum(window, 0.0)
        root = lax.rsqrt((1.0 + SOFT_CORE) - window)
        depth = grams[TILE + start : TILE + start + chunk]
        charge = grams[2 * TILE + start : 2 * TILE + start + chunk]
        parts = two_pieces(inside * inside * (depth + charge * (root * root * root)))
        high.append(parts[0])
        low.append(parts[1])
        yield
    both = jnp.dot(jnp.concatenate(high + low, axis=0), others, preferred_element_type=F32)
    yield
    sums[...] = both[0:TILE] + both[TILE:]


def weave(stages, copies, parts):
    size = -(-len(copies) // parts)
    for turn, _ in enumerate(stages):
        for copy in copies[turn * size : (turn + 1) * size]:
            copy()
    for copy in copies[parts * size :]:
        copy()


def force_kernel(
    rows, partner_ref, entry_ref, order_ref, lower_ref, upper_ref, place_ref, eye_ref, left_ref, own_ref,
    force_ref, solute_ref, table, forces, planes, far_a, far_b, sum_a, sum_b, arrival,
):
    turn = pl.program_id(0)
    partners = far_a.shape[0]
    own = rows * LANES

    masks = sublane_masks()

    def load(tile, far):
        def entry_of(k):
            return entry_ref[partner_ref[tile * partners + k]]

        return [
            functools.partial(copy_rows, table, entry_of, far, start, masks)
            for start in range(0, partners, 16)
        ]

    def save(tile, sums):
        def copy(block):
            value = sums[block * 8 : block * 8 + 8, :]
            for k in range(8):
                place = order_ref[tile * TILE + block * 8 + k] + (FORCE_PAD - k)
                pltpu.store(forces.at[pl.ds(place, 8), :], value, mask=masks[k])

        return [functools.partial(copy, block) for block in range(TILE // 8)]

    @pl.when(turn == 0)
    def _():
        own_copy = pltpu.make_async_copy(own_ref, table.at[pl.ds(own + PAD, own), :], arrival)
        own_copy.start()
        planes[...] = jnp.zeros_like(planes)

        def fill(group, carry):
            for side, ref, first, shift in ((0, lower_ref, 0, -SLAB_WIDTH), (1, upper_ref, 2 * own, SLAB_WIDTH)):
                fields = [
                    ref[pl.ds(pl.multiple_of(field * rows + group * 8, 8), 8), :] for field in range(FIELDS)
                ]
                fields[0] = fields[0] + shift
                fill_blocks(fields, eye_ref[...], planes.at[side], table, first + group * 8 * LANES)
            return carry

        lax.fori_loop(0, rows // 8, fill, 0)
        own_copy.wait()
        sum_b[...] = jnp.zeros_like(sum_b)
        for copy in load(0, far_a):
            copy()

    def step(pair, carry):
        tile = turn * 8 + pair * 2
        copies = save(jnp.maximum(tile - 1, 0), sum_b) + load(tile + 1, far_b)
        weave(tile_sums(left_ref, pair * 2, far_a, sum_a), copies, 7)
        copies = save(tile, sum_a) + load(jnp.minimum(tile + 2, rows - 1), far_a)
        weave(tile_sums(left_ref, pair * 2 + 1, far_b, sum_b), copies, 7)
        return carry

    lax.fori_loop(0, 4, step, 0)

    @pl.when(turn == pl.num_programs(0) - 1)
    def _():
        for copy in save(rows - 1, sum_b):
            copy()

        send = pltpu.make_async_copy(forces, force_ref, arrival)
        send.start()
        for row in range(SOL_DEV // LANES):
            start = FORCE_PAD + row * LANES
            force = row_forces(forces[start : start + LANES, :], [place_ref[axis, row : row + 1, :] for axis in range(3)])
            for axis in range(3):
                solute_ref[axis, row : row + 1, :] = place_ref[axis, row : row + 1, :] + STEP_SIZE * force[axis]
        send.wait()


def row_forces(sums, places):
    across = sums.T
    result = []
    for axis, place in enumerate(places):
        first = 6 * axis
        moment = across[first : first + 1] + across[first + 1 : first + 2] + across[first + 3 : first + 4]
        result.append((place - CENTRE) * across[ONES : ONES + 1] - moment)
    return result


def relax_kernel(place_ref, force_ref, out_ref):
    for row in range(8):
        places = [place_ref[axis, row : row + 1, :] for axis in range(3)]
        for axis, force in enumerate(row_forces(force_ref[row * LANES : (row + 1) * LANES, :], places)):
            out_ref[axis, row : row + 1, :] = places[axis] + STEP_SIZE * force


def product_kernel(images, index_ref, *refs):
    pushed_refs, path_refs = refs[:images], refs[images : 2 * images]
    sums_ref, pushed, path = refs[2 * images :]
    index = index_ref[0]
    for by in range(images):
        place = lax.rem(index + images - by, images)
        pushed[place] = pushed_refs[by][...]
        path[place] = path_refs[by][...]
    sums_ref[...] = jnp.zeros_like(sums_ref)
    last = images - 1
    tangents = [path[min(k + 1, last)] - path[max(k - 1, 0)] for k in range(images)]

    def put(kind, image, left, right):
        total = jnp.sum(left * right, axis=0)
        sums_ref[kind * images + image : kind * images + image + 1, :] = jnp.sum(total, axis=0, keepdims=True)

    for k in range(images):
        put(0, k, tangents[k], tangents[k])
        put(1, k, pushed[k] - path[k], tangents[k])
        if k < last:
            step = path[k + 1] - path[k]
            gap = pushed[k + 1] - pushed[k]
            put(2, k, step, step)
            put(3, k, gap, gap)
            put(4, k, gap, tangents[k + 1])
            put(5, k, gap, tangents[k])
            put(6, k, tangents[k + 1], tangents[k])


def blend_kernel(images, index_ref, sums_ref, pushed, path, out_in, out_ref):
    del out_in
    index = index_ref[0]
    last = images - 1
    totals = jnp.sum(sums_ref[...], axis=1, keepdims=True)

    def total(kind, image):
        row = kind * images + image
        return totals[row : row + 1, :]

    step_root = [jnp.sqrt(total(2, k) + EPSILON) for k in range(last)]
    shift = []
    for k in range(images):
        tangent_sq = total(0, k)
        value = -total(1, k) / (tangent_sq + EPSILON)
        if 0 < k < last:
            spring = SPRING_COEF * (step_root[k] - step_root[k - 1]) / jnp.sqrt(tangent_sq + EPSILON)
            value = value + STEP_SIZE * spring
        shift.append(value)
    lengths = []
    for k in range(last):
        there, here = shift[k + 1], shift[k]
        length_sq = (
            total(3, k)
            + there * there * total(0, k + 1)
            + here * here * total(0, k)
            + 2.0 * (there * total(4, k) - here * total(5, k) - there * here * total(6, k))
        )
        lengths.append(jnp.sqrt(jnp.maximum(length_sq, 0.0) + EPSILON))
    knots = [jnp.zeros_like(lengths[0])]
    for length in lengths:
        knots.append(knots[-1] + length)

    def pick(values):
        result = values[0]
        for k in range(1, images):
            result = jnp.where(index == k, values[k], result)
        return result

    none = jnp.zeros_like(lengths[0])
    excess = [knots[k] - knots[last] * (k / last) for k in range(images)]
    back = pick([none] + [jnp.clip(excess[k] / lengths[k - 1], 0.0, 1.0) for k in range(1, images)])
    ahead = pick([jnp.clip(-excess[k] / lengths[k], 0.0, 1.0) for k in range(last)] + [none])
    shifts = [pick([shift[min(max(k + by, 0), last)] for k in range(images)]) for by in (-1, 0, 1)]

    def moved(by):
        place = jnp.clip(index + by, 0, last)
        tangent = path[jnp.minimum(place + 1, last)] - path[jnp.maximum(place - 1, 0)]
        return pushed[place] + shifts[by + 1] * tangent

    here = moved(0)
    blended = here + back * (moved(-1) - here) + ahead * (moved(1) - here)
    out_ref[...] = blended


def whole(*shape, dtype=F32):
    return jax.ShapeDtypeStruct(shape, dtype)


def turned(array, axis, by):
    count = lax.axis_size(axis)
    return lax.ppermute(array, axis, [(i, (i + by) % count) for i in range(count)])


def summed(array, axis):
    count = lax.axis_size(axis)
    if count & (count - 1):
        return lax.psum(array, axis)
    by = 1
    while by < count:
        array = array + lax.ppermute(array, axis, [(i, i ^ by) for i in range(count)])
        by *= 2
    return array


def round_trip(array, axis):
    return [array] + [turned(array, axis, by) for by in range(1, lax.axis_size(axis))]


def per_device(positions, strength, charge, rest_scale, cell_order, ghost_index, tile_atoms):
    atoms = positions.shape[2]
    rows = atoms // LANES
    half = atoms // 2
    partners = tile_atoms.shape[2]
    images = lax.axis_size("image")
    index = lax.axis_index("image").reshape(1)

    factor = jnp.where(jnp.arange(atoms) < SOL_DEV, jnp.sqrt(rest_scale[0]), 1.0)
    scaled = jnp.stack([strength * factor, charge * factor]).reshape(2, rows, LANES)
    places = positions.reshape(3, rows, LANES)
    fields = jnp.concatenate([places, scaled])
    paths = round_trip(places[:, : SOL_DEV // LANES], "image")
    shell = ghost_index.reshape(2, rows // 2, LANES).astype(F32)
    planes = fields.reshape(FIELDS * rows, LANES)
    lower = turned(jnp.concatenate([planes, shell[1]]), "space", 1)
    upper = turned(jnp.concatenate([planes, shell[0]]), "space", -1)
    entries = jnp.concatenate(
        [
            lower[FIELDS * rows :].astype(I32).reshape(half),
            jnp.arange(atoms, 2 * atoms, dtype=I32),
            upper[FIELDS * rows :].astype(I32).reshape(half) + 2 * atoms,
        ]
    )
    order = cell_order.reshape(atoms)
    eye = jnp.eye(LANES, dtype=BF16)
    scalar = pl.BlockSpec(memory_space=pltpu.SMEM)
    vector = pl.BlockSpec(memory_space=pltpu.VMEM)
    params = pltpu.CompilerParams(vmem_limit_bytes=VMEM_LIMIT)
    table, left = pl.pallas_call(
        functools.partial(near_kernel, rows),
        grid=(rows // 8,),
        out_shape=[whole(atoms, LANES), whole(rows, 3 * TILE, LANES, dtype=BF16)],
        in_specs=[scalar] + [vector] * 3,
        out_specs=[
            pl.BlockSpec((8 * LANES, LANES), lambda i: (i, 0)),
            pl.BlockSpec((8, 3 * TILE, LANES), lambda i: (i, 0, 0)),
        ],
        scratch_shapes=[
            pltpu.VMEM((atoms + 2 * PAD, LANES), F32),
            pltpu.VMEM((2, 8 * STRIDE, LANES), F32),
            pltpu.VMEM((2, TILE, LANES), BF16),
        ],
        compiler_params=params,
        cost_estimate=pl.CostEstimate(flops=25 * 10**9, bytes_accessed=3 * 10**7, transcendentals=0),
    )(order, fields, near_selector(), eye)
    forces, solute = pl.pallas_call(
        functools.partial(force_kernel, rows),
        grid=(rows // 8,),
        out_shape=[whole(atoms + 2 * FORCE_PAD, LANES), whole(3, SOL_DEV // LANES, LANES)],
        in_specs=[scalar] * 3
        + [vector] * 4
        + [pl.BlockSpec((8, 3 * TILE, LANES), lambda i: (i, 0, 0)), pl.BlockSpec(memory_space=pl.ANY)],
        out_specs=[pl.BlockSpec(memory_space=pl.ANY), vector],
        scratch_shapes=[
            pltpu.VMEM((3 * atoms + 2 * PAD, LANES), F32),
            pltpu.VMEM((atoms + 2 * FORCE_PAD, LANES), F32),
            pltpu.VMEM((2, 8 * STRIDE, LANES), F32),
            pltpu.VMEM((partners, LANES), BF16),
            pltpu.VMEM((partners, LANES), BF16),
            pltpu.VMEM((TILE, LANES), F32),
            pltpu.VMEM((TILE, LANES), F32),
            pltpu.SemaphoreType.DMA,
        ],
        compiler_params=params,
        cost_estimate=pl.CostEstimate(flops=25 * 10**9, bytes_accessed=3 * 10**7, transcendentals=0),
    )(tile_atoms.reshape(rows * partners), entries, order, lower, upper, places, eye, left, table)
    solutes = round_trip(solute, "image")
    block = pl.BlockSpec((3, 8, LANES), lambda i: (0, i, 0))
    small = pltpu.CompilerParams(vmem_limit_bytes=8 * 1024 * 1024)
    out = pl.pallas_call(
        relax_kernel,
        grid=(rows // 8,),
        out_shape=whole(3, rows, LANES),
        in_specs=[block, pl.BlockSpec((8 * LANES, LANES), lambda i: (i + FORCE_PAD // (8 * LANES), 0))],
        out_specs=block,
        compiler_params=small,
        cost_estimate=pl.CostEstimate(flops=10**9, bytes_accessed=2 * 10**7, transcendentals=0),
    )(places, forces)
    solute_shape = whole(images, 3, SOL_DEV // LANES, LANES)
    sums, pushed, path = pl.pallas_call(
        functools.partial(product_kernel, images),
        out_shape=[whole(-(-7 * images // 8) * 8, LANES), solute_shape, solute_shape],
        in_specs=[scalar] + [vector] * (2 * images),
        out_specs=[vector] * 3,
        compiler_params=small,
    )(index, *solutes, *paths)
    out = pl.pallas_call(
        functools.partial(blend_kernel, images),
        grid=(1,),
        out_shape=whole(3, rows, LANES),
        in_specs=[scalar] + [vector] * 3 + [pl.BlockSpec(memory_space=pl.ANY)],
        out_specs=pl.BlockSpec((3, SOL_DEV // LANES, LANES), lambda i: (0, 0, 0)),
        input_output_aliases={4: 0},
        compiler_params=small,
    )(index, summed(sums, "space"), pushed, path, out)
    return out.reshape(1, 3, atoms)


def solution(mesh):
    placed = (
        P("image", None, "space"),
        P("space"),
        P("space"),
        P("image"),
        P("image", "space", None),
        P("image", "space", None),
        P("image", "space", None),
    )
    return jax.shard_map(
        per_device, mesh=mesh, in_specs=placed, out_specs=P("image", None, "space"), check_vma=False
    )
```

```python
import functools

import jax
import jax.numpy as jnp
import numpy as np
from jax import lax
from jax.experimental import pallas as pl
from jax.experimental.pallas import tpu as pltpu
from jax.sharding import PartitionSpec as P

SOL_DEV = 1024
TILE = 128
LANES = 128
FIELDS = 5
STRIDE = 48
FORCE_PAD = 1024
PAD = 8

LJ_COEF = 0.5
CHARGE_COEF = 0.1
SOFT_CORE = 0.09
SLAB_WIDTH = 1.0
STEP_SIZE = 0.2
SPRING_COEF = 1.0
EPSILON = 1e-06
CENTRE = 0.5

F32 = jnp.float32
BF16 = jnp.bfloat16
I32 = jnp.int32
VMEM_LIMIT = 58 * 1024 * 1024

ONES = 18
NORM = 21
DEPTH = 24
CHARGE = 28
LAST = 32


def near_selector():
    chosen = np.zeros((LANES, 3 * LANES), np.float32)
    for axis in range(3):
        high, middle, low = 6 * axis, 6 * axis + 1, 6 * axis + 3
        for k, source in enumerate((high, high, middle, high, low, middle)):
            chosen[source, 6 * axis + k] = 2.0
    for k in range(3):
        chosen[NORM + k, ONES + k] = 1.0
        chosen[ONES, NORM + k] = 1.0
    chosen[ONES, LAST] = 1.0
    for block, first in ((1, DEPTH), (2, CHARGE)):
        for k, source in enumerate((first, first, first + 1, first + 1)):
            chosen[source, block * LANES + first + k] = 1.0
    return jnp.asarray(chosen, BF16)


def pieces(value, count):
    result = []
    for _ in range(count - 1):
        part = value.astype(BF16).astype(F32)
        result.append(part)
        value = value - part
    return result + [value]


def features(fields):
    rows = []
    for axis in range(3):
        high, middle, low = pieces(fields[axis], 3)
        rows += [high, middle, high, low, high, middle]
    one = jnp.ones_like(fields[0])
    rows += [one] * 3
    rows += pieces(-(fields[0] * fields[0] + fields[1] * fields[1] + fields[2] * fields[2]), 3)
    for value in fields[3:]:
        high, low = pieces(value, 2)
        rows += [high, low, high, low]
    return rows + [one]


def two_pieces(values):
    high = values.astype(BF16)
    low = (values - high.astype(F32)).astype(BF16)
    return high, low


def nt_dot(left, right):
    return lax.dot_general(left, right, (((1,), (1,)), ((), ())), preferred_element_type=F32)


def fill_blocks(fields, planes, table, first):
    fields = [field - CENTRE for field in fields[:3]] + fields[3:]
    fields[3] = fields[3] * LJ_COEF**0.5
    fields[4] = fields[4] * CHARGE_COEF**0.5
    for k, row in enumerate(features(fields)):
        planes[pl.ds(k, 8, stride=STRIDE), :] = row
    blank = jnp.zeros((LANES - STRIDE, LANES), F32)
    for block in range(8):
        part = jnp.concatenate([planes[block * STRIDE : (block + 1) * STRIDE, :], blank], axis=0)
        start = pl.multiple_of(first + block * LANES + PAD, PAD)
        table[pl.ds(start, LANES), :] = part.T


def sublane_masks():
    sublane = lax.broadcasted_iota(I32, (8, LANES), 0)
    return [sublane == k for k in range(8)]


def merged(table, entries, masks):
    result = table[pl.ds(entries[0] + PAD, 8), :]
    for k in range(1, 8):
        result = jnp.where(masks[k], table[pl.ds(entries[k] + (PAD - k), 8), :], result)
    return result


def copy_rows(table, entry_of, stage, start, masks):
    parts = [merged(table, [entry_of(start + half + k) for k in range(8)], masks) for half in (0, 8)]
    stage[start : start + 16, :] = jnp.concatenate(parts, axis=0).astype(BF16)


def near_kernel(rows, order_ref, fields_ref, select_ref, table_ref, left_ref, table, planes, stage):
    turn = pl.program_id(0)

    @pl.when(turn == 0)
    def _():
        planes[...] = jnp.zeros_like(planes)

        def fill(turn, carry):
            for side in range(2):
                group = turn * 2 + side
                spot = pl.ds(pl.multiple_of(group * 8, 8), 8)
                fields = [fields_ref[field, spot, :] for field in range(FIELDS)]
                fill_blocks(fields, planes.at[side], table, group * 8 * LANES)
            return carry

        lax.fori_loop(0, rows // 16, fill, 0)

    masks = sublane_masks()

    def tile_step(local, carry):
        for side in range(2):
            tile = turn * 8 + local * 2 + side
            for start in range(0, TILE, 16):
                copy_rows(table, lambda k: order_ref[tile * TILE + k], stage.at[side], start, masks)
        for side in range(2):
            left = jnp.dot(stage[side], select_ref[...], preferred_element_type=F32).astype(BF16)
            for block in range(3):
                left_ref[local * 2 + side, block * TILE : (block + 1) * TILE, :] = left[
                    :, block * LANES : (block + 1) * LANES
                ]
        return carry

    lax.fori_loop(0, 4, tile_step, 0)
    table_ref[...] = table[pl.ds(pl.multiple_of(turn * 8 * LANES + PAD, PAD), 8 * LANES), :]


def tile_sums(left_ref, place, far, sums):
    others = far[...]
    yield
    grams = nt_dot(left_ref[place], others)
    yield
    chunk = 32
    high, low = [], []
    for start in range(0, TILE, chunk):
        window = grams[start : start + chunk]
        inside = jnp.maximum(window, 0.0)
        root = lax.rsqrt((1.0 + SOFT_CORE) - window)
        depth = grams[TILE + start : TILE + start + chunk]
        charge = grams[2 * TILE + start : 2 * TILE + start + chunk]
        parts = two_pieces(inside * inside * (depth + charge * (root * root * root)))
        high.append(parts[0])
        low.append(parts[1])
        yield
    both = jnp.dot(jnp.concatenate(high + low, axis=0), others, preferred_element_type=F32)
    yield
    sums[...] = both[0:TILE] + both[TILE:]


def weave(stages, copies, parts):
    size = -(-len(copies) // parts)
    for turn, _ in enumerate(stages):
        for copy in copies[turn * size : (turn + 1) * size]:
            copy()
    for copy in copies[parts * size :]:
        copy()


def force_kernel(
    rows, partner_ref, entry_ref, order_ref, lower_ref, upper_ref, place_ref, left_ref, own_ref,
    force_ref, solute_ref, table, forces, planes, far_a, far_b, sum_a, sum_b, arrival,
):
    turn = pl.program_id(0)
    partners = far_a.shape[0]
    own = rows * LANES

    masks = sublane_masks()

    def load(tile, far):
        def entry_of(k):
            return entry_ref[partner_ref[tile * partners + k]]

        return [
            functools.partial(copy_rows, table, entry_of, far, start, masks)
            for start in range(0, partners, 16)
        ]

    def save(tile, sums):
        def copy(block):
            value = sums[block * 8 : block * 8 + 8, :]
            for k in range(8):
                place = order_ref[tile * TILE + block * 8 + k] + (FORCE_PAD - k)
                pltpu.store(forces.at[pl.ds(place, 8), :], value, mask=masks[k])

        return [functools.partial(copy, block) for block in range(TILE // 8)]

    @pl.when(turn == 0)
    def _():
        own_copy = pltpu.make_async_copy(own_ref, table.at[pl.ds(own + PAD, own), :], arrival)
        own_copy.start()
        planes[...] = jnp.zeros_like(planes)

        def fill(group, carry):
            for side, ref, first, shift in ((0, lower_ref, 0, -SLAB_WIDTH), (1, upper_ref, 2 * own, SLAB_WIDTH)):
                fields = [
                    ref[pl.ds(pl.multiple_of(field * rows + group * 8, 8), 8), :] for field in range(FIELDS)
                ]
                fields[0] = fields[0] + shift
                fill_blocks(fields, planes.at[side], table, first + group * 8 * LANES)
            return carry

        lax.fori_loop(0, rows // 8, fill, 0)
        own_copy.wait()
        sum_b[...] = jnp.zeros_like(sum_b)
        for copy in load(0, far_a):
            copy()

    def step(pair, carry):
        tile = turn * 8 + pair * 2
        copies = save(jnp.maximum(tile - 1, 0), sum_b) + load(tile + 1, far_b)
        weave(tile_sums(left_ref, pair * 2, far_a, sum_a), copies, 7)
        copies = save(tile, sum_a) + load(jnp.minimum(tile + 2, rows - 1), far_a)
        weave(tile_sums(left_ref, pair * 2 + 1, far_b, sum_b), copies, 7)
        return carry

    lax.fori_loop(0, 4, step, 0)

    @pl.when(turn == pl.num_programs(0) - 1)
    def _():
        for copy in save(rows - 1, sum_b):
            copy()

        send = pltpu.make_async_copy(forces, force_ref, arrival)
        send.start()
        for row in range(SOL_DEV // LANES):
            start = FORCE_PAD + row * LANES
            force = row_forces(forces[start : start + LANES, :], [place_ref[axis, row : row + 1, :] for axis in range(3)])
            for axis in range(3):
                solute_ref[axis, row : row + 1, :] = place_ref[axis, row : row + 1, :] + STEP_SIZE * force[axis]
        send.wait()


def row_forces(sums, places):
    across = sums.T
    result = []
    for axis, place in enumerate(places):
        first = 6 * axis
        moment = across[first : first + 1] + across[first + 1 : first + 2] + across[first + 3 : first + 4]
        result.append((place - CENTRE) * across[ONES : ONES + 1] - moment)
    return result


def relax_kernel(place_ref, force_ref, out_ref):
    for row in range(8):
        places = [place_ref[axis, row : row + 1, :] for axis in range(3)]
        for axis, force in enumerate(row_forces(force_ref[row * LANES : (row + 1) * LANES, :], places)):
            out_ref[axis, row : row + 1, :] = places[axis] + STEP_SIZE * force


def product_kernel(images, index_ref, *refs):
    pushed_refs, path_refs = refs[:images], refs[images : 2 * images]
    sums_ref, pushed, path = refs[2 * images :]
    index = index_ref[0]
    for by in range(images):
        place = lax.rem(index + images - by, images)
        pushed[place] = pushed_refs[by][...]
        path[place] = path_refs[by][...]
    sums_ref[...] = jnp.zeros_like(sums_ref)
    last = images - 1
    tangents = [path[min(k + 1, last)] - path[max(k - 1, 0)] for k in range(images)]

    def put(kind, image, left, right):
        total = jnp.sum(left * right, axis=0)
        sums_ref[kind * images + image : kind * images + image + 1, :] = jnp.sum(total, axis=0, keepdims=True)

    for k in range(images):
        put(0, k, tangents[k], tangents[k])
        put(1, k, pushed[k] - path[k], tangents[k])
        if k < last:
            step = path[k + 1] - path[k]
            gap = pushed[k + 1] - pushed[k]
            put(2, k, step, step)
            put(3, k, gap, gap)
            put(4, k, gap, tangents[k + 1])
            put(5, k, gap, tangents[k])
            put(6, k, tangents[k + 1], tangents[k])


def blend_kernel(images, index_ref, sums_ref, pushed, path, out_in, out_ref):
    del out_in
    index = index_ref[0]
    last = images - 1
    totals = jnp.sum(sums_ref[...], axis=1, keepdims=True)

    def total(kind, image):
        row = kind * images + image
        return totals[row : row + 1, :]

    step_root = [jnp.sqrt(total(2, k) + EPSILON) for k in range(last)]
    shift = []
    for k in range(images):
        tangent_sq = total(0, k)
        value = -total(1, k) / (tangent_sq + EPSILON)
        if 0 < k < last:
            spring = SPRING_COEF * (step_root[k] - step_root[k - 1]) / jnp.sqrt(tangent_sq + EPSILON)
            value = value + STEP_SIZE * spring
        shift.append(value)
    lengths = []
    for k in range(last):
        there, here = shift[k + 1], shift[k]
        length_sq = (
            total(3, k)
            + there * there * total(0, k + 1)
            + here * here * total(0, k)
            + 2.0 * (there * total(4, k) - here * total(5, k) - there * here * total(6, k))
        )
        lengths.append(jnp.sqrt(jnp.maximum(length_sq, 0.0) + EPSILON))
    knots = [jnp.zeros_like(lengths[0])]
    for length in lengths:
        knots.append(knots[-1] + length)

    def pick(values):
        result = values[0]
        for k in range(1, images):
            result = jnp.where(index == k, values[k], result)
        return result

    none = jnp.zeros_like(lengths[0])
    excess = [knots[k] - knots[last] * (k / last) for k in range(images)]
    back = pick([none] + [jnp.clip(excess[k] / lengths[k - 1], 0.0, 1.0) for k in range(1, images)])
    ahead = pick([jnp.clip(-excess[k] / lengths[k], 0.0, 1.0) for k in range(last)] + [none])
    shifts = [pick([shift[min(max(k + by, 0), last)] for k in range(images)]) for by in (-1, 0, 1)]

    def moved(by):
        place = jnp.clip(index + by, 0, last)
        tangent = path[jnp.minimum(place + 1, last)] - path[jnp.maximum(place - 1, 0)]
        return pushed[place] + shifts[by + 1] * tangent

    here = moved(0)
    blended = here + back * (moved(-1) - here) + ahead * (moved(1) - here)
    out_ref[...] = blended


def whole(*shape, dtype=F32):
    return jax.ShapeDtypeStruct(shape, dtype)


def turned(array, axis, by):
    count = lax.axis_size(axis)
    return lax.ppermute(array, axis, [(i, (i + by) % count) for i in range(count)])


def summed(array, axis):
    count = lax.axis_size(axis)
    if count & (count - 1):
        return lax.psum(array, axis)
    by = 1
    while by < count:
        array = array + lax.ppermute(array, axis, [(i, i ^ by) for i in range(count)])
        by *= 2
    return array


def round_trip(array, axis):
    return [array] + [turned(array, axis, by) for by in range(1, lax.axis_size(axis))]


def per_device(positions, strength, charge, rest_scale, cell_order, ghost_index, tile_atoms):
    atoms = positions.shape[2]
    rows = atoms // LANES
    half = atoms // 2
    partners = tile_atoms.shape[2]
    images = lax.axis_size("image")
    index = lax.axis_index("image").reshape(1)

    factor = jnp.where(jnp.arange(atoms) < SOL_DEV, jnp.sqrt(rest_scale[0]), 1.0)
    scaled = jnp.stack([strength * factor, charge * factor]).reshape(2, rows, LANES)
    places = positions.reshape(3, rows, LANES)
    fields = jnp.concatenate([places, scaled])
    paths = round_trip(places[:, : SOL_DEV // LANES], "image")
    shell = ghost_index.reshape(2, rows // 2, LANES).astype(F32)
    planes = fields.reshape(FIELDS * rows, LANES)
    lower = turned(jnp.concatenate([planes, shell[1]]), "space", 1)
    upper = turned(jnp.concatenate([planes, shell[0]]), "space", -1)
    entries = jnp.concatenate(
        [
            lower[FIELDS * rows :].astype(I32).reshape(half),
            jnp.arange(atoms, 2 * atoms, dtype=I32),
            upper[FIELDS * rows :].astype(I32).reshape(half) + 2 * atoms,
        ]
    )
    order = cell_order.reshape(atoms)
    scalar = pl.BlockSpec(memory_space=pltpu.SMEM)
    vector = pl.BlockSpec(memory_space=pltpu.VMEM)
    params = pltpu.CompilerParams(vmem_limit_bytes=VMEM_LIMIT)
    table, left = pl.pallas_call(
        functools.partial(near_kernel, rows),
        grid=(rows // 8,),
        out_shape=[whole(atoms, LANES), whole(rows, 3 * TILE, LANES, dtype=BF16)],
        in_specs=[scalar] + [vector] * 2,
        out_specs=[
            pl.BlockSpec((8 * LANES, LANES), lambda i: (i, 0)),
            pl.BlockSpec((8, 3 * TILE, LANES), lambda i: (i, 0, 0)),
        ],
        scratch_shapes=[
            pltpu.VMEM((atoms + 2 * PAD, LANES), F32),
            pltpu.VMEM((2, 8 * STRIDE, LANES), F32),
            pltpu.VMEM((2, TILE, LANES), BF16),
        ],
        compiler_params=params,
        cost_estimate=pl.CostEstimate(flops=25 * 10**9, bytes_accessed=3 * 10**7, transcendentals=0),
    )(order, fields, near_selector())
    forces, solute = pl.pallas_call(
        functools.partial(force_kernel, rows),
        grid=(rows // 8,),
        out_shape=[whole(atoms + 2 * FORCE_PAD, LANES), whole(3, SOL_DEV // LANES, LANES)],
        in_specs=[scalar] * 3
        + [vector] * 3
        + [pl.BlockSpec((8, 3 * TILE, LANES), lambda i: (i, 0, 0)), pl.BlockSpec(memory_space=pl.ANY)],
        out_specs=[pl.BlockSpec(memory_space=pl.ANY), vector],
        scratch_shapes=[
            pltpu.VMEM((3 * atoms + 2 * PAD, LANES), F32),
            pltpu.VMEM((atoms + 2 * FORCE_PAD, LANES), F32),
            pltpu.VMEM((2, 8 * STRIDE, LANES), F32),
            pltpu.VMEM((partners, LANES), BF16),
            pltpu.VMEM((partners, LANES), BF16),
            pltpu.VMEM((TILE, LANES), F32),
            pltpu.VMEM((TILE, LANES), F32),
            pltpu.SemaphoreType.DMA,
        ],
        compiler_params=params,
        cost_estimate=pl.CostEstimate(flops=25 * 10**9, bytes_accessed=3 * 10**7, transcendentals=0),
    )(tile_atoms.reshape(rows * partners), entries, order, lower, upper, places, left, table)
    solutes = round_trip(solute, "image")
    block = pl.BlockSpec((3, 8, LANES), lambda i: (0, i, 0))
    small = pltpu.CompilerParams(vmem_limit_bytes=8 * 1024 * 1024)
    out = pl.pallas_call(
        relax_kernel,
        grid=(rows // 8,),
        out_shape=whole(3, rows, LANES),
        in_specs=[block, pl.BlockSpec((8 * LANES, LANES), lambda i: (i + FORCE_PAD // (8 * LANES), 0))],
        out_specs=block,
        compiler_params=small,
        cost_estimate=pl.CostEstimate(flops=10**9, bytes_accessed=2 * 10**7, transcendentals=0),
    )(places, forces)
    solute_shape = whole(images, 3, SOL_DEV // LANES, LANES)
    sums, pushed, path = pl.pallas_call(
        functools.partial(product_kernel, images),
        out_shape=[whole(-(-7 * images // 8) * 8, LANES), solute_shape, solute_shape],
        in_specs=[scalar] + [vector] * (2 * images),
        out_specs=[vector] * 3,
        compiler_params=small,
    )(index, *solutes, *paths)
    out = pl.pallas_call(
        functools.partial(blend_kernel, images),
        grid=(1,),
        out_shape=whole(3, rows, LANES),
        in_specs=[scalar] + [vector] * 3 + [pl.BlockSpec(memory_space=pl.ANY)],
        out_specs=pl.BlockSpec((3, SOL_DEV // LANES, LANES), lambda i: (0, 0, 0)),
        input_output_aliases={4: 0},
        compiler_params=small,
    )(index, summed(sums, "space"), pushed, path, out)
    return out.reshape(1, 3, atoms)


def solution(mesh):
    placed = (
        P("image", None, "space"),
        P("space"),
        P("space"),
        P("image"),
        P("image", "space", None),
        P("image", "space", None),
        P("image", "space", None),
    )
    return jax.shard_map(
        per_device, mesh=mesh, in_specs=placed, out_specs=P("image", None, "space"), check_vma=False
    )
```

```python
import functools

import jax
import jax.numpy as jnp
import numpy as np
from jax import lax
from jax.experimental import pallas as pl
from jax.experimental.pallas import tpu as pltpu
from jax.sharding import PartitionSpec as P

SOL_DEV = 1024
TILE = 128
LANES = 128
FIELDS = 5
STRIDE = 48

LJ_COEF = 0.5
CHARGE_COEF = 0.1
SOFT_CORE = 0.09
SLAB_WIDTH = 1.0
STEP_SIZE = 0.2
SPRING_COEF = 1.0
EPSILON = 1e-06
CENTRE = 0.5

F32 = jnp.float32
BF16 = jnp.bfloat16
I32 = jnp.int32
VMEM_LIMIT = 58 * 1024 * 1024

ONES = 18
NORM = 21
DEPTH = 24
CHARGE = 28
LAST = 32


def near_selector():
    chosen = np.zeros((LANES, 3 * LANES), np.float32)
    for axis in range(3):
        high, middle, low = 6 * axis, 6 * axis + 1, 6 * axis + 3
        for k, source in enumerate((high, high, middle, high, low, middle)):
            chosen[source, 6 * axis + k] = 2.0
    for k in range(3):
        chosen[NORM + k, ONES + k] = 1.0
        chosen[ONES, NORM + k] = 1.0
    chosen[ONES, LAST] = 1.0
    for block, first in ((1, DEPTH), (2, CHARGE)):
        for k, source in enumerate((first, first, first + 1, first + 1)):
            chosen[source, block * LANES + first + k] = 1.0
    return jnp.asarray(chosen, BF16)


def pieces(value, count):
    result = []
    for _ in range(count - 1):
        part = value.astype(BF16).astype(F32)
        result.append(part)
        value = value - part
    return result + [value]


def features(fields):
    rows = []
    for axis in range(3):
        high, middle, low = pieces(fields[axis], 3)
        rows += [high, middle, high, low, high, middle]
    one = jnp.ones_like(fields[0])
    rows += [one] * 3
    rows += pieces(-(fields[0] * fields[0] + fields[1] * fields[1] + fields[2] * fields[2]), 3)
    for value in fields[3:]:
        high, low = pieces(value, 2)
        rows += [high, low, high, low]
    return rows + [one]


def two_pieces(values):
    high = values.astype(BF16)
    low = (values - high.astype(F32)).astype(BF16)
    return high, low


def nt_dot(left, right):
    return lax.dot_general(left, right, (((1,), (1,)), ((), ())), preferred_element_type=F32)


def fill_blocks(fields, planes, table, first):
    fields = [field - CENTRE for field in fields[:3]] + fields[3:]
    fields[3] = fields[3] * LJ_COEF**0.5
    fields[4] = fields[4] * CHARGE_COEF**0.5
    for k, row in enumerate(features(fields)):
        planes[pl.ds(k, 8, stride=STRIDE), :] = row
    blank = jnp.zeros((LANES - STRIDE, LANES), F32)
    for block in range(8):
        part = jnp.concatenate([planes[block * STRIDE : (block + 1) * STRIDE, :], blank], axis=0)
        start = pl.multiple_of(first + block * LANES, LANES)
        flat(table)[pl.ds(start, LANES), :] = part.T


def flat(ref):
    return ref.reshape(ref.shape[0], LANES)


def near_kernel(rows, order_ref, fields_ref, select_ref, table_ref, left_ref, table, planes, stage):
    turn = pl.program_id(0)

    @pl.when(turn == 0)
    def _():
        planes[...] = jnp.zeros_like(planes)

        def fill(turn, carry):
            for side in range(2):
                group = turn * 2 + side
                spot = pl.ds(pl.multiple_of(group * 8, 8), 8)
                fields = [fields_ref[field, spot, :] for field in range(FIELDS)]
                fill_blocks(fields, planes.at[side], table, group * 8 * LANES)
            return carry

        lax.fori_loop(0, rows // 16, fill, 0)

    def tile_step(local, carry):
        for side in range(2):
            tile = turn * 8 + local * 2 + side
            for k in range(TILE):
                stage[side, k : k + 1, :] = table[order_ref[tile * TILE + k]]
        for side in range(2):
            left = jnp.dot(stage[side].astype(BF16), select_ref[...], preferred_element_type=F32).astype(BF16)
            for block in range(3):
                left_ref[local * 2 + side, block * TILE : (block + 1) * TILE, :] = left[
                    :, block * LANES : (block + 1) * LANES
                ]
        return carry

    lax.fori_loop(0, 4, tile_step, 0)
    table_ref[...] = flat(table)[pl.ds(pl.multiple_of(turn * 8 * LANES, 8 * LANES), 8 * LANES), :]


def tile_sums(left_ref, place, far, sums):
    others = far[...].astype(BF16)
    yield
    grams = nt_dot(left_ref[place], others)
    yield
    chunk = 32
    high, low = [], []
    for start in range(0, TILE, chunk):
        window = grams[start : start + chunk]
        inside = jnp.maximum(window, 0.0)
        root = lax.rsqrt((1.0 + SOFT_CORE) - window)
        depth = grams[TILE + start : TILE + start + chunk]
        charge = grams[2 * TILE + start : 2 * TILE + start + chunk]
        parts = two_pieces(inside * inside * (depth + charge * (root * root * root)))
        high.append(parts[0])
        low.append(parts[1])
        yield
    both = jnp.dot(jnp.concatenate(high + low, axis=0), others, preferred_element_type=F32)
    yield
    sums[...] = both[0:TILE] + both[TILE:]


def weave(stages, copies, parts):
    size = -(-len(copies) // parts)
    for turn, _ in enumerate(stages):
        for copy in copies[turn * size : (turn + 1) * size]:
            copy()
    for copy in copies[parts * size :]:
        copy()


def force_kernel(
    rows, partner_ref, entry_ref, order_ref, lower_ref, upper_ref, place_ref, left_ref, own_ref,
    force_ref, solute_ref, table, forces, planes, far_a, far_b, sum_a, sum_b, arrival,
):
    turn = pl.program_id(0)
    partners = far_a.shape[0]
    own = rows * LANES

    def load(tile, far):
        def copy(k):
            far[k : k + 1, :] = table[entry_ref[partner_ref[tile * partners + k]]]

        return [functools.partial(copy, k) for k in range(partners)]

    def save(tile, sums):
        def copy(k):
            forces[order_ref[tile * TILE + k]] = sums[k : k + 1, :]

        return [functools.partial(copy, k) for k in range(TILE)]

    @pl.when(turn == 0)
    def _():
        own_copy = pltpu.make_async_copy(own_ref, flat(table).at[pl.ds(own, own), :], arrival)
        own_copy.start()
        planes[...] = jnp.zeros_like(planes)

        def fill(group, carry):
            for side, ref, first, shift in ((0, lower_ref, 0, -SLAB_WIDTH), (1, upper_ref, 2 * own, SLAB_WIDTH)):
                fields = [
                    ref[pl.ds(pl.multiple_of(field * rows + group * 8, 8), 8), :] for field in range(FIELDS)
                ]
                fields[0] = fields[0] + shift
                fill_blocks(fields, planes.at[side], table, first + group * 8 * LANES)
            return carry

        lax.fori_loop(0, rows // 8, fill, 0)
        own_copy.wait()
        sum_b[...] = jnp.zeros_like(sum_b)
        for copy in load(0, far_a):
            copy()

    def step(pair, carry):
        tile = turn * 8 + pair * 2
        copies = save(jnp.maximum(tile - 1, 0), sum_b) + load(tile + 1, far_b)
        weave(tile_sums(left_ref, pair * 2, far_a, sum_a), copies, 7)
        copies = save(tile, sum_a) + load(jnp.minimum(tile + 2, rows - 1), far_a)
        weave(tile_sums(left_ref, pair * 2 + 1, far_b, sum_b), copies, 7)
        return carry

    lax.fori_loop(0, 4, step, 0)

    @pl.when(turn == pl.num_programs(0) - 1)
    def _():
        for copy in save(rows - 1, sum_b):
            copy()

        send = pltpu.make_async_copy(flat(forces), force_ref, arrival)
        send.start()
        for row in range(SOL_DEV // LANES):
            sums = flat(forces)[row * LANES : (row + 1) * LANES, :]
            force = row_forces(sums, [place_ref[axis, row : row + 1, :] for axis in range(3)])
            for axis in range(3):
                solute_ref[axis, row : row + 1, :] = place_ref[axis, row : row + 1, :] + STEP_SIZE * force[axis]
        send.wait()


def row_forces(sums, places):
    across = sums.T
    result = []
    for axis, place in enumerate(places):
        first = 6 * axis
        moment = across[first : first + 1] + across[first + 1 : first + 2] + across[first + 3 : first + 4]
        result.append((place - CENTRE) * across[ONES : ONES + 1] - moment)
    return result


def relax_kernel(place_ref, force_ref, out_ref):
    for row in range(8):
        places = [place_ref[axis, row : row + 1, :] for axis in range(3)]
        for axis, force in enumerate(row_forces(force_ref[row * LANES : (row + 1) * LANES, :], places)):
            out_ref[axis, row : row + 1, :] = places[axis] + STEP_SIZE * force


def product_kernel(images, index_ref, *refs):
    pushed_refs, path_refs = refs[:images], refs[images : 2 * images]
    sums_ref, pushed, path = refs[2 * images :]
    index = index_ref[0]
    for by in range(images):
        place = lax.rem(index + images - by, images)
        pushed[place] = pushed_refs[by][...]
        path[place] = path_refs[by][...]
    sums_ref[...] = jnp.zeros_like(sums_ref)
    last = images - 1
    tangents = [path[min(k + 1, last)] - path[max(k - 1, 0)] for k in range(images)]

    def put(kind, image, left, right):
        total = jnp.sum(left * right, axis=0)
        sums_ref[kind * images + image : kind * images + image + 1, :] = jnp.sum(total, axis=0, keepdims=True)

    for k in range(images):
        put(0, k, tangents[k], tangents[k])
        put(1, k, pushed[k] - path[k], tangents[k])
        if k < last:
            step = path[k + 1] - path[k]
            gap = pushed[k + 1] - pushed[k]
            put(2, k, step, step)
            put(3, k, gap, gap)
            put(4, k, gap, tangents[k + 1])
            put(5, k, gap, tangents[k])
            put(6, k, tangents[k + 1], tangents[k])


def blend_kernel(images, index_ref, sums_ref, pushed, path, out_in, out_ref):
    del out_in
    index = index_ref[0]
    last = images - 1
    totals = jnp.sum(sums_ref[...], axis=1, keepdims=True)

    def total(kind, image):
        row = kind * images + image
        return totals[row : row + 1, :]

    step_root = [jnp.sqrt(total(2, k) + EPSILON) for k in range(last)]
    shift = []
    for k in range(images):
        tangent_sq = total(0, k)
        value = -total(1, k) / (tangent_sq + EPSILON)
        if 0 < k < last:
            spring = SPRING_COEF * (step_root[k] - step_root[k - 1]) / jnp.sqrt(tangent_sq + EPSILON)
            value = value + STEP_SIZE * spring
        shift.append(value)
    lengths = []
    for k in range(last):
        there, here = shift[k + 1], shift[k]
        length_sq = (
            total(3, k)
            + there * there * total(0, k + 1)
            + here * here * total(0, k)
            + 2.0 * (there * total(4, k) - here * total(5, k) - there * here * total(6, k))
        )
        lengths.append(jnp.sqrt(jnp.maximum(length_sq, 0.0) + EPSILON))
    knots = [jnp.zeros_like(lengths[0])]
    for length in lengths:
        knots.append(knots[-1] + length)

    def pick(values):
        result = values[0]
        for k in range(1, images):
            result = jnp.where(index == k, values[k], result)
        return result

    none = jnp.zeros_like(lengths[0])
    excess = [knots[k] - knots[last] * (k / last) for k in range(images)]
    back = pick([none] + [jnp.clip(excess[k] / lengths[k - 1], 0.0, 1.0) for k in range(1, images)])
    ahead = pick([jnp.clip(-excess[k] / lengths[k], 0.0, 1.0) for k in range(last)] + [none])
    shifts = [pick([shift[min(max(k + by, 0), last)] for k in range(images)]) for by in (-1, 0, 1)]

    def moved(by):
        place = jnp.clip(index + by, 0, last)
        tangent = path[jnp.minimum(place + 1, last)] - path[jnp.maximum(place - 1, 0)]
        return pushed[place] + shifts[by + 1] * tangent

    here = moved(0)
    blended = here + back * (moved(-1) - here) + ahead * (moved(1) - here)
    out_ref[...] = blended


def whole(*shape, dtype=F32):
    return jax.ShapeDtypeStruct(shape, dtype)


def turned(array, axis, by):
    count = lax.axis_size(axis)
    return lax.ppermute(array, axis, [(i, (i + by) % count) for i in range(count)])


def summed(array, axis):
    count = lax.axis_size(axis)
    if count & (count - 1):
        return lax.psum(array, axis)
    by = 1
    while by < count:
        array = array + lax.ppermute(array, axis, [(i, i ^ by) for i in range(count)])
        by *= 2
    return array


def round_trip(array, axis):
    return [array] + [turned(array, axis, by) for by in range(1, lax.axis_size(axis))]


def per_device(positions, strength, charge, rest_scale, cell_order, ghost_index, tile_atoms):
    atoms = positions.shape[2]
    rows = atoms // LANES
    half = atoms // 2
    partners = tile_atoms.shape[2]
    images = lax.axis_size("image")
    index = lax.axis_index("image").reshape(1)

    factor = jnp.where(jnp.arange(atoms) < SOL_DEV, jnp.sqrt(rest_scale[0]), 1.0)
    scaled = jnp.stack([strength * factor, charge * factor]).reshape(2, rows, LANES)
    places = positions.reshape(3, rows, LANES)
    fields = jnp.concatenate([places, scaled])
    paths = round_trip(places[:, : SOL_DEV // LANES], "image")
    shell = ghost_index.reshape(2, rows // 2, LANES).astype(F32)
    planes = fields.reshape(FIELDS * rows, LANES)
    lower = turned(jnp.concatenate([planes, shell[1]]), "space", 1)
    upper = turned(jnp.concatenate([planes, shell[0]]), "space", -1)
    entries = jnp.concatenate(
        [
            lower[FIELDS * rows :].astype(I32).reshape(half),
            jnp.arange(atoms, 2 * atoms, dtype=I32),
            upper[FIELDS * rows :].astype(I32).reshape(half) + 2 * atoms,
        ]
    )
    order = cell_order.reshape(atoms)
    scalar = pl.BlockSpec(memory_space=pltpu.SMEM)
    vector = pl.BlockSpec(memory_space=pltpu.VMEM)
    params = pltpu.CompilerParams(vmem_limit_bytes=VMEM_LIMIT)
    table, left = pl.pallas_call(
        functools.partial(near_kernel, rows),
        grid=(rows // 8,),
        out_shape=[whole(atoms, LANES), whole(rows, 3 * TILE, LANES, dtype=BF16)],
        in_specs=[scalar] + [vector] * 2,
        out_specs=[
            pl.BlockSpec((8 * LANES, LANES), lambda i: (i, 0)),
            pl.BlockSpec((8, 3 * TILE, LANES), lambda i: (i, 0, 0)),
        ],
        scratch_shapes=[
            pltpu.VMEM((atoms, 1, LANES), F32),
            pltpu.VMEM((2, 8 * STRIDE, LANES), F32),
            pltpu.VMEM((2, TILE, LANES), F32),
        ],
        compiler_params=params,
        cost_estimate=pl.CostEstimate(flops=25 * 10**9, bytes_accessed=3 * 10**7, transcendentals=0),
    )(order, fields, near_selector())
    forces, solute = pl.pallas_call(
        functools.partial(force_kernel, rows),
        grid=(rows // 8,),
        out_shape=[whole(atoms, LANES), whole(3, SOL_DEV // LANES, LANES)],
        in_specs=[scalar] * 3
        + [vector] * 3
        + [pl.BlockSpec((8, 3 * TILE, LANES), lambda i: (i, 0, 0)), pl.BlockSpec(memory_space=pl.ANY)],
        out_specs=[pl.BlockSpec(memory_space=pl.ANY), vector],
        scratch_shapes=[
            pltpu.VMEM((3 * atoms, 1, LANES), F32),
            pltpu.VMEM((atoms, 1, LANES), F32),
            pltpu.VMEM((2, 8 * STRIDE, LANES), F32),
            pltpu.VMEM((partners, LANES), F32),
            pltpu.VMEM((partners, LANES), F32),
            pltpu.VMEM((TILE, LANES), F32),
            pltpu.VMEM((TILE, LANES), F32),
            pltpu.SemaphoreType.DMA,
        ],
        compiler_params=params,
        cost_estimate=pl.CostEstimate(flops=25 * 10**9, bytes_accessed=3 * 10**7, transcendentals=0),
    )(tile_atoms.reshape(rows * partners), entries, order, lower, upper, places, left, table)
    solutes = round_trip(solute, "image")
    block = pl.BlockSpec((3, 8, LANES), lambda i: (0, i, 0))
    small = pltpu.CompilerParams(vmem_limit_bytes=8 * 1024 * 1024)
    out = pl.pallas_call(
        relax_kernel,
        grid=(rows // 8,),
        out_shape=whole(3, rows, LANES),
        in_specs=[block, pl.BlockSpec((8 * LANES, LANES), lambda i: (i, 0))],
        out_specs=block,
        compiler_params=small,
        cost_estimate=pl.CostEstimate(flops=10**9, bytes_accessed=2 * 10**7, transcendentals=0),
    )(places, forces)
    solute_shape = whole(images, 3, SOL_DEV // LANES, LANES)
    sums, pushed, path = pl.pallas_call(
        functools.partial(product_kernel, images),
        out_shape=[whole(-(-7 * images // 8) * 8, LANES), solute_shape, solute_shape],
        in_specs=[scalar] + [vector] * (2 * images),
        out_specs=[vector] * 3,
        compiler_params=small,
    )(index, *solutes, *paths)
    out = pl.pallas_call(
        functools.partial(blend_kernel, images),
        grid=(1,),
        out_shape=whole(3, rows, LANES),
        in_specs=[scalar] + [vector] * 3 + [pl.BlockSpec(memory_space=pl.ANY)],
        out_specs=pl.BlockSpec((3, SOL_DEV // LANES, LANES), lambda i: (0, 0, 0)),
        input_output_aliases={4: 0},
        compiler_params=small,
    )(index, summed(sums, "space"), pushed, path, out)
    return out.reshape(1, 3, atoms)


def solution(mesh):
    placed = (
        P("image", None, "space"),
        P("space"),
        P("space"),
        P("image"),
        P("image", "space", None),
        P("image", "space", None),
        P("image", "space", None),
    )
    return jax.shard_map(
        per_device, mesh=mesh, in_specs=placed, out_specs=P("image", None, "space"), check_vma=False
    )
```

```python
import functools

import jax
import jax.numpy as jnp
import numpy as np
from jax import lax
from jax.experimental import pallas as pl
from jax.experimental.pallas import tpu as pltpu
from jax.sharding import PartitionSpec as P

SOL_DEV = 1024
TILE = 128
LANES = 128
FIELDS = 5
FORCE_PAD = 1024
PAD = 8

LJ_COEF = 0.5
CHARGE_COEF = 0.1
SOFT_CORE = 0.09
SLAB_WIDTH = 1.0
STEP_SIZE = 0.2
SPRING_COEF = 1.0
EPSILON = 1e-06
CENTRE = 0.5

F32 = jnp.float32
BF16 = jnp.bfloat16
I32 = jnp.int32
VMEM_LIMIT = 58 * 1024 * 1024

DEPTH, CHARGE, ONE, NORM, LAST = 3, 4, 5, 6, 7
FAR_PIECES = (0, 1, 2, 0, 1, 0)
NEAR_PIECES = (0, 0, 0, 1, 1, 2)


def near_selector():
    chosen = np.zeros((LANES, 3 * LANES), np.float32)
    for group, piece in enumerate(NEAR_PIECES):
        for axis in range(3):
            chosen[piece * 8 + axis, group * 8 + axis] = 2.0
        for block, field in ((1, DEPTH), (2, CHARGE)):
            chosen[piece * 8 + field, block * LANES + group * 8 + field] = 1.0
    for piece, group in ((0, 0), (1, 3), (2, 5)):
        chosen[piece * 8 + NORM, group * 8 + ONE] = 1.0
        chosen[ONE, piece * 8 + NORM] = 1.0
    chosen[ONE, LAST] = 1.0
    return jnp.asarray(chosen, BF16)


def two_pieces(values):
    high = values.astype(BF16)
    low = (values - high.astype(F32)).astype(BF16)
    return high, low


def nt_dot(left, right):
    return lax.dot_general(left, right, (((1,), (1,)), ((), ())), preferred_element_type=F32)


def fill_blocks(block_at, count, shift, table, first):
    sublane = lax.broadcasted_iota(I32, (8, LANES), 0)
    move = jnp.where(sublane < 3, jnp.where(sublane == 0, shift - CENTRE, -CENTRE), 0.0)
    blank = jnp.zeros((LANES - 8 * len(FAR_PIECES), LANES), F32)
    for block in range(count):
        values = block_at(block) + move
        norm = jnp.sum(jnp.where(sublane < 3, values * values, 0.0), axis=0, keepdims=True)
        rest = jnp.where(sublane == NORM, -norm, values)
        parts = []
        for _ in range(2):
            parts.append(rest.astype(BF16).astype(F32))
            rest = rest - parts[-1]
        parts.append(rest)
        rows = jnp.concatenate([parts[piece] for piece in FAR_PIECES] + [blank], axis=0)
        start = pl.multiple_of(first + block * LANES + PAD, PAD)
        table[pl.ds(start, LANES), :] = rows.T


def sublane_masks():
    sublane = lax.broadcasted_iota(I32, (8, LANES), 0)
    return [sublane == k for k in range(8)]


def merged(table, entries, masks):
    result = table[pl.ds(entries[0] + PAD, 8), :]
    for k in range(1, 8):
        result = jnp.where(masks[k], table[pl.ds(entries[k] + (PAD - k), 8), :], result)
    return result


def copy_rows(table, entry_of, stage, start, masks):
    parts = [merged(table, [entry_of(start + half + k) for k in range(8)], masks) for half in (0, 8)]
    stage[start : start + 16, :] = jnp.concatenate(parts, axis=0).astype(BF16)


def near_kernel(rows, order_ref, fields_ref, select_ref, table_ref, left_ref, table, stage):
    turn = pl.program_id(0)

    @pl.when(turn == 0)
    def _():
        def fill(group, carry):
            fill_blocks(lambda block: fields_ref[group * 8 + block], 8, 0.0, table, group * 8 * LANES)
            return carry

        lax.fori_loop(0, rows // 8, fill, 0)

    masks = sublane_masks()

    def tile_step(local, carry):
        for side in range(2):
            tile = turn * 8 + local * 2 + side
            for start in range(0, TILE, 16):
                copy_rows(table, lambda k: order_ref[tile * TILE + k], stage.at[side], start, masks)
        for side in range(2):
            left = jnp.dot(stage[side], select_ref[...], preferred_element_type=F32).astype(BF16)
            for block in range(3):
                left_ref[local * 2 + side, block * TILE : (block + 1) * TILE, :] = left[
                    :, block * LANES : (block + 1) * LANES
                ]
        return carry

    lax.fori_loop(0, 4, tile_step, 0)
    table_ref[...] = table[pl.ds(pl.multiple_of(turn * 8 * LANES + PAD, PAD), 8 * LANES), :]


def tile_sums(left_ref, place, far, sums):
    others = far[...]
    yield
    grams = nt_dot(left_ref[place], others)
    yield
    chunk = 32
    high, low = [], []
    for start in range(0, TILE, chunk):
        window = grams[start : start + chunk]
        inside = jnp.maximum(window, 0.0)
        root = lax.rsqrt((1.0 + SOFT_CORE) - window)
        depth = grams[TILE + start : TILE + start + chunk]
        charge = grams[2 * TILE + start : 2 * TILE + start + chunk]
        parts = two_pieces(inside * inside * (depth + charge * (root * root * root)))
        high.append(parts[0])
        low.append(parts[1])
        yield
    both = jnp.dot(jnp.concatenate(high + low, axis=0), others, preferred_element_type=F32)
    yield
    sums[...] = both[0:TILE] + both[TILE:]


def weave(stages, copies, parts):
    size = -(-len(copies) // parts)
    for turn, _ in enumerate(stages):
        for copy in copies[turn * size : (turn + 1) * size]:
            copy()
    for copy in copies[parts * size :]:
        copy()


def force_kernel(
    rows, partner_ref, entry_ref, order_ref, lower_ref, upper_ref, place_ref, left_ref, own_ref,
    force_ref, solute_ref, table, forces, far_a, far_b, sum_a, sum_b, arrival,
):
    turn = pl.program_id(0)
    partners = far_a.shape[0]
    own = rows * LANES

    masks = sublane_masks()

    def load(tile, far):
        def entry_of(k):
            return entry_ref[partner_ref[tile * partners + k]]

        return [
            functools.partial(copy_rows, table, entry_of, far, start, masks)
            for start in range(0, partners, 16)
        ]

    def save(tile, sums):
        def copy(block):
            value = sums[block * 8 : block * 8 + 8, :]
            for k in range(8):
                place = order_ref[tile * TILE + block * 8 + k] + (FORCE_PAD - k)
                pltpu.store(forces.at[pl.ds(place, 8), :], value, mask=masks[k])

        return [functools.partial(copy, block) for block in range(TILE // 8)]

    @pl.when(turn == 0)
    def _():
        own_copy = pltpu.make_async_copy(own_ref, table.at[pl.ds(own + PAD, own), :], arrival)
        own_copy.start()

        def fill(group, carry):
            for ref, first, shift in ((lower_ref, 0, -SLAB_WIDTH), (upper_ref, 2 * own, SLAB_WIDTH)):
                fill_blocks(lambda block: ref[group * 4 + block], 4, shift, table, first + group * 4 * LANES)
            return carry

        lax.fori_loop(0, rows // 4, fill, 0)
        own_copy.wait()
        sum_b[...] = jnp.zeros_like(sum_b)
        for copy in load(0, far_a):
            copy()

    def step(pair, carry):
        tile = turn * 8 + pair * 2
        copies = save(jnp.maximum(tile - 1, 0), sum_b) + load(tile + 1, far_b)
        weave(tile_sums(left_ref, pair * 2, far_a, sum_a), copies, 7)
        copies = save(tile, sum_a) + load(jnp.minimum(tile + 2, rows - 1), far_a)
        weave(tile_sums(left_ref, pair * 2 + 1, far_b, sum_b), copies, 7)
        return carry

    lax.fori_loop(0, 4, step, 0)

    @pl.when(turn == pl.num_programs(0) - 1)
    def _():
        for copy in save(rows - 1, sum_b):
            copy()

        send = pltpu.make_async_copy(forces, force_ref, arrival)
        send.start()
        for row in range(SOL_DEV // LANES):
            start = FORCE_PAD + row * LANES
            force = row_forces(forces[start : start + LANES, :], [place_ref[axis, row : row + 1, :] for axis in range(3)])
            for axis in range(3):
                solute_ref[axis, row : row + 1, :] = place_ref[axis, row : row + 1, :] + STEP_SIZE * force[axis]
        send.wait()


def row_forces(sums, places):
    across = sums.T
    result = []
    for axis, place in enumerate(places):
        moment = sum(across[first + axis : first + axis + 1] for first in (0, 8, 16))
        result.append((place - CENTRE) * across[ONE : ONE + 1] - moment)
    return result


def relax_kernel(place_ref, force_ref, out_ref):
    for row in range(8):
        places = [place_ref[axis, row : row + 1, :] for axis in range(3)]
        for axis, force in enumerate(row_forces(force_ref[row * LANES : (row + 1) * LANES, :], places)):
            out_ref[axis, row : row + 1, :] = places[axis] + STEP_SIZE * force


def product_kernel(images, index_ref, *refs):
    pushed_refs, path_refs = refs[:images], refs[images : 2 * images]
    sums_ref, pushed, path = refs[2 * images :]
    index = index_ref[0]
    for by in range(images):
        place = lax.rem(index + images - by, images)
        pushed[place] = pushed_refs[by][...]
        path[place] = path_refs[by][...]
    sums_ref[...] = jnp.zeros_like(sums_ref)
    last = images - 1
    tangents = [path[min(k + 1, last)] - path[max(k - 1, 0)] for k in range(images)]

    def put(kind, image, left, right):
        total = jnp.sum(left * right, axis=0)
        sums_ref[kind * images + image : kind * images + image + 1, :] = jnp.sum(total, axis=0, keepdims=True)

    for k in range(images):
        put(0, k, tangents[k], tangents[k])
        put(1, k, pushed[k] - path[k], tangents[k])
        if k < last:
            step = path[k + 1] - path[k]
            gap = pushed[k + 1] - pushed[k]
            put(2, k, step, step)
            put(3, k, gap, gap)
            put(4, k, gap, tangents[k + 1])
            put(5, k, gap, tangents[k])
            put(6, k, tangents[k + 1], tangents[k])


def blend_kernel(images, index_ref, sums_ref, pushed, path, out_in, out_ref):
    del out_in
    index = index_ref[0]
    last = images - 1
    totals = jnp.sum(sums_ref[...], axis=1, keepdims=True)

    def total(kind, image):
        row = kind * images + image
        return totals[row : row + 1, :]

    step_root = [jnp.sqrt(total(2, k) + EPSILON) for k in range(last)]
    shift = []
    for k in range(images):
        tangent_sq = total(0, k)
        value = -total(1, k) / (tangent_sq + EPSILON)
        if 0 < k < last:
            spring = SPRING_COEF * (step_root[k] - step_root[k - 1]) / jnp.sqrt(tangent_sq + EPSILON)
            value = value + STEP_SIZE * spring
        shift.append(value)
    lengths = []
    for k in range(last):
        there, here = shift[k + 1], shift[k]
        length_sq = (
            total(3, k)
            + there * there * total(0, k + 1)
            + here * here * total(0, k)
            + 2.0 * (there * total(4, k) - here * total(5, k) - there * here * total(6, k))
        )
        lengths.append(jnp.sqrt(jnp.maximum(length_sq, 0.0) + EPSILON))
    knots = [jnp.zeros_like(lengths[0])]
    for length in lengths:
        knots.append(knots[-1] + length)

    def pick(values):
        result = values[0]
        for k in range(1, images):
            result = jnp.where(index == k, values[k], result)
        return result

    none = jnp.zeros_like(lengths[0])
    excess = [knots[k] - knots[last] * (k / last) for k in range(images)]
    back = pick([none] + [jnp.clip(excess[k] / lengths[k - 1], 0.0, 1.0) for k in range(1, images)])
    ahead = pick([jnp.clip(-excess[k] / lengths[k], 0.0, 1.0) for k in range(last)] + [none])
    shifts = [pick([shift[min(max(k + by, 0), last)] for k in range(images)]) for by in (-1, 0, 1)]

    def moved(by):
        place = jnp.clip(index + by, 0, last)
        tangent = path[jnp.minimum(place + 1, last)] - path[jnp.maximum(place - 1, 0)]
        return pushed[place] + shifts[by + 1] * tangent

    here = moved(0)
    blended = here + back * (moved(-1) - here) + ahead * (moved(1) - here)
    out_ref[...] = blended


def whole(*shape, dtype=F32):
    return jax.ShapeDtypeStruct(shape, dtype)


def turned(array, axis, by):
    count = lax.axis_size(axis)
    return lax.ppermute(array, axis, [(i, (i + by) % count) for i in range(count)])


def summed(array, axis):
    count = lax.axis_size(axis)
    if count & (count - 1):
        return lax.psum(array, axis)
    by = 1
    while by < count:
        array = array + lax.ppermute(array, axis, [(i, i ^ by) for i in range(count)])
        by *= 2
    return array


def round_trip(array, axis):
    return [array] + [turned(array, axis, by) for by in range(1, lax.axis_size(axis))]


def per_device(positions, strength, charge, rest_scale, cell_order, ghost_index, tile_atoms):
    atoms = positions.shape[2]
    rows = atoms // LANES
    half = atoms // 2
    partners = tile_atoms.shape[2]
    images = lax.axis_size("image")
    index = lax.axis_index("image").reshape(1)

    factor = jnp.where(jnp.arange(atoms) < SOL_DEV, jnp.sqrt(rest_scale[0]), 1.0)
    scaled = jnp.stack([strength * factor * LJ_COEF**0.5, charge * factor * CHARGE_COEF**0.5])
    places = positions.reshape(3, rows, LANES)
    fields = jnp.concatenate([places, scaled.reshape(2, rows, LANES)])
    constant = jnp.stack([jnp.full((rows, LANES), value, F32) for value in (1.0, 0.0, 1.0)])

    def blocks(planes):
        return jnp.concatenate([planes, constant]).transpose(1, 0, 2)

    paths = round_trip(places[:, : SOL_DEV // LANES], "image")
    shell = ghost_index.reshape(2, rows // 2, LANES).astype(F32)
    planes = fields.reshape(FIELDS * rows, LANES)
    lower = turned(jnp.concatenate([planes, shell[1]]), "space", 1)
    upper = turned(jnp.concatenate([planes, shell[0]]), "space", -1)
    entries = jnp.concatenate(
        [
            lower[FIELDS * rows :].astype(I32).reshape(half),
            jnp.arange(atoms, 2 * atoms, dtype=I32),
            upper[FIELDS * rows :].astype(I32).reshape(half) + 2 * atoms,
        ]
    )
    lower, upper = (blocks(side[: FIELDS * rows].reshape(FIELDS, rows, LANES)) for side in (lower, upper))
    order = cell_order.reshape(atoms)
    scalar = pl.BlockSpec(memory_space=pltpu.SMEM)
    vector = pl.BlockSpec(memory_space=pltpu.VMEM)
    params = pltpu.CompilerParams(vmem_limit_bytes=VMEM_LIMIT)
    table, left = pl.pallas_call(
        functools.partial(near_kernel, rows),
        grid=(rows // 8,),
        out_shape=[whole(atoms, LANES), whole(rows, 3 * TILE, LANES, dtype=BF16)],
        in_specs=[scalar] + [vector] * 2,
        out_specs=[
            pl.BlockSpec((8 * LANES, LANES), lambda i: (i, 0)),
            pl.BlockSpec((8, 3 * TILE, LANES), lambda i: (i, 0, 0)),
        ],
        scratch_shapes=[
            pltpu.VMEM((atoms + 2 * PAD, LANES), F32),
            pltpu.VMEM((2, TILE, LANES), BF16),
        ],
        compiler_params=params,
        cost_estimate=pl.CostEstimate(flops=25 * 10**9, bytes_accessed=3 * 10**7, transcendentals=0),
    )(order, blocks(fields), near_selector())
    forces, solute = pl.pallas_call(
        functools.partial(force_kernel, rows),
        grid=(rows // 8,),
        out_shape=[whole(atoms + 2 * FORCE_PAD, LANES), whole(3, SOL_DEV // LANES, LANES)],
        in_specs=[scalar] * 3
        + [vector] * 3
        + [pl.BlockSpec((8, 3 * TILE, LANES), lambda i: (i, 0, 0)), pl.BlockSpec(memory_space=pl.ANY)],
        out_specs=[pl.BlockSpec(memory_space=pl.ANY), vector],
        scratch_shapes=[
            pltpu.VMEM((3 * atoms + 2 * PAD, LANES), F32),
            pltpu.VMEM((atoms + 2 * FORCE_PAD, LANES), F32),
            pltpu.VMEM((partners, LANES), BF16),
            pltpu.VMEM((partners, LANES), BF16),
            pltpu.VMEM((TILE, LANES), F32),
            pltpu.VMEM((TILE, LANES), F32),
            pltpu.SemaphoreType.DMA,
        ],
        compiler_params=params,
        cost_estimate=pl.CostEstimate(flops=25 * 10**9, bytes_accessed=3 * 10**7, transcendentals=0),
    )(tile_atoms.reshape(rows * partners), entries, order, lower, upper, places, left, table)
    solutes = round_trip(solute, "image")
    block = pl.BlockSpec((3, 8, LANES), lambda i: (0, i, 0))
    small = pltpu.CompilerParams(vmem_limit_bytes=8 * 1024 * 1024)
    out = pl.pallas_call(
        relax_kernel,
        grid=(rows // 8,),
        out_shape=whole(3, rows, LANES),
        in_specs=[block, pl.BlockSpec((8 * LANES, LANES), lambda i: (i + FORCE_PAD // (8 * LANES), 0))],
        out_specs=block,
        compiler_params=small,
        cost_estimate=pl.CostEstimate(flops=10**9, bytes_accessed=2 * 10**7, transcendentals=0),
    )(places, forces)
    solute_shape = whole(images, 3, SOL_DEV // LANES, LANES)
    sums, pushed, path = pl.pallas_call(
        functools.partial(product_kernel, images),
        out_shape=[whole(-(-7 * images // 8) * 8, LANES), solute_shape, solute_shape],
        in_specs=[scalar] + [vector] * (2 * images),
        out_specs=[vector] * 3,
        compiler_params=small,
    )(index, *solutes, *paths)
    out = pl.pallas_call(
        functools.partial(blend_kernel, images),
        grid=(1,),
        out_shape=whole(3, rows, LANES),
        in_specs=[scalar] + [vector] * 3 + [pl.BlockSpec(memory_space=pl.ANY)],
        out_specs=pl.BlockSpec((3, SOL_DEV // LANES, LANES), lambda i: (0, 0, 0)),
        input_output_aliases={4: 0},
        compiler_params=small,
    )(index, summed(sums, "space"), pushed, path, out)
    return out.reshape(1, 3, atoms)


def solution(mesh):
    placed = (
        P("image", None, "space"),
        P("space"),
        P("space"),
        P("image"),
        P("image", "space", None),
        P("image", "space", None),
        P("image", "space", None),
    )
    return jax.shard_map(
        per_device, mesh=mesh, in_specs=placed, out_specs=P("image", None, "space"), check_vma=False
    )
```

```python
import functools

import jax
import jax.numpy as jnp
import numpy as np
from jax import lax
from jax.experimental import pallas as pl
from jax.experimental.pallas import tpu as pltpu
from jax.sharding import PartitionSpec as P

SOL_DEV = 1024
TILE = 128
LANES = 128
FIELDS = 5
FORCE_PAD = 1024
PAD = 8

LJ_COEF = 0.5
CHARGE_COEF = 0.1
SOFT_CORE = 0.09
SLAB_WIDTH = 1.0
STEP_SIZE = 0.2
SPRING_COEF = 1.0
EPSILON = 1e-06
CENTRE = 0.5

F32 = jnp.float32
BF16 = jnp.bfloat16
I32 = jnp.int32
VMEM_LIMIT = 58 * 1024 * 1024

DEPTH, CHARGE, ONE, NORM, LAST = 3, 4, 5, 6, 7
FAR_PIECES = (0, 1, 2, 0, 1, 0)
NEAR_PIECES = (0, 0, 0, 1, 1, 2)


def near_selector():
    chosen = np.zeros((LANES, LANES), np.float32)
    for group, piece in enumerate(NEAR_PIECES):
        for axis in range(3):
            chosen[piece * 8 + axis, group * 8 + axis] = 2.0
        for field in (DEPTH, CHARGE):
            chosen[piece * 8 + field, group * 8 + field] = 1.0
    for piece, group in ((0, 0), (1, 3), (2, 5)):
        chosen[piece * 8 + NORM, group * 8 + ONE] = 1.0
        chosen[ONE, piece * 8 + NORM] = 1.0
    chosen[ONE, LAST] = 1.0
    return jnp.asarray(chosen, BF16)


def near_masks():
    field = np.arange(LANES) % 8
    kinds = [(field != DEPTH) & (field != CHARGE), field == DEPTH, field == CHARGE]
    return jnp.asarray(np.stack([np.tile(kind, (TILE, 1)) for kind in kinds]), BF16)


def two_pieces(values):
    high = values.astype(BF16)
    low = (values - high.astype(F32)).astype(BF16)
    return high, low


def nt_dot(left, right):
    return lax.dot_general(left, right, (((1,), (1,)), ((), ())), preferred_element_type=F32)


def fill_blocks(block_at, count, shift, table, first):
    sublane = lax.broadcasted_iota(I32, (8, LANES), 0)
    move = jnp.where(sublane < 3, jnp.where(sublane == 0, shift - CENTRE, -CENTRE), 0.0)
    blank = jnp.zeros((LANES - 8 * len(FAR_PIECES), LANES), F32)
    for block in range(count):
        values = block_at(block) + move
        norm = jnp.sum(jnp.where(sublane < 3, values * values, 0.0), axis=0, keepdims=True)
        rest = jnp.where(sublane == NORM, -norm, values)
        parts = []
        for _ in range(2):
            parts.append(rest.astype(BF16).astype(F32))
            rest = rest - parts[-1]
        parts.append(rest)
        rows = jnp.concatenate([parts[piece] for piece in FAR_PIECES] + [blank], axis=0)
        start = pl.multiple_of(first + block * LANES + PAD, PAD)
        table[pl.ds(start, LANES), :] = rows.T


def sublane_masks():
    sublane = lax.broadcasted_iota(I32, (8, LANES), 0)
    return [sublane == k for k in range(8)]


def merged(table, entries, masks):
    result = table[pl.ds(entries[0] + PAD, 8), :]
    for k in range(1, 8):
        result = jnp.where(masks[k], table[pl.ds(entries[k] + (PAD - k), 8), :], result)
    return result


def copy_rows(table, entry_of, stage, start, masks):
    parts = [merged(table, [entry_of(start + half + k) for k in range(8)], masks) for half in (0, 8)]
    stage[start : start + 16, :] = jnp.concatenate(parts, axis=0).astype(BF16)


def near_kernel(rows, order_ref, fields_ref, select_ref, table_ref, left_ref, table, stage_a, stage_b):
    turn = pl.program_id(0)

    @pl.when(turn == 0)
    def _():
        def fill(group, carry):
            fill_blocks(lambda block: fields_ref[group * 8 + block], 8, 0.0, table, group * 8 * LANES)
            return carry

        lax.fori_loop(0, rows // 8, fill, 0)

    masks = sublane_masks()

    def load(tile, stage):
        def entry_of(k):
            return order_ref[tile * TILE + k]

        return [
            functools.partial(copy_rows, table, entry_of, stage, start, masks) for start in range(0, TILE, 16)
        ]

    def factors(place, stage):
        left = jnp.dot(stage[...], select_ref[...], preferred_element_type=F32)
        yield
        left_ref[place] = left.astype(BF16)

    @pl.when(turn == 0)
    def _():
        for side in range(2):
            for copy in load(side, stage_a.at[side]):
                copy()

    def step(part, carry):
        tile = turn * 8 + part * 4
        last = rows - 1
        weave(
            [factors(part * 4 + side, stage_a.at[side]) for side in range(2)],
            load(tile + 2, stage_b.at[0]) + load(tile + 3, stage_b.at[1]),
            1,
        )
        weave(
            [factors(part * 4 + 2 + side, stage_b.at[side]) for side in range(2)],
            load(jnp.minimum(tile + 4, last), stage_a.at[0]) + load(jnp.minimum(tile + 5, last), stage_a.at[1]),
            1,
        )
        return carry

    lax.fori_loop(0, 2, step, 0)
    table_ref[...] = table[pl.ds(pl.multiple_of(turn * 8 * LANES + PAD, PAD), 8 * LANES), :]


def tile_sums(left_ref, kinds_ref, place, far, sums):
    others = far[...]
    left = left_ref[place]
    left = jnp.concatenate([left * kinds_ref[kind] for kind in range(3)], axis=0)
    yield
    grams = nt_dot(left, others)
    yield
    chunk = 32
    high, low = [], []
    for start in range(0, TILE, chunk):
        window = grams[start : start + chunk]
        inside = jnp.maximum(window, 0.0)
        root = lax.rsqrt((1.0 + SOFT_CORE) - window)
        depth = grams[TILE + start : TILE + start + chunk]
        charge = grams[2 * TILE + start : 2 * TILE + start + chunk]
        parts = two_pieces(inside * inside * (depth + charge * (root * root * root)))
        high.append(parts[0])
        low.append(parts[1])
        yield
    both = jnp.dot(jnp.concatenate(high + low, axis=0), others, preferred_element_type=F32)
    yield
    sums[...] = both[0:TILE] + both[TILE:]


def weave(stages, copies, parts):
    size = -(-len(copies) // parts)
    for turn, _ in enumerate(zip(*stages)):
        for copy in copies[turn * size : (turn + 1) * size]:
            copy()
    for copy in copies[parts * size :]:
        copy()
    for stage in stages:
        for _ in stage:
            pass


def force_kernel(
    rows, partner_ref, entry_ref, order_ref, lower_ref, upper_ref, place_ref, kinds_ref, left_ref, own_ref,
    force_ref, solute_ref, table, forces, far_a, far_b, sum_a, sum_b, arrival,
):
    turn = pl.program_id(0)
    partners = far_a.shape[1]
    own = rows * LANES

    masks = sublane_masks()

    def load(tile, far):
        def entry_of(k):
            return entry_ref[partner_ref[tile * partners + k]]

        return [
            functools.partial(copy_rows, table, entry_of, far, start, masks)
            for start in range(0, partners, 16)
        ]

    def save(tile, sums):
        def copy(block):
            value = sums[block * 8 : block * 8 + 8, :]
            for k in range(8):
                place = order_ref[tile * TILE + block * 8 + k] + (FORCE_PAD - k)
                pltpu.store(forces.at[pl.ds(place, 8), :], value, mask=masks[k])

        return [functools.partial(copy, block) for block in range(TILE // 8)]

    @pl.when(turn == 0)
    def _():
        own_copy = pltpu.make_async_copy(own_ref, table.at[pl.ds(own + PAD, own), :], arrival)
        own_copy.start()

        def fill(group, carry):
            for ref, first, shift in ((lower_ref, 0, -SLAB_WIDTH), (upper_ref, 2 * own, SLAB_WIDTH)):
                fill_blocks(lambda block: ref[group * 4 + block], 4, shift, table, first + group * 4 * LANES)
            return carry

        lax.fori_loop(0, rows // 4, fill, 0)
        own_copy.wait()
        sum_b[...] = jnp.zeros_like(sum_b)
        for side in range(2):
            for copy in load(side, far_a.at[side]):
                copy()

    def step(part, carry):
        tile = turn * 8 + part * 4
        last = rows - 1
        copies = save(jnp.maximum(tile - 2, 0), sum_b.at[0]) + save(jnp.maximum(tile - 1, 0), sum_b.at[1])
        copies += load(tile + 2, far_b.at[0]) + load(tile + 3, far_b.at[1])
        weave(
            [tile_sums(left_ref, kinds_ref, part * 4 + side, far_a.at[side], sum_a.at[side]) for side in range(2)],
            copies,
            7,
        )
        copies = save(tile, sum_a.at[0]) + save(tile + 1, sum_a.at[1])
        copies += load(jnp.minimum(tile + 4, last), far_a.at[0]) + load(jnp.minimum(tile + 5, last), far_a.at[1])
        weave(
            [tile_sums(left_ref, kinds_ref, part * 4 + 2 + side, far_b.at[side], sum_b.at[side]) for side in range(2)],
            copies,
            7,
        )
        return carry

    lax.fori_loop(0, 2, step, 0)

    @pl.when(turn == pl.num_programs(0) - 1)
    def _():
        for side in range(2):
            for copy in save(rows - 2 + side, sum_b.at[side]):
                copy()

        send = pltpu.make_async_copy(forces, force_ref, arrival)
        send.start()
        for row in range(SOL_DEV // LANES):
            start = FORCE_PAD + row * LANES
            force = row_forces(forces[start : start + LANES, :], [place_ref[axis, row : row + 1, :] for axis in range(3)])
            for axis in range(3):
                solute_ref[axis, row : row + 1, :] = place_ref[axis, row : row + 1, :] + STEP_SIZE * force[axis]
        send.wait()


def row_forces(sums, places):
    across = sums.T
    result = []
    for axis, place in enumerate(places):
        moment = sum(across[first + axis : first + axis + 1] for first in (0, 8, 16))
        result.append((place - CENTRE) * across[ONE : ONE + 1] - moment)
    return result


def relax_kernel(place_ref, force_ref, out_ref):
    for row in range(8):
        places = [place_ref[axis, row : row + 1, :] for axis in range(3)]
        for axis, force in enumerate(row_forces(force_ref[row * LANES : (row + 1) * LANES, :], places)):
            out_ref[axis, row : row + 1, :] = places[axis] + STEP_SIZE * force


def product_kernel(images, index_ref, *refs):
    pushed_refs, path_refs = refs[:images], refs[images : 2 * images]
    sums_ref, pushed, path = refs[2 * images :]
    index = index_ref[0]
    for by in range(images):
        place = lax.rem(index + images - by, images)
        pushed[place] = pushed_refs[by][...]
        path[place] = path_refs[by][...]
    sums_ref[...] = jnp.zeros_like(sums_ref)
    last = images - 1
    tangents = [path[min(k + 1, last)] - path[max(k - 1, 0)] for k in range(images)]

    def put(kind, image, left, right):
        total = jnp.sum(left * right, axis=0)
        sums_ref[kind * images + image : kind * images + image + 1, :] = jnp.sum(total, axis=0, keepdims=True)

    for k in range(images):
        put(0, k, tangents[k], tangents[k])
        put(1, k, pushed[k] - path[k], tangents[k])
        if k < last:
            step = path[k + 1] - path[k]
            gap = pushed[k + 1] - pushed[k]
            put(2, k, step, step)
            put(3, k, gap, gap)
            put(4, k, gap, tangents[k + 1])
            put(5, k, gap, tangents[k])
            put(6, k, tangents[k + 1], tangents[k])


def blend_kernel(images, index_ref, sums_ref, pushed, path, out_in, out_ref):
    del out_in
    index = index_ref[0]
    last = images - 1
    totals = jnp.sum(sums_ref[...], axis=1, keepdims=True)

    def total(kind, image):
        row = kind * images + image
        return totals[row : row + 1, :]

    step_root = [jnp.sqrt(total(2, k) + EPSILON) for k in range(last)]
    shift = []
    for k in range(images):
        tangent_sq = total(0, k)
        value = -total(1, k) / (tangent_sq + EPSILON)
        if 0 < k < last:
            spring = SPRING_COEF * (step_root[k] - step_root[k - 1]) / jnp.sqrt(tangent_sq + EPSILON)
            value = value + STEP_SIZE * spring
        shift.append(value)
    lengths = []
    for k in range(last):
        there, here = shift[k + 1], shift[k]
        length_sq = (
            total(3, k)
            + there * there * total(0, k + 1)
            + here * here * total(0, k)
            + 2.0 * (there * total(4, k) - here * total(5, k) - there * here * total(6, k))
        )
        lengths.append(jnp.sqrt(jnp.maximum(length_sq, 0.0) + EPSILON))
    knots = [jnp.zeros_like(lengths[0])]
    for length in lengths:
        knots.append(knots[-1] + length)

    def pick(values):
        result = values[0]
        for k in range(1, images):
            result = jnp.where(index == k, values[k], result)
        return result

    none = jnp.zeros_like(lengths[0])
    excess = [knots[k] - knots[last] * (k / last) for k in range(images)]
    back = pick([none] + [jnp.clip(excess[k] / lengths[k - 1], 0.0, 1.0) for k in range(1, images)])
    ahead = pick([jnp.clip(-excess[k] / lengths[k], 0.0, 1.0) for k in range(last)] + [none])
    shifts = [pick([shift[min(max(k + by, 0), last)] for k in range(images)]) for by in (-1, 0, 1)]

    def moved(by):
        place = jnp.clip(index + by, 0, last)
        tangent = path[jnp.minimum(place + 1, last)] - path[jnp.maximum(place - 1, 0)]
        return pushed[place] + shifts[by + 1] * tangent

    here = moved(0)
    blended = here + back * (moved(-1) - here) + ahead * (moved(1) - here)
    out_ref[...] = blended


def whole(*shape, dtype=F32):
    return jax.ShapeDtypeStruct(shape, dtype)


def turned(array, axis, by):
    count = lax.axis_size(axis)
    return lax.ppermute(array, axis, [(i, (i + by) % count) for i in range(count)])


def summed(array, axis):
    count = lax.axis_size(axis)
    if count & (count - 1):
        return lax.psum(array, axis)
    by = 1
    while by < count:
        array = array + lax.ppermute(array, axis, [(i, i ^ by) for i in range(count)])
        by *= 2
    return array


def round_trip(array, axis):
    return [array] + [turned(array, axis, by) for by in range(1, lax.axis_size(axis))]


def per_device(positions, strength, charge, rest_scale, cell_order, ghost_index, tile_atoms):
    atoms = positions.shape[2]
    rows = atoms // LANES
    half = atoms // 2
    partners = tile_atoms.shape[2]
    images = lax.axis_size("image")
    index = lax.axis_index("image").reshape(1)

    factor = jnp.where(jnp.arange(atoms) < SOL_DEV, jnp.sqrt(rest_scale[0]), 1.0)
    scaled = jnp.stack([strength * factor * LJ_COEF**0.5, charge * factor * CHARGE_COEF**0.5])
    places = positions.reshape(3, rows, LANES)
    fields = jnp.concatenate([places, scaled.reshape(2, rows, LANES)])
    constant = jnp.stack([jnp.full((rows, LANES), value, F32) for value in (1.0, 0.0, 1.0)])

    def blocks(planes):
        return jnp.concatenate([planes, constant]).transpose(1, 0, 2)

    paths = round_trip(places[:, : SOL_DEV // LANES], "image")
    shell = ghost_index.reshape(2, rows // 2, LANES).astype(F32)
    planes = fields.reshape(FIELDS * rows, LANES)
    lower = turned(jnp.concatenate([planes, shell[1]]), "space", 1)
    upper = turned(jnp.concatenate([planes, shell[0]]), "space", -1)
    entries = jnp.concatenate(
        [
            lower[FIELDS * rows :].astype(I32).reshape(half),
            jnp.arange(atoms, 2 * atoms, dtype=I32),
            upper[FIELDS * rows :].astype(I32).reshape(half) + 2 * atoms,
        ]
    )
    lower, upper = (blocks(side[: FIELDS * rows].reshape(FIELDS, rows, LANES)) for side in (lower, upper))
    order = cell_order.reshape(atoms)
    scalar = pl.BlockSpec(memory_space=pltpu.SMEM)
    vector = pl.BlockSpec(memory_space=pltpu.VMEM)
    params = pltpu.CompilerParams(vmem_limit_bytes=VMEM_LIMIT)
    table, left = pl.pallas_call(
        functools.partial(near_kernel, rows),
        grid=(rows // 8,),
        out_shape=[whole(atoms, LANES), whole(rows, TILE, LANES, dtype=BF16)],
        in_specs=[scalar] + [vector] * 2,
        out_specs=[
            pl.BlockSpec((8 * LANES, LANES), lambda i: (i, 0)),
            pl.BlockSpec((8, TILE, LANES), lambda i: (i, 0, 0)),
        ],
        scratch_shapes=[
            pltpu.VMEM((atoms + 2 * PAD, LANES), F32),
            pltpu.VMEM((2, TILE, LANES), BF16),
            pltpu.VMEM((2, TILE, LANES), BF16),
        ],
        compiler_params=params,
        cost_estimate=pl.CostEstimate(flops=25 * 10**9, bytes_accessed=3 * 10**7, transcendentals=0),
    )(order, blocks(fields), near_selector())
    forces, solute = pl.pallas_call(
        functools.partial(force_kernel, rows),
        grid=(rows // 8,),
        out_shape=[whole(atoms + 2 * FORCE_PAD, LANES), whole(3, SOL_DEV // LANES, LANES)],
        in_specs=[scalar] * 3
        + [vector] * 4
        + [pl.BlockSpec((8, TILE, LANES), lambda i: (i, 0, 0)), pl.BlockSpec(memory_space=pl.ANY)],
        out_specs=[pl.BlockSpec(memory_space=pl.ANY), vector],
        scratch_shapes=[
            pltpu.VMEM((3 * atoms + 2 * PAD, LANES), F32),
            pltpu.VMEM((atoms + 2 * FORCE_PAD, LANES), F32),
            pltpu.VMEM((2, partners, LANES), BF16),
            pltpu.VMEM((2, partners, LANES), BF16),
            pltpu.VMEM((2, TILE, LANES), F32),
            pltpu.VMEM((2, TILE, LANES), F32),
            pltpu.SemaphoreType.DMA,
        ],
        compiler_params=params,
        cost_estimate=pl.CostEstimate(flops=25 * 10**9, bytes_accessed=3 * 10**7, transcendentals=0),
    )(tile_atoms.reshape(rows * partners), entries, order, lower, upper, places, near_masks(), left, table)
    solutes = round_trip(solute, "image")
    block = pl.BlockSpec((3, 8, LANES), lambda i: (0, i, 0))
    small = pltpu.CompilerParams(vmem_limit_bytes=8 * 1024 * 1024)
    out = pl.pallas_call(
        relax_kernel,
        grid=(rows // 8,),
        out_shape=whole(3, rows, LANES),
        in_specs=[block, pl.BlockSpec((8 * LANES, LANES), lambda i: (i + FORCE_PAD // (8 * LANES), 0))],
        out_specs=block,
        compiler_params=small,
        cost_estimate=pl.CostEstimate(flops=10**9, bytes_accessed=2 * 10**7, transcendentals=0),
    )(places, forces)
    solute_shape = whole(images, 3, SOL_DEV // LANES, LANES)
    sums, pushed, path = pl.pallas_call(
        functools.partial(product_kernel, images),
        out_shape=[whole(-(-7 * images // 8) * 8, LANES), solute_shape, solute_shape],
        in_specs=[scalar] + [vector] * (2 * images),
        out_specs=[vector] * 3,
        compiler_params=small,
    )(index, *solutes, *paths)
    out = pl.pallas_call(
        functools.partial(blend_kernel, images),
        grid=(1,),
        out_shape=whole(3, rows, LANES),
        in_specs=[scalar] + [vector] * 3 + [pl.BlockSpec(memory_space=pl.ANY)],
        out_specs=pl.BlockSpec((3, SOL_DEV // LANES, LANES), lambda i: (0, 0, 0)),
        input_output_aliases={4: 0},
        compiler_params=small,
    )(index, summed(sums, "space"), pushed, path, out)
    return out.reshape(1, 3, atoms)


def solution(mesh):
    placed = (
        P("image", None, "space"),
        P("space"),
        P("space"),
        P("image"),
        P("image", "space", None),
        P("image", "space", None),
        P("image", "space", None),
    )
    return jax.shard_map(
        per_device, mesh=mesh, in_specs=placed, out_specs=P("image", None, "space"), check_vma=False
    )
```

```python
import functools

import jax
import jax.numpy as jnp
import numpy as np
from jax import lax
from jax.experimental import pallas as pl
from jax.experimental.pallas import tpu as pltpu
from jax.sharding import PartitionSpec as P

SOL_DEV = 1024
TILE = 128
LANES = 128
FIELDS = 5
FORCE_PAD = 1024
PAD = 8

LJ_COEF = 0.5
CHARGE_COEF = 0.1
SOFT_CORE = 0.09
SLAB_WIDTH = 1.0
STEP_SIZE = 0.2
SPRING_COEF = 1.0
EPSILON = 1e-06
CENTRE = 0.5

F32 = jnp.float32
BF16 = jnp.bfloat16
I32 = jnp.int32
VMEM_LIMIT = 58 * 1024 * 1024

DEPTH, CHARGE, ONE, NORM, LAST = 3, 4, 5, 6, 7
FAR_PIECES = (0, 1, 2, 0, 1, 0)
USED = 8 * len(FAR_PIECES)
NEAR_PIECES = (0, 0, 0, 1, 1, 2)


def near_selector():
    chosen = np.zeros((LANES, LANES), np.float32)
    for group, piece in enumerate(NEAR_PIECES):
        for axis in range(3):
            chosen[piece * 8 + axis, group * 8 + axis] = 2.0
        for field in (DEPTH, CHARGE):
            chosen[piece * 8 + field, group * 8 + field] = 1.0
    for piece, group in ((0, 0), (1, 3), (2, 5)):
        chosen[piece * 8 + NORM, group * 8 + ONE] = 1.0
        chosen[ONE, piece * 8 + NORM] = 1.0
    chosen[ONE, LAST] = 1.0
    return jnp.asarray(chosen, BF16)


def near_masks():
    field = np.arange(LANES) % 8
    kinds = [(field != DEPTH) & (field != CHARGE), field == DEPTH, field == CHARGE]
    return jnp.asarray(np.stack([np.tile(kind, (TILE, 1)) for kind in kinds]), BF16)


def two_pieces(values):
    high = values.astype(BF16)
    low = (values - high.astype(F32)).astype(BF16)
    return high, low


def nt_dot(left, right):
    return lax.dot_general(left, right, (((1,), (1,)), ((), ())), preferred_element_type=F32)


def fill_blocks(block_at, count, shift, table, first):
    sublane = lax.broadcasted_iota(I32, (8, LANES), 0)
    move = jnp.where(sublane < 3, jnp.where(sublane == 0, shift - CENTRE, -CENTRE), 0.0)
    for block in range(count):
        values = block_at(block) + move
        norm = jnp.sum(jnp.where(sublane < 3, values * values, 0.0), axis=0, keepdims=True)
        rest = jnp.where(sublane == NORM, -norm, values)
        parts = []
        for _ in range(2):
            parts.append(rest.astype(BF16).astype(F32))
            rest = rest - parts[-1]
        parts.append(rest)
        rows = jnp.concatenate([parts[piece] for piece in FAR_PIECES], axis=0)
        start = pl.multiple_of(first + block * LANES + PAD, PAD)
        table[pl.ds(start, LANES), 0:USED] = rows.T


def sublane_masks():
    sublane = lax.broadcasted_iota(I32, (8, LANES), 0)
    used = lax.broadcasted_iota(I32, (8, LANES), 1) < USED
    return [sublane == k for k in range(8)] + [used]


def merged(table, entries, masks):
    result = table[pl.ds(entries[0] + PAD, 8), :]
    for k in range(1, 8):
        result = jnp.where(masks[k], table[pl.ds(entries[k] + (PAD - k), 8), :], result)
    return jnp.where(masks[8], result, 0.0)


def copy_rows(table, entry_of, stage, start, masks):
    parts = [merged(table, [entry_of(start + half + k) for k in range(8)], masks) for half in (0, 8)]
    stage[start : start + 16, :] = jnp.concatenate(parts, axis=0).astype(BF16)


def near_kernel(rows, order_ref, next_ref, fields_ref, select_ref, table_ref, left_ref, table, stage_a, stage_b):
    turn = pl.program_id(0)

    @pl.when(turn == 0)
    def _():
        def fill(group, carry):
            fill_blocks(lambda block: fields_ref[group * 8 + block], 8, 0.0, table, group * 8 * LANES)
            return carry

        lax.fori_loop(0, rows // 8, fill, 0)

    masks = sublane_masks()

    def load(local, stage):
        ref, first = (order_ref, local) if local < 8 else (next_ref, local - 8)

        def entry_of(k):
            return ref[first * TILE + k]

        return [
            functools.partial(copy_rows, table, entry_of, stage, start, masks) for start in range(0, TILE, 16)
        ]

    def factors(place, stage):
        left = jnp.dot(stage[...], select_ref[...], preferred_element_type=F32)
        yield
        left_ref[place] = left.astype(BF16)

    @pl.when(turn == 0)
    def _():
        for side in range(2):
            for copy in load(side, stage_a.at[side]):
                copy()

    for tile in range(0, 8, 2):
        here, there = (stage_a, stage_b) if tile % 4 == 0 else (stage_b, stage_a)
        weave(
            [factors(tile + side, here.at[side]) for side in range(2)],
            load(tile + 2, there.at[0]) + load(tile + 3, there.at[1]),
            1,
        )
    table_ref[...] = table[pl.ds(pl.multiple_of(turn * 8 * LANES + PAD, PAD), 8 * LANES), :]


def tile_sums(left_ref, kinds_ref, place, far, sums):
    others = far[...]
    left = left_ref[place]
    left = jnp.concatenate([left * kinds_ref[kind] for kind in range(3)], axis=0)
    yield
    grams = nt_dot(left, others)
    yield
    chunk = 32
    high, low = [], []
    for start in range(0, TILE, chunk):
        window = grams[start : start + chunk]
        inside = jnp.maximum(window, 0.0)
        root = lax.rsqrt((1.0 + SOFT_CORE) - window)
        depth = grams[TILE + start : TILE + start + chunk]
        charge = grams[2 * TILE + start : 2 * TILE + start + chunk]
        parts = two_pieces(inside * inside * (depth + charge * (root * root * root)))
        high.append(parts[0])
        low.append(parts[1])
        yield
    both = jnp.dot(jnp.concatenate(high + low, axis=0), others, preferred_element_type=F32)
    yield
    sums[...] = both[0:TILE] + both[TILE:]


def weave(stages, copies, parts):
    size = -(-len(copies) // parts)
    for turn, _ in enumerate(zip(*stages)):
        for copy in copies[turn * size : (turn + 1) * size]:
            copy()
    for copy in copies[parts * size :]:
        copy()
    for stage in stages:
        for _ in stage:
            pass


def force_kernel(
    rows, partner_ref, next_ref, entry_ref, order_ref, before_ref, lower_ref, upper_ref, place_ref, kinds_ref, left_ref, own_ref,
    force_ref, solute_ref, table, forces, far_a, far_b, sum_a, sum_b, arrival,
):
    turn = pl.program_id(0)
    partners = far_a.shape[1]
    own = rows * LANES

    masks = sublane_masks()

    def load(local, far):
        ref, first = (partner_ref, local) if local < 8 else (next_ref, local - 8)

        def entry_of(k):
            return entry_ref[ref[first * partners + k]]

        return [
            functools.partial(copy_rows, table, entry_of, far, start, masks)
            for start in range(0, partners, 16)
        ]

    def save(local, sums):
        ref, first = (order_ref, local) if local >= 0 else (before_ref, local + 8)

        def copy(block):
            value = sums[block * 8 : block * 8 + 8, :]
            for k in range(8):
                place = ref[first * TILE + block * 8 + k] + (FORCE_PAD - k)
                pltpu.store(forces.at[pl.ds(place, 8), :], value, mask=masks[k])

        return [functools.partial(copy, block) for block in range(TILE // 8)]

    @pl.when(turn == 0)
    def _():
        own_copy = pltpu.make_async_copy(own_ref, table.at[pl.ds(own + PAD, own), :], arrival)
        own_copy.start()

        def fill(group, carry):
            for ref, first, shift in ((lower_ref, 0, -SLAB_WIDTH), (upper_ref, 2 * own, SLAB_WIDTH)):
                fill_blocks(lambda block: ref[group * 4 + block], 4, shift, table, first + group * 4 * LANES)
            return carry

        lax.fori_loop(0, rows // 4, fill, 0)
        own_copy.wait()
        sum_b[...] = jnp.zeros_like(sum_b)
        for side in range(2):
            for copy in load(side, far_a.at[side]):
                copy()

    for tile in range(0, 8, 2):
        far, far_next, sums, sums_before = (
            (far_a, far_b, sum_a, sum_b) if tile % 4 == 0 else (far_b, far_a, sum_b, sum_a)
        )
        copies = save(tile - 2, sums_before.at[0]) + save(tile - 1, sums_before.at[1])
        copies += load(tile + 2, far_next.at[0]) + load(tile + 3, far_next.at[1])
        weave(
            [tile_sums(left_ref, kinds_ref, tile + side, far.at[side], sums.at[side]) for side in range(2)],
            copies,
            7,
        )

    @pl.when(turn == pl.num_programs(0) - 1)
    def _():
        for side in range(2):
            for copy in save(6 + side, sum_b.at[side]):
                copy()

        send = pltpu.make_async_copy(forces, force_ref, arrival)
        send.start()
        for row in range(SOL_DEV // LANES):
            start = FORCE_PAD + row * LANES
            force = row_forces(forces[start : start + LANES, :], [place_ref[axis, row : row + 1, :] for axis in range(3)])
            for axis in range(3):
                solute_ref[axis, row : row + 1, :] = place_ref[axis, row : row + 1, :] + STEP_SIZE * force[axis]
        send.wait()


def row_forces(sums, places):
    across = sums.T
    result = []
    for axis, place in enumerate(places):
        moment = sum(across[first + axis : first + axis + 1] for first in (0, 8, 16))
        result.append((place - CENTRE) * across[ONE : ONE + 1] - moment)
    return result


def relax_kernel(place_ref, force_ref, out_ref):
    for row in range(8):
        places = [place_ref[axis, row : row + 1, :] for axis in range(3)]
        for axis, force in enumerate(row_forces(force_ref[row * LANES : (row + 1) * LANES, :], places)):
            out_ref[axis, row : row + 1, :] = places[axis] + STEP_SIZE * force


def product_kernel(images, index_ref, *refs):
    pushed_refs, path_refs = refs[:images], refs[images : 2 * images]
    sums_ref, pushed, path = refs[2 * images :]
    index = index_ref[0]
    for by in range(images):
        place = lax.rem(index + images - by, images)
        pushed[place] = pushed_refs[by][...]
        path[place] = path_refs[by][...]
    sums_ref[...] = jnp.zeros_like(sums_ref)
    last = images - 1
    tangents = [path[min(k + 1, last)] - path[max(k - 1, 0)] for k in range(images)]

    def put(kind, image, left, right):
        total = jnp.sum(left * right, axis=0)
        sums_ref[kind * images + image : kind * images + image + 1, :] = jnp.sum(total, axis=0, keepdims=True)

    for k in range(images):
        put(0, k, tangents[k], tangents[k])
        put(1, k, pushed[k] - path[k], tangents[k])
        if k < last:
            step = path[k + 1] - path[k]
            gap = pushed[k + 1] - pushed[k]
            put(2, k, step, step)
            put(3, k, gap, gap)
            put(4, k, gap, tangents[k + 1])
            put(5, k, gap, tangents[k])
            put(6, k, tangents[k + 1], tangents[k])


def blend_kernel(images, index_ref, sums_ref, pushed, path, out_in, out_ref):
    del out_in
    index = index_ref[0]
    last = images - 1
    totals = jnp.sum(sums_ref[...], axis=1, keepdims=True)

    def total(kind, image):
        row = kind * images + image
        return totals[row : row + 1, :]

    step_root = [jnp.sqrt(total(2, k) + EPSILON) for k in range(last)]
    shift = []
    for k in range(images):
        tangent_sq = total(0, k)
        value = -total(1, k) / (tangent_sq + EPSILON)
        if 0 < k < last:
            spring = SPRING_COEF * (step_root[k] - step_root[k - 1]) / jnp.sqrt(tangent_sq + EPSILON)
            value = value + STEP_SIZE * spring
        shift.append(value)
    lengths = []
    for k in range(last):
        there, here = shift[k + 1], shift[k]
        length_sq = (
            total(3, k)
            + there * there * total(0, k + 1)
            + here * here * total(0, k)
            + 2.0 * (there * total(4, k) - here * total(5, k) - there * here * total(6, k))
        )
        lengths.append(jnp.sqrt(jnp.maximum(length_sq, 0.0) + EPSILON))
    knots = [jnp.zeros_like(lengths[0])]
    for length in lengths:
        knots.append(knots[-1] + length)

    def pick(values):
        result = values[0]
        for k in range(1, images):
            result = jnp.where(index == k, values[k], result)
        return result

    none = jnp.zeros_like(lengths[0])
    excess = [knots[k] - knots[last] * (k / last) for k in range(images)]
    back = pick([none] + [jnp.clip(excess[k] / lengths[k - 1], 0.0, 1.0) for k in range(1, images)])
    ahead = pick([jnp.clip(-excess[k] / lengths[k], 0.0, 1.0) for k in range(last)] + [none])
    shifts = [pick([shift[min(max(k + by, 0), last)] for k in range(images)]) for by in (-1, 0, 1)]

    def moved(by):
        place = jnp.clip(index + by, 0, last)
        tangent = path[jnp.minimum(place + 1, last)] - path[jnp.maximum(place - 1, 0)]
        return pushed[place] + shifts[by + 1] * tangent

    here = moved(0)
    blended = here + back * (moved(-1) - here) + ahead * (moved(1) - here)
    out_ref[...] = blended


def whole(*shape, dtype=F32):
    return jax.ShapeDtypeStruct(shape, dtype)


def turned(array, axis, by):
    count = lax.axis_size(axis)
    return lax.ppermute(array, axis, [(i, (i + by) % count) for i in range(count)])


def summed(array, axis):
    count = lax.axis_size(axis)
    if count & (count - 1):
        return lax.psum(array, axis)
    by = 1
    while by < count:
        array = array + lax.ppermute(array, axis, [(i, i ^ by) for i in range(count)])
        by *= 2
    return array


def round_trip(array, axis):
    return [array] + [turned(array, axis, by) for by in range(1, lax.axis_size(axis))]


def per_device(positions, strength, charge, rest_scale, cell_order, ghost_index, tile_atoms):
    atoms = positions.shape[2]
    rows = atoms // LANES
    half = atoms // 2
    partners = tile_atoms.shape[2]
    images = lax.axis_size("image")
    index = lax.axis_index("image").reshape(1)

    factor = jnp.where(jnp.arange(atoms) < SOL_DEV, jnp.sqrt(rest_scale[0]), 1.0)
    scaled = jnp.stack([strength * factor * LJ_COEF**0.5, charge * factor * CHARGE_COEF**0.5])
    places = positions.reshape(3, rows, LANES)
    fields = jnp.concatenate([places, scaled.reshape(2, rows, LANES)])
    constant = jnp.stack([jnp.full((rows, LANES), value, F32) for value in (1.0, 0.0, 1.0)])

    def blocks(planes):
        return jnp.concatenate([planes, constant]).transpose(1, 0, 2)

    paths = round_trip(places[:, : SOL_DEV // LANES], "image")
    shell = ghost_index.reshape(2, rows // 2, LANES).astype(F32)
    planes = fields.reshape(FIELDS * rows, LANES)
    lower = turned(jnp.concatenate([planes, shell[1]]), "space", 1)
    upper = turned(jnp.concatenate([planes, shell[0]]), "space", -1)
    entries = jnp.concatenate(
        [
            lower[FIELDS * rows :].astype(I32).reshape(half),
            jnp.arange(atoms, 2 * atoms, dtype=I32),
            upper[FIELDS * rows :].astype(I32).reshape(half) + 2 * atoms,
        ]
    )
    lower, upper = (blocks(side[: FIELDS * rows].reshape(FIELDS, rows, LANES)) for side in (lower, upper))
    order = cell_order.reshape(atoms)
    pairs = tile_atoms.reshape(rows * partners)
    scalar = pl.BlockSpec(memory_space=pltpu.SMEM)
    vector = pl.BlockSpec(memory_space=pltpu.VMEM)
    params = pltpu.CompilerParams(vmem_limit_bytes=VMEM_LIMIT)
    last = rows // 8 - 1

    def listed(size, by):
        return pl.BlockSpec((8 * size,), lambda i: (jnp.clip(i + by, 0, last),), memory_space=pltpu.SMEM)

    table, left = pl.pallas_call(
        functools.partial(near_kernel, rows),
        grid=(rows // 8,),
        out_shape=[whole(atoms, LANES), whole(rows, TILE, LANES, dtype=BF16)],
        in_specs=[listed(TILE, 0), listed(TILE, 1)] + [vector] * 2,
        out_specs=[
            pl.BlockSpec((8 * LANES, LANES), lambda i: (i, 0)),
            pl.BlockSpec((8, TILE, LANES), lambda i: (i, 0, 0)),
        ],
        scratch_shapes=[
            pltpu.VMEM((atoms + 2 * PAD, LANES), F32),
            pltpu.VMEM((2, TILE, LANES), BF16),
            pltpu.VMEM((2, TILE, LANES), BF16),
        ],
        compiler_params=params,
        cost_estimate=pl.CostEstimate(flops=25 * 10**9, bytes_accessed=3 * 10**7, transcendentals=0),
    )(order, order, blocks(fields), near_selector())
    forces, solute = pl.pallas_call(
        functools.partial(force_kernel, rows),
        grid=(rows // 8,),
        out_shape=[whole(atoms + 2 * FORCE_PAD, LANES), whole(3, SOL_DEV // LANES, LANES)],
        in_specs=[listed(partners, 0), listed(partners, 1), scalar, listed(TILE, 0), listed(TILE, -1)]
        + [vector] * 4
        + [pl.BlockSpec((8, TILE, LANES), lambda i: (i, 0, 0)), pl.BlockSpec(memory_space=pl.ANY)],
        out_specs=[pl.BlockSpec(memory_space=pl.ANY), vector],
        scratch_shapes=[
            pltpu.VMEM((3 * atoms + 2 * PAD, LANES), F32),
            pltpu.VMEM((atoms + 2 * FORCE_PAD, LANES), F32),
            pltpu.VMEM((2, partners, LANES), BF16),
            pltpu.VMEM((2, partners, LANES), BF16),
            pltpu.VMEM((2, TILE, LANES), F32),
            pltpu.VMEM((2, TILE, LANES), F32),
            pltpu.SemaphoreType.DMA,
        ],
        compiler_params=params,
        cost_estimate=pl.CostEstimate(flops=25 * 10**9, bytes_accessed=3 * 10**7, transcendentals=0),
    )(pairs, pairs, entries, order, order, lower, upper, places, near_masks(), left, table)
    solutes = round_trip(solute, "image")
    block = pl.BlockSpec((3, 8, LANES), lambda i: (0, i, 0))
    small = pltpu.CompilerParams(vmem_limit_bytes=8 * 1024 * 1024)
    out = pl.pallas_call(
        relax_kernel,
        grid=(rows // 8,),
        out_shape=whole(3, rows, LANES),
        in_specs=[block, pl.BlockSpec((8 * LANES, LANES), lambda i: (i + FORCE_PAD // (8 * LANES), 0))],
        out_specs=block,
        compiler_params=small,
        cost_estimate=pl.CostEstimate(flops=10**9, bytes_accessed=2 * 10**7, transcendentals=0),
    )(places, forces)
    solute_shape = whole(images, 3, SOL_DEV // LANES, LANES)
    sums, pushed, path = pl.pallas_call(
        functools.partial(product_kernel, images),
        out_shape=[whole(-(-7 * images // 8) * 8, LANES), solute_shape, solute_shape],
        in_specs=[scalar] + [vector] * (2 * images),
        out_specs=[vector] * 3,
        compiler_params=small,
    )(index, *solutes, *paths)
    out = pl.pallas_call(
        functools.partial(blend_kernel, images),
        grid=(1,),
        out_shape=whole(3, rows, LANES),
        in_specs=[scalar] + [vector] * 3 + [pl.BlockSpec(memory_space=pl.ANY)],
        out_specs=pl.BlockSpec((3, SOL_DEV // LANES, LANES), lambda i: (0, 0, 0)),
        input_output_aliases={4: 0},
        compiler_params=small,
    )(index, summed(sums, "space"), pushed, path, out)
    return out.reshape(1, 3, atoms)


def solution(mesh):
    placed = (
        P("image", None, "space"),
        P("space"),
        P("space"),
        P("image"),
        P("image", "space", None),
        P("image", "space", None),
        P("image", "space", None),
    )
    return jax.shard_map(
        per_device, mesh=mesh, in_specs=placed, out_specs=P("image", None, "space"), check_vma=False
    )
```

```python
import functools
import itertools

import jax
import jax.numpy as jnp
import numpy as np
from jax import lax
from jax.experimental import pallas as pl
from jax.experimental.pallas import tpu as pltpu
from jax.sharding import PartitionSpec as P

SOL_DEV = 1024
TILE = 128
LANES = 128
FIELDS = 5
PAD = 8

LJ_COEF = 0.5
CHARGE_COEF = 0.1
SOFT_CORE = 0.09
SLAB_WIDTH = 1.0
STEP_SIZE = 0.2
SPRING_COEF = 1.0
EPSILON = 1e-06
CENTRE = 0.5

F32 = jnp.float32
BF16 = jnp.bfloat16
I32 = jnp.int32
VMEM_LIMIT = 58 * 1024 * 1024

DEPTH, CHARGE, ONE, NORM, LAST = 3, 4, 5, 6, 7
FAR_PIECES = (0, 1, 2, 0, 1, 0)
USED = 8 * len(FAR_PIECES)
NEAR_PIECES = (0, 0, 0, 1, 1, 2)


def near_selector():
    chosen = np.zeros((LANES, LANES), np.float32)
    for group, piece in enumerate(NEAR_PIECES):
        for axis in range(3):
            chosen[piece * 8 + axis, group * 8 + axis] = 2.0
        for field in (DEPTH, CHARGE):
            chosen[piece * 8 + field, group * 8 + field] = 1.0
    for piece, group in ((0, 0), (1, 3), (2, 5)):
        chosen[piece * 8 + NORM, group * 8 + ONE] = 1.0
        chosen[ONE, piece * 8 + NORM] = 1.0
    chosen[ONE, LAST] = 1.0
    return jnp.asarray(chosen, BF16)


def near_masks():
    field = np.arange(LANES) % 8
    kinds = [(field != DEPTH) & (field != CHARGE), field == DEPTH, field == CHARGE]
    return jnp.asarray(np.stack([np.tile(kind, (TILE, 1)) for kind in kinds]), BF16)


def two_pieces(values):
    high = values.astype(BF16)
    low = (values - high.astype(F32)).astype(BF16)
    return high, low


def nt_dot(left, right):
    return lax.dot_general(left, right, (((1,), (1,)), ((), ())), preferred_element_type=F32)


def fill_blocks(fields_ref, rows, start_row, count, shift, table, first):
    sublane = lax.broadcasted_iota(I32, (8, LANES), 0)
    move = jnp.where(sublane < 3, jnp.where(sublane == 0, shift - CENTRE, -CENTRE), 0.0)
    ones = jnp.ones((8 - FIELDS, LANES), F32)
    for block in range(count):
        values = fields_ref[pl.ds(start_row + block, FIELDS, stride=rows), :]
        values = jnp.concatenate([values, ones], axis=0) + move
        norm = jnp.sum(jnp.where(sublane < 3, values * values, 0.0), axis=0, keepdims=True)
        rest = jnp.where(sublane == NORM, -norm, values)
        parts = []
        for _ in range(2):
            parts.append(rest.astype(BF16).astype(F32))
            rest = rest - parts[-1]
        parts.append(rest)
        used = jnp.concatenate([parts[piece] for piece in FAR_PIECES], axis=0)
        start = pl.multiple_of(first + (start_row + block) * LANES + PAD, PAD)
        table[pl.ds(start, LANES), 0:USED] = used.T


def sublane_masks():
    sublane = lax.broadcasted_iota(I32, (8, LANES), 0)
    used = lax.broadcasted_iota(I32, (8, LANES), 1) < USED
    return [sublane == k for k in range(8)] + [used]


def merged(table, entries, masks):
    result = table[pl.ds(entries[0], 8), :]
    for k in range(1, 8):
        result = jnp.where(masks[k], table[pl.ds(entries[k], 8), :], result)
    return jnp.where(masks[8], result, 0.0)


def copy_rows(table, entry_of, stage, start, masks):
    parts = [merged(table, [entry_of(start + half + k) for k in range(8)], masks) for half in (0, 8)]
    stage[start : start + 16, :] = jnp.concatenate(parts, axis=0).astype(BF16)


def near_kernel(
    rows, order_ref, next_ref, lower_ref, upper_ref, partner_ref, fields_ref, select_ref, left_ref, list_ref,
    table, stage_a, stage_b, lists,
):
    turn = pl.program_id(0)
    half = rows // 2

    @pl.when(turn == 0)
    def _():
        for side, ref in enumerate((lower_ref, upper_ref)):
            spot = slice(side * half, (side + 1) * half)
            low = ref[...] & 255
            lists[spot, 0:LANES] = (ref[...] - low).astype(F32).astype(BF16)
            lists[spot, LANES:] = low.astype(F32).astype(BF16)

        def fill(group, carry):
            fill_blocks(fields_ref, rows, group * 8, 8, 0.0, table, 0)
            return carry

        lax.fori_loop(0, rows // 8, fill, 0)

    def compose(tile):
        entries = partner_ref[0, tile : tile + 1, :]
        width = entries.shape[1]
        grid = lax.broadcasted_iota(I32, (LANES, width), 0)
        hot = jnp.where(grid == (entries & (LANES - 1)), 1.0, 0.0).astype(BF16)
        found = jnp.dot(lists[...], jnp.concatenate([hot, hot], axis=0), preferred_element_type=F32)
        yield
        block = entries >> 7
        low, high = block < half, block >= half + rows
        chosen = jnp.where(low, block, jnp.where(high, block - rows, -8)) - lax.broadcasted_iota(I32, (8, width), 0)
        picked = jnp.zeros((8, width), F32)
        for start in range(0, rows, 8):
            picked = jnp.where(chosen == start, found[start : start + 8], picked)
        atom = jnp.sum(picked, axis=0, keepdims=True).astype(I32)
        yield
        atom = jnp.where(low, atom, jnp.where(high, atom + 2 * rows * LANES, entries + half * LANES))
        atom = atom + PAD - (lax.broadcasted_iota(I32, (1, width), 1) & 7)
        for side in range(width // LANES):
            row = tile * (width // LANES) + side
            list_ref[row : row + 1, :] = atom[:, side * LANES : (side + 1) * LANES]

    masks = sublane_masks()

    def load(local, stage):
        ref, first = (order_ref, local) if local < 8 else (next_ref, local - 8)

        def entry_of(k):
            return ref[first * TILE + k]

        return [
            functools.partial(copy_rows, table, entry_of, stage, start, masks) for start in range(0, TILE, 16)
        ]

    def factors(place, stage):
        left = jnp.dot(stage[...], select_ref[...], preferred_element_type=F32)
        yield
        left_ref[place] = left.astype(BF16)

    @pl.when(turn == 0)
    def _():
        for side in range(2):
            for copy in load(side, stage_a.at[side]):
                copy()

    for tile in range(0, 8, 2):
        here, there = (stage_a, stage_b) if tile % 4 == 0 else (stage_b, stage_a)
        weave(
            [factors(tile + side, here.at[side]) for side in range(2)] + [compose(tile + side) for side in range(2)],
            load(tile + 2, there.at[0]) + load(tile + 3, there.at[1]),
            2,
        )


def tile_sums(left_ref, kinds_ref, place, far, sums):
    others = far[...]
    left = left_ref[place]
    left = jnp.concatenate([left * kinds_ref[kind] for kind in range(3)], axis=0)
    yield
    grams = nt_dot(left, others)
    yield
    chunk = 32
    high, low = [], []
    for start in range(0, TILE, chunk):
        window = grams[start : start + chunk]
        inside = jnp.maximum(window, 0.0)
        root = lax.rsqrt((1.0 + SOFT_CORE) - window)
        depth = grams[TILE + start : TILE + start + chunk]
        charge = grams[2 * TILE + start : 2 * TILE + start + chunk]
        parts = two_pieces(inside * inside * (depth + charge * (root * root * root)))
        high.append(parts[0])
        low.append(parts[1])
        yield
    both = jnp.dot(jnp.concatenate(high + low, axis=0), others, preferred_element_type=F32)
    yield
    sums[...] = both[0:TILE] + both[TILE:]


def weave(stages, copies, parts):
    size = -(-len(copies) // parts)
    for turn, _ in enumerate(itertools.zip_longest(*stages)):
        for copy in copies[turn * size : (turn + 1) * size]:
            copy()


def force_kernel(
    rows, list_ref, next_ref, order_ref, before_ref, lower_ref, fields_ref, upper_ref, kinds_ref, left_ref,
    out_ref, solute_ref, table, forces, far_a, far_b, sum_a, sum_b,
):
    turn = pl.program_id(0)
    partners = far_a.shape[1]
    own = rows * LANES
    masks = sublane_masks()

    def load(local, far):
        ref, first = (list_ref, local) if local < 8 else (next_ref, local - 8)

        def entry_of(k):
            return ref[first * partners + k]

        return [
            functools.partial(copy_rows, table, entry_of, far, start, masks)
            for start in range(0, partners, 16)
        ]

    def save(local, sums):
        ref, first = (order_ref, local) if local >= 0 else (before_ref, local + 8)

        def copy(block):
            value = sums[block * 8 : block * 8 + 8, :]
            for k in range(8):
                place = ref[first * TILE + block * 8 + k]
                pltpu.store(forces.at[pl.ds(place, 8), :], value, mask=masks[k])

        return [functools.partial(copy, block) for block in range(TILE // 8)]

    @pl.when(turn == 0)
    def _():
        def fill(group, carry):
            for domain, ref in enumerate((lower_ref, fields_ref, upper_ref)):
                fill_blocks(ref, rows, group * 4, 4, (domain - 1) * SLAB_WIDTH, table, domain * own)
            return carry

        lax.fori_loop(0, rows // 4, fill, 0)
        sum_b[...] = jnp.zeros_like(sum_b)
        for side in range(2):
            for copy in load(side, far_a.at[side]):
                copy()

    for tile in range(0, 8, 2):
        far, far_next, sums, sums_before = (
            (far_a, far_b, sum_a, sum_b) if tile % 4 == 0 else (far_b, far_a, sum_b, sum_a)
        )
        copies = save(tile - 2, sums_before.at[0]) + save(tile - 1, sums_before.at[1])
        copies += load(tile + 2, far_next.at[0]) + load(tile + 3, far_next.at[1])
        weave(
            [tile_sums(left_ref, kinds_ref, tile + side, far.at[side], sums.at[side]) for side in range(2)],
            copies,
            7,
        )

    @pl.when(turn == pl.num_programs(0) - 1)
    def _():
        for side in range(2):
            for copy in save(6 + side, sum_b.at[side]):
                copy()

        def finish(group, carry):
            for local in range(8):
                row = group * 8 + local
                sums = forces[pl.ds(pl.multiple_of(row * LANES + PAD, PAD), LANES), :]
                places = [fields_ref[pl.ds(axis * rows + row, 1), :] for axis in range(3)]
                for axis, force in enumerate(row_forces(sums, places)):
                    out_ref[axis, pl.ds(row, 1), :] = places[axis] + STEP_SIZE * force
            return carry

        lax.fori_loop(0, rows // 8, finish, 0)
        solute = SOL_DEV // LANES
        solute_ref[0:3] = out_ref[:, 0:solute, :]
        for axis in range(3):
            solute_ref[3 + axis] = fields_ref[axis * rows : axis * rows + solute, :]


def row_forces(sums, places):
    across = sums.T
    result = []
    for axis, place in enumerate(places):
        moment = sum(across[first + axis : first + axis + 1] for first in (0, 8, 16))
        result.append((place - CENTRE) * across[ONE : ONE + 1] - moment)
    return result


def product_kernel(images, index_ref, *refs):
    solute_refs, (sums_ref, pushed, path) = refs[:images], refs[images:]
    index = index_ref[0]
    for by in range(images):
        place = lax.rem(index + images - by, images)
        pushed[place] = solute_refs[by][0:3]
        path[place] = solute_refs[by][3:6]
    sums_ref[...] = jnp.zeros_like(sums_ref)
    last = images - 1
    tangents = [path[min(k + 1, last)] - path[max(k - 1, 0)] for k in range(images)]

    def put(kind, image, left, right):
        total = jnp.sum(left * right, axis=0)
        sums_ref[kind * images + image : kind * images + image + 1, :] = jnp.sum(total, axis=0, keepdims=True)

    for k in range(images):
        put(0, k, tangents[k], tangents[k])
        put(1, k, pushed[k] - path[k], tangents[k])
        if k < last:
            step = path[k + 1] - path[k]
            gap = pushed[k + 1] - pushed[k]
            put(2, k, step, step)
            put(3, k, gap, gap)
            put(4, k, gap, tangents[k + 1])
            put(5, k, gap, tangents[k])
            put(6, k, tangents[k + 1], tangents[k])


def blend_kernel(images, index_ref, sums_ref, pushed, path, out_in, out_ref):
    del out_in
    index = index_ref[0]
    last = images - 1
    totals = jnp.sum(sums_ref[...], axis=1, keepdims=True)

    def total(kind, image):
        row = kind * images + image
        return totals[row : row + 1, :]

    step_root = [jnp.sqrt(total(2, k) + EPSILON) for k in range(last)]
    shift = []
    for k in range(images):
        tangent_sq = total(0, k)
        value = -total(1, k) / (tangent_sq + EPSILON)
        if 0 < k < last:
            spring = SPRING_COEF * (step_root[k] - step_root[k - 1]) / jnp.sqrt(tangent_sq + EPSILON)
            value = value + STEP_SIZE * spring
        shift.append(value)
    lengths = []
    for k in range(last):
        there, here = shift[k + 1], shift[k]
        length_sq = (
            total(3, k)
            + there * there * total(0, k + 1)
            + here * here * total(0, k)
            + 2.0 * (there * total(4, k) - here * total(5, k) - there * here * total(6, k))
        )
        lengths.append(jnp.sqrt(jnp.maximum(length_sq, 0.0) + EPSILON))
    knots = [jnp.zeros_like(lengths[0])]
    for length in lengths:
        knots.append(knots[-1] + length)

    def pick(values):
        result = values[0]
        for k in range(1, images):
            result = jnp.where(index == k, values[k], result)
        return result

    none = jnp.zeros_like(lengths[0])
    excess = [knots[k] - knots[last] * (k / last) for k in range(images)]
    back = pick([none] + [jnp.clip(excess[k] / lengths[k - 1], 0.0, 1.0) for k in range(1, images)])
    ahead = pick([jnp.clip(-excess[k] / lengths[k], 0.0, 1.0) for k in range(last)] + [none])
    shifts = [pick([shift[min(max(k + by, 0), last)] for k in range(images)]) for by in (-1, 0, 1)]

    def moved(by):
        place = jnp.clip(index + by, 0, last)
        tangent = path[jnp.minimum(place + 1, last)] - path[jnp.maximum(place - 1, 0)]
        return pushed[place] + shifts[by + 1] * tangent

    here = moved(0)
    blended = here + back * (moved(-1) - here) + ahead * (moved(1) - here)
    out_ref[...] = blended


def whole(*shape, dtype=F32):
    return jax.ShapeDtypeStruct(shape, dtype)


def turned(array, axis, by):
    count = lax.axis_size(axis)
    return lax.ppermute(array, axis, [(i, (i + by) % count) for i in range(count)])


def summed(array, axis):
    count = lax.axis_size(axis)
    if count & (count - 1):
        return lax.psum(array, axis)
    by = 1
    while by < count:
        array = array + lax.ppermute(array, axis, [(i, i ^ by) for i in range(count)])
        by *= 2
    return array


def round_trip(array, axis):
    return [array] + [turned(array, axis, by) for by in range(1, lax.axis_size(axis))]


def per_device(positions, strength, charge, rest_scale, cell_order, ghost_index, tile_atoms):
    atoms = positions.shape[2]
    rows = atoms // LANES
    partners = tile_atoms.shape[2]
    images = lax.axis_size("image")
    index = lax.axis_index("image").reshape(1)

    factor = jnp.where(jnp.arange(atoms) < SOL_DEV, jnp.sqrt(rest_scale[0]), 1.0)
    scaled = jnp.stack([strength * factor * LJ_COEF**0.5, charge * factor * CHARGE_COEF**0.5])
    places = positions.reshape(3, rows, LANES)
    fields = jnp.concatenate([places, scaled.reshape(2, rows, LANES)]).reshape(FIELDS * rows, LANES)
    shell = ghost_index.reshape(2, rows // 2, LANES)
    lower_list, upper_list = turned(shell[1], "space", 1), turned(shell[0], "space", -1)
    lower, upper = turned(fields, "space", 1), turned(fields, "space", -1)
    order = cell_order.reshape(atoms) + (PAD - jnp.arange(atoms, dtype=I32) % 8)
    scalar = pl.BlockSpec(memory_space=pltpu.SMEM)
    vector = pl.BlockSpec(memory_space=pltpu.VMEM)
    params = pltpu.CompilerParams(vmem_limit_bytes=VMEM_LIMIT)
    last = rows // 8 - 1

    def listed(size, by):
        return pl.BlockSpec((8 * size,), lambda i: (jnp.clip(i + by, 0, last),), memory_space=pltpu.SMEM)

    table = (atoms + 2 * PAD, LANES)
    left, partner_rows = pl.pallas_call(
        functools.partial(near_kernel, rows),
        grid=(rows // 8,),
        out_shape=[whole(rows, TILE, LANES, dtype=BF16), whole(rows * partners // LANES, LANES, dtype=I32)],
        in_specs=[listed(TILE, 0), listed(TILE, 1)]
        + [vector] * 2
        + [pl.BlockSpec((1, 8, partners), lambda i: (0, i, 0))]
        + [vector] * 2,
        out_specs=[
            pl.BlockSpec((8, TILE, LANES), lambda i: (i, 0, 0)),
            pl.BlockSpec((8 * partners // LANES, LANES), lambda i: (i, 0)),
        ],
        scratch_shapes=[
            pltpu.VMEM(table, F32),
            pltpu.VMEM((2, TILE, LANES), BF16),
            pltpu.VMEM((2, TILE, LANES), BF16),
            pltpu.VMEM((rows, 2 * LANES), BF16),
        ],
        compiler_params=params,
        cost_estimate=pl.CostEstimate(flops=25 * 10**9, bytes_accessed=10**7, transcendentals=0),
    )(order, order, lower_list, upper_list, tile_atoms, fields, near_selector())
    pairs = partner_rows.reshape(rows * partners)
    out, solute = pl.pallas_call(
        functools.partial(force_kernel, rows),
        grid=(rows // 8,),
        out_shape=[whole(3, rows, LANES), whole(6, SOL_DEV // LANES, LANES)],
        in_specs=[listed(partners, 0), listed(partners, 1), listed(TILE, 0), listed(TILE, -1)]
        + [vector] * 4
        + [pl.BlockSpec((8, TILE, LANES), lambda i: (i, 0, 0))],
        out_specs=[vector] * 2,
        scratch_shapes=[
            pltpu.VMEM((3 * atoms + 2 * PAD, LANES), F32),
            pltpu.VMEM(table, F32),
            pltpu.VMEM((2, partners, LANES), BF16),
            pltpu.VMEM((2, partners, LANES), BF16),
            pltpu.VMEM((2, TILE, LANES), F32),
            pltpu.VMEM((2, TILE, LANES), F32),
        ],
        compiler_params=params,
        cost_estimate=pl.CostEstimate(flops=25 * 10**9, bytes_accessed=10**7, transcendentals=0),
    )(pairs, pairs, order, order, lower, fields, upper, near_masks(), left)
    solutes = round_trip(solute, "image")
    small = pltpu.CompilerParams(vmem_limit_bytes=8 * 1024 * 1024)
    solute_shape = whole(images, 3, SOL_DEV // LANES, LANES)
    sums, pushed, path = pl.pallas_call(
        functools.partial(product_kernel, images),
        out_shape=[whole(-(-7 * images // 8) * 8, LANES), solute_shape, solute_shape],
        in_specs=[scalar] + [vector] * images,
        out_specs=[vector] * 3,
        compiler_params=small,
    )(index, *solutes)
    out = pl.pallas_call(
        functools.partial(blend_kernel, images),
        grid=(1,),
        out_shape=whole(3, rows, LANES),
        in_specs=[scalar] + [vector] * 3 + [pl.BlockSpec(memory_space=pl.ANY)],
        out_specs=pl.BlockSpec((3, SOL_DEV // LANES, LANES), lambda i: (0, 0, 0)),
        input_output_aliases={4: 0},
        compiler_params=small,
    )(index, summed(sums, "space"), pushed, path, out)
    return out.reshape(1, 3, atoms)


def solution(mesh):
    placed = (
        P("image", None, "space"),
        P("space"),
        P("space"),
        P("image"),
        P("image", "space", None),
        P("image", "space", None),
        P("image", "space", None),
    )
    return jax.shard_map(
        per_device, mesh=mesh, in_specs=placed, out_specs=P("image", None, "space"), check_vma=False
    )
```

```python
import functools
import itertools

import jax
import jax.numpy as jnp
import numpy as np
from jax import lax
from jax.experimental import pallas as pl
from jax.experimental.pallas import tpu as pltpu
from jax.sharding import PartitionSpec as P

SOL_DEV = 1024
TILE = 128
LANES = 128
FIELDS = 5
PAD = 8

LJ_COEF = 0.5
CHARGE_COEF = 0.1
SOFT_CORE = 0.09
SLAB_WIDTH = 1.0
STEP_SIZE = 0.2
SPRING_COEF = 1.0
EPSILON = 1e-06
CENTRE = 0.5

F32 = jnp.float32
BF16 = jnp.bfloat16
I32 = jnp.int32
VMEM_LIMIT = 58 * 1024 * 1024

DEPTH, CHARGE, ONE, NORM, LAST = 3, 4, 5, 6, 7
FAR_PIECES = (0, 1, 2, 0, 1, 0)
USED = 8 * len(FAR_PIECES)
NEAR_PIECES = (0, 0, 0, 1, 1, 2)


def near_selector():
    chosen = np.zeros((LANES, LANES), np.float32)
    for group, piece in enumerate(NEAR_PIECES):
        for axis in range(3):
            chosen[piece * 8 + axis, group * 8 + axis] = 2.0
        for field in (DEPTH, CHARGE):
            chosen[piece * 8 + field, group * 8 + field] = 1.0
    for piece, group in ((0, 0), (1, 3), (2, 5)):
        chosen[piece * 8 + NORM, group * 8 + ONE] = 1.0
        chosen[ONE, piece * 8 + NORM] = 1.0
    chosen[ONE, LAST] = 1.0
    return jnp.asarray(chosen, BF16)


def near_masks():
    field = np.arange(LANES) % 8
    kinds = [(field != DEPTH) & (field != CHARGE), field == DEPTH, field == CHARGE]
    return jnp.asarray(np.stack([np.tile(kind, (TILE, 1)) for kind in kinds]), BF16)


def two_pieces(values):
    high = values.astype(BF16)
    low = (values - high.astype(F32)).astype(BF16)
    return high, low


def nt_dot(left, right):
    return lax.dot_general(left, right, (((1,), (1,)), ((), ())), preferred_element_type=F32)


def fill_blocks(fields_ref, rows, start_row, count, shift, table, first):
    sublane = lax.broadcasted_iota(I32, (8, LANES), 0)
    move = jnp.where(sublane < 3, jnp.where(sublane == 0, shift - CENTRE, -CENTRE), 0.0)
    ones = jnp.ones((8 - FIELDS, LANES), F32)
    for block in range(count):
        values = fields_ref[pl.ds(start_row + block, FIELDS, stride=rows), :]
        values = jnp.concatenate([values, ones], axis=0) + move
        norm = jnp.sum(jnp.where(sublane < 3, values * values, 0.0), axis=0, keepdims=True)
        rest = jnp.where(sublane == NORM, -norm, values)
        parts = []
        for _ in range(2):
            parts.append(rest.astype(BF16).astype(F32))
            rest = rest - parts[-1]
        parts.append(rest)
        used = jnp.concatenate([parts[piece] for piece in FAR_PIECES], axis=0)
        start = pl.multiple_of(first + (start_row + block) * LANES + PAD, PAD)
        table[pl.ds(start, LANES), 0:USED] = used.T


def sublane_masks():
    sublane = lax.broadcasted_iota(I32, (8, LANES), 0)
    used = lax.broadcasted_iota(I32, (8, LANES), 1) < USED
    return [sublane == k for k in range(8)] + [used]


def merged(table, entries, masks):
    result = table[pl.ds(entries[0], 8), :]
    for k in range(1, 8):
        result = jnp.where(masks[k], table[pl.ds(entries[k], 8), :], result)
    return jnp.where(masks[8], result, 0.0)


def copy_rows(table, entry_of, stage, start, masks):
    parts = [merged(table, [entry_of(start + half + k) for k in range(8)], masks) for half in (0, 8)]
    stage[start : start + 16, :] = jnp.concatenate(parts, axis=0).astype(BF16)


def near_kernel(
    rows, order_ref, next_ref, lower_ref, upper_ref, partner_ref, fields_ref, select_ref, left_ref, list_ref,
    table, stage_a, stage_b, lists,
):
    turn = pl.program_id(0)
    half = rows // 2

    @pl.when(turn == 0)
    def _():
        for side, ref in enumerate((lower_ref, upper_ref)):
            spot = slice(side * half, (side + 1) * half)
            low = ref[...] & 255
            lists[spot, 0:LANES] = (ref[...] - low).astype(F32).astype(BF16)
            lists[spot, LANES:] = low.astype(F32).astype(BF16)

        def fill(group, carry):
            fill_blocks(fields_ref, rows, group * 8, 8, 0.0, table, 0)
            return carry

        lax.fori_loop(0, rows // 8, fill, 0)

    def compose(tile):
        entries = partner_ref[0, tile : tile + 1, :]
        width = entries.shape[1]
        grid = lax.broadcasted_iota(I32, (LANES, width), 0)
        hot = jnp.where(grid == (entries & (LANES - 1)), 1.0, 0.0).astype(BF16)
        found = jnp.dot(lists[...], jnp.concatenate([hot, hot], axis=0), preferred_element_type=F32)
        yield
        block = entries >> 7
        low, high = block < half, block >= half + rows
        chosen = jnp.where(low, block, jnp.where(high, block - rows, -8)) - lax.broadcasted_iota(I32, (8, width), 0)
        picked = jnp.zeros((8, width), F32)
        for start in range(0, rows, 8):
            picked = jnp.where(chosen == start, found[start : start + 8], picked)
        atom = jnp.sum(picked, axis=0, keepdims=True).astype(I32)
        yield
        atom = jnp.where(low, atom, jnp.where(high, atom + 2 * rows * LANES, entries + half * LANES))
        atom = atom + PAD - (lax.broadcasted_iota(I32, (1, width), 1) & 7)
        for side in range(width // LANES):
            row = tile * (width // LANES) + side
            list_ref[row : row + 1, :] = atom[:, side * LANES : (side + 1) * LANES]

    masks = sublane_masks()

    def load(local, stage):
        ref, first = (order_ref, local) if local < 8 else (next_ref, local - 8)

        def entry_of(k):
            return ref[first * TILE + k]

        return [
            functools.partial(copy_rows, table, entry_of, stage, start, masks) for start in range(0, TILE, 16)
        ]

    def factors(place, stage):
        left = jnp.dot(stage[...], select_ref[...], preferred_element_type=F32)
        yield
        left_ref[place] = left.astype(BF16)

    @pl.when(turn == 0)
    def _():
        for side in range(2):
            for copy in load(side, stage_a.at[side]):
                copy()

    for tile in range(0, 8, 2):
        here, there = (stage_a, stage_b) if tile % 4 == 0 else (stage_b, stage_a)
        weave(
            [factors(tile + side, here.at[side]) for side in range(2)] + [compose(tile + side) for side in range(2)],
            load(tile + 2, there.at[0]) + load(tile + 3, there.at[1]),
            2,
        )


def tile_sums(left_ref, kinds_ref, place, far, sums):
    others = far[...]
    left = left_ref[place]
    left = jnp.concatenate([left * kinds_ref[kind] for kind in range(3)], axis=0)
    yield
    grams = nt_dot(left, others)
    yield
    chunk = 32
    high, low = [], []
    for start in range(0, TILE, chunk):
        window = grams[start : start + chunk]
        inside = jnp.maximum(window, 0.0)
        root = lax.rsqrt((1.0 + SOFT_CORE) - window)
        depth = grams[TILE + start : TILE + start + chunk]
        charge = grams[2 * TILE + start : 2 * TILE + start + chunk]
        parts = two_pieces(inside * inside * (depth + charge * (root * root * root)))
        high.append(parts[0])
        low.append(parts[1])
        yield
    both = jnp.dot(jnp.concatenate(high + low, axis=0), others, preferred_element_type=F32)
    yield
    sums[...] = both[0:TILE] + both[TILE:]


def weave(stages, copies, parts):
    size = -(-len(copies) // parts)
    for turn, _ in enumerate(itertools.zip_longest(*stages)):
        for copy in copies[turn * size : (turn + 1) * size]:
            copy()


def force_kernel(
    rows, list_ref, next_ref, order_ref, before_ref, lower_ref, fields_ref, upper_ref, kinds_ref, left_ref,
    out_ref, solute_ref, table, forces, far_a, far_b, sum_a, sum_b,
):
    turn = pl.program_id(0)
    partners = far_a.shape[1]
    own = rows * LANES
    masks = sublane_masks()

    def load(local, far):
        ref, first = (list_ref, local) if local < 8 else (next_ref, local - 8)

        def entry_of(k):
            return ref[first * partners + k]

        return [
            functools.partial(copy_rows, table, entry_of, far, start, masks)
            for start in range(0, partners, 16)
        ]

    def save(local, sums):
        ref, first = (order_ref, local) if local >= 0 else (before_ref, local + 8)

        def copy(block):
            value = sums[block * 8 : block * 8 + 8, :]
            for k in range(8):
                place = ref[first * TILE + block * 8 + k]
                pltpu.store(forces.at[pl.ds(place, 8), :], value, mask=masks[k])

        return [functools.partial(copy, block) for block in range(TILE // 8)]

    @pl.when(turn == 0)
    def _():
        def fill(group, carry):
            for domain, ref in enumerate((lower_ref, fields_ref, upper_ref)):
                fill_blocks(ref, rows, group * 4, 4, (domain - 1) * SLAB_WIDTH, table, domain * own)
            return carry

        lax.fori_loop(0, rows // 4, fill, 0)
        sum_b[...] = jnp.zeros_like(sum_b)
        for side in range(2):
            for copy in load(side, far_a.at[side]):
                copy()

    for tile in range(0, 8, 2):
        far, far_next, sums, sums_before = (
            (far_a, far_b, sum_a, sum_b) if tile % 4 == 0 else (far_b, far_a, sum_b, sum_a)
        )
        copies = save(tile - 2, sums_before.at[0]) + save(tile - 1, sums_before.at[1])
        copies += load(tile + 2, far_next.at[0]) + load(tile + 3, far_next.at[1])
        weave(
            [tile_sums(left_ref, kinds_ref, tile + side, far.at[side], sums.at[side]) for side in range(2)],
            copies,
            7,
        )

    @pl.when(turn == pl.num_programs(0) - 1)
    def _():
        for side in range(2):
            for copy in save(6 + side, sum_b.at[side]):
                copy()

        def finish(group, carry):
            for local in range(8):
                row = group * 8 + local
                sums = forces[pl.ds(pl.multiple_of(row * LANES + PAD, PAD), LANES), :]
                places = [fields_ref[pl.ds(axis * rows + row, 1), :] for axis in range(3)]
                for axis, force in enumerate(row_forces(sums, places)):
                    out_ref[axis, pl.ds(row, 1), :] = places[axis] + STEP_SIZE * force
            return carry

        lax.fori_loop(0, rows // 8, finish, 0)
        solute = SOL_DEV // LANES
        solute_ref[0:3] = out_ref[:, 0:solute, :]
        for axis in range(3):
            solute_ref[3 + axis] = fields_ref[axis * rows : axis * rows + solute, :]


def row_forces(sums, places):
    across = sums.T
    result = []
    for axis, place in enumerate(places):
        moment = sum(across[first + axis : first + axis + 1] for first in (0, 8, 16))
        result.append((place - CENTRE) * across[ONE : ONE + 1] - moment)
    return result


def product_kernel(images, index_ref, *refs):
    solute_refs, (sums_ref, pushed, path) = refs[:images], refs[images:]
    index = index_ref[0]
    for by in range(images):
        place = lax.rem(index + images - by, images)
        pushed[place] = solute_refs[by][0:3]
        path[place] = solute_refs[by][3:6]
    sums_ref[...] = jnp.zeros_like(sums_ref)
    last = images - 1
    tangents = [path[min(k + 1, last)] - path[max(k - 1, 0)] for k in range(images)]

    def put(kind, image, left, right):
        total = jnp.sum(left * right, axis=0)
        sums_ref[kind * images + image : kind * images + image + 1, :] = jnp.sum(total, axis=0, keepdims=True)

    for k in range(images):
        put(0, k, tangents[k], tangents[k])
        put(1, k, pushed[k] - path[k], tangents[k])
        if k < last:
            step = path[k + 1] - path[k]
            gap = pushed[k + 1] - pushed[k]
            put(2, k, step, step)
            put(3, k, gap, gap)
            put(4, k, gap, tangents[k + 1])
            put(5, k, gap, tangents[k])
            put(6, k, tangents[k + 1], tangents[k])


def blend_kernel(images, index_ref, sums_ref, pushed, path, out_in, out_ref):
    del out_in
    index = index_ref[0]
    last = images - 1
    totals = jnp.sum(sums_ref[...], axis=1, keepdims=True)

    def total(kind, image):
        row = kind * images + image
        return totals[row : row + 1, :]

    step_root = [jnp.sqrt(total(2, k) + EPSILON) for k in range(last)]
    shift = []
    for k in range(images):
        tangent_sq = total(0, k)
        value = -total(1, k) / (tangent_sq + EPSILON)
        if 0 < k < last:
            spring = SPRING_COEF * (step_root[k] - step_root[k - 1]) / jnp.sqrt(tangent_sq + EPSILON)
            value = value + STEP_SIZE * spring
        shift.append(value)
    lengths = []
    for k in range(last):
        there, here = shift[k + 1], shift[k]
        length_sq = (
            total(3, k)
            + there * there * total(0, k + 1)
            + here * here * total(0, k)
            + 2.0 * (there * total(4, k) - here * total(5, k) - there * here * total(6, k))
        )
        lengths.append(jnp.sqrt(jnp.maximum(length_sq, 0.0) + EPSILON))
    knots = [jnp.zeros_like(lengths[0])]
    for length in lengths:
        knots.append(knots[-1] + length)

    def pick(values):
        result = values[0]
        for k in range(1, images):
            result = jnp.where(index == k, values[k], result)
        return result

    none = jnp.zeros_like(lengths[0])
    excess = [knots[k] - knots[last] * (k / last) for k in range(images)]
    back = pick([none] + [jnp.clip(excess[k] / lengths[k - 1], 0.0, 1.0) for k in range(1, images)])
    ahead = pick([jnp.clip(-excess[k] / lengths[k], 0.0, 1.0) for k in range(last)] + [none])
    shifts = [pick([shift[min(max(k + by, 0), last)] for k in range(images)]) for by in (-1, 0, 1)]

    def moved(by):
        place = jnp.clip(index + by, 0, last)
        tangent = path[jnp.minimum(place + 1, last)] - path[jnp.maximum(place - 1, 0)]
        return pushed[place] + shifts[by + 1] * tangent

    here = moved(0)
    blended = here + back * (moved(-1) - here) + ahead * (moved(1) - here)
    out_ref[...] = blended


def whole(*shape, dtype=F32):
    return jax.ShapeDtypeStruct(shape, dtype)


def turned(array, axis, by):
    count = lax.axis_size(axis)
    return lax.ppermute(array, axis, [(i, (i + by) % count) for i in range(count)])


def summed(array, axis):
    count = lax.axis_size(axis)
    if count & (count - 1):
        return lax.psum(array, axis)
    by = 1
    while by < count:
        array = array + lax.ppermute(array, axis, [(i, i ^ by) for i in range(count)])
        by *= 2
    return array


def round_trip(array, axis):
    return [array] + [turned(array, axis, by) for by in range(1, lax.axis_size(axis))]


def per_device(positions, strength, charge, rest_scale, cell_order, ghost_index, tile_atoms):
    atoms = positions.shape[2]
    rows = atoms // LANES
    partners = tile_atoms.shape[2]
    images = lax.axis_size("image")
    index = lax.axis_index("image").reshape(1)

    factor = jnp.where(jnp.arange(atoms) < SOL_DEV, jnp.sqrt(rest_scale[0]), 1.0)
    scaled = jnp.stack([strength * factor * LJ_COEF**0.5, charge * factor * CHARGE_COEF**0.5])
    places = positions.reshape(3, rows, LANES)
    fields = jnp.concatenate([places, scaled.reshape(2, rows, LANES)]).reshape(FIELDS * rows, LANES)
    shell = ghost_index.reshape(2, rows // 2, LANES)
    lower_list, upper_list = turned(shell[1], "space", 1), turned(shell[0], "space", -1)
    fields, lower_list, upper_list = lax.optimization_barrier((fields, lower_list, upper_list))
    lower, upper = turned(fields, "space", 1), turned(fields, "space", -1)
    order = cell_order.reshape(atoms) + (PAD - jnp.arange(atoms, dtype=I32) % 8)
    scalar = pl.BlockSpec(memory_space=pltpu.SMEM)
    vector = pl.BlockSpec(memory_space=pltpu.VMEM)
    params = pltpu.CompilerParams(vmem_limit_bytes=VMEM_LIMIT)
    last = rows // 8 - 1

    def listed(size, by):
        return pl.BlockSpec((8 * size,), lambda i: (jnp.clip(i + by, 0, last),), memory_space=pltpu.SMEM)

    table = (atoms + 2 * PAD, LANES)
    left, partner_rows = pl.pallas_call(
        functools.partial(near_kernel, rows),
        grid=(rows // 8,),
        out_shape=[whole(rows, TILE, LANES, dtype=BF16), whole(rows * partners // LANES, LANES, dtype=I32)],
        in_specs=[listed(TILE, 0), listed(TILE, 1)]
        + [vector] * 2
        + [pl.BlockSpec((1, 8, partners), lambda i: (0, i, 0))]
        + [vector] * 2,
        out_specs=[
            pl.BlockSpec((8, TILE, LANES), lambda i: (i, 0, 0)),
            pl.BlockSpec((8 * partners // LANES, LANES), lambda i: (i, 0)),
        ],
        scratch_shapes=[
            pltpu.VMEM(table, F32),
            pltpu.VMEM((2, TILE, LANES), BF16),
            pltpu.VMEM((2, TILE, LANES), BF16),
            pltpu.VMEM((rows, 2 * LANES), BF16),
        ],
        compiler_params=params,
        cost_estimate=pl.CostEstimate(flops=25 * 10**9, bytes_accessed=10**7, transcendentals=0),
    )(order, order, lower_list, upper_list, tile_atoms, fields, near_selector())
    pairs = partner_rows.reshape(rows * partners)
    out, solute = pl.pallas_call(
        functools.partial(force_kernel, rows),
        grid=(rows // 8,),
        out_shape=[whole(3, rows, LANES), whole(6, SOL_DEV // LANES, LANES)],
        in_specs=[listed(partners, 0), listed(partners, 1), listed(TILE, 0), listed(TILE, -1)]
        + [vector] * 4
        + [pl.BlockSpec((8, TILE, LANES), lambda i: (i, 0, 0))],
        out_specs=[vector] * 2,
        scratch_shapes=[
            pltpu.VMEM((3 * atoms + 2 * PAD, LANES), F32),
            pltpu.VMEM(table, F32),
            pltpu.VMEM((2, partners, LANES), BF16),
            pltpu.VMEM((2, partners, LANES), BF16),
            pltpu.VMEM((2, TILE, LANES), F32),
            pltpu.VMEM((2, TILE, LANES), F32),
        ],
        compiler_params=params,
        cost_estimate=pl.CostEstimate(flops=25 * 10**9, bytes_accessed=10**7, transcendentals=0),
    )(pairs, pairs, order, order, lower, fields, upper, near_masks(), left)
    solutes = round_trip(solute, "image")
    small = pltpu.CompilerParams(vmem_limit_bytes=8 * 1024 * 1024)
    solute_shape = whole(images, 3, SOL_DEV // LANES, LANES)
    sums, pushed, path = pl.pallas_call(
        functools.partial(product_kernel, images),
        out_shape=[whole(-(-7 * images // 8) * 8, LANES), solute_shape, solute_shape],
        in_specs=[scalar] + [vector] * images,
        out_specs=[vector] * 3,
        compiler_params=small,
    )(index, *solutes)
    out = pl.pallas_call(
        functools.partial(blend_kernel, images),
        grid=(1,),
        out_shape=whole(3, rows, LANES),
        in_specs=[scalar] + [vector] * 3 + [pl.BlockSpec(memory_space=pl.ANY)],
        out_specs=pl.BlockSpec((3, SOL_DEV // LANES, LANES), lambda i: (0, 0, 0)),
        input_output_aliases={4: 0},
        compiler_params=small,
    )(index, summed(sums, "space"), pushed, path, out)
    return out.reshape(1, 3, atoms)


def solution(mesh):
    placed = (
        P("image", None, "space"),
        P("space"),
        P("space"),
        P("image"),
        P("image", "space", None),
        P("image", "space", None),
        P("image", "space", None),
    )
    return jax.shard_map(
        per_device, mesh=mesh, in_specs=placed, out_specs=P("image", None, "space"), check_vma=False
    )
```

```python
import functools
import itertools

import jax
import jax.numpy as jnp
import numpy as np
from jax import lax
from jax.experimental import pallas as pl
from jax.experimental.pallas import tpu as pltpu
from jax.sharding import PartitionSpec as P

SOL_DEV = 1024
TILE = 128
LANES = 128
FIELDS = 5
PAD = 8

LJ_COEF = 0.5
CHARGE_COEF = 0.1
SOFT_CORE = 0.09
SLAB_WIDTH = 1.0
STEP_SIZE = 0.2
SPRING_COEF = 1.0
EPSILON = 1e-06
CENTRE = 0.5

F32 = jnp.float32
BF16 = jnp.bfloat16
I32 = jnp.int32
VMEM_LIMIT = 58 * 1024 * 1024

DEPTH, CHARGE, ONE, NORM, LAST = 3, 4, 5, 6, 7
FAR_PIECES = (0, 1, 2, 0, 1, 0)
ROW = 256
COPY = 64
USED = 8 * len(FAR_PIECES)
NEAR_PIECES = (0, 0, 0, 1, 1, 2)


def near_selector():
    chosen = np.zeros((LANES, LANES), np.float32)
    for group, piece in enumerate(NEAR_PIECES):
        for axis in range(3):
            chosen[piece * 8 + axis, group * 8 + axis] = 2.0
        for field in (DEPTH, CHARGE):
            chosen[piece * 8 + field, group * 8 + field] = 1.0
    for piece in range(3):
        for axis in range(3):
            chosen[piece * 8 + axis, COPY + piece * 8 + axis] = 1.0
    for piece, group in ((0, 0), (1, 3), (2, 5)):
        chosen[piece * 8 + NORM, group * 8 + ONE] = 1.0
        chosen[ONE, piece * 8 + NORM] = 1.0
    chosen[ONE, LAST] = 1.0
    return jnp.asarray(chosen, BF16)


def near_masks():
    lane = np.arange(LANES)
    field = lane % 8
    kinds = [(field != DEPTH) & (field != CHARGE), field == DEPTH, field == CHARGE, lane >= COPY]
    return jnp.asarray(np.stack([np.tile(kind, (TILE, 1)) for kind in kinds]), BF16)


def two_pieces(values):
    high = values.astype(BF16)
    low = (values - high.astype(F32)).astype(BF16)
    return high, low


def nt_dot(left, right):
    return lax.dot_general(left, right, (((1,), (1,)), ((), ())), preferred_element_type=F32)


def fill_blocks(fields_ref, rows, start_row, count, shift, table, first):
    sublane = lax.broadcasted_iota(I32, (8, LANES), 0)
    move = jnp.where(sublane < 3, jnp.where(sublane == 0, shift - CENTRE, -CENTRE), 0.0)
    ones = jnp.ones((8 - FIELDS, LANES), F32)
    for block in range(count):
        values = fields_ref[pl.ds(start_row + block, FIELDS, stride=rows), :]
        values = jnp.concatenate([values, ones], axis=0) + move
        norm = jnp.sum(jnp.where(sublane < 3, values * values, 0.0), axis=0, keepdims=True)
        rest = jnp.where(sublane == NORM, -norm, values)
        parts = []
        for _ in range(2):
            parts.append(rest.astype(BF16).astype(F32))
            rest = rest - parts[-1]
        parts.append(rest)
        used = jnp.concatenate([parts[piece] for piece in FAR_PIECES], axis=0)
        start = pl.multiple_of(first + (start_row + block) * LANES + PAD, PAD)
        table[pl.ds(start, LANES), 0:USED] = used.T


def sublane_masks():
    sublane = lax.broadcasted_iota(I32, (8, LANES), 0)
    used = lax.broadcasted_iota(I32, (8, LANES), 1) < USED
    return [sublane == k for k in range(8)] + [used]


def merged(table, entries, masks):
    result = table[pl.ds(entries[0], 8), :]
    for k in range(1, 8):
        result = jnp.where(masks[k], table[pl.ds(entries[k], 8), :], result)
    return jnp.where(masks[8], result, 0.0)


def copy_rows(table, entry_of, stage, start, masks):
    parts = [merged(table, [entry_of(start + half + k) for k in range(8)], masks) for half in (0, 8)]
    stage[start : start + 16, :] = jnp.concatenate(parts, axis=0).astype(BF16)


def near_kernel(
    rows, order_ref, next_ref, lower_ref, upper_ref, partner_ref, fields_ref, select_ref, left_ref, list_ref,
    table, stage_a, stage_b, lists,
):
    turn = pl.program_id(0)
    half = rows // 2

    @pl.when(turn == 0)
    def _():
        for side, ref in enumerate((lower_ref, upper_ref)):
            spot = slice(side * half, (side + 1) * half)
            low = ref[...] & 255
            lists[spot, 0:LANES] = (ref[...] - low).astype(F32).astype(BF16)
            lists[spot, LANES:] = low.astype(F32).astype(BF16)

        def fill(group, carry):
            fill_blocks(fields_ref, rows, group * 8, 8, 0.0, table, 0)
            return carry

        lax.fori_loop(0, rows // 8, fill, 0)

    def compose(tile):
        entries = partner_ref[0, tile : tile + 1, :]
        width = entries.shape[1]
        grid = lax.broadcasted_iota(I32, (LANES, width), 0)
        hot = jnp.where(grid == (entries & (LANES - 1)), 1.0, 0.0).astype(BF16)
        found = jnp.dot(lists[...], jnp.concatenate([hot, hot], axis=0), preferred_element_type=F32)
        yield
        block = entries >> 7
        low, high = block < half, block >= half + rows
        chosen = jnp.where(low, block, jnp.where(high, block - rows, -8)) - lax.broadcasted_iota(I32, (8, width), 0)
        picked = jnp.zeros((8, width), F32)
        for start in range(0, rows, 8):
            picked = jnp.where(chosen == start, found[start : start + 8], picked)
        atom = jnp.sum(picked, axis=0, keepdims=True).astype(I32)
        yield
        atom = jnp.where(low, atom, jnp.where(high, atom + 2 * rows * LANES, entries + half * LANES))
        atom = atom + PAD - (lax.broadcasted_iota(I32, (1, width), 1) & 7)
        for side in range(width // LANES):
            row = tile * (width // LANES) + side
            list_ref[row : row + 1, :] = atom[:, side * LANES : (side + 1) * LANES]

    masks = sublane_masks()

    def load(local, stage):
        ref, first = (order_ref, local) if local < 8 else (next_ref, local - 8)

        def entry_of(k):
            return ref[first * TILE + k]

        return [
            functools.partial(copy_rows, table, entry_of, stage, start, masks) for start in range(0, TILE, 16)
        ]

    def factors(place, stage):
        left = jnp.dot(stage[...], select_ref[...], preferred_element_type=F32)
        yield
        left_ref[place] = left.astype(BF16)

    @pl.when(turn == 0)
    def _():
        for side in range(2):
            for copy in load(side, stage_a.at[side]):
                copy()

    for tile in range(0, 8, 2):
        here, there = (stage_a, stage_b) if tile % 4 == 0 else (stage_b, stage_a)
        weave(
            [factors(tile + side, here.at[side]) for side in range(2)] + [compose(tile + side) for side in range(2)],
            load(tile + 2, there.at[0]) + load(tile + 3, there.at[1]),
            2,
        )


def tile_sums(left_ref, kinds_ref, place, far, sums):
    others = far[...]
    left = left_ref[place]
    left = jnp.concatenate([left * kinds_ref[kind] for kind in range(3)], axis=0)
    yield
    grams = nt_dot(left, others)
    yield
    chunk = 32
    high, low = [], []
    for start in range(0, TILE, chunk):
        window = grams[start : start + chunk]
        inside = jnp.maximum(window, 0.0)
        root = lax.rsqrt((1.0 + SOFT_CORE) - window)
        depth = grams[TILE + start : TILE + start + chunk]
        charge = grams[2 * TILE + start : 2 * TILE + start + chunk]
        parts = two_pieces(inside * inside * (depth + charge * (root * root * root)))
        high.append(parts[0])
        low.append(parts[1])
        yield
    both = jnp.dot(jnp.concatenate(high + low, axis=0), others, preferred_element_type=F32)
    yield
    sums[...] = both[0:TILE] + both[TILE:] + (left_ref[place] * kinds_ref[3]).astype(F32)


def pair_scatter(numbers, sums, total):
    entries = jnp.concatenate(numbers, axis=1)
    forces = [[], [], []]
    for side in range(2):
        across = sums[side].T
        for axis in range(3):
            moment, place = (
                sum(across[first + axis + 8 * piece : first + axis + 8 * piece + 1] for piece in range(3))
                for first in (0, COPY)
            )
            forces[axis].append(place * across[ONE : ONE + 1] - moment)
    yield
    grid = lax.broadcasted_iota(I32, (ROW, ROW), 0)
    hot = jnp.where(grid == (entries & (ROW - 1)), 1.0, 0.0).astype(BF16)
    yield
    count = total.shape[0] // 3
    mask = lax.broadcasted_iota(I32, (count, ROW), 0) == (entries >> 8)
    high, low = [], []
    for axis in range(3):
        force = jnp.concatenate(forces[axis], axis=1)
        part = force.astype(BF16).astype(F32)
        high.append(jnp.where(mask, part, 0.0).astype(BF16))
        low.append(jnp.where(mask, force - part, 0.0).astype(BF16))
        yield
    parts = [jnp.concatenate(piece, axis=0) for piece in (high, low)]
    total[...] += nt_dot(jnp.concatenate(parts, axis=1), jnp.concatenate([hot, hot], axis=1))


def weave(stages, copies, parts):
    size = -(-len(copies) // parts)
    for turn, _ in enumerate(itertools.zip_longest(*stages)):
        for copy in copies[turn * size : (turn + 1) * size]:
            copy()


def force_kernel(
    rows, list_ref, next_ref, order_ref, before_ref, lower_ref, fields_ref, upper_ref, kinds_ref, left_ref,
    out_ref, solute_ref, table, total, far_a, far_b, sum_a, sum_b,
):
    turn = pl.program_id(0)
    partners = far_a.shape[1]
    own = rows * LANES
    masks = sublane_masks()

    def load(local, far):
        ref, first = (list_ref, local) if local < 8 else (next_ref, local - 8)

        def entry_of(k):
            return ref[first * partners + k]

        return [
            functools.partial(copy_rows, table, entry_of, far, start, masks)
            for start in range(0, partners, 16)
        ]

    def scatter(local, sums):
        ref, first = (order_ref, local) if local >= 0 else (before_ref, local + 8)
        return pair_scatter([ref[first + side : first + side + 1, :] for side in range(2)], sums, total)

    @pl.when(turn == 0)
    def _():
        def fill(group, carry):
            for domain, ref in enumerate((lower_ref, fields_ref, upper_ref)):
                fill_blocks(ref, rows, group * 4, 4, (domain - 1) * SLAB_WIDTH, table, domain * own)
            return carry

        lax.fori_loop(0, rows // 4, fill, 0)
        sum_b[...] = jnp.zeros_like(sum_b)
        total[...] = jnp.zeros_like(total)
        for side in range(2):
            for copy in load(side, far_a.at[side]):
                copy()

    for tile in range(0, 8, 2):
        far, far_next, sums, sums_before = (
            (far_a, far_b, sum_a, sum_b) if tile % 4 == 0 else (far_b, far_a, sum_b, sum_a)
        )
        weave(
            [tile_sums(left_ref, kinds_ref, tile + side, far.at[side], sums.at[side]) for side in range(2)]
            + [scatter(tile - 2, sums_before)],
            load(tile + 2, far_next.at[0]) + load(tile + 3, far_next.at[1]),
            7,
        )

    @pl.when(turn == pl.num_programs(0) - 1)
    def _():
        for _ in scatter(6, sum_b):
            pass
        count = rows * LANES // ROW
        for axis in range(3):
            force = total[axis * count : (axis + 1) * count, :]
            for side in range(ROW // LANES):
                spot = pl.ds(axis * rows + side, count, stride=ROW // LANES)
                out_ref[spot, :] = fields_ref[spot, :] + STEP_SIZE * force[:, side * LANES : (side + 1) * LANES]
        solute = SOL_DEV // LANES
        for axis in range(3):
            solute_ref[axis] = out_ref[axis * rows : axis * rows + solute, :]
            solute_ref[3 + axis] = fields_ref[axis * rows : axis * rows + solute, :]


def product_kernel(images, index_ref, *refs):
    solute_refs, (sums_ref, pushed, path) = refs[:images], refs[images:]
    index = index_ref[0]
    for by in range(images):
        place = lax.rem(index + images - by, images)
        pushed[place] = solute_refs[by][0:3]
        path[place] = solute_refs[by][3:6]
    sums_ref[...] = jnp.zeros_like(sums_ref)
    last = images - 1
    tangents = [path[min(k + 1, last)] - path[max(k - 1, 0)] for k in range(images)]

    def put(kind, image, left, right):
        total = jnp.sum(left * right, axis=0)
        sums_ref[kind * images + image : kind * images + image + 1, :] = jnp.sum(total, axis=0, keepdims=True)

    for k in range(images):
        put(0, k, tangents[k], tangents[k])
        put(1, k, pushed[k] - path[k], tangents[k])
        if k < last:
            step = path[k + 1] - path[k]
            gap = pushed[k + 1] - pushed[k]
            put(2, k, step, step)
            put(3, k, gap, gap)
            put(4, k, gap, tangents[k + 1])
            put(5, k, gap, tangents[k])
            put(6, k, tangents[k + 1], tangents[k])


def blend_kernel(images, index_ref, sums_ref, pushed, path, out_in, out_ref):
    del out_in
    index = index_ref[0]
    last = images - 1
    totals = jnp.sum(sums_ref[...], axis=1, keepdims=True)

    def total(kind, image):
        row = kind * images + image
        return totals[row : row + 1, :]

    step_root = [jnp.sqrt(total(2, k) + EPSILON) for k in range(last)]
    shift = []
    for k in range(images):
        tangent_sq = total(0, k)
        value = -total(1, k) / (tangent_sq + EPSILON)
        if 0 < k < last:
            spring = SPRING_COEF * (step_root[k] - step_root[k - 1]) / jnp.sqrt(tangent_sq + EPSILON)
            value = value + STEP_SIZE * spring
        shift.append(value)
    lengths = []
    for k in range(last):
        there, here = shift[k + 1], shift[k]
        length_sq = (
            total(3, k)
            + there * there * total(0, k + 1)
            + here * here * total(0, k)
            + 2.0 * (there * total(4, k) - here * total(5, k) - there * here * total(6, k))
        )
        lengths.append(jnp.sqrt(jnp.maximum(length_sq, 0.0) + EPSILON))
    knots = [jnp.zeros_like(lengths[0])]
    for length in lengths:
        knots.append(knots[-1] + length)

    def pick(values):
        result = values[0]
        for k in range(1, images):
            result = jnp.where(index == k, values[k], result)
        return result

    none = jnp.zeros_like(lengths[0])
    excess = [knots[k] - knots[last] * (k / last) for k in range(images)]
    back = pick([none] + [jnp.clip(excess[k] / lengths[k - 1], 0.0, 1.0) for k in range(1, images)])
    ahead = pick([jnp.clip(-excess[k] / lengths[k], 0.0, 1.0) for k in range(last)] + [none])
    shifts = [pick([shift[min(max(k + by, 0), last)] for k in range(images)]) for by in (-1, 0, 1)]

    def moved(by):
        place = jnp.clip(index + by, 0, last)
        tangent = path[jnp.minimum(place + 1, last)] - path[jnp.maximum(place - 1, 0)]
        return pushed[place] + shifts[by + 1] * tangent

    here = moved(0)
    blended = here + back * (moved(-1) - here) + ahead * (moved(1) - here)
    out_ref[...] = blended


def whole(*shape, dtype=F32):
    return jax.ShapeDtypeStruct(shape, dtype)


def turned(array, axis, by):
    count = lax.axis_size(axis)
    return lax.ppermute(array, axis, [(i, (i + by) % count) for i in range(count)])


def summed(array, axis):
    count = lax.axis_size(axis)
    if count & (count - 1):
        return lax.psum(array, axis)
    by = 1
    while by < count:
        array = array + lax.ppermute(array, axis, [(i, i ^ by) for i in range(count)])
        by *= 2
    return array


def round_trip(array, axis):
    return [array] + [turned(array, axis, by) for by in range(1, lax.axis_size(axis))]


def per_device(positions, strength, charge, rest_scale, cell_order, ghost_index, tile_atoms):
    atoms = positions.shape[2]
    rows = atoms // LANES
    partners = tile_atoms.shape[2]
    images = lax.axis_size("image")
    index = lax.axis_index("image").reshape(1)

    factor = jnp.where(jnp.arange(atoms) < SOL_DEV, jnp.sqrt(rest_scale[0]), 1.0)
    scaled = jnp.stack([strength * factor * LJ_COEF**0.5, charge * factor * CHARGE_COEF**0.5])
    places = positions.reshape(3, rows, LANES)
    fields = jnp.concatenate([places, scaled.reshape(2, rows, LANES)]).reshape(FIELDS * rows, LANES)
    shell = ghost_index.reshape(2, rows // 2, LANES)
    lower_list, upper_list = turned(shell[1], "space", 1), turned(shell[0], "space", -1)
    fields, lower_list, upper_list = lax.optimization_barrier((fields, lower_list, upper_list))
    lower, upper = turned(fields, "space", 1), turned(fields, "space", -1)
    tile_order = cell_order.reshape(rows, LANES)
    order = cell_order.reshape(atoms) + (PAD - jnp.arange(atoms, dtype=I32) % 8)
    scalar = pl.BlockSpec(memory_space=pltpu.SMEM)
    vector = pl.BlockSpec(memory_space=pltpu.VMEM)
    params = pltpu.CompilerParams(vmem_limit_bytes=VMEM_LIMIT)
    last = rows // 8 - 1

    def listed(size, by):
        return pl.BlockSpec((8 * size,), lambda i: (jnp.clip(i + by, 0, last),), memory_space=pltpu.SMEM)

    table = (atoms + 2 * PAD, LANES)
    left, partner_rows = pl.pallas_call(
        functools.partial(near_kernel, rows),
        grid=(rows // 8,),
        out_shape=[whole(rows, TILE, LANES, dtype=BF16), whole(rows * partners // LANES, LANES, dtype=I32)],
        in_specs=[listed(TILE, 0), listed(TILE, 1)]
        + [vector] * 2
        + [pl.BlockSpec((1, 8, partners), lambda i: (0, i, 0))]
        + [vector] * 2,
        out_specs=[
            pl.BlockSpec((8, TILE, LANES), lambda i: (i, 0, 0)),
            pl.BlockSpec((8 * partners // LANES, LANES), lambda i: (i, 0)),
        ],
        scratch_shapes=[
            pltpu.VMEM(table, F32),
            pltpu.VMEM((2, TILE, LANES), BF16),
            pltpu.VMEM((2, TILE, LANES), BF16),
            pltpu.VMEM((rows, 2 * LANES), BF16),
        ],
        compiler_params=params,
        cost_estimate=pl.CostEstimate(flops=25 * 10**9, bytes_accessed=10**7, transcendentals=0),
    )(order, order, lower_list, upper_list, tile_atoms, fields, near_selector())
    pairs = partner_rows.reshape(rows * partners)
    out, solute = pl.pallas_call(
        functools.partial(force_kernel, rows),
        grid=(rows // 8,),
        out_shape=[whole(3 * rows, LANES), whole(6, SOL_DEV // LANES, LANES)],
        in_specs=[listed(partners, 0), listed(partners, 1)]
        + [pl.BlockSpec((8, LANES), lambda i, by=by: (jnp.maximum(i - by, 0), 0)) for by in (0, 1)]
        + [vector] * 4
        + [pl.BlockSpec((8, TILE, LANES), lambda i: (i, 0, 0))],
        out_specs=[vector] * 2,
        scratch_shapes=[
            pltpu.VMEM((3 * atoms + 2 * PAD, LANES), F32),
            pltpu.VMEM((3 * atoms // ROW, ROW), F32),
            pltpu.VMEM((2, partners, LANES), BF16),
            pltpu.VMEM((2, partners, LANES), BF16),
            pltpu.VMEM((2, TILE, LANES), F32),
            pltpu.VMEM((2, TILE, LANES), F32),
        ],
        compiler_params=params,
        cost_estimate=pl.CostEstimate(flops=25 * 10**9, bytes_accessed=10**7, transcendentals=0),
    )(pairs, pairs, tile_order, tile_order, lower, fields, upper, near_masks(), left)
    out = out.reshape(3, rows, LANES)
    solutes = round_trip(solute, "image")
    small = pltpu.CompilerParams(vmem_limit_bytes=8 * 1024 * 1024)
    solute_shape = whole(images, 3, SOL_DEV // LANES, LANES)
    sums, pushed, path = pl.pallas_call(
        functools.partial(product_kernel, images),
        out_shape=[whole(-(-7 * images // 8) * 8, LANES), solute_shape, solute_shape],
        in_specs=[scalar] + [vector] * images,
        out_specs=[vector] * 3,
        compiler_params=small,
    )(index, *solutes)
    out = pl.pallas_call(
        functools.partial(blend_kernel, images),
        grid=(1,),
        out_shape=whole(3, rows, LANES),
        in_specs=[scalar] + [vector] * 3 + [pl.BlockSpec(memory_space=pl.ANY)],
        out_specs=pl.BlockSpec((3, SOL_DEV // LANES, LANES), lambda i: (0, 0, 0)),
        input_output_aliases={4: 0},
        compiler_params=small,
    )(index, summed(sums, "space"), pushed, path, out)
    return out.reshape(1, 3, atoms)


def solution(mesh):
    placed = (
        P("image", None, "space"),
        P("space"),
        P("space"),
        P("image"),
        P("image", "space", None),
        P("image", "space", None),
        P("image", "space", None),
    )
    return jax.shard_map(
        per_device, mesh=mesh, in_specs=placed, out_specs=P("image", None, "space"), check_vma=False
    )
```

```python
import functools
import itertools

import jax
import jax.numpy as jnp
import numpy as np
from jax import lax
from jax.experimental import pallas as pl
from jax.experimental.pallas import tpu as pltpu
from jax.sharding import PartitionSpec as P

SOL_DEV = 1024
TILE = 128
LANES = 128
FIELDS = 5
PAD = 8

LJ_COEF = 0.5
CHARGE_COEF = 0.1
SOFT_CORE = 0.09
SLAB_WIDTH = 1.0
STEP_SIZE = 0.2
SPRING_COEF = 1.0
EPSILON = 1e-06
CENTRE = 0.5

F32 = jnp.float32
BF16 = jnp.bfloat16
I32 = jnp.int32
VMEM_LIMIT = 58 * 1024 * 1024

DEPTH, CHARGE, ONE, NORM, LAST = 3, 4, 5, 6, 7
FAR_PIECES = (0, 1, 2, 0, 1, 0)
ROW = 256
COPY = 64
USED = 8 * len(FAR_PIECES)
NEAR_PIECES = (0, 0, 0, 1, 1, 2)


def near_selector():
    chosen = np.zeros((LANES, LANES), np.float32)
    for group, piece in enumerate(NEAR_PIECES):
        for axis in range(3):
            chosen[piece * 8 + axis, group * 8 + axis] = 2.0
        for field in (DEPTH, CHARGE):
            chosen[piece * 8 + field, group * 8 + field] = 1.0
    for piece in range(3):
        for axis in range(3):
            chosen[piece * 8 + axis, COPY + piece * 8 + axis] = 1.0
    for piece, group in ((0, 0), (1, 3), (2, 5)):
        chosen[piece * 8 + NORM, group * 8 + ONE] = 1.0
        chosen[ONE, piece * 8 + NORM] = 1.0
    chosen[ONE, LAST] = 1.0
    return jnp.asarray(chosen, BF16)


def near_masks():
    lane = np.arange(LANES)
    field = lane % 8
    kinds = [(field != DEPTH) & (field != CHARGE), field == DEPTH, field == CHARGE, lane >= COPY]
    return jnp.asarray(np.stack([np.tile(kind, (16, 1)) for kind in kinds]), BF16)


def two_pieces(values):
    high = values.astype(BF16)
    low = (values - high.astype(F32)).astype(BF16)
    return high, low


def nt_dot(left, right):
    return lax.dot_general(left, right, (((1,), (1,)), ((), ())), preferred_element_type=F32)


def fill_blocks(fields_ref, rows, start_row, count, shift, table, first):
    sublane = lax.broadcasted_iota(I32, (8, LANES), 0)
    move = jnp.where(sublane < 3, jnp.where(sublane == 0, shift - CENTRE, -CENTRE), 0.0)
    ones = jnp.ones((8 - FIELDS, LANES), F32)
    for block in range(count):
        values = fields_ref[pl.ds(start_row + block, FIELDS, stride=rows), :]
        values = jnp.concatenate([values, ones], axis=0) + move
        norm = jnp.sum(jnp.where(sublane < 3, values * values, 0.0), axis=0, keepdims=True)
        rest = jnp.where(sublane == NORM, -norm, values)
        parts = []
        for _ in range(2):
            parts.append(rest.astype(BF16).astype(F32))
            rest = rest - parts[-1]
        parts.append(rest)
        used = jnp.concatenate([parts[piece] for piece in FAR_PIECES], axis=0)
        start = pl.multiple_of(first + (start_row + block) * LANES + PAD, PAD)
        table[pl.ds(start, LANES), 0:USED] = used.T


def sublane_masks():
    sublane = lax.broadcasted_iota(I32, (8, LANES), 0)
    used = lax.broadcasted_iota(I32, (8, LANES), 1) < USED
    return [sublane == k for k in range(8)] + [used]


def merged(table, entries, masks):
    result = table[pl.ds(entries[0], 8), :]
    for k in range(1, 8):
        result = jnp.where(masks[k], table[pl.ds(entries[k], 8), :], result)
    return jnp.where(masks[8], result, 0.0)


def copy_rows(table, entry_of, stage, start, masks):
    parts = [merged(table, [entry_of(start + half + k) for k in range(8)], masks) for half in (0, 8)]
    stage[start : start + 16, :] = jnp.concatenate(parts, axis=0).astype(BF16)


def near_kernel(
    rows, order_ref, next_ref, lower_ref, upper_ref, partner_ref, fields_ref, select_ref, left_ref, list_ref,
    table, stage_a, stage_b, lists,
):
    turn = pl.program_id(0)
    half = rows // 2

    @pl.when(turn == 0)
    def _():
        for side, ref in enumerate((lower_ref, upper_ref)):
            spot = slice(side * half, (side + 1) * half)
            low = ref[...] & 255
            lists[spot, 0:LANES] = (ref[...] - low).astype(F32).astype(BF16)
            lists[spot, LANES:] = low.astype(F32).astype(BF16)

        def fill(group, carry):
            fill_blocks(fields_ref, rows, group * 8, 8, 0.0, table, 0)
            return carry

        lax.fori_loop(0, rows // 8, fill, 0)

    def compose(tile):
        entries = partner_ref[0, tile : tile + 1, :]
        width = entries.shape[1]
        grid = lax.broadcasted_iota(I32, (LANES, width), 0)
        hot = jnp.where(grid == (entries & (LANES - 1)), 1.0, 0.0).astype(BF16)
        found = jnp.dot(lists[...], jnp.concatenate([hot, hot], axis=0), preferred_element_type=F32)
        yield
        block = entries >> 7
        low, high = block < half, block >= half + rows
        chosen = jnp.where(low, block, jnp.where(high, block - rows, -8)) - lax.broadcasted_iota(I32, (8, width), 0)
        picked = jnp.zeros((8, width), F32)
        for start in range(0, rows, 8):
            picked = jnp.where(chosen == start, found[start : start + 8], picked)
        atom = jnp.sum(picked, axis=0, keepdims=True).astype(I32)
        yield
        atom = jnp.where(low, atom, jnp.where(high, atom + 2 * rows * LANES, entries + half * LANES))
        atom = atom + PAD - (lax.broadcasted_iota(I32, (1, width), 1) & 7)
        for side in range(width // LANES):
            row = tile * (width // LANES) + side
            list_ref[row : row + 1, :] = atom[:, side * LANES : (side + 1) * LANES]

    masks = sublane_masks()

    def load(local, stage):
        ref, first = (order_ref, local) if local < 8 else (next_ref, local - 8)

        def entry_of(k):
            return ref[first * TILE + k]

        return [
            functools.partial(copy_rows, table, entry_of, stage, start, masks) for start in range(0, TILE, 16)
        ]

    def factors(place, stage):
        left = jnp.dot(stage[...], select_ref[...], preferred_element_type=F32)
        yield
        left_ref[place] = left.astype(BF16)

    @pl.when(turn == 0)
    def _():
        for side in range(2):
            for copy in load(side, stage_a.at[side]):
                copy()

    for tile in range(0, 8, 2):
        here, there = (stage_a, stage_b) if tile % 4 == 0 else (stage_b, stage_a)
        weave(
            [factors(tile + side, here.at[side]) for side in range(2)] + [compose(tile + side) for side in range(2)],
            load(tile + 2, there.at[0]) + load(tile + 3, there.at[1]),
            2,
        )


def masked(values, kind):
    blocks = values.reshape(TILE // 16, 16, LANES) * kind[None]
    return blocks.reshape(TILE, LANES)


def tile_sums(left_ref, kinds_ref, place, far, sums):
    others = far[...]
    left = left_ref[place]
    left = jnp.concatenate([masked(left, kinds_ref[kind]) for kind in range(3)], axis=0)
    yield
    grams = nt_dot(left, others)
    yield
    chunk = 32
    high, low = [], []
    for start in range(0, TILE, chunk):
        window = grams[start : start + chunk]
        inside = jnp.maximum(window, 0.0)
        root = lax.rsqrt((1.0 + SOFT_CORE) - window)
        depth = grams[TILE + start : TILE + start + chunk]
        charge = grams[2 * TILE + start : 2 * TILE + start + chunk]
        parts = two_pieces(inside * inside * (depth + charge * (root * root * root)))
        high.append(parts[0])
        low.append(parts[1])
        yield
    both = jnp.dot(jnp.concatenate(high + low, axis=0), others, preferred_element_type=F32)
    yield
    sums[...] = both[0:TILE] + both[TILE:] + masked(left_ref[place], kinds_ref[3]).astype(F32)


def pair_scatter(numbers, sums, total):
    entries = jnp.concatenate(numbers, axis=1)
    forces = [[], [], []]
    for side in range(2):
        across = sums[side].T
        for axis in range(3):
            moment, place = (
                sum(across[first + axis + 8 * piece : first + axis + 8 * piece + 1] for piece in range(3))
                for first in (0, COPY)
            )
            forces[axis].append(place * across[ONE : ONE + 1] - moment)
    yield
    grid = lax.broadcasted_iota(I32, (ROW, ROW), 0)
    hot = jnp.where(grid == (entries & (ROW - 1)), 1.0, 0.0).astype(BF16)
    yield
    count = total.shape[0] // 3
    mask = lax.broadcasted_iota(I32, (count, ROW), 0) == (entries >> 8)
    high, low = [], []
    for axis in range(3):
        force = jnp.concatenate(forces[axis], axis=1)
        part = force.astype(BF16).astype(F32)
        high.append(jnp.where(mask, part, 0.0).astype(BF16))
        low.append(jnp.where(mask, force - part, 0.0).astype(BF16))
        yield
    both = nt_dot(jnp.concatenate(high + low, axis=0), hot)
    total[...] += both[0 : 3 * count] + both[3 * count :]


def weave(stages, copies, parts):
    size = -(-len(copies) // parts)
    for turn, _ in enumerate(itertools.zip_longest(*stages)):
        for copy in copies[turn * size : (turn + 1) * size]:
            copy()


def force_kernel(
    rows, list_ref, next_ref, order_ref, before_ref, lower_ref, fields_ref, upper_ref, kinds_ref, left_ref,
    out_ref, solute_ref, table, total, far_a, far_b, sum_a, sum_b,
):
    turn = pl.program_id(0)
    partners = far_a.shape[1]
    own = rows * LANES
    masks = sublane_masks()

    def load(local, far):
        ref, first = (list_ref, local) if local < 8 else (next_ref, local - 8)

        def entry_of(k):
            return ref[first * partners + k]

        return [
            functools.partial(copy_rows, table, entry_of, far, start, masks)
            for start in range(0, partners, 16)
        ]

    def scatter(local, sums):
        ref, first = (order_ref, local) if local >= 0 else (before_ref, local + 8)
        return pair_scatter([ref[first + side : first + side + 1, :] for side in range(2)], sums, total)

    @pl.when(turn == 0)
    def _():
        def fill(group, carry):
            for domain, ref in enumerate((lower_ref, fields_ref, upper_ref)):
                fill_blocks(ref, rows, group * 4, 4, (domain - 1) * SLAB_WIDTH, table, domain * own)
            return carry

        lax.fori_loop(0, rows // 4, fill, 0)
        sum_b[...] = jnp.zeros_like(sum_b)
        total[...] = jnp.zeros_like(total)
        for side in range(2):
            for copy in load(side, far_a.at[side]):
                copy()

    for tile in range(0, 8, 2):
        far, far_next, sums, sums_before = (
            (far_a, far_b, sum_a, sum_b) if tile % 4 == 0 else (far_b, far_a, sum_b, sum_a)
        )
        weave(
            [tile_sums(left_ref, kinds_ref, tile + side, far.at[side], sums.at[side]) for side in range(2)]
            + [scatter(tile - 2, sums_before)],
            load(tile + 2, far_next.at[0]) + load(tile + 3, far_next.at[1]),
            7,
        )

    @pl.when(turn == pl.num_programs(0) - 1)
    def _():
        for _ in scatter(6, sum_b):
            pass
        count = rows * LANES // ROW
        for axis in range(3):
            force = total[axis * count : (axis + 1) * count, :]
            for side in range(ROW // LANES):
                spot = pl.ds(axis * rows + side, count, stride=ROW // LANES)
                out_ref[spot, :] = fields_ref[spot, :] + STEP_SIZE * force[:, side * LANES : (side + 1) * LANES]
        solute = SOL_DEV // LANES
        for axis in range(3):
            solute_ref[axis] = out_ref[axis * rows : axis * rows + solute, :]
            solute_ref[3 + axis] = fields_ref[axis * rows : axis * rows + solute, :]


def product_kernel(images, index_ref, *refs):
    solute_refs, (sums_ref, pushed, path) = refs[:images], refs[images:]
    index = index_ref[0]
    for by in range(images):
        place = lax.rem(index + images - by, images)
        pushed[place] = solute_refs[by][0:3]
        path[place] = solute_refs[by][3:6]
    sums_ref[...] = jnp.zeros_like(sums_ref)
    last = images - 1
    tangents = [path[min(k + 1, last)] - path[max(k - 1, 0)] for k in range(images)]

    def put(kind, image, left, right):
        total = jnp.sum(left * right, axis=0)
        sums_ref[kind * images + image : kind * images + image + 1, :] = jnp.sum(total, axis=0, keepdims=True)

    for k in range(images):
        put(0, k, tangents[k], tangents[k])
        put(1, k, pushed[k] - path[k], tangents[k])
        if k < last:
            step = path[k + 1] - path[k]
            gap = pushed[k + 1] - pushed[k]
            put(2, k, step, step)
            put(3, k, gap, gap)
            put(4, k, gap, tangents[k + 1])
            put(5, k, gap, tangents[k])
            put(6, k, tangents[k + 1], tangents[k])


def blend_kernel(images, index_ref, sums_ref, pushed, path, out_in, out_ref):
    del out_in
    index = index_ref[0]
    last = images - 1
    totals = jnp.sum(sums_ref[...], axis=1, keepdims=True)

    def total(kind, image):
        row = kind * images + image
        return totals[row : row + 1, :]

    step_root = [jnp.sqrt(total(2, k) + EPSILON) for k in range(last)]
    shift = []
    for k in range(images):
        tangent_sq = total(0, k)
        value = -total(1, k) / (tangent_sq + EPSILON)
        if 0 < k < last:
            spring = SPRING_COEF * (step_root[k] - step_root[k - 1]) / jnp.sqrt(tangent_sq + EPSILON)
            value = value + STEP_SIZE * spring
        shift.append(value)
    lengths = []
    for k in range(last):
        there, here = shift[k + 1], shift[k]
        length_sq = (
            total(3, k)
            + there * there * total(0, k + 1)
            + here * here * total(0, k)
            + 2.0 * (there * total(4, k) - here * total(5, k) - there * here * total(6, k))
        )
        lengths.append(jnp.sqrt(jnp.maximum(length_sq, 0.0) + EPSILON))
    knots = [jnp.zeros_like(lengths[0])]
    for length in lengths:
        knots.append(knots[-1] + length)

    def pick(values):
        result = values[0]
        for k in range(1, images):
            result = jnp.where(index == k, values[k], result)
        return result

    none = jnp.zeros_like(lengths[0])
    excess = [knots[k] - knots[last] * (k / last) for k in range(images)]
    back = pick([none] + [jnp.clip(excess[k] / lengths[k - 1], 0.0, 1.0) for k in range(1, images)])
    ahead = pick([jnp.clip(-excess[k] / lengths[k], 0.0, 1.0) for k in range(last)] + [none])
    shifts = [pick([shift[min(max(k + by, 0), last)] for k in range(images)]) for by in (-1, 0, 1)]

    def moved(by):
        place = jnp.clip(index + by, 0, last)
        tangent = path[jnp.minimum(place + 1, last)] - path[jnp.maximum(place - 1, 0)]
        return pushed[place] + shifts[by + 1] * tangent

    here = moved(0)
    blended = here + back * (moved(-1) - here) + ahead * (moved(1) - here)
    out_ref[...] = blended


def whole(*shape, dtype=F32):
    return jax.ShapeDtypeStruct(shape, dtype)


def turned(array, axis, by):
    count = lax.axis_size(axis)
    return lax.ppermute(array, axis, [(i, (i + by) % count) for i in range(count)])


def summed(array, axis):
    count = lax.axis_size(axis)
    if count & (count - 1):
        return lax.psum(array, axis)

    def crossed(by):
        return lax.ppermute(array, axis, [(i, i ^ by) for i in range(count)])

    array = array + crossed(1)
    return sum((crossed(by) for by in range(2, count, 2)), array)


def round_trip(array, axis):
    return [array] + [turned(array, axis, by) for by in range(1, lax.axis_size(axis))]


def per_device(positions, strength, charge, rest_scale, cell_order, ghost_index, tile_atoms):
    atoms = positions.shape[2]
    rows = atoms // LANES
    partners = tile_atoms.shape[2]
    images = lax.axis_size("image")
    index = lax.axis_index("image").reshape(1)

    factor = jnp.where(jnp.arange(atoms) < SOL_DEV, jnp.sqrt(rest_scale[0]), 1.0)
    scaled = jnp.stack([strength * factor * LJ_COEF**0.5, charge * factor * CHARGE_COEF**0.5])
    places = positions.reshape(3, rows, LANES)
    fields = jnp.concatenate([places, scaled.reshape(2, rows, LANES)]).reshape(FIELDS * rows, LANES)
    shell = ghost_index.reshape(2, rows // 2, LANES)
    lower_list, upper_list = turned(shell[1], "space", 1), turned(shell[0], "space", -1)
    fields, lower_list, upper_list = lax.optimization_barrier((fields, lower_list, upper_list))
    lower, upper = turned(fields, "space", 1), turned(fields, "space", -1)
    tile_order = cell_order.reshape(rows, LANES)
    order = cell_order.reshape(atoms) + (PAD - jnp.arange(atoms, dtype=I32) % 8)
    scalar = pl.BlockSpec(memory_space=pltpu.SMEM)
    vector = pl.BlockSpec(memory_space=pltpu.VMEM)
    params = pltpu.CompilerParams(vmem_limit_bytes=VMEM_LIMIT)
    last = rows // 8 - 1

    def listed(size, by):
        return pl.BlockSpec((8 * size,), lambda i: (jnp.clip(i + by, 0, last),), memory_space=pltpu.SMEM)

    table = (atoms + 2 * PAD, LANES)
    left, partner_rows = pl.pallas_call(
        functools.partial(near_kernel, rows),
        grid=(rows // 8,),
        out_shape=[whole(rows, TILE, LANES, dtype=BF16), whole(rows * partners // LANES, LANES, dtype=I32)],
        in_specs=[listed(TILE, 0), listed(TILE, 1)]
        + [vector] * 2
        + [pl.BlockSpec((1, 8, partners), lambda i: (0, i, 0))]
        + [vector] * 2,
        out_specs=[
            pl.BlockSpec((8, TILE, LANES), lambda i: (i, 0, 0)),
            pl.BlockSpec((8 * partners // LANES, LANES), lambda i: (i, 0)),
        ],
        scratch_shapes=[
            pltpu.VMEM(table, F32),
            pltpu.VMEM((2, TILE, LANES), BF16),
            pltpu.VMEM((2, TILE, LANES), BF16),
            pltpu.VMEM((rows, 2 * LANES), BF16),
        ],
        compiler_params=params,
        cost_estimate=pl.CostEstimate(flops=25 * 10**9, bytes_accessed=10**7, transcendentals=0),
    )(order, order, lower_list, upper_list, tile_atoms, fields, near_selector())
    pairs = partner_rows.reshape(rows * partners)
    out, solute = pl.pallas_call(
        functools.partial(force_kernel, rows),
        grid=(rows // 8,),
        out_shape=[whole(3 * rows, LANES), whole(6, SOL_DEV // LANES, LANES)],
        in_specs=[listed(partners, 0), listed(partners, 1)]
        + [pl.BlockSpec((8, LANES), lambda i, by=by: (jnp.maximum(i - by, 0), 0)) for by in (0, 1)]
        + [vector] * 4
        + [pl.BlockSpec((8, TILE, LANES), lambda i: (i, 0, 0))],
        out_specs=[vector] * 2,
        scratch_shapes=[
            pltpu.VMEM((3 * atoms + 2 * PAD, LANES), F32),
            pltpu.VMEM((3 * atoms // ROW, ROW), F32),
            pltpu.VMEM((2, partners, LANES), BF16),
            pltpu.VMEM((2, partners, LANES), BF16),
            pltpu.VMEM((2, TILE, LANES), F32),
            pltpu.VMEM((2, TILE, LANES), F32),
        ],
        compiler_params=params,
        cost_estimate=pl.CostEstimate(flops=25 * 10**9, bytes_accessed=10**7, transcendentals=0),
    )(pairs, pairs, tile_order, tile_order, lower, fields, upper, near_masks(), left)
    out = out.reshape(3, rows, LANES)
    solutes = round_trip(solute, "image")
    small = pltpu.CompilerParams(vmem_limit_bytes=8 * 1024 * 1024)
    solute_shape = whole(images, 3, SOL_DEV // LANES, LANES)
    sums, pushed, path = pl.pallas_call(
        functools.partial(product_kernel, images),
        out_shape=[whole(-(-7 * images // 8) * 8, LANES), solute_shape, solute_shape],
        in_specs=[scalar] + [vector] * images,
        out_specs=[vector] * 3,
        compiler_params=small,
    )(index, *solutes)
    out = pl.pallas_call(
        functools.partial(blend_kernel, images),
        grid=(1,),
        out_shape=whole(3, rows, LANES),
        in_specs=[scalar] + [vector] * 3 + [pl.BlockSpec(memory_space=pl.ANY)],
        out_specs=pl.BlockSpec((3, SOL_DEV // LANES, LANES), lambda i: (0, 0, 0)),
        input_output_aliases={4: 0},
        compiler_params=small,
    )(index, summed(sums, "space"), pushed, path, out)
    return out.reshape(1, 3, atoms)


def solution(mesh):
    placed = (
        P("image", None, "space"),
        P("space"),
        P("space"),
        P("image"),
        P("image", "space", None),
        P("image", "space", None),
        P("image", "space", None),
    )
    return jax.shard_map(
        per_device, mesh=mesh, in_specs=placed, out_specs=P("image", None, "space"), check_vma=False
    )
```

```python
import functools
import itertools

import jax
import jax.numpy as jnp
import numpy as np
from jax import lax
from jax.experimental import pallas as pl
from jax.experimental.pallas import tpu as pltpu
from jax.sharding import PartitionSpec as P

SOL_DEV = 1024
TILE = 128
LANES = 128
FIELDS = 5
PAD = 8

LJ_COEF = 0.5
CHARGE_COEF = 0.1
SOFT_CORE = 0.09
SLAB_WIDTH = 1.0
STEP_SIZE = 0.2
SPRING_COEF = 1.0
EPSILON = 1e-06
CENTRE = 0.5

F32 = jnp.float32
BF16 = jnp.bfloat16
I32 = jnp.int32
VMEM_LIMIT = 58 * 1024 * 1024

DEPTH, CHARGE, ONE, NORM, LAST = 3, 4, 5, 6, 7
FAR_PIECES = (0, 1, 2, 0, 1, 0)
ROW = 256
COPY = 64
USED = 8 * len(FAR_PIECES)
NEAR_PIECES = (0, 0, 0, 1, 1, 2)


def near_selector():
    chosen = np.zeros((LANES, LANES), np.float32)
    for group, piece in enumerate(NEAR_PIECES):
        for axis in range(3):
            chosen[piece * 8 + axis, group * 8 + axis] = 2.0
        for field in (DEPTH, CHARGE):
            chosen[piece * 8 + field, group * 8 + field] = 1.0
    for piece in range(3):
        for axis in range(3):
            chosen[piece * 8 + axis, COPY + piece * 8 + axis] = 1.0
    for piece, group in ((0, 0), (1, 3), (2, 5)):
        chosen[piece * 8 + NORM, group * 8 + ONE] = 1.0
        chosen[ONE, piece * 8 + NORM] = 1.0
    chosen[ONE, LAST] = 1.0
    return jnp.asarray(chosen, BF16)


def near_masks():
    lane = np.arange(LANES)
    field = lane % 8
    kinds = [(field != DEPTH) & (field != CHARGE), field == DEPTH, field == CHARGE, lane >= COPY]
    return jnp.asarray(np.stack([np.tile(kind, (16, 1)) for kind in kinds]), BF16)


def two_pieces(values):
    high = values.astype(BF16)
    low = (values - high.astype(F32)).astype(BF16)
    return high, low


def nt_dot(left, right):
    return lax.dot_general(left, right, (((1,), (1,)), ((), ())), preferred_element_type=F32)


def fill_blocks(fields_ref, rows, start_row, count, shift, table, first):
    sublane = lax.broadcasted_iota(I32, (8, LANES), 0)
    move = jnp.where(sublane < 3, jnp.where(sublane == 0, shift - CENTRE, -CENTRE), 0.0)
    ones = jnp.ones((8 - FIELDS, LANES), F32)
    corner = lax.broadcasted_iota(I32, (LANES, LANES), 0) == lax.broadcasted_iota(I32, (LANES, LANES), 1)
    eye = jnp.where(corner, 1.0, 0.0).astype(BF16)
    blank = jnp.zeros((LANES - USED, LANES), F32)

    def pieces(block):
        values = fields_ref[pl.ds(start_row + block, FIELDS, stride=rows), :]
        values = jnp.concatenate([values, ones], axis=0) + move
        norm = jnp.sum(jnp.where(sublane < 3, values * values, 0.0), axis=0, keepdims=True)
        rest = jnp.where(sublane == NORM, -norm, values)
        parts = []
        for _ in range(2):
            parts.append(rest.astype(BF16).astype(F32))
            rest = rest - parts[-1]
        parts.append(rest)
        return [parts[piece] for piece in FAR_PIECES]

    def put(block, value):
        start = pl.multiple_of(first + (start_row + block) * LANES + PAD, PAD)
        table[pl.ds(start, LANES), 0:USED] = value

    for block in range(0, count, 4):
        for side in range(2):
            put(block + side, jnp.concatenate(pieces(block + side), axis=0).T)
        both = jnp.concatenate(pieces(block + 2) + [blank] + pieces(block + 3) + [blank], axis=0)
        both = nt_dot(eye, both.astype(BF16))
        for side in range(2):
            put(block + 2 + side, both[:, side * LANES : side * LANES + USED])


def sublane_masks():
    sublane = lax.broadcasted_iota(I32, (8, LANES), 0)
    used = lax.broadcasted_iota(I32, (8, LANES), 1) < USED
    return [sublane == k for k in range(8)] + [used]


def merged(table, entries, masks):
    result = table[pl.ds(entries[0], 8), :]
    for k in range(1, 8):
        result = jnp.where(masks[k], table[pl.ds(entries[k], 8), :], result)
    return jnp.where(masks[8], result, 0.0)


def copy_rows(table, entry_of, stage, start, masks):
    parts = [merged(table, [entry_of(start + half + k) for k in range(8)], masks) for half in (0, 8)]
    stage[start : start + 16, :] = jnp.concatenate(parts, axis=0).astype(BF16)


def near_kernel(
    rows, order_ref, next_ref, lower_ref, upper_ref, partner_ref, fields_ref, select_ref, left_ref, list_ref,
    table, stage_a, stage_b, lists,
):
    turn = pl.program_id(0)
    half = rows // 2

    @pl.when(turn == 0)
    def _():
        for side, ref in enumerate((lower_ref, upper_ref)):
            spot = slice(side * half, (side + 1) * half)
            low = ref[...] & 255
            lists[spot, 0:LANES] = (ref[...] - low).astype(F32).astype(BF16)
            lists[spot, LANES:] = low.astype(F32).astype(BF16)

        def fill(group, carry):
            fill_blocks(fields_ref, rows, group * 8, 8, 0.0, table, 0)
            return carry

        lax.fori_loop(0, rows // 8, fill, 0)

    def compose(tile):
        entries = partner_ref[0, tile : tile + 1, :]
        width = entries.shape[1]
        grid = lax.broadcasted_iota(I32, (LANES, width), 0)
        hot = jnp.where(grid == (entries & (LANES - 1)), 1.0, 0.0).astype(BF16)
        found = jnp.dot(lists[...], jnp.concatenate([hot, hot], axis=0), preferred_element_type=F32)
        yield
        block = entries >> 7
        low, high = block < half, block >= half + rows
        chosen = jnp.where(low, block, jnp.where(high, block - rows, -8)) - lax.broadcasted_iota(I32, (8, width), 0)
        picked = jnp.zeros((8, width), F32)
        for start in range(0, rows, 8):
            picked = jnp.where(chosen == start, found[start : start + 8], picked)
        atom = jnp.sum(picked, axis=0, keepdims=True).astype(I32)
        yield
        atom = jnp.where(low, atom, jnp.where(high, atom + 2 * rows * LANES, entries + half * LANES))
        atom = atom + PAD - (lax.broadcasted_iota(I32, (1, width), 1) & 7)
        for side in range(width // LANES):
            row = tile * (width // LANES) + side
            list_ref[row : row + 1, :] = atom[:, side * LANES : (side + 1) * LANES]

    masks = sublane_masks()

    def load(local, stage):
        ref, first = (order_ref, local) if local < 8 else (next_ref, local - 8)

        def entry_of(k):
            return ref[first * TILE + k]

        return [
            functools.partial(copy_rows, table, entry_of, stage, start, masks) for start in range(0, TILE, 16)
        ]

    def factors(place, stage):
        left = jnp.dot(stage[...], select_ref[...], preferred_element_type=F32)
        yield
        left_ref[place] = left.astype(BF16)

    @pl.when(turn == 0)
    def _():
        for side in range(2):
            for copy in load(side, stage_a.at[side]):
                copy()

    for tile in range(0, 8, 2):
        here, there = (stage_a, stage_b) if tile % 4 == 0 else (stage_b, stage_a)
        weave(
            [factors(tile + side, here.at[side]) for side in range(2)] + [compose(tile + side) for side in range(2)],
            load(tile + 2, there.at[0]) + load(tile + 3, there.at[1]),
            2,
        )


def masked(values, kind):
    blocks = values.reshape(TILE // 16, 16, LANES) * kind[None]
    return blocks.reshape(TILE, LANES)


def tile_sums(left_ref, kinds_ref, place, far, sums):
    others = far[...]
    left = left_ref[place]
    left = jnp.concatenate([masked(left, kinds_ref[kind]) for kind in range(3)], axis=0)
    yield
    grams = nt_dot(left, others)
    yield
    chunk = 32
    high, low = [], []
    for start in range(0, TILE, chunk):
        window = grams[start : start + chunk]
        inside = jnp.maximum(window, 0.0)
        root = lax.rsqrt((1.0 + SOFT_CORE) - window)
        depth = grams[TILE + start : TILE + start + chunk]
        charge = grams[2 * TILE + start : 2 * TILE + start + chunk]
        parts = two_pieces(inside * inside * (depth + charge * (root * root * root)))
        high.append(parts[0])
        low.append(parts[1])
        yield
    both = jnp.dot(jnp.concatenate(high + low, axis=0), others, preferred_element_type=F32)
    yield
    sums[...] = both[0:TILE] + both[TILE:] + masked(left_ref[place], kinds_ref[3]).astype(F32)


def pair_scatter(numbers, sums, total):
    entries = jnp.concatenate(numbers, axis=1)
    forces = [[], [], []]
    for side in range(2):
        across = sums[side].T
        for axis in range(3):
            moment, place = (
                sum(across[first + axis + 8 * piece : first + axis + 8 * piece + 1] for piece in range(3))
                for first in (0, COPY)
            )
            forces[axis].append(place * across[ONE : ONE + 1] - moment)
    yield
    grid = lax.broadcasted_iota(I32, (ROW, ROW), 0)
    hot = jnp.where(grid == (entries & (ROW - 1)), 1.0, 0.0).astype(BF16)
    yield
    count = total.shape[0] // 3
    mask = lax.broadcasted_iota(I32, (count, ROW), 0) == (entries >> 8)
    high, low = [], []
    for axis in range(3):
        force = jnp.concatenate(forces[axis], axis=1)
        part = force.astype(BF16).astype(F32)
        high.append(jnp.where(mask, part, 0.0).astype(BF16))
        low.append(jnp.where(mask, force - part, 0.0).astype(BF16))
        yield
    both = nt_dot(jnp.concatenate(high + low, axis=0), hot)
    total[...] += both[0 : 3 * count] + both[3 * count :]


def weave(stages, copies, parts):
    size = -(-len(copies) // parts)
    for turn, _ in enumerate(itertools.zip_longest(*stages)):
        for copy in copies[turn * size : (turn + 1) * size]:
            copy()


def force_kernel(
    rows, list_ref, next_ref, order_ref, before_ref, lower_ref, fields_ref, upper_ref, kinds_ref, left_ref,
    out_ref, solute_ref, table, total, far_a, far_b, sum_a, sum_b,
):
    turn = pl.program_id(0)
    partners = far_a.shape[1]
    own = rows * LANES
    masks = sublane_masks()

    def load(local, far):
        ref, first = (list_ref, local) if local < 8 else (next_ref, local - 8)

        def entry_of(k):
            return ref[first * partners + k]

        return [
            functools.partial(copy_rows, table, entry_of, far, start, masks)
            for start in range(0, partners, 16)
        ]

    def scatter(local, sums):
        ref, first = (order_ref, local) if local >= 0 else (before_ref, local + 8)
        return pair_scatter([ref[first + side : first + side + 1, :] for side in range(2)], sums, total)

    @pl.when(turn == 0)
    def _():
        def fill(group, carry):
            for domain, ref in enumerate((lower_ref, fields_ref, upper_ref)):
                fill_blocks(ref, rows, group * 4, 4, (domain - 1) * SLAB_WIDTH, table, domain * own)
            return carry

        lax.fori_loop(0, rows // 4, fill, 0)
        sum_b[...] = jnp.zeros_like(sum_b)
        total[...] = jnp.zeros_like(total)
        for side in range(2):
            for copy in load(side, far_a.at[side]):
                copy()

    for tile in range(0, 8, 2):
        far, far_next, sums, sums_before = (
            (far_a, far_b, sum_a, sum_b) if tile % 4 == 0 else (far_b, far_a, sum_b, sum_a)
        )
        weave(
            [tile_sums(left_ref, kinds_ref, tile + side, far.at[side], sums.at[side]) for side in range(2)]
            + [scatter(tile - 2, sums_before)],
            load(tile + 2, far_next.at[0]) + load(tile + 3, far_next.at[1]),
            7,
        )

    @pl.when(turn == pl.num_programs(0) - 1)
    def _():
        for _ in scatter(6, sum_b):
            pass
        count = rows * LANES // ROW
        for axis in range(3):
            force = total[axis * count : (axis + 1) * count, :]
            for side in range(ROW // LANES):
                spot = pl.ds(axis * rows + side, count, stride=ROW // LANES)
                out_ref[spot, :] = fields_ref[spot, :] + STEP_SIZE * force[:, side * LANES : (side + 1) * LANES]
        solute = SOL_DEV // LANES
        for axis in range(3):
            solute_ref[axis] = out_ref[axis * rows : axis * rows + solute, :]
            solute_ref[3 + axis] = fields_ref[axis * rows : axis * rows + solute, :]


def product_kernel(images, index_ref, *refs):
    solute_refs, (sums_ref, pushed, path) = refs[:images], refs[images:]
    index = index_ref[0]
    for by in range(images):
        place = lax.rem(index + images - by, images)
        pushed[place] = solute_refs[by][0:3]
        path[place] = solute_refs[by][3:6]
    sums_ref[...] = jnp.zeros_like(sums_ref)
    last = images - 1
    tangents = [path[min(k + 1, last)] - path[max(k - 1, 0)] for k in range(images)]

    def put(kind, image, left, right):
        total = jnp.sum(left * right, axis=0)
        sums_ref[kind * images + image : kind * images + image + 1, :] = jnp.sum(total, axis=0, keepdims=True)

    for k in range(images):
        put(0, k, tangents[k], tangents[k])
        put(1, k, pushed[k] - path[k], tangents[k])
        if k < last:
            step = path[k + 1] - path[k]
            gap = pushed[k + 1] - pushed[k]
            put(2, k, step, step)
            put(3, k, gap, gap)
            put(4, k, gap, tangents[k + 1])
            put(5, k, gap, tangents[k])
            put(6, k, tangents[k + 1], tangents[k])


def blend_kernel(images, index_ref, sums_ref, pushed, path, out_in, out_ref):
    del out_in
    index = index_ref[0]
    last = images - 1
    totals = jnp.sum(sums_ref[...], axis=1, keepdims=True)

    def total(kind, image):
        row = kind * images + image
        return totals[row : row + 1, :]

    step_root = [jnp.sqrt(total(2, k) + EPSILON) for k in range(last)]
    shift = []
    for k in range(images):
        tangent_sq = total(0, k)
        value = -total(1, k) / (tangent_sq + EPSILON)
        if 0 < k < last:
            spring = SPRING_COEF * (step_root[k] - step_root[k - 1]) / jnp.sqrt(tangent_sq + EPSILON)
            value = value + STEP_SIZE * spring
        shift.append(value)
    lengths = []
    for k in range(last):
        there, here = shift[k + 1], shift[k]
        length_sq = (
            total(3, k)
            + there * there * total(0, k + 1)
            + here * here * total(0, k)
            + 2.0 * (there * total(4, k) - here * total(5, k) - there * here * total(6, k))
        )
        lengths.append(jnp.sqrt(jnp.maximum(length_sq, 0.0) + EPSILON))
    knots = [jnp.zeros_like(lengths[0])]
    for length in lengths:
        knots.append(knots[-1] + length)

    def pick(values):
        result = values[0]
        for k in range(1, images):
            result = jnp.where(index == k, values[k], result)
        return result

    none = jnp.zeros_like(lengths[0])
    excess = [knots[k] - knots[last] * (k / last) for k in range(images)]
    back = pick([none] + [jnp.clip(excess[k] / lengths[k - 1], 0.0, 1.0) for k in range(1, images)])
    ahead = pick([jnp.clip(-excess[k] / lengths[k], 0.0, 1.0) for k in range(last)] + [none])
    shifts = [pick([shift[min(max(k + by, 0), last)] for k in range(images)]) for by in (-1, 0, 1)]

    def moved(by):
        place = jnp.clip(index + by, 0, last)
        tangent = path[jnp.minimum(place + 1, last)] - path[jnp.maximum(place - 1, 0)]
        return pushed[place] + shifts[by + 1] * tangent

    here = moved(0)
    blended = here + back * (moved(-1) - here) + ahead * (moved(1) - here)
    out_ref[...] = blended


def whole(*shape, dtype=F32):
    return jax.ShapeDtypeStruct(shape, dtype)


def turned(array, axis, by):
    count = lax.axis_size(axis)
    return lax.ppermute(array, axis, [(i, (i + by) % count) for i in range(count)])


def summed(array, axis):
    count = lax.axis_size(axis)
    if count & (count - 1):
        return lax.psum(array, axis)

    def crossed(by):
        return lax.ppermute(array, axis, [(i, i ^ by) for i in range(count)])

    array = array + crossed(1)
    return sum((crossed(by) for by in range(2, count, 2)), array)


def round_trip(array, axis):
    return [array] + [turned(array, axis, by) for by in range(1, lax.axis_size(axis))]


def per_device(positions, strength, charge, rest_scale, cell_order, ghost_index, tile_atoms):
    atoms = positions.shape[2]
    rows = atoms // LANES
    partners = tile_atoms.shape[2]
    images = lax.axis_size("image")
    index = lax.axis_index("image").reshape(1)

    factor = jnp.where(jnp.arange(atoms) < SOL_DEV, jnp.sqrt(rest_scale[0]), 1.0)
    scaled = jnp.stack([strength * factor * LJ_COEF**0.5, charge * factor * CHARGE_COEF**0.5])
    places = positions.reshape(3, rows, LANES)
    fields = jnp.concatenate([places, scaled.reshape(2, rows, LANES)]).reshape(FIELDS * rows, LANES)
    shell = ghost_index.reshape(2, rows // 2, LANES)
    lower_list, upper_list = turned(shell[1], "space", 1), turned(shell[0], "space", -1)
    fields, lower_list, upper_list = lax.optimization_barrier((fields, lower_list, upper_list))
    lower, upper = turned(fields, "space", 1), turned(fields, "space", -1)
    tile_order = cell_order.reshape(rows, LANES)
    order = cell_order.reshape(atoms) + (PAD - jnp.arange(atoms, dtype=I32) % 8)
    scalar = pl.BlockSpec(memory_space=pltpu.SMEM)
    vector = pl.BlockSpec(memory_space=pltpu.VMEM)
    params = pltpu.CompilerParams(vmem_limit_bytes=VMEM_LIMIT)
    last = rows // 8 - 1

    def listed(size, by):
        return pl.BlockSpec((8 * size,), lambda i: (jnp.clip(i + by, 0, last),), memory_space=pltpu.SMEM)

    table = (atoms + 2 * PAD, LANES)
    left, partner_rows = pl.pallas_call(
        functools.partial(near_kernel, rows),
        grid=(rows // 8,),
        out_shape=[whole(rows, TILE, LANES, dtype=BF16), whole(rows * partners // LANES, LANES, dtype=I32)],
        in_specs=[listed(TILE, 0), listed(TILE, 1)]
        + [vector] * 2
        + [pl.BlockSpec((1, 8, partners), lambda i: (0, i, 0))]
        + [vector] * 2,
        out_specs=[
            pl.BlockSpec((8, TILE, LANES), lambda i: (i, 0, 0)),
            pl.BlockSpec((8 * partners // LANES, LANES), lambda i: (i, 0)),
        ],
        scratch_shapes=[
            pltpu.VMEM(table, F32),
            pltpu.VMEM((2, TILE, LANES), BF16),
            pltpu.VMEM((2, TILE, LANES), BF16),
            pltpu.VMEM((rows, 2 * LANES), BF16),
        ],
        compiler_params=params,
        cost_estimate=pl.CostEstimate(flops=25 * 10**9, bytes_accessed=10**7, transcendentals=0),
    )(order, order, lower_list, upper_list, tile_atoms, fields, near_selector())
    pairs = partner_rows.reshape(rows * partners)
    out, solute = pl.pallas_call(
        functools.partial(force_kernel, rows),
        grid=(rows // 8,),
        out_shape=[whole(3 * rows, LANES), whole(6, SOL_DEV // LANES, LANES)],
        in_specs=[listed(partners, 0), listed(partners, 1)]
        + [pl.BlockSpec((8, LANES), lambda i, by=by: (jnp.maximum(i - by, 0), 0)) for by in (0, 1)]
        + [vector] * 4
        + [pl.BlockSpec((8, TILE, LANES), lambda i: (i, 0, 0))],
        out_specs=[vector] * 2,
        scratch_shapes=[
            pltpu.VMEM((3 * atoms + 2 * PAD, LANES), F32),
            pltpu.VMEM((3 * atoms // ROW, ROW), F32),
            pltpu.VMEM((2, partners, LANES), BF16),
            pltpu.VMEM((2, partners, LANES), BF16),
            pltpu.VMEM((2, TILE, LANES), F32),
            pltpu.VMEM((2, TILE, LANES), F32),
        ],
        compiler_params=params,
        cost_estimate=pl.CostEstimate(flops=25 * 10**9, bytes_accessed=10**7, transcendentals=0),
    )(pairs, pairs, tile_order, tile_order, lower, fields, upper, near_masks(), left)
    out = out.reshape(3, rows, LANES)
    solutes = round_trip(solute, "image")
    small = pltpu.CompilerParams(vmem_limit_bytes=8 * 1024 * 1024)
    solute_shape = whole(images, 3, SOL_DEV // LANES, LANES)
    sums, pushed, path = pl.pallas_call(
        functools.partial(product_kernel, images),
        out_shape=[whole(-(-7 * images // 8) * 8, LANES), solute_shape, solute_shape],
        in_specs=[scalar] + [vector] * images,
        out_specs=[vector] * 3,
        compiler_params=small,
    )(index, *solutes)
    out = pl.pallas_call(
        functools.partial(blend_kernel, images),
        grid=(1,),
        out_shape=whole(3, rows, LANES),
        in_specs=[scalar] + [vector] * 3 + [pl.BlockSpec(memory_space=pl.ANY)],
        out_specs=pl.BlockSpec((3, SOL_DEV // LANES, LANES), lambda i: (0, 0, 0)),
        input_output_aliases={4: 0},
        compiler_params=small,
    )(index, summed(sums, "space"), pushed, path, out)
    return out.reshape(1, 3, atoms)


def solution(mesh):
    placed = (
        P("image", None, "space"),
        P("space"),
        P("space"),
        P("image"),
        P("image", "space", None),
        P("image", "space", None),
        P("image", "space", None),
    )
    return jax.shard_map(
        per_device, mesh=mesh, in_specs=placed, out_specs=P("image", None, "space"), check_vma=False
    )
```

```python
import functools
import itertools

import jax
import jax.numpy as jnp
import numpy as np
from jax import lax
from jax.experimental import pallas as pl
from jax.experimental.pallas import tpu as pltpu
from jax.sharding import PartitionSpec as P

SOL_DEV = 1024
TILE = 128
LANES = 128
FIELDS = 5
PAD = 8

LJ_COEF = 0.5
CHARGE_COEF = 0.1
SOFT_CORE = 0.09
SLAB_WIDTH = 1.0
STEP_SIZE = 0.2
SPRING_COEF = 1.0
EPSILON = 1e-06
CENTRE = 0.5

F32 = jnp.float32
BF16 = jnp.bfloat16
I32 = jnp.int32
VMEM_LIMIT = 58 * 1024 * 1024

DEPTH, CHARGE, ONE, NORM, LAST = 3, 4, 5, 6, 7
FAR_PIECES = (0, 1, 2, 0, 1, 0)
ROW = 256
COPY = 64
USED = 8 * len(FAR_PIECES)
NEAR_PIECES = (0, 0, 0, 1, 1, 2)


def near_selector():
    chosen = np.zeros((LANES, LANES), np.float32)
    for group, piece in enumerate(NEAR_PIECES):
        for axis in range(3):
            chosen[piece * 8 + axis, group * 8 + axis] = 2.0
        for field in (DEPTH, CHARGE):
            chosen[piece * 8 + field, group * 8 + field] = 1.0
    for piece in range(3):
        for axis in range(3):
            chosen[piece * 8 + axis, COPY + piece * 8 + axis] = 1.0
    for piece, group in ((0, 0), (1, 3), (2, 5)):
        chosen[piece * 8 + NORM, group * 8 + ONE] = 1.0
        chosen[ONE, piece * 8 + NORM] = 1.0
    chosen[ONE, LAST] = 1.0
    return jnp.asarray(chosen, BF16)


def near_masks():
    lane = np.arange(LANES)
    field = lane % 8
    kinds = [(field != DEPTH) & (field != CHARGE), field == DEPTH, field == CHARGE, lane >= COPY]
    return jnp.asarray(np.stack([np.tile(kind, (16, 1)) for kind in kinds]), BF16)


def sublane_numbers():
    return jnp.asarray(np.arange(ROW)[:, None] * np.ones((1, ROW)), BF16)


def equal_rows(numbers, row, value):
    return jnp.where(numbers == row.astype(F32).astype(BF16), value, jnp.zeros((), BF16))


def two_pieces(values):
    high = values.astype(BF16)
    low = (values - high.astype(F32)).astype(BF16)
    return high, low


def nt_dot(left, right):
    return lax.dot_general(left, right, (((1,), (1,)), ((), ())), preferred_element_type=F32)


def fill_blocks(fields_ref, rows, start_row, count, shift, table, first):
    sublane = lax.broadcasted_iota(I32, (8, LANES), 0)
    move = jnp.where(sublane < 3, jnp.where(sublane == 0, shift - CENTRE, -CENTRE), 0.0)
    ones = jnp.ones((8 - FIELDS, LANES), F32)
    corner = lax.broadcasted_iota(I32, (LANES, LANES), 0) == lax.broadcasted_iota(I32, (LANES, LANES), 1)
    eye = jnp.where(corner, 1.0, 0.0).astype(BF16)
    blank = jnp.zeros((LANES - USED, LANES), F32)

    def pieces(block):
        values = fields_ref[pl.ds(start_row + block, FIELDS, stride=rows), :]
        values = jnp.concatenate([values, ones], axis=0) + move
        norm = jnp.sum(jnp.where(sublane < 3, values * values, 0.0), axis=0, keepdims=True)
        rest = jnp.where(sublane == NORM, -norm, values)
        parts = []
        for _ in range(2):
            parts.append(rest.astype(BF16).astype(F32))
            rest = rest - parts[-1]
        parts.append(rest)
        return [parts[piece] for piece in FAR_PIECES]

    def put(block, value):
        start = pl.multiple_of(first + (start_row + block) * LANES + PAD, PAD)
        table[pl.ds(start, LANES), 0:USED] = value

    for block in range(0, count, 4):
        for side in range(2):
            put(block + side, jnp.concatenate(pieces(block + side), axis=0).T)
        both = jnp.concatenate(pieces(block + 2) + [blank] + pieces(block + 3) + [blank], axis=0)
        both = nt_dot(eye, both.astype(BF16))
        for side in range(2):
            put(block + 2 + side, both[:, side * LANES : side * LANES + USED])


def sublane_masks():
    sublane = lax.broadcasted_iota(I32, (8, LANES), 0)
    used = lax.broadcasted_iota(I32, (8, LANES), 1) < USED
    return [sublane == k for k in range(8)] + [used]


def merged(table, entries, masks):
    result = table[pl.ds(entries[0], 8), :]
    for k in range(1, 8):
        result = jnp.where(masks[k], table[pl.ds(entries[k], 8), :], result)
    return jnp.where(masks[8], result, 0.0)


def copy_rows(table, entry_of, stage, start, masks):
    parts = [merged(table, [entry_of(start + half + k) for k in range(8)], masks) for half in (0, 8)]
    stage[start : start + 16, :] = jnp.concatenate(parts, axis=0).astype(BF16)


def near_kernel(
    rows, order_ref, next_ref, lower_ref, upper_ref, partner_ref, fields_ref, select_ref, numbers_ref, left_ref, list_ref,
    table, stage_a, stage_b, lists,
):
    turn = pl.program_id(0)
    half = rows // 2

    @pl.when(turn == 0)
    def _():
        for side, ref in enumerate((lower_ref, upper_ref)):
            spot = slice(side * half, (side + 1) * half)
            low = ref[...] & 255
            lists[spot, 0:LANES] = (ref[...] - low).astype(F32).astype(BF16)
            lists[spot, LANES:] = low.astype(F32).astype(BF16)

        def fill(group, carry):
            fill_blocks(fields_ref, rows, group * 8, 8, 0.0, table, 0)
            return carry

        lax.fori_loop(0, rows // 8, fill, 0)

    def compose(tile):
        entries = partner_ref[0, tile : tile + 1, :]
        width = entries.shape[1]
        hot = equal_rows(numbers_ref[0:LANES, 0:width], entries & (LANES - 1), jnp.ones((), BF16))
        found = jnp.dot(lists[...], jnp.concatenate([hot, hot], axis=0), preferred_element_type=F32)
        yield
        block = entries >> 7
        low, high = block < half, block >= half + rows
        chosen = jnp.where(low, block, jnp.where(high, block - rows, -8)) - lax.broadcasted_iota(I32, (8, width), 0)
        picked = jnp.zeros((8, width), F32)
        for start in range(0, rows, 8):
            picked = jnp.where(chosen == start, found[start : start + 8], picked)
        atom = jnp.sum(picked, axis=0, keepdims=True).astype(I32)
        yield
        atom = jnp.where(low, atom, jnp.where(high, atom + 2 * rows * LANES, entries + half * LANES))
        atom = atom + PAD - (lax.broadcasted_iota(I32, (1, width), 1) & 7)
        for side in range(width // LANES):
            row = tile * (width // LANES) + side
            list_ref[row : row + 1, :] = atom[:, side * LANES : (side + 1) * LANES]

    masks = sublane_masks()

    def load(local, stage):
        ref, first = (order_ref, local) if local < 8 else (next_ref, local - 8)

        def entry_of(k):
            return ref[first * TILE + k]

        return [
            functools.partial(copy_rows, table, entry_of, stage, start, masks) for start in range(0, TILE, 16)
        ]

    def factors(place, stage):
        left = jnp.dot(stage[...], select_ref[...], preferred_element_type=F32)
        yield
        left_ref[place] = left.astype(BF16)

    @pl.when(turn == 0)
    def _():
        for side in range(2):
            for copy in load(side, stage_a.at[side]):
                copy()

    for tile in range(0, 8, 2):
        here, there = (stage_a, stage_b) if tile % 4 == 0 else (stage_b, stage_a)
        weave(
            [factors(tile + side, here.at[side]) for side in range(2)] + [compose(tile + side) for side in range(2)],
            load(tile + 2, there.at[0]) + load(tile + 3, there.at[1]),
            2,
        )


def masked(values, kind):
    blocks = values.reshape(TILE // 16, 16, LANES) * kind[None]
    return blocks.reshape(TILE, LANES)


def tile_sums(left_ref, kinds_ref, place, far, sums):
    others = far[...]
    left = left_ref[place]
    left = jnp.concatenate([masked(left, kinds_ref[kind]) for kind in range(3)], axis=0)
    yield
    grams = nt_dot(left, others)
    yield
    chunk = 32
    high, low = [], []
    for start in range(0, TILE, chunk):
        window = grams[start : start + chunk]
        inside = jnp.maximum(window, 0.0)
        root = lax.rsqrt((1.0 + SOFT_CORE) - window)
        depth = grams[TILE + start : TILE + start + chunk]
        charge = grams[2 * TILE + start : 2 * TILE + start + chunk]
        parts = two_pieces(inside * inside * (depth + charge * (root * root * root)))
        high.append(parts[0])
        low.append(parts[1])
        yield
    both = jnp.dot(jnp.concatenate(high + low, axis=0), others, preferred_element_type=F32)
    yield
    sums[...] = both[0:TILE] + both[TILE:] + masked(left_ref[place], kinds_ref[3]).astype(F32)


def pair_scatter(lists, numbers_ref, sums, total):
    entries = jnp.concatenate(lists, axis=1)
    forces = [[], [], []]
    for side in range(2):
        across = sums[side].T
        for axis in range(3):
            moment, place = (
                sum(across[first + axis + 8 * piece : first + axis + 8 * piece + 1] for piece in range(3))
                for first in (0, COPY)
            )
            forces[axis].append(place * across[ONE : ONE + 1] - moment)
    yield
    hot = equal_rows(numbers_ref[...], entries & (ROW - 1), jnp.ones((), BF16))
    yield
    count = total.shape[0] // 3
    high, low = [], []
    for axis in range(3):
        parts = two_pieces(jnp.concatenate(forces[axis], axis=1))
        for part, kept in zip(parts, (high, low)):
            kept.append(equal_rows(numbers_ref[0:count, :], entries >> 8, part))
        yield
    both = nt_dot(jnp.concatenate(high + low, axis=0), hot)
    total[...] += both[0 : 3 * count] + both[3 * count :]


def weave(stages, copies, parts):
    size = -(-len(copies) // parts)
    for turn, _ in enumerate(itertools.zip_longest(*stages)):
        for copy in copies[turn * size : (turn + 1) * size]:
            copy()


def force_kernel(
    rows, list_ref, next_ref, order_ref, before_ref, lower_ref, fields_ref, upper_ref, kinds_ref, numbers_ref, left_ref,
    out_ref, solute_ref, table, total, far_a, far_b, sum_a, sum_b,
):
    turn = pl.program_id(0)
    partners = far_a.shape[1]
    own = rows * LANES
    masks = sublane_masks()

    def load(local, far):
        ref, first = (list_ref, local) if local < 8 else (next_ref, local - 8)

        def entry_of(k):
            return ref[first * partners + k]

        return [
            functools.partial(copy_rows, table, entry_of, far, start, masks)
            for start in range(0, partners, 16)
        ]

    def scatter(local, sums):
        ref, first = (order_ref, local) if local >= 0 else (before_ref, local + 8)
        return pair_scatter([ref[first + side : first + side + 1, :] for side in range(2)], numbers_ref, sums, total)

    @pl.when(turn == 0)
    def _():
        def fill(group, carry):
            for domain, ref in enumerate((lower_ref, fields_ref, upper_ref)):
                fill_blocks(ref, rows, group * 4, 4, (domain - 1) * SLAB_WIDTH, table, domain * own)
            return carry

        lax.fori_loop(0, rows // 4, fill, 0)
        sum_b[...] = jnp.zeros_like(sum_b)
        total[...] = jnp.zeros_like(total)
        for side in range(2):
            for copy in load(side, far_a.at[side]):
                copy()

    for tile in range(0, 8, 2):
        far, far_next, sums, sums_before = (
            (far_a, far_b, sum_a, sum_b) if tile % 4 == 0 else (far_b, far_a, sum_b, sum_a)
        )
        weave(
            [tile_sums(left_ref, kinds_ref, tile + side, far.at[side], sums.at[side]) for side in range(2)]
            + [scatter(tile - 2, sums_before)],
            load(tile + 2, far_next.at[0]) + load(tile + 3, far_next.at[1]),
            7,
        )

    @pl.when(turn == pl.num_programs(0) - 1)
    def _():
        for _ in scatter(6, sum_b):
            pass
        count = rows * LANES // ROW
        for axis in range(3):
            force = total[axis * count : (axis + 1) * count, :]
            for side in range(ROW // LANES):
                spot = pl.ds(axis * rows + side, count, stride=ROW // LANES)
                out_ref[spot, :] = fields_ref[spot, :] + STEP_SIZE * force[:, side * LANES : (side + 1) * LANES]
        solute = SOL_DEV // LANES
        for axis in range(3):
            solute_ref[axis] = out_ref[axis * rows : axis * rows + solute, :]
            solute_ref[3 + axis] = fields_ref[axis * rows : axis * rows + solute, :]


def product_kernel(images, index_ref, *refs):
    solute_refs, (sums_ref, pushed, path) = refs[:images], refs[images:]
    index = index_ref[0]
    for by in range(images):
        place = lax.rem(index + images - by, images)
        pushed[place] = solute_refs[by][0:3]
        path[place] = solute_refs[by][3:6]
    sums_ref[...] = jnp.zeros_like(sums_ref)
    last = images - 1
    tangents = [path[min(k + 1, last)] - path[max(k - 1, 0)] for k in range(images)]

    def put(kind, image, left, right):
        total = jnp.sum(left * right, axis=0)
        sums_ref[kind * images + image : kind * images + image + 1, :] = jnp.sum(total, axis=0, keepdims=True)

    for k in range(images):
        put(0, k, tangents[k], tangents[k])
        put(1, k, pushed[k] - path[k], tangents[k])
        if k < last:
            step = path[k + 1] - path[k]
            gap = pushed[k + 1] - pushed[k]
            put(2, k, step, step)
            put(3, k, gap, gap)
            put(4, k, gap, tangents[k + 1])
            put(5, k, gap, tangents[k])
            put(6, k, tangents[k + 1], tangents[k])


def blend_kernel(images, index_ref, sums_ref, pushed, path, out_in, out_ref):
    del out_in
    index = index_ref[0]
    last = images - 1
    totals = jnp.sum(sums_ref[...], axis=1, keepdims=True)

    def total(kind, image):
        row = kind * images + image
        return totals[row : row + 1, :]

    step_root = [jnp.sqrt(total(2, k) + EPSILON) for k in range(last)]
    shift = []
    for k in range(images):
        tangent_sq = total(0, k)
        value = -total(1, k) / (tangent_sq + EPSILON)
        if 0 < k < last:
            spring = SPRING_COEF * (step_root[k] - step_root[k - 1]) / jnp.sqrt(tangent_sq + EPSILON)
            value = value + STEP_SIZE * spring
        shift.append(value)
    lengths = []
    for k in range(last):
        there, here = shift[k + 1], shift[k]
        length_sq = (
            total(3, k)
            + there * there * total(0, k + 1)
            + here * here * total(0, k)
            + 2.0 * (there * total(4, k) - here * total(5, k) - there * here * total(6, k))
        )
        lengths.append(jnp.sqrt(jnp.maximum(length_sq, 0.0) + EPSILON))
    knots = [jnp.zeros_like(lengths[0])]
    for length in lengths:
        knots.append(knots[-1] + length)

    def pick(values):
        result = values[0]
        for k in range(1, images):
            result = jnp.where(index == k, values[k], result)
        return result

    none = jnp.zeros_like(lengths[0])
    excess = [knots[k] - knots[last] * (k / last) for k in range(images)]
    back = pick([none] + [jnp.clip(excess[k] / lengths[k - 1], 0.0, 1.0) for k in range(1, images)])
    ahead = pick([jnp.clip(-excess[k] / lengths[k], 0.0, 1.0) for k in range(last)] + [none])
    shifts = [pick([shift[min(max(k + by, 0), last)] for k in range(images)]) for by in (-1, 0, 1)]

    def moved(by):
        place = jnp.clip(index + by, 0, last)
        tangent = path[jnp.minimum(place + 1, last)] - path[jnp.maximum(place - 1, 0)]
        return pushed[place] + shifts[by + 1] * tangent

    here = moved(0)
    blended = here + back * (moved(-1) - here) + ahead * (moved(1) - here)
    out_ref[...] = blended


def whole(*shape, dtype=F32):
    return jax.ShapeDtypeStruct(shape, dtype)


def turned(array, axis, by):
    count = lax.axis_size(axis)
    return lax.ppermute(array, axis, [(i, (i + by) % count) for i in range(count)])


def summed(array, axis):
    count = lax.axis_size(axis)
    if count & (count - 1):
        return lax.psum(array, axis)

    def crossed(by):
        return lax.ppermute(array, axis, [(i, i ^ by) for i in range(count)])

    array = array + crossed(1)
    return sum((crossed(by) for by in range(2, count, 2)), array)


def round_trip(array, axis):
    return [array] + [turned(array, axis, by) for by in range(1, lax.axis_size(axis))]


def per_device(positions, strength, charge, rest_scale, cell_order, ghost_index, tile_atoms):
    atoms = positions.shape[2]
    rows = atoms // LANES
    partners = tile_atoms.shape[2]
    images = lax.axis_size("image")
    index = lax.axis_index("image").reshape(1)

    factor = jnp.where(jnp.arange(atoms) < SOL_DEV, jnp.sqrt(rest_scale[0]), 1.0)
    scaled = jnp.stack([strength * factor * LJ_COEF**0.5, charge * factor * CHARGE_COEF**0.5])
    places = positions.reshape(3, rows, LANES)
    fields = jnp.concatenate([places, scaled.reshape(2, rows, LANES)]).reshape(FIELDS * rows, LANES)
    shell = ghost_index.reshape(2, rows // 2, LANES)
    lower_list, upper_list = turned(shell[1], "space", 1), turned(shell[0], "space", -1)
    fields, lower_list, upper_list = lax.optimization_barrier((fields, lower_list, upper_list))
    lower, upper = turned(fields, "space", 1), turned(fields, "space", -1)
    tile_order = cell_order.reshape(rows, LANES)
    order = cell_order.reshape(atoms) + (PAD - jnp.arange(atoms, dtype=I32) % 8)
    scalar = pl.BlockSpec(memory_space=pltpu.SMEM)
    vector = pl.BlockSpec(memory_space=pltpu.VMEM)
    params = pltpu.CompilerParams(vmem_limit_bytes=VMEM_LIMIT)
    last = rows // 8 - 1

    def listed(size, by):
        return pl.BlockSpec((8 * size,), lambda i: (jnp.clip(i + by, 0, last),), memory_space=pltpu.SMEM)

    table = (atoms + 2 * PAD, LANES)
    left, partner_rows = pl.pallas_call(
        functools.partial(near_kernel, rows),
        grid=(rows // 8,),
        out_shape=[whole(rows, TILE, LANES, dtype=BF16), whole(rows * partners // LANES, LANES, dtype=I32)],
        in_specs=[listed(TILE, 0), listed(TILE, 1)]
        + [vector] * 2
        + [pl.BlockSpec((1, 8, partners), lambda i: (0, i, 0))]
        + [vector] * 3,
        out_specs=[
            pl.BlockSpec((8, TILE, LANES), lambda i: (i, 0, 0)),
            pl.BlockSpec((8 * partners // LANES, LANES), lambda i: (i, 0)),
        ],
        scratch_shapes=[
            pltpu.VMEM(table, F32),
            pltpu.VMEM((2, TILE, LANES), BF16),
            pltpu.VMEM((2, TILE, LANES), BF16),
            pltpu.VMEM((rows, 2 * LANES), BF16),
        ],
        compiler_params=params,
        cost_estimate=pl.CostEstimate(flops=25 * 10**9, bytes_accessed=10**7, transcendentals=0),
    )(order, order, lower_list, upper_list, tile_atoms, fields, near_selector(), sublane_numbers())
    pairs = partner_rows.reshape(rows * partners)
    out, solute = pl.pallas_call(
        functools.partial(force_kernel, rows),
        grid=(rows // 8,),
        out_shape=[whole(3 * rows, LANES), whole(6, SOL_DEV // LANES, LANES)],
        in_specs=[listed(partners, 0), listed(partners, 1)]
        + [pl.BlockSpec((8, LANES), lambda i, by=by: (jnp.maximum(i - by, 0), 0)) for by in (0, 1)]
        + [vector] * 5
        + [pl.BlockSpec((8, TILE, LANES), lambda i: (i, 0, 0))],
        out_specs=[vector] * 2,
        scratch_shapes=[
            pltpu.VMEM((3 * atoms + 2 * PAD, LANES), F32),
            pltpu.VMEM((3 * atoms // ROW, ROW), F32),
            pltpu.VMEM((2, partners, LANES), BF16),
            pltpu.VMEM((2, partners, LANES), BF16),
            pltpu.VMEM((2, TILE, LANES), F32),
            pltpu.VMEM((2, TILE, LANES), F32),
        ],
        compiler_params=params,
        cost_estimate=pl.CostEstimate(flops=25 * 10**9, bytes_accessed=10**7, transcendentals=0),
    )(pairs, pairs, tile_order, tile_order, lower, fields, upper, near_masks(), sublane_numbers(), left)
    out = out.reshape(3, rows, LANES)
    solutes = round_trip(solute, "image")
    small = pltpu.CompilerParams(vmem_limit_bytes=8 * 1024 * 1024)
    solute_shape = whole(images, 3, SOL_DEV // LANES, LANES)
    sums, pushed, path = pl.pallas_call(
        functools.partial(product_kernel, images),
        out_shape=[whole(-(-7 * images // 8) * 8, LANES), solute_shape, solute_shape],
        in_specs=[scalar] + [vector] * images,
        out_specs=[vector] * 3,
        compiler_params=small,
    )(index, *solutes)
    out = pl.pallas_call(
        functools.partial(blend_kernel, images),
        grid=(1,),
        out_shape=whole(3, rows, LANES),
        in_specs=[scalar] + [vector] * 3 + [pl.BlockSpec(memory_space=pl.ANY)],
        out_specs=pl.BlockSpec((3, SOL_DEV // LANES, LANES), lambda i: (0, 0, 0)),
        input_output_aliases={4: 0},
        compiler_params=small,
    )(index, summed(sums, "space"), pushed, path, out)
    return out.reshape(1, 3, atoms)


def solution(mesh):
    placed = (
        P("image", None, "space"),
        P("space"),
        P("space"),
        P("image"),
        P("image", "space", None),
        P("image", "space", None),
        P("image", "space", None),
    )
    return jax.shard_map(
        per_device, mesh=mesh, in_specs=placed, out_specs=P("image", None, "space"), check_vma=False
    )
```

```python
import functools
import itertools

import jax
import jax.numpy as jnp
import numpy as np
from jax import lax
from jax.experimental import pallas as pl
from jax.experimental.pallas import tpu as pltpu
from jax.sharding import PartitionSpec as P

SOL_DEV = 1024
TILE = 128
LANES = 128
FIELDS = 5

LJ_COEF = 0.5
CHARGE_COEF = 0.1
SOFT_CORE = 0.09
SLAB_WIDTH = 1.0
STEP_SIZE = 0.2
SPRING_COEF = 1.0
EPSILON = 1e-06
CENTRE = 0.5

F32 = jnp.float32
BF16 = jnp.bfloat16
I32 = jnp.int32
VMEM_LIMIT = 58 * 1024 * 1024

DEPTH, CHARGE, ONE, NORM, LAST = 3, 4, 5, 6, 7
FAR_PIECES = (0, 1, 2, 0, 1, 0)
ROW = 256
COPY = 64
USED = 8 * len(FAR_PIECES)
NEAR_PIECES = (0, 0, 0, 1, 1, 2)


def near_selector():
    chosen = np.zeros((LANES, LANES), np.float32)
    for group, piece in enumerate(NEAR_PIECES):
        for axis in range(3):
            chosen[piece * 8 + axis, group * 8 + axis] = 2.0
        for field in (DEPTH, CHARGE):
            chosen[piece * 8 + field, group * 8 + field] = 1.0
    for piece in range(3):
        for axis in range(3):
            chosen[piece * 8 + axis, COPY + piece * 8 + axis] = 1.0
    for piece, group in ((0, 0), (1, 3), (2, 5)):
        chosen[piece * 8 + NORM, group * 8 + ONE] = 1.0
        chosen[ONE, piece * 8 + NORM] = 1.0
    chosen[ONE, LAST] = 1.0
    return jnp.asarray(chosen, BF16)


def near_masks():
    lane = np.arange(LANES)
    field = lane % 8
    kinds = [(field != DEPTH) & (field != CHARGE), field == DEPTH, field == CHARGE, lane >= COPY]
    return jnp.asarray(np.stack([np.tile(kind, (16, 1)) for kind in kinds]), BF16)


def sublane_numbers():
    return jnp.asarray(np.arange(ROW)[:, None] * np.ones((1, ROW)), BF16)


def equal_rows(numbers, row, value):
    return jnp.where(numbers == row.astype(F32).astype(BF16), value, jnp.zeros((), BF16))


def two_pieces(values):
    high = values.astype(BF16)
    low = (values - high.astype(F32)).astype(BF16)
    return high, low


def nt_dot(left, right):
    return lax.dot_general(left, right, (((1,), (1,)), ((), ())), preferred_element_type=F32)


def fill_blocks(fields_ref, rows, start_row, count, shift, table, first):
    sublane = lax.broadcasted_iota(I32, (8, LANES), 0)
    move = jnp.where(sublane < 3, jnp.where(sublane == 0, shift - CENTRE, -CENTRE), 0.0)
    ones = jnp.ones((8 - FIELDS, LANES), F32)
    corner = lax.broadcasted_iota(I32, (LANES, LANES), 0) == lax.broadcasted_iota(I32, (LANES, LANES), 1)
    eye = jnp.where(corner, 1.0, 0.0).astype(BF16)
    blank = jnp.zeros((LANES - USED, LANES), F32)

    def pieces(block):
        values = fields_ref[pl.ds(start_row + block, FIELDS, stride=rows), :]
        values = jnp.concatenate([values, ones], axis=0) + move
        norm = jnp.sum(jnp.where(sublane < 3, values * values, 0.0), axis=0, keepdims=True)
        rest = jnp.where(sublane == NORM, -norm, values)
        parts = []
        for _ in range(2):
            parts.append(rest.astype(BF16).astype(F32))
            rest = rest - parts[-1]
        parts.append(rest)
        return [parts[piece] for piece in FAR_PIECES]

    def put(block, value):
        start = pl.multiple_of(first + (start_row + block) * LANES, LANES)
        flat(table)[pl.ds(start, LANES), 0:USED] = value

    for block in range(0, count, 4):
        for side in range(2):
            put(block + side, jnp.concatenate(pieces(block + side), axis=0).T)
        both = jnp.concatenate(pieces(block + 2) + [blank] + pieces(block + 3) + [blank], axis=0)
        both = nt_dot(eye, both.astype(BF16))
        for side in range(2):
            put(block + 2 + side, both[:, side * LANES : side * LANES + USED])


def flat(table):
    return table.reshape(table.shape[0], LANES)


def copy_rows(table, entry_of, stage, start):
    for k in range(start, start + 16):
        stage[k : k + 1, :] = table[entry_of(k)]


def used_lanes(stage):
    used = lax.broadcasted_iota(I32, stage.shape, 1) < USED
    return jnp.where(used, stage[...], 0.0).astype(BF16)


def near_kernel(
    rows, order_ref, next_ref, lower_ref, upper_ref, partner_ref, fields_ref, select_ref, numbers_ref, left_ref, list_ref,
    table, stage_a, stage_b, lists,
):
    turn = pl.program_id(0)
    half = rows // 2

    @pl.when(turn == 0)
    def _():
        for side, ref in enumerate((lower_ref, upper_ref)):
            spot = slice(side * half, (side + 1) * half)
            low = ref[...] & 255
            lists[spot, 0:LANES] = (ref[...] - low).astype(F32).astype(BF16)
            lists[spot, LANES:] = low.astype(F32).astype(BF16)

        def fill(group, carry):
            fill_blocks(fields_ref, rows, group * 8, 8, 0.0, table, 0)
            return carry

        lax.fori_loop(0, rows // 8, fill, 0)

    def compose(tile):
        entries = partner_ref[0, tile : tile + 1, :]
        width = entries.shape[1]
        hot = equal_rows(numbers_ref[0:LANES, 0:width], entries & (LANES - 1), jnp.ones((), BF16))
        found = jnp.dot(lists[...], jnp.concatenate([hot, hot], axis=0), preferred_element_type=F32)
        yield
        block = entries >> 7
        low, high = block < half, block >= half + rows
        chosen = jnp.where(low, block, jnp.where(high, block - rows, -8)) - lax.broadcasted_iota(I32, (8, width), 0)
        picked = jnp.zeros((8, width), F32)
        for start in range(0, rows, 8):
            picked = jnp.where(chosen == start, found[start : start + 8], picked)
        atom = jnp.sum(picked, axis=0, keepdims=True).astype(I32)
        yield
        atom = jnp.where(low, atom, jnp.where(high, atom + 2 * rows * LANES, entries + half * LANES))
        for side in range(width // LANES):
            row = tile * (width // LANES) + side
            list_ref[row : row + 1, :] = atom[:, side * LANES : (side + 1) * LANES]

    def load(local, stage):
        ref, first = (order_ref, local) if local < 8 else (next_ref, local - 8)

        def entry_of(k):
            return ref[first * TILE + k]

        return [
            functools.partial(copy_rows, table, entry_of, stage, start) for start in range(0, TILE, 16)
        ]

    def factors(place, stage):
        left = jnp.dot(used_lanes(stage), select_ref[...], preferred_element_type=F32)
        yield
        left_ref[place] = left.astype(BF16)

    @pl.when(turn == 0)
    def _():
        for side in range(2):
            for copy in load(side, stage_a.at[side]):
                copy()

    for tile in range(0, 8, 2):
        here, there = (stage_a, stage_b) if tile % 4 == 0 else (stage_b, stage_a)
        weave(
            [factors(tile + side, here.at[side]) for side in range(2)] + [compose(tile + side) for side in range(2)],
            load(tile + 2, there.at[0]) + load(tile + 3, there.at[1]),
            2,
        )


def masked(values, kind):
    blocks = values.reshape(TILE // 16, 16, LANES) * kind[None]
    return blocks.reshape(TILE, LANES)


def tile_sums(left_ref, kinds_ref, place, far, sums):
    others = used_lanes(far)
    left = left_ref[place]
    left = jnp.concatenate([masked(left, kinds_ref[kind]) for kind in range(3)], axis=0)
    yield
    grams = nt_dot(left, others)
    yield
    chunk = 32
    high, low = [], []
    for start in range(0, TILE, chunk):
        window = grams[start : start + chunk]
        inside = jnp.maximum(window, 0.0)
        root = lax.rsqrt((1.0 + SOFT_CORE) - window)
        depth = grams[TILE + start : TILE + start + chunk]
        charge = grams[2 * TILE + start : 2 * TILE + start + chunk]
        parts = two_pieces(inside * inside * (depth + charge * (root * root * root)))
        high.append(parts[0])
        low.append(parts[1])
        yield
    both = jnp.dot(jnp.concatenate(high + low, axis=0), others, preferred_element_type=F32)
    yield
    sums[...] = both[0:TILE] + both[TILE:] + masked(left_ref[place], kinds_ref[3]).astype(F32)


def pair_scatter(lists, numbers_ref, sums, total):
    entries = jnp.concatenate(lists, axis=1)
    forces = [[], [], []]
    for side in range(2):
        across = sums[side].T
        for axis in range(3):
            moment, place = (
                sum(across[first + axis + 8 * piece : first + axis + 8 * piece + 1] for piece in range(3))
                for first in (0, COPY)
            )
            forces[axis].append(place * across[ONE : ONE + 1] - moment)
    yield
    hot = equal_rows(numbers_ref[...], entries & (ROW - 1), jnp.ones((), BF16))
    yield
    count = total.shape[0] // 3
    high, low = [], []
    for axis in range(3):
        parts = two_pieces(jnp.concatenate(forces[axis], axis=1))
        for part, kept in zip(parts, (high, low)):
            kept.append(equal_rows(numbers_ref[0:count, :], entries >> 8, part))
        yield
    both = nt_dot(jnp.concatenate(high + low, axis=0), hot)
    total[...] += both[0 : 3 * count] + both[3 * count :]


def weave(stages, copies, parts):
    size = -(-len(copies) // parts)
    for turn, _ in enumerate(itertools.zip_longest(*stages)):
        for copy in copies[turn * size : (turn + 1) * size]:
            copy()


def force_kernel(
    rows, list_ref, next_ref, order_ref, before_ref, lower_ref, fields_ref, upper_ref, kinds_ref, numbers_ref, left_ref,
    out_ref, solute_ref, table, total, far_a, far_b, sum_a, sum_b,
):
    turn = pl.program_id(0)
    partners = far_a.shape[1]
    own = rows * LANES
    def load(local, far):
        ref, first = (list_ref, local) if local < 8 else (next_ref, local - 8)

        def entry_of(k):
            return ref[first * partners + k]

        return [
            functools.partial(copy_rows, table, entry_of, far, start)
            for start in range(0, partners, 16)
        ]

    def scatter(local, sums):
        ref, first = (order_ref, local) if local >= 0 else (before_ref, local + 8)
        return pair_scatter([ref[first + side : first + side + 1, :] for side in range(2)], numbers_ref, sums, total)

    @pl.when(turn == 0)
    def _():
        def fill(group, carry):
            for domain, ref in enumerate((lower_ref, fields_ref, upper_ref)):
                fill_blocks(ref, rows, group * 4, 4, (domain - 1) * SLAB_WIDTH, table, domain * own)
            return carry

        lax.fori_loop(0, rows // 4, fill, 0)
        sum_b[...] = jnp.zeros_like(sum_b)
        total[...] = jnp.zeros_like(total)
        for side in range(2):
            for copy in load(side, far_a.at[side]):
                copy()

    for tile in range(0, 8, 2):
        far, far_next, sums, sums_before = (
            (far_a, far_b, sum_a, sum_b) if tile % 4 == 0 else (far_b, far_a, sum_b, sum_a)
        )
        weave(
            [tile_sums(left_ref, kinds_ref, tile + side, far.at[side], sums.at[side]) for side in range(2)]
            + [scatter(tile - 2, sums_before)],
            load(tile + 2, far_next.at[0]) + load(tile + 3, far_next.at[1]),
            7,
        )

    @pl.when(turn == pl.num_programs(0) - 1)
    def _():
        for _ in scatter(6, sum_b):
            pass
        count = rows * LANES // ROW
        for axis in range(3):
            force = total[axis * count : (axis + 1) * count, :]
            for side in range(ROW // LANES):
                spot = pl.ds(axis * rows + side, count, stride=ROW // LANES)
                out_ref[spot, :] = fields_ref[spot, :] + STEP_SIZE * force[:, side * LANES : (side + 1) * LANES]
        solute = SOL_DEV // LANES
        for axis in range(3):
            solute_ref[axis] = out_ref[axis * rows : axis * rows + solute, :]
            solute_ref[3 + axis] = fields_ref[axis * rows : axis * rows + solute, :]


def product_kernel(images, index_ref, *refs):
    solute_refs, (sums_ref, pushed, path) = refs[:images], refs[images:]
    index = index_ref[0]
    for by in range(images):
        place = lax.rem(index + images - by, images)
        pushed[place] = solute_refs[by][0:3]
        path[place] = solute_refs[by][3:6]
    sums_ref[...] = jnp.zeros_like(sums_ref)
    last = images - 1
    tangents = [path[min(k + 1, last)] - path[max(k - 1, 0)] for k in range(images)]

    def put(kind, image, left, right):
        total = jnp.sum(left * right, axis=0)
        sums_ref[kind * images + image : kind * images + image + 1, :] = jnp.sum(total, axis=0, keepdims=True)

    for k in range(images):
        put(0, k, tangents[k], tangents[k])
        put(1, k, pushed[k] - path[k], tangents[k])
        if k < last:
            step = path[k + 1] - path[k]
            gap = pushed[k + 1] - pushed[k]
            put(2, k, step, step)
            put(3, k, gap, gap)
            put(4, k, gap, tangents[k + 1])
            put(5, k, gap, tangents[k])
            put(6, k, tangents[k + 1], tangents[k])


def blend_kernel(images, index_ref, sums_ref, pushed, path, out_in, out_ref):
    del out_in
    index = index_ref[0]
    last = images - 1
    totals = jnp.sum(sums_ref[...], axis=1, keepdims=True)

    def total(kind, image):
        row = kind * images + image
        return totals[row : row + 1, :]

    step_root = [jnp.sqrt(total(2, k) + EPSILON) for k in range(last)]
    shift = []
    for k in range(images):
        tangent_sq = total(0, k)
        value = -total(1, k) / (tangent_sq + EPSILON)
        if 0 < k < last:
            spring = SPRING_COEF * (step_root[k] - step_root[k - 1]) / jnp.sqrt(tangent_sq + EPSILON)
            value = value + STEP_SIZE * spring
        shift.append(value)
    lengths = []
    for k in range(last):
        there, here = shift[k + 1], shift[k]
        length_sq = (
            total(3, k)
            + there * there * total(0, k + 1)
            + here * here * total(0, k)
            + 2.0 * (there * total(4, k) - here * total(5, k) - there * here * total(6, k))
        )
        lengths.append(jnp.sqrt(jnp.maximum(length_sq, 0.0) + EPSILON))
    knots = [jnp.zeros_like(lengths[0])]
    for length in lengths:
        knots.append(knots[-1] + length)

    def pick(values):
        result = values[0]
        for k in range(1, images):
            result = jnp.where(index == k, values[k], result)
        return result

    none = jnp.zeros_like(lengths[0])
    excess = [knots[k] - knots[last] * (k / last) for k in range(images)]
    back = pick([none] + [jnp.clip(excess[k] / lengths[k - 1], 0.0, 1.0) for k in range(1, images)])
    ahead = pick([jnp.clip(-excess[k] / lengths[k], 0.0, 1.0) for k in range(last)] + [none])
    shifts = [pick([shift[min(max(k + by, 0), last)] for k in range(images)]) for by in (-1, 0, 1)]

    def moved(by):
        place = jnp.clip(index + by, 0, last)
        tangent = path[jnp.minimum(place + 1, last)] - path[jnp.maximum(place - 1, 0)]
        return pushed[place] + shifts[by + 1] * tangent

    here = moved(0)
    blended = here + back * (moved(-1) - here) + ahead * (moved(1) - here)
    out_ref[...] = blended


def whole(*shape, dtype=F32):
    return jax.ShapeDtypeStruct(shape, dtype)


def turned(array, axis, by):
    count = lax.axis_size(axis)
    return lax.ppermute(array, axis, [(i, (i + by) % count) for i in range(count)])


def summed(array, axis):
    count = lax.axis_size(axis)
    if count & (count - 1):
        return lax.psum(array, axis)

    def crossed(by):
        return lax.ppermute(array, axis, [(i, i ^ by) for i in range(count)])

    array = array + crossed(1)
    return sum((crossed(by) for by in range(2, count, 2)), array)


def round_trip(array, axis):
    return [array] + [turned(array, axis, by) for by in range(1, lax.axis_size(axis))]


def per_device(positions, strength, charge, rest_scale, cell_order, ghost_index, tile_atoms):
    atoms = positions.shape[2]
    rows = atoms // LANES
    partners = tile_atoms.shape[2]
    images = lax.axis_size("image")
    index = lax.axis_index("image").reshape(1)

    factor = jnp.where(jnp.arange(atoms) < SOL_DEV, jnp.sqrt(rest_scale[0]), 1.0)
    scaled = jnp.stack([strength * factor * LJ_COEF**0.5, charge * factor * CHARGE_COEF**0.5])
    places = positions.reshape(3, rows, LANES)
    fields = jnp.concatenate([places, scaled.reshape(2, rows, LANES)]).reshape(FIELDS * rows, LANES)
    shell = ghost_index.reshape(2, rows // 2, LANES)
    lower_list, upper_list = turned(shell[1], "space", 1), turned(shell[0], "space", -1)
    fields, lower_list, upper_list = lax.optimization_barrier((fields, lower_list, upper_list))
    lower, upper = turned(fields, "space", 1), turned(fields, "space", -1)
    tile_order = cell_order.reshape(rows, LANES)
    order = cell_order.reshape(atoms)
    scalar = pl.BlockSpec(memory_space=pltpu.SMEM)
    vector = pl.BlockSpec(memory_space=pltpu.VMEM)
    params = pltpu.CompilerParams(vmem_limit_bytes=VMEM_LIMIT)
    last = rows // 8 - 1

    def listed(size, by):
        return pl.BlockSpec((8 * size,), lambda i: (jnp.clip(i + by, 0, last),), memory_space=pltpu.SMEM)

    left, partner_rows = pl.pallas_call(
        functools.partial(near_kernel, rows),
        grid=(rows // 8,),
        out_shape=[whole(rows, TILE, LANES, dtype=BF16), whole(rows * partners // LANES, LANES, dtype=I32)],
        in_specs=[listed(TILE, 0), listed(TILE, 1)]
        + [vector] * 2
        + [pl.BlockSpec((1, 8, partners), lambda i: (0, i, 0))]
        + [vector] * 3,
        out_specs=[
            pl.BlockSpec((8, TILE, LANES), lambda i: (i, 0, 0)),
            pl.BlockSpec((8 * partners // LANES, LANES), lambda i: (i, 0)),
        ],
        scratch_shapes=[
            pltpu.VMEM((atoms, 1, LANES), F32),
            pltpu.VMEM((2, TILE, LANES), F32),
            pltpu.VMEM((2, TILE, LANES), F32),
            pltpu.VMEM((rows, 2 * LANES), BF16),
        ],
        compiler_params=params,
        cost_estimate=pl.CostEstimate(flops=25 * 10**9, bytes_accessed=10**7, transcendentals=0),
    )(order, order, lower_list, upper_list, tile_atoms, fields, near_selector(), sublane_numbers())
    pairs = partner_rows.reshape(rows * partners)
    out, solute = pl.pallas_call(
        functools.partial(force_kernel, rows),
        grid=(rows // 8,),
        out_shape=[whole(3 * rows, LANES), whole(6, SOL_DEV // LANES, LANES)],
        in_specs=[listed(partners, 0), listed(partners, 1)]
        + [pl.BlockSpec((8, LANES), lambda i, by=by: (jnp.maximum(i - by, 0), 0)) for by in (0, 1)]
        + [vector] * 5
        + [pl.BlockSpec((8, TILE, LANES), lambda i: (i, 0, 0))],
        out_specs=[vector] * 2,
        scratch_shapes=[
            pltpu.VMEM((3 * atoms, 1, LANES), F32),
            pltpu.VMEM((3 * atoms // ROW, ROW), F32),
            pltpu.VMEM((2, partners, LANES), F32),
            pltpu.VMEM((2, partners, LANES), F32),
            pltpu.VMEM((2, TILE, LANES), F32),
            pltpu.VMEM((2, TILE, LANES), F32),
        ],
        compiler_params=params,
        cost_estimate=pl.CostEstimate(flops=25 * 10**9, bytes_accessed=10**7, transcendentals=0),
    )(pairs, pairs, tile_order, tile_order, lower, fields, upper, near_masks(), sublane_numbers(), left)
    out = out.reshape(3, rows, LANES)
    solutes = round_trip(solute, "image")
    small = pltpu.CompilerParams(vmem_limit_bytes=8 * 1024 * 1024)
    solute_shape = whole(images, 3, SOL_DEV // LANES, LANES)
    sums, pushed, path = pl.pallas_call(
        functools.partial(product_kernel, images),
        out_shape=[whole(-(-7 * images // 8) * 8, LANES), solute_shape, solute_shape],
        in_specs=[scalar] + [vector] * images,
        out_specs=[vector] * 3,
        compiler_params=small,
    )(index, *solutes)
    out = pl.pallas_call(
        functools.partial(blend_kernel, images),
        grid=(1,),
        out_shape=whole(3, rows, LANES),
        in_specs=[scalar] + [vector] * 3 + [pl.BlockSpec(memory_space=pl.ANY)],
        out_specs=pl.BlockSpec((3, SOL_DEV // LANES, LANES), lambda i: (0, 0, 0)),
        input_output_aliases={4: 0},
        compiler_params=small,
    )(index, summed(sums, "space"), pushed, path, out)
    return out.reshape(1, 3, atoms)


def solution(mesh):
    placed = (
        P("image", None, "space"),
        P("space"),
        P("space"),
        P("image"),
        P("image", "space", None),
        P("image", "space", None),
        P("image", "space", None),
    )
    return jax.shard_map(
        per_device, mesh=mesh, in_specs=placed, out_specs=P("image", None, "space"), check_vma=False
    )
```

```python
import functools
import itertools

import jax
import jax.numpy as jnp
import numpy as np
from jax import lax
from jax.experimental import pallas as pl
from jax.experimental.pallas import tpu as pltpu
from jax.sharding import PartitionSpec as P

SOL_DEV = 1024
TILE = 128
LANES = 128
FIELDS = 5
PAD = 8

LJ_COEF = 0.5
CHARGE_COEF = 0.1
SOFT_CORE = 0.09
SLAB_WIDTH = 1.0
STEP_SIZE = 0.2
SPRING_COEF = 1.0
EPSILON = 1e-06
CENTRE = 0.5

F32 = jnp.float32
BF16 = jnp.bfloat16
I32 = jnp.int32
VMEM_LIMIT = 58 * 1024 * 1024

DEPTH, CHARGE, ONE, NORM, LAST = 3, 4, 5, 6, 7
FAR_PIECES = (0, 1, 2, 0, 1, 0)
STEP = 16
ROW = 256
COPY = 64
USED = 8 * len(FAR_PIECES)
NEAR_PIECES = (0, 0, 0, 1, 1, 2)


def near_selector():
    chosen = np.zeros((LANES, LANES), np.float32)
    for group, piece in enumerate(NEAR_PIECES):
        for axis in range(3):
            chosen[piece * 8 + axis, group * 8 + axis] = 2.0
        for field in (DEPTH, CHARGE):
            chosen[piece * 8 + field, group * 8 + field] = 1.0
    for piece in range(3):
        for axis in range(3):
            chosen[piece * 8 + axis, COPY + piece * 8 + axis] = 1.0
    for piece, group in ((0, 0), (1, 3), (2, 5)):
        chosen[piece * 8 + NORM, group * 8 + ONE] = 1.0
        chosen[ONE, piece * 8 + NORM] = 1.0
    chosen[ONE, LAST] = 1.0
    return jnp.asarray(chosen, BF16)


def near_masks():
    lane = np.arange(LANES)
    field = lane % 8
    kinds = [(field != DEPTH) & (field != CHARGE), field == DEPTH, field == CHARGE, lane >= COPY]
    return jnp.asarray(np.stack([np.tile(kind, (16, 1)) for kind in kinds]), BF16)


def two_pieces(values):
    high = values.astype(BF16)
    low = (values - high.astype(F32)).astype(BF16)
    return high, low


def nt_dot(left, right):
    return lax.dot_general(left, right, (((1,), (1,)), ((), ())), preferred_element_type=F32)


def fill_blocks(fields_ref, rows, start_row, count, shift, table, first):
    sublane = lax.broadcasted_iota(I32, (8, LANES), 0)
    move = jnp.where(sublane < 3, jnp.where(sublane == 0, shift - CENTRE, -CENTRE), 0.0)
    ones = jnp.ones((8 - FIELDS, LANES), F32)
    corner = lax.broadcasted_iota(I32, (LANES, LANES), 0) == lax.broadcasted_iota(I32, (LANES, LANES), 1)
    eye = jnp.where(corner, 1.0, 0.0).astype(BF16)
    blank = jnp.zeros((LANES - USED, LANES), F32)

    def pieces(block):
        values = fields_ref[pl.ds(start_row + block, FIELDS, stride=rows), :]
        values = jnp.concatenate([values, ones], axis=0) + move
        norm = jnp.sum(jnp.where(sublane < 3, values * values, 0.0), axis=0, keepdims=True)
        rest = jnp.where(sublane == NORM, -norm, values)
        parts = []
        for _ in range(2):
            parts.append(rest.astype(BF16).astype(F32))
            rest = rest - parts[-1]
        parts.append(rest)
        return [parts[piece] for piece in FAR_PIECES]

    def put(block, value):
        start = pl.multiple_of(first + (start_row + block) * LANES + PAD, PAD)
        table[pl.ds(start, LANES), 0:USED] = value

    for block in range(0, count, 4):
        for side in range(2):
            put(block + side, jnp.concatenate(pieces(block + side), axis=0).T)
        both = jnp.concatenate(pieces(block + 2) + [blank] + pieces(block + 3) + [blank], axis=0)
        both = nt_dot(eye, both.astype(BF16))
        for side in range(2):
            put(block + 2 + side, both[:, side * LANES : side * LANES + USED])


def sublane_masks():
    sublane = lax.broadcasted_iota(I32, (8, LANES), 0)
    used = lax.broadcasted_iota(I32, (8, LANES), 1) < USED
    return [sublane == k for k in range(8)] + [used]


def merged(table, entries, masks):
    result = table[pl.ds(entries[0], 8), :]
    for k in range(1, 8):
        result = jnp.where(masks[k], table[pl.ds(entries[k], 8), :], result)
    return jnp.where(masks[8], result, 0.0)


def copy_rows(table, entry_of, stage, start, masks):
    parts = [merged(table, [entry_of(start + half + k) for k in range(8)], masks) for half in (0, 8)]
    stage[start : start + 16, :] = jnp.concatenate(parts, axis=0).astype(BF16)


def near_kernel(
    rows, order_ref, next_ref, lower_ref, upper_ref, partner_ref, fields_ref, select_ref, left_ref, list_ref,
    table, stage_a, stage_b, lists,
):
    turn = pl.program_id(0)
    half = rows // 2

    @pl.when(turn == 0)
    def _():
        for side, ref in enumerate((lower_ref, upper_ref)):
            spot = slice(side * half, (side + 1) * half)
            low = ref[...] & 255
            lists[spot, 0:LANES] = (ref[...] - low).astype(F32).astype(BF16)
            lists[spot, LANES:] = low.astype(F32).astype(BF16)

        def fill(group, carry):
            fill_blocks(fields_ref, rows, group * 8, 8, 0.0, table, 0)
            return carry

        lax.fori_loop(0, rows // 8, fill, 0)

    def compose(tile):
        entries = partner_ref[0, tile : tile + 1, :]
        width = entries.shape[1]
        grid = lax.broadcasted_iota(I32, (LANES, width), 0)
        hot = jnp.where(grid == (entries & (LANES - 1)), 1.0, 0.0).astype(BF16)
        found = jnp.dot(lists[...], jnp.concatenate([hot, hot], axis=0), preferred_element_type=F32)
        yield
        block = entries >> 7
        low, high = block < half, block >= half + rows
        chosen = jnp.where(low, block, jnp.where(high, block - rows, -8)) - lax.broadcasted_iota(I32, (8, width), 0)
        picked = jnp.zeros((8, width), F32)
        for start in range(0, rows, 8):
            picked = jnp.where(chosen == start, found[start : start + 8], picked)
        atom = jnp.sum(picked, axis=0, keepdims=True).astype(I32)
        yield
        atom = jnp.where(low, atom, jnp.where(high, atom + 2 * rows * LANES, entries + half * LANES))
        atom = atom + PAD - (lax.broadcasted_iota(I32, (1, width), 1) & 7)
        for side in range(width // LANES):
            row = tile * (width // LANES) + side
            list_ref[row : row + 1, :] = atom[:, side * LANES : (side + 1) * LANES]

    masks = sublane_masks()

    def load(local, stage):
        ref, first = (order_ref, local) if local < STEP else (next_ref, local - STEP)

        def entry_of(k):
            return ref[first * TILE + k]

        return [
            functools.partial(copy_rows, table, entry_of, stage, start, masks) for start in range(0, TILE, 16)
        ]

    def factors(place, stage):
        left = jnp.dot(stage[...], select_ref[...], preferred_element_type=F32)
        yield
        left_ref[place] = left.astype(BF16)

    @pl.when(turn == 0)
    def _():
        for side in range(2):
            for copy in load(side, stage_a.at[side]):
                copy()

    for tile in range(0, STEP, 2):
        here, there = (stage_a, stage_b) if tile % 4 == 0 else (stage_b, stage_a)
        weave(
            [factors(tile + side, here.at[side]) for side in range(2)] + [compose(tile + side) for side in range(2)],
            load(tile + 2, there.at[0]) + load(tile + 3, there.at[1]),
            2,
        )


def masked(values, kind):
    blocks = values.reshape(TILE // 16, 16, LANES) * kind[None]
    return blocks.reshape(TILE, LANES)


def tile_sums(left_ref, kinds_ref, place, far, sums):
    others = far[...]
    left = left_ref[place]
    left = jnp.concatenate([masked(left, kinds_ref[kind]) for kind in range(3)], axis=0)
    yield
    grams = nt_dot(left, others)
    yield
    chunk = 32
    high, low = [], []
    for start in range(0, TILE, chunk):
        window = grams[start : start + chunk]
        inside = jnp.maximum(window, 0.0)
        root = lax.rsqrt((1.0 + SOFT_CORE) - window)
        depth = grams[TILE + start : TILE + start + chunk]
        charge = grams[2 * TILE + start : 2 * TILE + start + chunk]
        parts = two_pieces(inside * inside * (depth + charge * (root * root * root)))
        high.append(parts[0])
        low.append(parts[1])
        yield
    both = jnp.dot(jnp.concatenate(high + low, axis=0), others, preferred_element_type=F32)
    yield
    sums[...] = both[0:TILE] + both[TILE:] + masked(left_ref[place], kinds_ref[3]).astype(F32)


def pair_scatter(numbers, sums, total):
    entries = jnp.concatenate(numbers, axis=1)
    forces = [[], [], []]
    for side in range(2):
        across = sums[side].T
        for axis in range(3):
            moment, place = (
                sum(across[first + axis + 8 * piece : first + axis + 8 * piece + 1] for piece in range(3))
                for first in (0, COPY)
            )
            forces[axis].append(place * across[ONE : ONE + 1] - moment)
    yield
    grid = lax.broadcasted_iota(I32, (ROW, ROW), 0)
    hot = jnp.where(grid == (entries & (ROW - 1)), 1.0, 0.0).astype(BF16)
    yield
    count = total.shape[0] // 3
    mask = lax.broadcasted_iota(I32, (count, ROW), 0) == (entries >> 8)
    high, low = [], []
    for axis in range(3):
        force = jnp.concatenate(forces[axis], axis=1)
        part = force.astype(BF16).astype(F32)
        high.append(jnp.where(mask, part, 0.0).astype(BF16))
        low.append(jnp.where(mask, force - part, 0.0).astype(BF16))
        yield
    both = nt_dot(jnp.concatenate(high + low, axis=0), hot)
    total[...] += both[0 : 3 * count] + both[3 * count :]


def weave(stages, copies, parts):
    size = -(-len(copies) // parts)
    for turn, _ in enumerate(itertools.zip_longest(*stages)):
        for copy in copies[turn * size : (turn + 1) * size]:
            copy()


def force_kernel(
    rows, list_ref, next_ref, order_ref, before_ref, lower_ref, fields_ref, upper_ref, kinds_ref, left_ref,
    out_ref, solute_ref, table, total, far_a, far_b, sum_a, sum_b,
):
    turn = pl.program_id(0)
    partners = far_a.shape[1]
    own = rows * LANES
    masks = sublane_masks()

    def load(local, far):
        ref, first = (list_ref, local) if local < STEP else (next_ref, local - STEP)

        def entry_of(k):
            return ref[first * partners + k]

        return [
            functools.partial(copy_rows, table, entry_of, far, start, masks)
            for start in range(0, partners, 16)
        ]

    def scatter(local, sums):
        ref, first = (order_ref, local) if local >= 0 else (before_ref, local + STEP)
        return pair_scatter([ref[first + side : first + side + 1, :] for side in range(2)], sums, total)

    @pl.when(turn == 0)
    def _():
        def fill(group, carry):
            for domain, ref in enumerate((lower_ref, fields_ref, upper_ref)):
                fill_blocks(ref, rows, group * 4, 4, (domain - 1) * SLAB_WIDTH, table, domain * own)
            return carry

        lax.fori_loop(0, rows // 4, fill, 0)
        sum_b[...] = jnp.zeros_like(sum_b)
        total[...] = jnp.zeros_like(total)
        for side in range(2):
            for copy in load(side, far_a.at[side]):
                copy()

    for tile in range(0, STEP, 2):
        far, far_next, sums, sums_before = (
            (far_a, far_b, sum_a, sum_b) if tile % 4 == 0 else (far_b, far_a, sum_b, sum_a)
        )
        weave(
            [tile_sums(left_ref, kinds_ref, tile + side, far.at[side], sums.at[side]) for side in range(2)]
            + [scatter(tile - 2, sums_before)],
            load(tile + 2, far_next.at[0]) + load(tile + 3, far_next.at[1]),
            7,
        )

    @pl.when(turn == pl.num_programs(0) - 1)
    def _():
        for _ in scatter(STEP - 2, sum_b):
            pass
        count = rows * LANES // ROW
        for axis in range(3):
            force = total[axis * count : (axis + 1) * count, :]
            for side in range(ROW // LANES):
                spot = pl.ds(axis * rows + side, count, stride=ROW // LANES)
                out_ref[spot, :] = fields_ref[spot, :] + STEP_SIZE * force[:, side * LANES : (side + 1) * LANES]
        solute = SOL_DEV // LANES
        for axis in range(3):
            solute_ref[axis] = out_ref[axis * rows : axis * rows + solute, :]
            solute_ref[3 + axis] = fields_ref[axis * rows : axis * rows + solute, :]


def product_kernel(images, index_ref, *refs):
    solute_refs, (sums_ref, pushed, path) = refs[:images], refs[images:]
    index = index_ref[0]
    for by in range(images):
        place = lax.rem(index + images - by, images)
        pushed[place] = solute_refs[by][0:3]
        path[place] = solute_refs[by][3:6]
    sums_ref[...] = jnp.zeros_like(sums_ref)
    last = images - 1
    tangents = [path[min(k + 1, last)] - path[max(k - 1, 0)] for k in range(images)]

    def put(kind, image, left, right):
        total = jnp.sum(left * right, axis=0)
        sums_ref[kind * images + image : kind * images + image + 1, :] = jnp.sum(total, axis=0, keepdims=True)

    for k in range(images):
        put(0, k, tangents[k], tangents[k])
        put(1, k, pushed[k] - path[k], tangents[k])
        if k < last:
            step = path[k + 1] - path[k]
            gap = pushed[k + 1] - pushed[k]
            put(2, k, step, step)
            put(3, k, gap, gap)
            put(4, k, gap, tangents[k + 1])
            put(5, k, gap, tangents[k])
            put(6, k, tangents[k + 1], tangents[k])


def blend_kernel(images, index_ref, sums_ref, pushed, path, out_in, out_ref):
    del out_in
    index = index_ref[0]
    last = images - 1
    totals = jnp.sum(sums_ref[...], axis=1, keepdims=True)

    def total(kind, image):
        row = kind * images + image
        return totals[row : row + 1, :]

    step_root = [jnp.sqrt(total(2, k) + EPSILON) for k in range(last)]
    shift = []
    for k in range(images):
        tangent_sq = total(0, k)
        value = -total(1, k) / (tangent_sq + EPSILON)
        if 0 < k < last:
            spring = SPRING_COEF * (step_root[k] - step_root[k - 1]) / jnp.sqrt(tangent_sq + EPSILON)
            value = value + STEP_SIZE * spring
        shift.append(value)
    lengths = []
    for k in range(last):
        there, here = shift[k + 1], shift[k]
        length_sq = (
            total(3, k)
            + there * there * total(0, k + 1)
            + here * here * total(0, k)
            + 2.0 * (there * total(4, k) - here * total(5, k) - there * here * total(6, k))
        )
        lengths.append(jnp.sqrt(jnp.maximum(length_sq, 0.0) + EPSILON))
    knots = [jnp.zeros_like(lengths[0])]
    for length in lengths:
        knots.append(knots[-1] + length)

    def pick(values):
        result = values[0]
        for k in range(1, images):
            result = jnp.where(index == k, values[k], result)
        return result

    none = jnp.zeros_like(lengths[0])
    excess = [knots[k] - knots[last] * (k / last) for k in range(images)]
    back = pick([none] + [jnp.clip(excess[k] / lengths[k - 1], 0.0, 1.0) for k in range(1, images)])
    ahead = pick([jnp.clip(-excess[k] / lengths[k], 0.0, 1.0) for k in range(last)] + [none])
    shifts = [pick([shift[min(max(k + by, 0), last)] for k in range(images)]) for by in (-1, 0, 1)]

    def moved(by):
        place = jnp.clip(index + by, 0, last)
        tangent = path[jnp.minimum(place + 1, last)] - path[jnp.maximum(place - 1, 0)]
        return pushed[place] + shifts[by + 1] * tangent

    here = moved(0)
    blended = here + back * (moved(-1) - here) + ahead * (moved(1) - here)
    out_ref[...] = blended


def whole(*shape, dtype=F32):
    return jax.ShapeDtypeStruct(shape, dtype)


def turned(array, axis, by):
    count = lax.axis_size(axis)
    return lax.ppermute(array, axis, [(i, (i + by) % count) for i in range(count)])


def summed(array, axis):
    count = lax.axis_size(axis)
    if count & (count - 1):
        return lax.psum(array, axis)

    def crossed(by):
        return lax.ppermute(array, axis, [(i, i ^ by) for i in range(count)])

    array = array + crossed(1)
    return sum((crossed(by) for by in range(2, count, 2)), array)


def round_trip(array, axis):
    return [array] + [turned(array, axis, by) for by in range(1, lax.axis_size(axis))]


def per_device(positions, strength, charge, rest_scale, cell_order, ghost_index, tile_atoms):
    atoms = positions.shape[2]
    rows = atoms // LANES
    partners = tile_atoms.shape[2]
    images = lax.axis_size("image")
    index = lax.axis_index("image").reshape(1)

    factor = jnp.where(jnp.arange(atoms) < SOL_DEV, jnp.sqrt(rest_scale[0]), 1.0)
    scaled = jnp.stack([strength * factor * LJ_COEF**0.5, charge * factor * CHARGE_COEF**0.5])
    places = positions.reshape(3, rows, LANES)
    fields = jnp.concatenate([places, scaled.reshape(2, rows, LANES)]).reshape(FIELDS * rows, LANES)
    shell = ghost_index.reshape(2, rows // 2, LANES)
    lower_list, upper_list = turned(shell[1], "space", 1), turned(shell[0], "space", -1)
    fields, lower_list, upper_list = lax.optimization_barrier((fields, lower_list, upper_list))
    lower, upper = turned(fields, "space", 1), turned(fields, "space", -1)
    tile_order = cell_order.reshape(rows, LANES)
    order = cell_order.reshape(atoms) + (PAD - jnp.arange(atoms, dtype=I32) % 8)
    scalar = pl.BlockSpec(memory_space=pltpu.SMEM)
    vector = pl.BlockSpec(memory_space=pltpu.VMEM)
    params = pltpu.CompilerParams(vmem_limit_bytes=VMEM_LIMIT)
    last = rows // STEP - 1

    def listed(size, by):
        return pl.BlockSpec((STEP * size,), lambda i: (jnp.clip(i + by, 0, last),), memory_space=pltpu.SMEM)

    table = (atoms + 2 * PAD, LANES)
    left, partner_rows = pl.pallas_call(
        functools.partial(near_kernel, rows),
        grid=(rows // STEP,),
        out_shape=[whole(rows, TILE, LANES, dtype=BF16), whole(rows * partners // LANES, LANES, dtype=I32)],
        in_specs=[listed(TILE, 0), listed(TILE, 1)]
        + [vector] * 2
        + [pl.BlockSpec((1, STEP, partners), lambda i: (0, i, 0))]
        + [vector] * 2,
        out_specs=[
            pl.BlockSpec((STEP, TILE, LANES), lambda i: (i, 0, 0)),
            pl.BlockSpec((STEP * partners // LANES, LANES), lambda i: (i, 0)),
        ],
        scratch_shapes=[
            pltpu.VMEM(table, F32),
            pltpu.VMEM((2, TILE, LANES), BF16),
            pltpu.VMEM((2, TILE, LANES), BF16),
            pltpu.VMEM((rows, 2 * LANES), BF16),
        ],
        compiler_params=params,
        cost_estimate=pl.CostEstimate(flops=25 * 10**9, bytes_accessed=10**7, transcendentals=0),
    )(order, order, lower_list, upper_list, tile_atoms, fields, near_selector())
    pairs = partner_rows.reshape(rows * partners)
    out, solute = pl.pallas_call(
        functools.partial(force_kernel, rows),
        grid=(rows // STEP,),
        out_shape=[whole(3 * rows, LANES), whole(6, SOL_DEV // LANES, LANES)],
        in_specs=[listed(partners, 0), listed(partners, 1)]
        + [pl.BlockSpec((STEP, LANES), lambda i, by=by: (jnp.maximum(i - by, 0), 0)) for by in (0, 1)]
        + [vector] * 4
        + [pl.BlockSpec((STEP, TILE, LANES), lambda i: (i, 0, 0))],
        out_specs=[vector] * 2,
        scratch_shapes=[
            pltpu.VMEM((3 * atoms + 2 * PAD, LANES), F32),
            pltpu.VMEM((3 * atoms // ROW, ROW), F32),
            pltpu.VMEM((2, partners, LANES), BF16),
            pltpu.VMEM((2, partners, LANES), BF16),
            pltpu.VMEM((2, TILE, LANES), F32),
            pltpu.VMEM((2, TILE, LANES), F32),
        ],
        compiler_params=params,
        cost_estimate=pl.CostEstimate(flops=25 * 10**9, bytes_accessed=10**7, transcendentals=0),
    )(pairs, pairs, tile_order, tile_order, lower, fields, upper, near_masks(), left)
    out = out.reshape(3, rows, LANES)
    solutes = round_trip(solute, "image")
    small = pltpu.CompilerParams(vmem_limit_bytes=8 * 1024 * 1024)
    solute_shape = whole(images, 3, SOL_DEV // LANES, LANES)
    sums, pushed, path = pl.pallas_call(
        functools.partial(product_kernel, images),
        out_shape=[whole(-(-7 * images // 8) * 8, LANES), solute_shape, solute_shape],
        in_specs=[scalar] + [vector] * images,
        out_specs=[vector] * 3,
        compiler_params=small,
    )(index, *solutes)
    out = pl.pallas_call(
        functools.partial(blend_kernel, images),
        grid=(1,),
        out_shape=whole(3, rows, LANES),
        in_specs=[scalar] + [vector] * 3 + [pl.BlockSpec(memory_space=pl.ANY)],
        out_specs=pl.BlockSpec((3, SOL_DEV // LANES, LANES), lambda i: (0, 0, 0)),
        input_output_aliases={4: 0},
        compiler_params=small,
    )(index, summed(sums, "space"), pushed, path, out)
    return out.reshape(1, 3, atoms)


def solution(mesh):
    placed = (
        P("image", None, "space"),
        P("space"),
        P("space"),
        P("image"),
        P("image", "space", None),
        P("image", "space", None),
        P("image", "space", None),
    )
    return jax.shard_map(
        per_device, mesh=mesh, in_specs=placed, out_specs=P("image", None, "space"), check_vma=False
    )
```

```python
import functools
import itertools

import jax
import jax.numpy as jnp
import numpy as np
from jax import lax
from jax.experimental import pallas as pl
from jax.experimental.pallas import tpu as pltpu
from jax.sharding import PartitionSpec as P

SOL_DEV = 1024
TILE = 128
LANES = 128
FIELDS = 5
PAD = 8

LJ_COEF = 0.5
CHARGE_COEF = 0.1
SOFT_CORE = 0.09
SLAB_WIDTH = 1.0
STEP_SIZE = 0.2
SPRING_COEF = 1.0
EPSILON = 1e-06
CENTRE = 0.5

F32 = jnp.float32
BF16 = jnp.bfloat16
I32 = jnp.int32
VMEM_LIMIT = 58 * 1024 * 1024

DEPTH, CHARGE, ONE, NORM, LAST = 3, 4, 5, 6, 7
FAR_PIECES = (0, 1, 2, 0, 1, 0)
STEP = 40
ROW = 256
COPY = 64
USED = 8 * len(FAR_PIECES)
NEAR_PIECES = (0, 0, 0, 1, 1, 2)


def near_selector():
    chosen = np.zeros((LANES, LANES), np.float32)
    for group, piece in enumerate(NEAR_PIECES):
        for axis in range(3):
            chosen[piece * 8 + axis, group * 8 + axis] = 2.0
        for field in (DEPTH, CHARGE):
            chosen[piece * 8 + field, group * 8 + field] = 1.0
    for piece in range(3):
        for axis in range(3):
            chosen[piece * 8 + axis, COPY + piece * 8 + axis] = 1.0
    for piece, group in ((0, 0), (1, 3), (2, 5)):
        chosen[piece * 8 + NORM, group * 8 + ONE] = 1.0
        chosen[ONE, piece * 8 + NORM] = 1.0
    chosen[ONE, LAST] = 1.0
    return jnp.asarray(chosen, BF16)


def near_masks():
    lane = np.arange(LANES)
    field = lane % 8
    kinds = [(field != DEPTH) & (field != CHARGE), field == DEPTH, field == CHARGE, lane >= COPY]
    return jnp.asarray(np.stack([np.tile(kind, (16, 1)) for kind in kinds]), BF16)


def two_pieces(values):
    high = values.astype(BF16)
    low = (values - high.astype(F32)).astype(BF16)
    return high, low


def nt_dot(left, right):
    return lax.dot_general(left, right, (((1,), (1,)), ((), ())), preferred_element_type=F32)


def fill_blocks(fields_ref, rows, start_row, count, shift, table, first):
    sublane = lax.broadcasted_iota(I32, (8, LANES), 0)
    move = jnp.where(sublane < 3, jnp.where(sublane == 0, shift - CENTRE, -CENTRE), 0.0)
    ones = jnp.ones((8 - FIELDS, LANES), F32)
    corner = lax.broadcasted_iota(I32, (LANES, LANES), 0) == lax.broadcasted_iota(I32, (LANES, LANES), 1)
    eye = jnp.where(corner, 1.0, 0.0).astype(BF16)
    blank = jnp.zeros((LANES - USED, LANES), F32)

    def pieces(block):
        values = fields_ref[pl.ds(start_row + block, FIELDS, stride=rows), :]
        values = jnp.concatenate([values, ones], axis=0) + move
        norm = jnp.sum(jnp.where(sublane < 3, values * values, 0.0), axis=0, keepdims=True)
        rest = jnp.where(sublane == NORM, -norm, values)
        parts = []
        for _ in range(2):
            parts.append(rest.astype(BF16).astype(F32))
            rest = rest - parts[-1]
        parts.append(rest)
        return [parts[piece] for piece in FAR_PIECES]

    def put(block, value):
        start = pl.multiple_of(first + (start_row + block) * LANES + PAD, PAD)
        table[pl.ds(start, LANES), 0:USED] = value

    for block in range(0, count, 4):
        for side in range(2):
            put(block + side, jnp.concatenate(pieces(block + side), axis=0).T)
        both = jnp.concatenate(pieces(block + 2) + [blank] + pieces(block + 3) + [blank], axis=0)
        both = nt_dot(eye, both.astype(BF16))
        for side in range(2):
            put(block + 2 + side, both[:, side * LANES : side * LANES + USED])


def sublane_masks():
    sublane = lax.broadcasted_iota(I32, (8, LANES), 0)
    used = lax.broadcasted_iota(I32, (8, LANES), 1) < USED
    return [sublane == k for k in range(8)] + [used]


def merged(table, entries, masks):
    result = table[pl.ds(entries[0], 8), :]
    for k in range(1, 8):
        result = jnp.where(masks[k], table[pl.ds(entries[k], 8), :], result)
    return jnp.where(masks[8], result, 0.0)


def copy_rows(table, entry_of, stage, start, masks):
    parts = [merged(table, [entry_of(start + half + k) for k in range(8)], masks) for half in (0, 8)]
    stage[start : start + 16, :] = jnp.concatenate(parts, axis=0).astype(BF16)


def near_kernel(
    rows, order_ref, next_ref, lower_ref, upper_ref, partner_ref, fields_ref, select_ref, left_ref, list_ref,
    table, stage_a, stage_b, lists,
):
    turn = pl.program_id(0)
    half = rows // 2

    @pl.when(turn == 0)
    def _():
        for side, ref in enumerate((lower_ref, upper_ref)):
            spot = slice(side * half, (side + 1) * half)
            low = ref[...] & 255
            lists[spot, 0:LANES] = (ref[...] - low).astype(F32).astype(BF16)
            lists[spot, LANES:] = low.astype(F32).astype(BF16)

        def fill(group, carry):
            fill_blocks(fields_ref, rows, group * 8, 8, 0.0, table, 0)
            return carry

        lax.fori_loop(0, rows // 8, fill, 0)

    def compose(tile):
        entries = partner_ref[0, tile : tile + 1, :]
        width = entries.shape[1]
        grid = lax.broadcasted_iota(I32, (LANES, width), 0)
        hot = jnp.where(grid == (entries & (LANES - 1)), 1.0, 0.0).astype(BF16)
        found = jnp.dot(lists[...], jnp.concatenate([hot, hot], axis=0), preferred_element_type=F32)
        yield
        block = entries >> 7
        low, high = block < half, block >= half + rows
        chosen = jnp.where(low, block, jnp.where(high, block - rows, -8)) - lax.broadcasted_iota(I32, (8, width), 0)
        picked = jnp.zeros((8, width), F32)
        for start in range(0, rows, 8):
            picked = jnp.where(chosen == start, found[start : start + 8], picked)
        atom = jnp.sum(picked, axis=0, keepdims=True).astype(I32)
        yield
        atom = jnp.where(low, atom, jnp.where(high, atom + 2 * rows * LANES, entries + half * LANES))
        atom = atom + PAD - (lax.broadcasted_iota(I32, (1, width), 1) & 7)
        for side in range(width // LANES):
            row = tile * (width // LANES) + side
            list_ref[row : row + 1, :] = atom[:, side * LANES : (side + 1) * LANES]

    masks = sublane_masks()

    def load(local, stage):
        ref, first = (order_ref, local) if local < STEP else (next_ref, local - STEP)

        def entry_of(k):
            return ref[first * TILE + k]

        return [
            functools.partial(copy_rows, table, entry_of, stage, start, masks) for start in range(0, TILE, 16)
        ]

    def factors(place, stage):
        left = jnp.dot(stage[...], select_ref[...], preferred_element_type=F32)
        yield
        left_ref[place] = left.astype(BF16)

    @pl.when(turn == 0)
    def _():
        for side in range(2):
            for copy in load(side, stage_a.at[side]):
                copy()

    for tile in range(0, STEP, 2):
        here, there = (stage_a, stage_b) if tile % 4 == 0 else (stage_b, stage_a)
        weave(
            [factors(tile + side, here.at[side]) for side in range(2)] + [compose(tile + side) for side in range(2)],
            load(tile + 2, there.at[0]) + load(tile + 3, there.at[1]),
            2,
        )


def masked(values, kind):
    blocks = values.reshape(TILE // 16, 16, LANES) * kind[None]
    return blocks.reshape(TILE, LANES)


def tile_sums(left_ref, kinds_ref, place, far, sums):
    others = far[...]
    left = left_ref[place]
    left = jnp.concatenate([masked(left, kinds_ref[kind]) for kind in range(3)], axis=0)
    yield
    grams = nt_dot(left, others)
    yield
    chunk = 32
    high, low = [], []
    for start in range(0, TILE, chunk):
        window = grams[start : start + chunk]
        inside = jnp.maximum(window, 0.0)
        root = lax.rsqrt((1.0 + SOFT_CORE) - window)
        depth = grams[TILE + start : TILE + start + chunk]
        charge = grams[2 * TILE + start : 2 * TILE + start + chunk]
        parts = two_pieces(inside * inside * (depth + charge * (root * root * root)))
        high.append(parts[0])
        low.append(parts[1])
        yield
    both = jnp.dot(jnp.concatenate(high + low, axis=0), others, preferred_element_type=F32)
    yield
    sums[...] = both[0:TILE] + both[TILE:] + masked(left_ref[place], kinds_ref[3]).astype(F32)


def pair_scatter(numbers, sums, total):
    entries = jnp.concatenate(numbers, axis=1)
    forces = [[], [], []]
    for side in range(2):
        across = sums[side].T
        for axis in range(3):
            moment, place = (
                sum(across[first + axis + 8 * piece : first + axis + 8 * piece + 1] for piece in range(3))
                for first in (0, COPY)
            )
            forces[axis].append(place * across[ONE : ONE + 1] - moment)
    yield
    grid = lax.broadcasted_iota(I32, (ROW, ROW), 0)
    hot = jnp.where(grid == (entries & (ROW - 1)), 1.0, 0.0).astype(BF16)
    yield
    count = total.shape[0] // 3
    mask = lax.broadcasted_iota(I32, (count, ROW), 0) == (entries >> 8)
    high, low = [], []
    for axis in range(3):
        force = jnp.concatenate(forces[axis], axis=1)
        part = force.astype(BF16).astype(F32)
        high.append(jnp.where(mask, part, 0.0).astype(BF16))
        low.append(jnp.where(mask, force - part, 0.0).astype(BF16))
        yield
    both = nt_dot(jnp.concatenate(high + low, axis=0), hot)
    total[...] += both[0 : 3 * count] + both[3 * count :]


def weave(stages, copies, parts):
    size = -(-len(copies) // parts)
    for turn, _ in enumerate(itertools.zip_longest(*stages)):
        for copy in copies[turn * size : (turn + 1) * size]:
            copy()


def force_kernel(
    rows, list_ref, next_ref, order_ref, before_ref, lower_ref, fields_ref, upper_ref, kinds_ref, left_ref,
    out_ref, solute_ref, table, total, far_a, far_b, sum_a, sum_b,
):
    turn = pl.program_id(0)
    partners = far_a.shape[1]
    own = rows * LANES
    masks = sublane_masks()

    def load(local, far):
        ref, first = (list_ref, local) if local < STEP else (next_ref, local - STEP)

        def entry_of(k):
            return ref[first * partners + k]

        return [
            functools.partial(copy_rows, table, entry_of, far, start, masks)
            for start in range(0, partners, 16)
        ]

    def scatter(local, sums):
        ref, first = (order_ref, local) if local >= 0 else (before_ref, local + STEP)
        return pair_scatter([ref[first + side : first + side + 1, :] for side in range(2)], sums, total)

    @pl.when(turn == 0)
    def _():
        def fill(group, carry):
            for domain, ref in enumerate((lower_ref, fields_ref, upper_ref)):
                fill_blocks(ref, rows, group * 4, 4, (domain - 1) * SLAB_WIDTH, table, domain * own)
            return carry

        lax.fori_loop(0, rows // 4, fill, 0)
        sum_b[...] = jnp.zeros_like(sum_b)
        total[...] = jnp.zeros_like(total)
        for side in range(2):
            for copy in load(side, far_a.at[side]):
                copy()

    for tile in range(0, STEP, 2):
        far, far_next, sums, sums_before = (
            (far_a, far_b, sum_a, sum_b) if tile % 4 == 0 else (far_b, far_a, sum_b, sum_a)
        )
        weave(
            [tile_sums(left_ref, kinds_ref, tile + side, far.at[side], sums.at[side]) for side in range(2)]
            + [scatter(tile - 2, sums_before)],
            load(tile + 2, far_next.at[0]) + load(tile + 3, far_next.at[1]),
            7,
        )

    @pl.when(turn == pl.num_programs(0) - 1)
    def _():
        for _ in scatter(STEP - 2, sum_b):
            pass
        count = rows * LANES // ROW
        for axis in range(3):
            force = total[axis * count : (axis + 1) * count, :]
            for side in range(ROW // LANES):
                spot = pl.ds(axis * rows + side, count, stride=ROW // LANES)
                out_ref[spot, :] = fields_ref[spot, :] + STEP_SIZE * force[:, side * LANES : (side + 1) * LANES]
        solute = SOL_DEV // LANES
        for axis in range(3):
            solute_ref[axis] = out_ref[axis * rows : axis * rows + solute, :]
            solute_ref[3 + axis] = fields_ref[axis * rows : axis * rows + solute, :]


def product_kernel(images, index_ref, *refs):
    solute_refs, (sums_ref, pushed, path) = refs[:images], refs[images:]
    index = index_ref[0]
    for by in range(images):
        place = lax.rem(index + images - by, images)
        pushed[place] = solute_refs[by][0:3]
        path[place] = solute_refs[by][3:6]
    sums_ref[...] = jnp.zeros_like(sums_ref)
    last = images - 1
    tangents = [path[min(k + 1, last)] - path[max(k - 1, 0)] for k in range(images)]

    def put(kind, image, left, right):
        total = jnp.sum(left * right, axis=0)
        sums_ref[kind * images + image : kind * images + image + 1, :] = jnp.sum(total, axis=0, keepdims=True)

    for k in range(images):
        put(0, k, tangents[k], tangents[k])
        put(1, k, pushed[k] - path[k], tangents[k])
        if k < last:
            step = path[k + 1] - path[k]
            gap = pushed[k + 1] - pushed[k]
            put(2, k, step, step)
            put(3, k, gap, gap)
            put(4, k, gap, tangents[k + 1])
            put(5, k, gap, tangents[k])
            put(6, k, tangents[k + 1], tangents[k])


def blend_kernel(images, index_ref, sums_ref, pushed, path, out_in, out_ref):
    del out_in
    index = index_ref[0]
    last = images - 1
    totals = jnp.sum(sums_ref[...], axis=1, keepdims=True)

    def total(kind, image):
        row = kind * images + image
        return totals[row : row + 1, :]

    step_root = [jnp.sqrt(total(2, k) + EPSILON) for k in range(last)]
    shift = []
    for k in range(images):
        tangent_sq = total(0, k)
        value = -total(1, k) / (tangent_sq + EPSILON)
        if 0 < k < last:
            spring = SPRING_COEF * (step_root[k] - step_root[k - 1]) / jnp.sqrt(tangent_sq + EPSILON)
            value = value + STEP_SIZE * spring
        shift.append(value)
    lengths = []
    for k in range(last):
        there, here = shift[k + 1], shift[k]
        length_sq = (
            total(3, k)
            + there * there * total(0, k + 1)
            + here * here * total(0, k)
            + 2.0 * (there * total(4, k) - here * total(5, k) - there * here * total(6, k))
        )
        lengths.append(jnp.sqrt(jnp.maximum(length_sq, 0.0) + EPSILON))
    knots = [jnp.zeros_like(lengths[0])]
    for length in lengths:
        knots.append(knots[-1] + length)

    def pick(values):
        result = values[0]
        for k in range(1, images):
            result = jnp.where(index == k, values[k], result)
        return result

    none = jnp.zeros_like(lengths[0])
    excess = [knots[k] - knots[last] * (k / last) for k in range(images)]
    back = pick([none] + [jnp.clip(excess[k] / lengths[k - 1], 0.0, 1.0) for k in range(1, images)])
    ahead = pick([jnp.clip(-excess[k] / lengths[k], 0.0, 1.0) for k in range(last)] + [none])
    shifts = [pick([shift[min(max(k + by, 0), last)] for k in range(images)]) for by in (-1, 0, 1)]

    def moved(by):
        place = jnp.clip(index + by, 0, last)
        tangent = path[jnp.minimum(place + 1, last)] - path[jnp.maximum(place - 1, 0)]
        return pushed[place] + shifts[by + 1] * tangent

    here = moved(0)
    blended = here + back * (moved(-1) - here) + ahead * (moved(1) - here)
    out_ref[...] = blended


def whole(*shape, dtype=F32):
    return jax.ShapeDtypeStruct(shape, dtype)


def turned(array, axis, by):
    count = lax.axis_size(axis)
    return lax.ppermute(array, axis, [(i, (i + by) % count) for i in range(count)])


def summed(array, axis):
    count = lax.axis_size(axis)
    if count & (count - 1):
        return lax.psum(array, axis)

    def crossed(by):
        return lax.ppermute(array, axis, [(i, i ^ by) for i in range(count)])

    array = array + crossed(1)
    return sum((crossed(by) for by in range(2, count, 2)), array)


def round_trip(array, axis):
    return [array] + [turned(array, axis, by) for by in range(1, lax.axis_size(axis))]


def per_device(positions, strength, charge, rest_scale, cell_order, ghost_index, tile_atoms):
    atoms = positions.shape[2]
    rows = atoms // LANES
    partners = tile_atoms.shape[2]
    images = lax.axis_size("image")
    index = lax.axis_index("image").reshape(1)

    factor = jnp.where(jnp.arange(atoms) < SOL_DEV, jnp.sqrt(rest_scale[0]), 1.0)
    scaled = jnp.stack([strength * factor * LJ_COEF**0.5, charge * factor * CHARGE_COEF**0.5])
    places = positions.reshape(3, rows, LANES)
    fields = jnp.concatenate([places, scaled.reshape(2, rows, LANES)]).reshape(FIELDS * rows, LANES)
    shell = ghost_index.reshape(2, rows // 2, LANES)
    lower_list, upper_list = turned(shell[1], "space", 1), turned(shell[0], "space", -1)
    fields, lower_list, upper_list = lax.optimization_barrier((fields, lower_list, upper_list))
    lower, upper = turned(fields, "space", 1), turned(fields, "space", -1)
    tile_order = cell_order.reshape(rows, LANES)
    order = cell_order.reshape(atoms) + (PAD - jnp.arange(atoms, dtype=I32) % 8)
    scalar = pl.BlockSpec(memory_space=pltpu.SMEM)
    vector = pl.BlockSpec(memory_space=pltpu.VMEM)
    params = pltpu.CompilerParams(vmem_limit_bytes=VMEM_LIMIT)
    last = rows // STEP - 1

    def listed(size, by):
        return pl.BlockSpec((STEP * size,), lambda i: (jnp.clip(i + by, 0, last),), memory_space=pltpu.SMEM)

    table = (atoms + 2 * PAD, LANES)
    left, partner_rows = pl.pallas_call(
        functools.partial(near_kernel, rows),
        grid=(rows // STEP,),
        out_shape=[whole(rows, TILE, LANES, dtype=BF16), whole(rows * partners // LANES, LANES, dtype=I32)],
        in_specs=[listed(TILE, 0), listed(TILE, 1)]
        + [vector] * 2
        + [pl.BlockSpec((1, STEP, partners), lambda i: (0, i, 0))]
        + [vector] * 2,
        out_specs=[
            pl.BlockSpec((STEP, TILE, LANES), lambda i: (i, 0, 0)),
            pl.BlockSpec((STEP * partners // LANES, LANES), lambda i: (i, 0)),
        ],
        scratch_shapes=[
            pltpu.VMEM(table, F32),
            pltpu.VMEM((2, TILE, LANES), BF16),
            pltpu.VMEM((2, TILE, LANES), BF16),
            pltpu.VMEM((rows, 2 * LANES), BF16),
        ],
        compiler_params=params,
        cost_estimate=pl.CostEstimate(flops=25 * 10**9, bytes_accessed=10**7, transcendentals=0),
    )(order, order, lower_list, upper_list, tile_atoms, fields, near_selector())
    pairs = partner_rows.reshape(rows * partners)
    out, solute = pl.pallas_call(
        functools.partial(force_kernel, rows),
        grid=(rows // STEP,),
        out_shape=[whole(3 * rows, LANES), whole(6, SOL_DEV // LANES, LANES)],
        in_specs=[listed(partners, 0), listed(partners, 1)]
        + [pl.BlockSpec((STEP, LANES), lambda i, by=by: (jnp.maximum(i - by, 0), 0)) for by in (0, 1)]
        + [vector] * 4
        + [pl.BlockSpec((STEP, TILE, LANES), lambda i: (i, 0, 0))],
        out_specs=[vector] * 2,
        scratch_shapes=[
            pltpu.VMEM((3 * atoms + 2 * PAD, LANES), F32),
            pltpu.VMEM((3 * atoms // ROW, ROW), F32),
            pltpu.VMEM((2, partners, LANES), BF16),
            pltpu.VMEM((2, partners, LANES), BF16),
            pltpu.VMEM((2, TILE, LANES), F32),
            pltpu.VMEM((2, TILE, LANES), F32),
        ],
        compiler_params=params,
        cost_estimate=pl.CostEstimate(flops=25 * 10**9, bytes_accessed=10**7, transcendentals=0),
    )(pairs, pairs, tile_order, tile_order, lower, fields, upper, near_masks(), left)
    out = out.reshape(3, rows, LANES)
    solutes = round_trip(solute, "image")
    small = pltpu.CompilerParams(vmem_limit_bytes=8 * 1024 * 1024)
    solute_shape = whole(images, 3, SOL_DEV // LANES, LANES)
    sums, pushed, path = pl.pallas_call(
        functools.partial(product_kernel, images),
        out_shape=[whole(-(-7 * images // 8) * 8, LANES), solute_shape, solute_shape],
        in_specs=[scalar] + [vector] * images,
        out_specs=[vector] * 3,
        compiler_params=small,
    )(index, *solutes)
    out = pl.pallas_call(
        functools.partial(blend_kernel, images),
        grid=(1,),
        out_shape=whole(3, rows, LANES),
        in_specs=[scalar] + [vector] * 3 + [pl.BlockSpec(memory_space=pl.ANY)],
        out_specs=pl.BlockSpec((3, SOL_DEV // LANES, LANES), lambda i: (0, 0, 0)),
        input_output_aliases={4: 0},
        compiler_params=small,
    )(index, summed(sums, "space"), pushed, path, out)
    return out.reshape(1, 3, atoms)


def solution(mesh):
    placed = (
        P("image", None, "space"),
        P("space"),
        P("space"),
        P("image"),
        P("image", "space", None),
        P("image", "space", None),
        P("image", "space", None),
    )
    return jax.shard_map(
        per_device, mesh=mesh, in_specs=placed, out_specs=P("image", None, "space"), check_vma=False
    )
```

```python
import functools
import itertools

import jax
import jax.numpy as jnp
import numpy as np
from jax import lax
from jax.experimental import pallas as pl
from jax.experimental.pallas import tpu as pltpu
from jax.sharding import PartitionSpec as P

SOL_DEV = 1024
TILE = 128
LANES = 128
FIELDS = 5
PAD = 8

LJ_COEF = 0.5
CHARGE_COEF = 0.1
SOFT_CORE = 0.09
SLAB_WIDTH = 1.0
STEP_SIZE = 0.2
SPRING_COEF = 1.0
EPSILON = 1e-06
CENTRE = 0.5

F32 = jnp.float32
BF16 = jnp.bfloat16
I32 = jnp.int32
VMEM_LIMIT = 58 * 1024 * 1024

DEPTH, CHARGE, ONE, NORM, LAST = 3, 4, 5, 6, 7
FAR_PIECES = (0, 1, 2, 0, 1, 0)
STEP = 16
FLIGHT = 4
ROW = 256
COPY = 64
USED = 8 * len(FAR_PIECES)
NEAR_PIECES = (0, 0, 0, 1, 1, 2)


def near_selector():
    chosen = np.zeros((LANES, LANES), np.float32)
    for group, piece in enumerate(NEAR_PIECES):
        for axis in range(3):
            chosen[piece * 8 + axis, group * 8 + axis] = 2.0
        for field in (DEPTH, CHARGE):
            chosen[piece * 8 + field, group * 8 + field] = 1.0
    for piece in range(3):
        for axis in range(3):
            chosen[piece * 8 + axis, COPY + piece * 8 + axis] = 1.0
    for piece, group in ((0, 0), (1, 3), (2, 5)):
        chosen[piece * 8 + NORM, group * 8 + ONE] = 1.0
        chosen[ONE, piece * 8 + NORM] = 1.0
    chosen[ONE, LAST] = 1.0
    return jnp.asarray(chosen, BF16)


def near_masks():
    lane = np.arange(LANES)
    field = lane % 8
    kinds = [(field != DEPTH) & (field != CHARGE), field == DEPTH, field == CHARGE, lane >= COPY]
    return jnp.asarray(np.stack([np.tile(kind, (16, 1)) for kind in kinds]), BF16)


def two_pieces(values):
    high = values.astype(BF16)
    low = (values - high.astype(F32)).astype(BF16)
    return high, low


def nt_dot(left, right):
    return lax.dot_general(left, right, (((1,), (1,)), ((), ())), preferred_element_type=F32)


def fill_blocks(fields_ref, rows, start_row, count, shift, table, first):
    sublane = lax.broadcasted_iota(I32, (8, LANES), 0)
    move = jnp.where(sublane < 3, jnp.where(sublane == 0, shift - CENTRE, -CENTRE), 0.0)
    ones = jnp.ones((8 - FIELDS, LANES), F32)
    corner = lax.broadcasted_iota(I32, (LANES, LANES), 0) == lax.broadcasted_iota(I32, (LANES, LANES), 1)
    eye = jnp.where(corner, 1.0, 0.0).astype(BF16)
    blank = jnp.zeros((LANES - USED, LANES), F32)

    def pieces(block):
        values = fields_ref[pl.ds(start_row + block, FIELDS, stride=rows), :]
        values = jnp.concatenate([values, ones], axis=0) + move
        norm = jnp.sum(jnp.where(sublane < 3, values * values, 0.0), axis=0, keepdims=True)
        rest = jnp.where(sublane == NORM, -norm, values)
        parts = []
        for _ in range(2):
            parts.append(rest.astype(BF16).astype(F32))
            rest = rest - parts[-1]
        parts.append(rest)
        return [parts[piece] for piece in FAR_PIECES]

    def put(block, value):
        start = pl.multiple_of(first + (start_row + block) * LANES + PAD, PAD)
        table[pl.ds(start, LANES), 0:USED] = value

    for block in range(0, count, 4):
        for side in range(2):
            put(block + side, jnp.concatenate(pieces(block + side), axis=0).T)
        both = jnp.concatenate(pieces(block + 2) + [blank] + pieces(block + 3) + [blank], axis=0)
        both = nt_dot(eye, both.astype(BF16))
        for side in range(2):
            put(block + 2 + side, both[:, side * LANES : side * LANES + USED])


def sublane_masks():
    sublane = lax.broadcasted_iota(I32, (8, LANES), 0)
    used = lax.broadcasted_iota(I32, (8, LANES), 1) < USED
    return [sublane == k for k in range(8)] + [used]


def merged(table, entries, masks):
    result = table[pl.ds(entries[0], 8), :]
    for k in range(1, 8):
        result = jnp.where(masks[k], table[pl.ds(entries[k], 8), :], result)
    return jnp.where(masks[8], result, 0.0)


def copy_rows(table, entry_of, stage, start, masks):
    parts = [merged(table, [entry_of(start + half + k) for k in range(8)], masks) for half in (0, 8)]
    stage[start : start + 16, :] = jnp.concatenate(parts, axis=0).astype(BF16)


def near_kernel(
    rows, order_ref, next_ref, lower_ref, upper_ref, partner_ref, fields_ref, select_ref, left_ref, list_ref,
    table, stage_a, stage_b, lists,
):
    turn = pl.program_id(0)
    half = rows // 2

    @pl.when(turn == 0)
    def _():
        for side, ref in enumerate((lower_ref, upper_ref)):
            spot = slice(side * half, (side + 1) * half)
            low = ref[...] & 255
            lists[spot, 0:LANES] = (ref[...] - low).astype(F32).astype(BF16)
            lists[spot, LANES:] = low.astype(F32).astype(BF16)

        def fill(group, carry):
            fill_blocks(fields_ref, rows, group * 8, 8, 0.0, table, 0)
            return carry

        lax.fori_loop(0, rows // 8, fill, 0)

    def compose(tile):
        entries = partner_ref[0, tile : tile + 1, :]
        width = entries.shape[1]
        grid = lax.broadcasted_iota(I32, (LANES, width), 0)
        hot = jnp.where(grid == (entries & (LANES - 1)), 1.0, 0.0).astype(BF16)
        found = jnp.dot(lists[...], jnp.concatenate([hot, hot], axis=0), preferred_element_type=F32)
        yield
        block = entries >> 7
        low, high = block < half, block >= half + rows
        chosen = jnp.where(low, block, jnp.where(high, block - rows, -8)) - lax.broadcasted_iota(I32, (8, width), 0)
        picked = jnp.zeros((8, width), F32)
        for start in range(0, rows, 8):
            picked = jnp.where(chosen == start, found[start : start + 8], picked)
        atom = jnp.sum(picked, axis=0, keepdims=True).astype(I32)
        yield
        atom = jnp.where(low, atom, jnp.where(high, atom + 2 * rows * LANES, entries + half * LANES))
        atom = atom + PAD - (lax.broadcasted_iota(I32, (1, width), 1) & 7)
        for side in range(width // LANES):
            row = tile * (width // LANES) + side
            list_ref[row : row + 1, :] = atom[:, side * LANES : (side + 1) * LANES]

    masks = sublane_masks()

    def load(local, stage):
        ref, first = (order_ref, local) if local < STEP else (next_ref, local - STEP)

        def entry_of(k):
            return ref[first * TILE + k] + (PAD - k % 8)

        return [
            functools.partial(copy_rows, table, entry_of, stage, start, masks) for start in range(0, TILE, 16)
        ]

    def factors(place, stage):
        left = jnp.dot(stage[...], select_ref[...], preferred_element_type=F32)
        yield
        left_ref[place] = left.astype(BF16)

    @pl.when(turn == 0)
    def _():
        for side in range(2):
            for copy in load(side, stage_a.at[side]):
                copy()

    for tile in range(0, STEP, 2):
        here, there = (stage_a, stage_b) if tile % 4 == 0 else (stage_b, stage_a)
        weave(
            [factors(tile + side, here.at[side]) for side in range(2)] + [compose(tile + side) for side in range(2)],
            load(tile + 2, there.at[0]) + load(tile + 3, there.at[1]),
            2,
        )


def masked(values, kind):
    blocks = values.reshape(TILE // 16, 16, LANES) * kind[None]
    return blocks.reshape(TILE, LANES)


def tile_sums(left_ref, kinds_ref, place, far, sums):
    others = far[...]
    left = left_ref[place]
    left = jnp.concatenate([masked(left, kinds_ref[kind]) for kind in range(3)], axis=0)
    yield
    grams = nt_dot(left, others)
    yield
    chunk = 32
    high, low = [], []
    for start in range(0, TILE, chunk):
        window = grams[start : start + chunk]
        inside = jnp.maximum(window, 0.0)
        root = lax.rsqrt((1.0 + SOFT_CORE) - window)
        depth = grams[TILE + start : TILE + start + chunk]
        charge = grams[2 * TILE + start : 2 * TILE + start + chunk]
        parts = two_pieces(inside * inside * (depth + charge * (root * root * root)))
        high.append(parts[0])
        low.append(parts[1])
        yield
    both = jnp.dot(jnp.concatenate(high + low, axis=0), others, preferred_element_type=F32)
    yield
    sums[...] = both[0:TILE] + both[TILE:] + masked(left_ref[place], kinds_ref[3]).astype(F32)


def pair_scatter(numbers, sums, total):
    entries = jnp.concatenate(numbers, axis=1)
    forces = [[], [], []]
    for side in range(2):
        across = sums[side].T
        for axis in range(3):
            moment, place = (
                sum(across[first + axis + 8 * piece : first + axis + 8 * piece + 1] for piece in range(3))
                for first in (0, COPY)
            )
            forces[axis].append(place * across[ONE : ONE + 1] - moment)
    yield
    grid = lax.broadcasted_iota(I32, (ROW, ROW), 0)
    hot = jnp.where(grid == (entries & (ROW - 1)), 1.0, 0.0).astype(BF16)
    yield
    count = total.shape[0] // 3
    mask = lax.broadcasted_iota(I32, (count, ROW), 0) == (entries >> 8)
    high, low = [], []
    for axis in range(3):
        force = jnp.concatenate(forces[axis], axis=1)
        part = force.astype(BF16).astype(F32)
        high.append(jnp.where(mask, part, 0.0).astype(BF16))
        low.append(jnp.where(mask, force - part, 0.0).astype(BF16))
        yield
    both = nt_dot(jnp.concatenate(high + low, axis=0), hot)
    total[...] += both[0 : 3 * count] + both[3 * count :]


def weave(stages, copies, parts):
    size = -(-len(copies) // parts)
    for turn, _ in enumerate(itertools.zip_longest(*stages)):
        for copy in copies[turn * size : (turn + 1) * size]:
            copy()


def force_kernel(
    rows, list_ref, next_ref, order_ref, before_ref, lower_ref, fields_ref, upper_ref, kinds_ref, left_ref,
    out_ref, solute_ref, table, total, far_a, far_b, sum_a, sum_b,
):
    turn = pl.program_id(0)
    partners = far_a.shape[1]
    own = rows * LANES
    masks = sublane_masks()

    def load(local, far):
        ref, first = (list_ref, local) if local < STEP else (next_ref, local - STEP)

        def entry_of(k):
            return ref[first * partners + k]

        return [
            functools.partial(copy_rows, table, entry_of, far, start, masks)
            for start in range(0, partners, 16)
        ]

    def scatter(local, sums):
        ref, first = (order_ref, local) if local >= 0 else (before_ref, local + STEP)
        return pair_scatter([ref[first + side : first + side + 1, :] for side in range(2)], sums, total)

    @pl.when(turn == 0)
    def _():
        def fill(group, carry):
            for domain, ref in enumerate((lower_ref, fields_ref, upper_ref)):
                fill_blocks(ref, rows, group * 4, 4, (domain - 1) * SLAB_WIDTH, table, domain * own)
            return carry

        lax.fori_loop(0, rows // 4, fill, 0)
        sum_b[...] = jnp.zeros_like(sum_b)
        total[...] = jnp.zeros_like(total)
        for side in range(FLIGHT):
            for copy in load(side, far_a.at[side]):
                copy()

    flight = range(FLIGHT)
    for tile in range(0, STEP, FLIGHT):
        far, far_next, sums, sums_before = (
            (far_a, far_b, sum_a, sum_b) if tile % (2 * FLIGHT) == 0 else (far_b, far_a, sum_b, sum_a)
        )
        weave(
            [tile_sums(left_ref, kinds_ref, tile + side, far.at[side], sums.at[side]) for side in flight]
            + [scatter(tile - FLIGHT + side, sums_before.at[pl.ds(side, 2)]) for side in flight[::2]],
            [copy for side in flight for copy in load(tile + FLIGHT + side, far_next.at[side])],
            7,
        )

    @pl.when(turn == pl.num_programs(0) - 1)
    def _():
        for side in range(0, FLIGHT, 2):
            for _ in scatter(STEP - FLIGHT + side, sum_b.at[pl.ds(side, 2)]):
                pass
        count = rows * LANES // ROW
        for axis in range(3):
            force = total[axis * count : (axis + 1) * count, :]
            for side in range(ROW // LANES):
                spot = pl.ds(axis * rows + side, count, stride=ROW // LANES)
                out_ref[spot, :] = fields_ref[spot, :] + STEP_SIZE * force[:, side * LANES : (side + 1) * LANES]
        solute = SOL_DEV // LANES
        for axis in range(3):
            solute_ref[axis] = out_ref[axis * rows : axis * rows + solute, :]
            solute_ref[3 + axis] = fields_ref[axis * rows : axis * rows + solute, :]


def product_kernel(images, index_ref, *refs):
    solute_refs, (sums_ref, pushed, path) = refs[:images], refs[images:]
    index = index_ref[0]
    for by in range(images):
        place = lax.rem(index + images - by, images)
        pushed[place] = solute_refs[by][0:3]
        path[place] = solute_refs[by][3:6]
    sums_ref[...] = jnp.zeros_like(sums_ref)
    last = images - 1
    tangents = [path[min(k + 1, last)] - path[max(k - 1, 0)] for k in range(images)]

    def put(kind, image, left, right):
        total = jnp.sum(left * right, axis=0)
        sums_ref[kind * images + image : kind * images + image + 1, :] = jnp.sum(total, axis=0, keepdims=True)

    for k in range(images):
        put(0, k, tangents[k], tangents[k])
        put(1, k, pushed[k] - path[k], tangents[k])
        if k < last:
            step = path[k + 1] - path[k]
            gap = pushed[k + 1] - pushed[k]
            put(2, k, step, step)
            put(3, k, gap, gap)
            put(4, k, gap, tangents[k + 1])
            put(5, k, gap, tangents[k])
            put(6, k, tangents[k + 1], tangents[k])


def blend_kernel(images, index_ref, sums_ref, pushed, path, out_in, out_ref):
    del out_in
    index = index_ref[0]
    last = images - 1
    totals = jnp.sum(sums_ref[...], axis=1, keepdims=True)

    def total(kind, image):
        row = kind * images + image
        return totals[row : row + 1, :]

    step_root = [jnp.sqrt(total(2, k) + EPSILON) for k in range(last)]
    shift = []
    for k in range(images):
        tangent_sq = total(0, k)
        value = -total(1, k) / (tangent_sq + EPSILON)
        if 0 < k < last:
            spring = SPRING_COEF * (step_root[k] - step_root[k - 1]) / jnp.sqrt(tangent_sq + EPSILON)
            value = value + STEP_SIZE * spring
        shift.append(value)
    lengths = []
    for k in range(last):
        there, here = shift[k + 1], shift[k]
        length_sq = (
            total(3, k)
            + there * there * total(0, k + 1)
            + here * here * total(0, k)
            + 2.0 * (there * total(4, k) - here * total(5, k) - there * here * total(6, k))
        )
        lengths.append(jnp.sqrt(jnp.maximum(length_sq, 0.0) + EPSILON))
    knots = [jnp.zeros_like(lengths[0])]
    for length in lengths:
        knots.append(knots[-1] + length)

    def pick(values):
        result = values[0]
        for k in range(1, images):
            result = jnp.where(index == k, values[k], result)
        return result

    none = jnp.zeros_like(lengths[0])
    excess = [knots[k] - knots[last] * (k / last) for k in range(images)]
    back = pick([none] + [jnp.clip(excess[k] / lengths[k - 1], 0.0, 1.0) for k in range(1, images)])
    ahead = pick([jnp.clip(-excess[k] / lengths[k], 0.0, 1.0) for k in range(last)] + [none])
    shifts = [pick([shift[min(max(k + by, 0), last)] for k in range(images)]) for by in (-1, 0, 1)]

    def moved(by):
        place = jnp.clip(index + by, 0, last)
        tangent = path[jnp.minimum(place + 1, last)] - path[jnp.maximum(place - 1, 0)]
        return pushed[place] + shifts[by + 1] * tangent

    here = moved(0)
    blended = here + back * (moved(-1) - here) + ahead * (moved(1) - here)
    out_ref[...] = blended


def whole(*shape, dtype=F32):
    return jax.ShapeDtypeStruct(shape, dtype)


def turned(array, axis, by):
    count = lax.axis_size(axis)
    return lax.ppermute(array, axis, [(i, (i + by) % count) for i in range(count)])


def summed(array, axis):
    count = lax.axis_size(axis)
    if count & (count - 1):
        return lax.psum(array, axis)

    def crossed(by):
        return lax.ppermute(array, axis, [(i, i ^ by) for i in range(count)])

    array = array + crossed(1)
    return sum((crossed(by) for by in range(2, count, 2)), array)


def round_trip(array, axis):
    return [array] + [turned(array, axis, by) for by in range(1, lax.axis_size(axis))]


def per_device(positions, strength, charge, rest_scale, cell_order, ghost_index, tile_atoms):
    atoms = positions.shape[2]
    rows = atoms // LANES
    partners = tile_atoms.shape[2]
    images = lax.axis_size("image")
    index = lax.axis_index("image").reshape(1)

    factor = jnp.where(jnp.arange(atoms) < SOL_DEV, jnp.sqrt(rest_scale[0]), 1.0)
    scaled = jnp.stack([strength * factor * LJ_COEF**0.5, charge * factor * CHARGE_COEF**0.5])
    places = positions.reshape(3, rows, LANES)
    fields = jnp.concatenate([places, scaled.reshape(2, rows, LANES)]).reshape(FIELDS * rows, LANES)
    shell = ghost_index.reshape(2, rows // 2, LANES)
    lower_list, upper_list = turned(shell[1], "space", 1), turned(shell[0], "space", -1)
    fields, lower_list, upper_list = lax.optimization_barrier((fields, lower_list, upper_list))
    lower, upper = turned(fields, "space", 1), turned(fields, "space", -1)
    tile_order = cell_order.reshape(rows, LANES)
    order = cell_order.reshape(atoms)
    scalar = pl.BlockSpec(memory_space=pltpu.SMEM)
    vector = pl.BlockSpec(memory_space=pltpu.VMEM)
    params = pltpu.CompilerParams(vmem_limit_bytes=VMEM_LIMIT)
    last = rows // STEP - 1

    def listed(size, by):
        return pl.BlockSpec((STEP * size,), lambda i: (jnp.clip(i + by, 0, last),), memory_space=pltpu.SMEM)

    table = (atoms + 2 * PAD, LANES)
    left, partner_rows = pl.pallas_call(
        functools.partial(near_kernel, rows),
        grid=(rows // STEP,),
        out_shape=[whole(rows, TILE, LANES, dtype=BF16), whole(rows * partners // LANES, LANES, dtype=I32)],
        in_specs=[listed(TILE, 0), listed(TILE, 1)]
        + [vector] * 2
        + [pl.BlockSpec((1, STEP, partners), lambda i: (0, i, 0))]
        + [vector] * 2,
        out_specs=[
            pl.BlockSpec((STEP, TILE, LANES), lambda i: (i, 0, 0)),
            pl.BlockSpec((STEP * partners // LANES, LANES), lambda i: (i, 0)),
        ],
        scratch_shapes=[
            pltpu.VMEM(table, F32),
            pltpu.VMEM((2, TILE, LANES), BF16),
            pltpu.VMEM((2, TILE, LANES), BF16),
            pltpu.VMEM((rows, 2 * LANES), BF16),
        ],
        compiler_params=params,
        cost_estimate=pl.CostEstimate(flops=25 * 10**9, bytes_accessed=10**7, transcendentals=0),
    )(order, order, lower_list, upper_list, tile_atoms, fields, near_selector())
    pairs = partner_rows.reshape(rows * partners)
    out, solute = pl.pallas_call(
        functools.partial(force_kernel, rows),
        grid=(rows // STEP,),
        out_shape=[whole(3 * rows, LANES), whole(6, SOL_DEV // LANES, LANES)],
        in_specs=[listed(partners, 0), listed(partners, 1)]
        + [pl.BlockSpec((STEP, LANES), lambda i, by=by: (jnp.maximum(i - by, 0), 0)) for by in (0, 1)]
        + [vector] * 4
        + [pl.BlockSpec((STEP, TILE, LANES), lambda i: (i, 0, 0))],
        out_specs=[vector] * 2,
        scratch_shapes=[
            pltpu.VMEM((3 * atoms + 2 * PAD, LANES), F32),
            pltpu.VMEM((3 * atoms // ROW, ROW), F32),
            pltpu.VMEM((FLIGHT, partners, LANES), BF16),
            pltpu.VMEM((FLIGHT, partners, LANES), BF16),
            pltpu.VMEM((FLIGHT, TILE, LANES), F32),
            pltpu.VMEM((FLIGHT, TILE, LANES), F32),
        ],
        compiler_params=params,
        cost_estimate=pl.CostEstimate(flops=25 * 10**9, bytes_accessed=10**7, transcendentals=0),
    )(pairs, pairs, tile_order, tile_order, lower, fields, upper, near_masks(), left)
    out = out.reshape(3, rows, LANES)
    solutes = round_trip(solute, "image")
    small = pltpu.CompilerParams(vmem_limit_bytes=8 * 1024 * 1024)
    solute_shape = whole(images, 3, SOL_DEV // LANES, LANES)
    sums, pushed, path = pl.pallas_call(
        functools.partial(product_kernel, images),
        out_shape=[whole(-(-7 * images // 8) * 8, LANES), solute_shape, solute_shape],
        in_specs=[scalar] + [vector] * images,
        out_specs=[vector] * 3,
        compiler_params=small,
    )(index, *solutes)
    out = pl.pallas_call(
        functools.partial(blend_kernel, images),
        grid=(1,),
        out_shape=whole(3, rows, LANES),
        in_specs=[scalar] + [vector] * 3 + [pl.BlockSpec(memory_space=pl.ANY)],
        out_specs=pl.BlockSpec((3, SOL_DEV // LANES, LANES), lambda i: (0, 0, 0)),
        input_output_aliases={4: 0},
        compiler_params=small,
    )(index, summed(sums, "space"), pushed, path, out)
    return out.reshape(1, 3, atoms)


def solution(mesh):
    placed = (
        P("image", None, "space"),
        P("space"),
        P("space"),
        P("image"),
        P("image", "space", None),
        P("image", "space", None),
        P("image", "space", None),
    )
    return jax.shard_map(
        per_device, mesh=mesh, in_specs=placed, out_specs=P("image", None, "space"), check_vma=False
    )
```

```python
import functools
import itertools

import jax
import jax.numpy as jnp
import numpy as np
from jax import lax
from jax.experimental import pallas as pl
from jax.experimental.pallas import tpu as pltpu
from jax.sharding import PartitionSpec as P

SOL_DEV = 1024
TILE = 128
LANES = 128
FIELDS = 5
PAD = 8

LJ_COEF = 0.5
CHARGE_COEF = 0.1
SOFT_CORE = 0.09
SLAB_WIDTH = 1.0
STEP_SIZE = 0.2
SPRING_COEF = 1.0
EPSILON = 1e-06
CENTRE = 0.5

F32 = jnp.float32
BF16 = jnp.bfloat16
I32 = jnp.int32
VMEM_LIMIT = 58 * 1024 * 1024

DEPTH, CHARGE, ONE, NORM, LAST = 3, 4, 5, 6, 7
FAR_PIECES = (0, 1, 2, 0, 1, 0)
STEP = 16
FLIGHT = 2
ROW = 256
COPY = 64
USED = 8 * len(FAR_PIECES)
NEAR_PIECES = (0, 0, 0, 1, 1, 2)


def near_selector():
    chosen = np.zeros((LANES, LANES), np.float32)
    for group, piece in enumerate(NEAR_PIECES):
        for axis in range(3):
            chosen[piece * 8 + axis, group * 8 + axis] = 2.0
        for field in (DEPTH, CHARGE):
            chosen[piece * 8 + field, group * 8 + field] = 1.0
    for piece in range(3):
        for axis in range(3):
            chosen[piece * 8 + axis, COPY + piece * 8 + axis] = 1.0
    for piece, group in ((0, 0), (1, 3), (2, 5)):
        chosen[piece * 8 + NORM, group * 8 + ONE] = 1.0
        chosen[ONE, piece * 8 + NORM] = 1.0
    chosen[ONE, LAST] = 1.0
    return jnp.asarray(chosen, BF16)


def near_masks():
    lane = np.arange(LANES)
    field = lane % 8
    kinds = [(field != DEPTH) & (field != CHARGE), field == DEPTH, field == CHARGE, lane >= COPY]
    return jnp.asarray(np.stack([np.tile(kind, (16, 1)) for kind in kinds]), BF16)


def two_pieces(values):
    high = values.astype(BF16)
    low = (values - high.astype(F32)).astype(BF16)
    return high, low


def nt_dot(left, right):
    return lax.dot_general(left, right, (((1,), (1,)), ((), ())), preferred_element_type=F32)


def fill_blocks(fields_ref, rows, start_row, count, shift, table, first):
    sublane = lax.broadcasted_iota(I32, (8, LANES), 0)
    move = jnp.where(sublane < 3, jnp.where(sublane == 0, shift - CENTRE, -CENTRE), 0.0)
    ones = jnp.ones((8 - FIELDS, LANES), F32)
    corner = lax.broadcasted_iota(I32, (LANES, LANES), 0) == lax.broadcasted_iota(I32, (LANES, LANES), 1)
    eye = jnp.where(corner, 1.0, 0.0).astype(BF16)
    blank = jnp.zeros((LANES - USED, LANES), F32)

    def pieces(block):
        values = fields_ref[pl.ds(start_row + block, FIELDS, stride=rows), :]
        values = jnp.concatenate([values, ones], axis=0) + move
        norm = jnp.sum(jnp.where(sublane < 3, values * values, 0.0), axis=0, keepdims=True)
        rest = jnp.where(sublane == NORM, -norm, values)
        parts = []
        for _ in range(2):
            parts.append(rest.astype(BF16).astype(F32))
            rest = rest - parts[-1]
        parts.append(rest)
        return [parts[piece] for piece in FAR_PIECES]

    def put(block, value):
        start = pl.multiple_of(first + (start_row + block) * LANES + PAD, PAD)
        table[pl.ds(start, LANES), 0:USED] = value

    for block in range(0, count, 4):
        for side in range(2):
            put(block + side, jnp.concatenate(pieces(block + side), axis=0).T)
        both = jnp.concatenate(pieces(block + 2) + [blank] + pieces(block + 3) + [blank], axis=0)
        both = nt_dot(eye, both.astype(BF16))
        for side in range(2):
            put(block + 2 + side, both[:, side * LANES : side * LANES + USED])


def sublane_masks():
    sublane = lax.broadcasted_iota(I32, (8, LANES), 0)
    used = lax.broadcasted_iota(I32, (8, LANES), 1) < USED
    return [sublane == k for k in range(8)] + [used]


def merged(table, entries, masks):
    result = table[pl.ds(entries[0], 8), :]
    for k in range(1, 8):
        result = jnp.where(masks[k], table[pl.ds(entries[k], 8), :], result)
    return jnp.where(masks[8], result, 0.0)


def copy_rows(table, entry_of, stage, start, masks):
    parts = [merged(table, [entry_of(start + half + k) for k in range(8)], masks) for half in (0, 8)]
    stage[start : start + 16, :] = jnp.concatenate(parts, axis=0).astype(BF16)


def near_kernel(
    rows, order_ref, next_ref, lower_ref, upper_ref, partner_ref, fields_ref, select_ref, left_ref, list_ref,
    table, stage_a, stage_b, lists,
):
    turn = pl.program_id(0)
    half = rows // 2

    @pl.when(turn == 0)
    def _():
        for side, ref in enumerate((lower_ref, upper_ref)):
            spot = slice(side * half, (side + 1) * half)
            low = ref[...] & 255
            lists[spot, 0:LANES] = (ref[...] - low).astype(F32).astype(BF16)
            lists[spot, LANES:] = low.astype(F32).astype(BF16)

        def fill(group, carry):
            fill_blocks(fields_ref, rows, group * 8, 8, 0.0, table, 0)
            return carry

        lax.fori_loop(0, rows // 8, fill, 0)

    def compose(tile):
        entries = partner_ref[0, tile : tile + 1, :]
        width = entries.shape[1]
        grid = lax.broadcasted_iota(I32, (LANES, width), 0)
        hot = jnp.where(grid == (entries & (LANES - 1)), 1.0, 0.0).astype(BF16)
        found = jnp.dot(lists[...], jnp.concatenate([hot, hot], axis=0), preferred_element_type=F32)
        yield
        block = entries >> 7
        low, high = block < half, block >= half + rows
        chosen = jnp.where(low, block, jnp.where(high, block - rows, -8)) - lax.broadcasted_iota(I32, (8, width), 0)
        picked = jnp.zeros((8, width), F32)
        for start in range(0, rows, 8):
            picked = jnp.where(chosen == start, found[start : start + 8], picked)
        atom = jnp.sum(picked, axis=0, keepdims=True).astype(I32)
        yield
        atom = jnp.where(low, atom, jnp.where(high, atom + 2 * rows * LANES, entries + half * LANES))
        atom = atom + PAD - (lax.broadcasted_iota(I32, (1, width), 1) & 7)
        for side in range(width // LANES):
            row = tile * (width // LANES) + side
            list_ref[row : row + 1, :] = atom[:, side * LANES : (side + 1) * LANES]

    masks = sublane_masks()

    def load(local, stage):
        ref, first = (order_ref, local) if local < STEP else (next_ref, local - STEP)

        def entry_of(k):
            return ref[first * TILE + k] + (PAD - k % 8)

        return [
            functools.partial(copy_rows, table, entry_of, stage, start, masks) for start in range(0, TILE, 16)
        ]

    def factors(place, stage):
        left = jnp.dot(stage[...], select_ref[...], preferred_element_type=F32)
        yield
        left_ref[place] = left.astype(BF16)

    @pl.when(turn == 0)
    def _():
        for side in range(2):
            for copy in load(side, stage_a.at[side]):
                copy()

    for tile in range(0, STEP, 2):
        here, there = (stage_a, stage_b) if tile % 4 == 0 else (stage_b, stage_a)
        weave(
            [factors(tile + side, here.at[side]) for side in range(2)] + [compose(tile + side) for side in range(2)],
            load(tile + 2, there.at[0]) + load(tile + 3, there.at[1]),
            2,
        )


def masked(values, kind):
    blocks = values.reshape(TILE // 16, 16, LANES) * kind[None]
    return blocks.reshape(TILE, LANES)


def tile_sums(left_ref, kinds_ref, place, far, sums):
    others = far[...]
    left = left_ref[place]
    left = jnp.concatenate([masked(left, kinds_ref[kind]) for kind in range(3)], axis=0)
    yield
    grams = nt_dot(left, others)
    yield
    chunk = 32
    high, low = [], []
    for start in range(0, TILE, chunk):
        window = grams[start : start + chunk]
        inside = jnp.maximum(window, 0.0)
        root = lax.rsqrt((1.0 + SOFT_CORE) - window)
        depth = grams[TILE + start : TILE + start + chunk]
        charge = grams[2 * TILE + start : 2 * TILE + start + chunk]
        parts = two_pieces(inside * inside * (depth + charge * (root * root * root)))
        high.append(parts[0])
        low.append(parts[1])
        yield
    both = jnp.dot(jnp.concatenate(high + low, axis=0), others, preferred_element_type=F32)
    yield
    sums[...] = both[0:TILE] + both[TILE:] + masked(left_ref[place], kinds_ref[3]).astype(F32)


def pair_scatter(numbers, sums, total):
    entries = jnp.concatenate(numbers, axis=1)
    forces = [[], [], []]
    for side in range(2):
        across = sums[side].T
        for axis in range(3):
            moment, place = (
                sum(across[first + axis + 8 * piece : first + axis + 8 * piece + 1] for piece in range(3))
                for first in (0, COPY)
            )
            forces[axis].append(place * across[ONE : ONE + 1] - moment)
    yield
    grid = lax.broadcasted_iota(I32, (ROW, ROW), 0)
    hot = jnp.where(grid == (entries & (ROW - 1)), 1.0, 0.0).astype(BF16)
    yield
    count = total.shape[0] // 3
    mask = lax.broadcasted_iota(I32, (count, ROW), 0) == (entries >> 8)
    high, low = [], []
    for axis in range(3):
        force = jnp.concatenate(forces[axis], axis=1)
        part = force.astype(BF16).astype(F32)
        high.append(jnp.where(mask, part, 0.0).astype(BF16))
        low.append(jnp.where(mask, force - part, 0.0).astype(BF16))
        yield
    both = nt_dot(jnp.concatenate(high + low, axis=0), hot)
    total[...] += both[0 : 3 * count] + both[3 * count :]


def weave(stages, copies, parts):
    size = -(-len(copies) // parts)
    for turn, _ in enumerate(itertools.zip_longest(*stages)):
        for copy in copies[turn * size : (turn + 1) * size]:
            copy()


def force_kernel(
    rows, list_ref, next_ref, order_ref, before_ref, lower_ref, fields_ref, upper_ref, kinds_ref, left_ref,
    out_ref, solute_ref, table, total, far_a, far_b, sum_a, sum_b,
):
    turn = pl.program_id(0)
    partners = far_a.shape[1]
    own = rows * LANES
    masks = sublane_masks()

    def load(local, far):
        ref, first = (list_ref, local) if local < STEP else (next_ref, local - STEP)

        def entry_of(k):
            return ref[first * partners + k]

        return [
            functools.partial(copy_rows, table, entry_of, far, start, masks)
            for start in range(0, partners, 16)
        ]

    def scatter(local, sums):
        ref, first = (order_ref, local) if local >= 0 else (before_ref, local + STEP)
        return pair_scatter([ref[first + side : first + side + 1, :] for side in range(2)], sums, total)

    @pl.when(turn == 0)
    def _():
        def fill(group, carry):
            for domain, ref in enumerate((lower_ref, fields_ref, upper_ref)):
                fill_blocks(ref, rows, group * 4, 4, (domain - 1) * SLAB_WIDTH, table, domain * own)
            return carry

        lax.fori_loop(0, rows // 4, fill, 0)
        sum_b[...] = jnp.zeros_like(sum_b)
        total[...] = jnp.zeros_like(total)
        for side in range(FLIGHT):
            for copy in load(side, far_a.at[side]):
                copy()

    flight = range(FLIGHT)
    for tile in range(0, STEP, FLIGHT):
        far, far_next, sums, sums_before = (
            (far_a, far_b, sum_a, sum_b) if tile % (2 * FLIGHT) == 0 else (far_b, far_a, sum_b, sum_a)
        )
        weave(
            [tile_sums(left_ref, kinds_ref, tile + side, far.at[side], sums.at[side]) for side in flight]
            + [scatter(tile - FLIGHT + side, sums_before.at[pl.ds(side, 2)]) for side in flight[::2]],
            [copy for side in flight for copy in load(tile + FLIGHT + side, far_next.at[side])],
            7,
        )

    @pl.when(turn == pl.num_programs(0) - 1)
    def _():
        for side in range(0, FLIGHT, 2):
            for _ in scatter(STEP - FLIGHT + side, sum_b.at[pl.ds(side, 2)]):
                pass
        count = rows * LANES // ROW
        for axis in range(3):
            force = total[axis * count : (axis + 1) * count, :]
            for side in range(ROW // LANES):
                spot = pl.ds(axis * rows + side, count, stride=ROW // LANES)
                out_ref[spot, :] = fields_ref[spot, :] + STEP_SIZE * force[:, side * LANES : (side + 1) * LANES]
        solute = SOL_DEV // LANES
        for axis in range(3):
            solute_ref[axis] = out_ref[axis * rows : axis * rows + solute, :]
            solute_ref[3 + axis] = fields_ref[axis * rows : axis * rows + solute, :]


def product_kernel(images, index_ref, *refs):
    solute_refs, (sums_ref, pushed, path) = refs[:images], refs[images:]
    index = index_ref[0]
    for by in range(images):
        place = lax.rem(index + images - by, images)
        pushed[place] = solute_refs[by][0:3]
        path[place] = solute_refs[by][3:6]
    sums_ref[...] = jnp.zeros_like(sums_ref)
    last = images - 1
    tangents = [path[min(k + 1, last)] - path[max(k - 1, 0)] for k in range(images)]

    def put(kind, image, left, right):
        total = jnp.sum(left * right, axis=0)
        sums_ref[kind * images + image : kind * images + image + 1, :] = jnp.sum(total, axis=0, keepdims=True)

    for k in range(images):
        put(0, k, tangents[k], tangents[k])
        put(1, k, pushed[k] - path[k], tangents[k])
        if k < last:
            step = path[k + 1] - path[k]
            gap = pushed[k + 1] - pushed[k]
            put(2, k, step, step)
            put(3, k, gap, gap)
            put(4, k, gap, tangents[k + 1])
            put(5, k, gap, tangents[k])
            put(6, k, tangents[k + 1], tangents[k])


def blend_kernel(images, index_ref, sums_ref, pushed, path, out_in, out_ref):
    del out_in
    index = index_ref[0]
    last = images - 1
    totals = jnp.sum(sums_ref[...], axis=1, keepdims=True)

    def total(kind, image):
        row = kind * images + image
        return totals[row : row + 1, :]

    step_root = [jnp.sqrt(total(2, k) + EPSILON) for k in range(last)]
    shift = []
    for k in range(images):
        tangent_sq = total(0, k)
        value = -total(1, k) / (tangent_sq + EPSILON)
        if 0 < k < last:
            spring = SPRING_COEF * (step_root[k] - step_root[k - 1]) / jnp.sqrt(tangent_sq + EPSILON)
            value = value + STEP_SIZE * spring
        shift.append(value)
    lengths = []
    for k in range(last):
        there, here = shift[k + 1], shift[k]
        length_sq = (
            total(3, k)
            + there * there * total(0, k + 1)
            + here * here * total(0, k)
            + 2.0 * (there * total(4, k) - here * total(5, k) - there * here * total(6, k))
        )
        lengths.append(jnp.sqrt(jnp.maximum(length_sq, 0.0) + EPSILON))
    knots = [jnp.zeros_like(lengths[0])]
    for length in lengths:
        knots.append(knots[-1] + length)

    def pick(values):
        result = values[0]
        for k in range(1, images):
            result = jnp.where(index == k, values[k], result)
        return result

    none = jnp.zeros_like(lengths[0])
    excess = [knots[k] - knots[last] * (k / last) for k in range(images)]
    back = pick([none] + [jnp.clip(excess[k] / lengths[k - 1], 0.0, 1.0) for k in range(1, images)])
    ahead = pick([jnp.clip(-excess[k] / lengths[k], 0.0, 1.0) for k in range(last)] + [none])
    shifts = [pick([shift[min(max(k + by, 0), last)] for k in range(images)]) for by in (-1, 0, 1)]

    def moved(by):
        place = jnp.clip(index + by, 0, last)
        tangent = path[jnp.minimum(place + 1, last)] - path[jnp.maximum(place - 1, 0)]
        return pushed[place] + shifts[by + 1] * tangent

    here = moved(0)
    blended = here + back * (moved(-1) - here) + ahead * (moved(1) - here)
    out_ref[...] = blended


def whole(*shape, dtype=F32):
    return jax.ShapeDtypeStruct(shape, dtype)


def turned(array, axis, by):
    count = lax.axis_size(axis)
    return lax.ppermute(array, axis, [(i, (i + by) % count) for i in range(count)])


def summed(array, axis):
    count = lax.axis_size(axis)
    if count & (count - 1):
        return lax.psum(array, axis)

    def crossed(by):
        return lax.ppermute(array, axis, [(i, i ^ by) for i in range(count)])

    array = array + crossed(1)
    return sum((crossed(by) for by in range(2, count, 2)), array)


def round_trip(array, axis):
    return [array] + [turned(array, axis, by) for by in range(1, lax.axis_size(axis))]


def per_device(positions, strength, charge, rest_scale, cell_order, ghost_index, tile_atoms):
    atoms = positions.shape[2]
    rows = atoms // LANES
    partners = tile_atoms.shape[2]
    images = lax.axis_size("image")
    index = lax.axis_index("image").reshape(1)

    factor = jnp.where(jnp.arange(atoms) < SOL_DEV, jnp.sqrt(rest_scale[0]), 1.0)
    scaled = jnp.stack([strength * factor * LJ_COEF**0.5, charge * factor * CHARGE_COEF**0.5])
    places = positions.reshape(3, rows, LANES)
    fields = jnp.concatenate([places, scaled.reshape(2, rows, LANES)]).reshape(FIELDS * rows, LANES)
    shell = ghost_index.reshape(2, rows // 2, LANES)
    lower_list, upper_list = turned(shell[1], "space", 1), turned(shell[0], "space", -1)
    fields, lower_list, upper_list = lax.optimization_barrier((fields, lower_list, upper_list))
    lower, upper = turned(fields, "space", 1), turned(fields, "space", -1)
    tile_order = cell_order.reshape(rows, LANES)
    order = cell_order.reshape(atoms)
    scalar = pl.BlockSpec(memory_space=pltpu.SMEM)
    vector = pl.BlockSpec(memory_space=pltpu.VMEM)
    params = pltpu.CompilerParams(vmem_limit_bytes=VMEM_LIMIT)
    last = rows // STEP - 1

    def listed(size, by):
        return pl.BlockSpec((STEP * size,), lambda i: (jnp.clip(i + by, 0, last),), memory_space=pltpu.SMEM)

    table = (atoms + 2 * PAD, LANES)
    left, partner_rows = pl.pallas_call(
        functools.partial(near_kernel, rows),
        grid=(rows // STEP,),
        out_shape=[whole(rows, TILE, LANES, dtype=BF16), whole(rows * partners // LANES, LANES, dtype=I32)],
        in_specs=[listed(TILE, 0), listed(TILE, 1)]
        + [vector] * 2
        + [pl.BlockSpec((1, STEP, partners), lambda i: (0, i, 0))]
        + [vector] * 2,
        out_specs=[
            pl.BlockSpec((STEP, TILE, LANES), lambda i: (i, 0, 0)),
            pl.BlockSpec((STEP * partners // LANES, LANES), lambda i: (i, 0)),
        ],
        scratch_shapes=[
            pltpu.VMEM(table, F32),
            pltpu.VMEM((2, TILE, LANES), BF16),
            pltpu.VMEM((2, TILE, LANES), BF16),
            pltpu.VMEM((rows, 2 * LANES), BF16),
        ],
        compiler_params=params,
        cost_estimate=pl.CostEstimate(flops=25 * 10**9, bytes_accessed=10**7, transcendentals=0),
    )(order, order, lower_list, upper_list, tile_atoms, fields, near_selector())
    pairs = partner_rows.reshape(rows * partners)
    out, solute = pl.pallas_call(
        functools.partial(force_kernel, rows),
        grid=(rows // STEP,),
        out_shape=[whole(3 * rows, LANES), whole(6, SOL_DEV // LANES, LANES)],
        in_specs=[listed(partners, 0), listed(partners, 1)]
        + [pl.BlockSpec((STEP, LANES), lambda i, by=by: (jnp.maximum(i - by, 0), 0)) for by in (0, 1)]
        + [vector] * 4
        + [pl.BlockSpec((STEP, TILE, LANES), lambda i: (i, 0, 0))],
        out_specs=[vector] * 2,
        scratch_shapes=[
            pltpu.VMEM((3 * atoms + 2 * PAD, LANES), F32),
            pltpu.VMEM((3 * atoms // ROW, ROW), F32),
            pltpu.VMEM((FLIGHT, partners, LANES), BF16),
            pltpu.VMEM((FLIGHT, partners, LANES), BF16),
            pltpu.VMEM((FLIGHT, TILE, LANES), F32),
            pltpu.VMEM((FLIGHT, TILE, LANES), F32),
        ],
        compiler_params=params,
        cost_estimate=pl.CostEstimate(flops=25 * 10**9, bytes_accessed=10**7, transcendentals=0),
    )(pairs, pairs, tile_order, tile_order, lower, fields, upper, near_masks(), left)
    out = out.reshape(3, rows, LANES)
    solutes = round_trip(solute, "image")
    small = pltpu.CompilerParams(vmem_limit_bytes=8 * 1024 * 1024)
    solute_shape = whole(images, 3, SOL_DEV // LANES, LANES)
    sums, pushed, path = pl.pallas_call(
        functools.partial(product_kernel, images),
        out_shape=[whole(-(-7 * images // 8) * 8, LANES), solute_shape, solute_shape],
        in_specs=[scalar] + [vector] * images,
        out_specs=[vector] * 3,
        compiler_params=small,
    )(index, *solutes)
    out = pl.pallas_call(
        functools.partial(blend_kernel, images),
        grid=(1,),
        out_shape=whole(3, rows, LANES),
        in_specs=[scalar] + [vector] * 3 + [pl.BlockSpec(memory_space=pl.ANY)],
        out_specs=pl.BlockSpec((3, SOL_DEV // LANES, LANES), lambda i: (0, 0, 0)),
        input_output_aliases={4: 0},
        compiler_params=small,
    )(index, summed(sums, "space"), pushed, path, out)
    return out.reshape(1, 3, atoms)


def solution(mesh):
    placed = (
        P("image", None, "space"),
        P("space"),
        P("space"),
        P("image"),
        P("image", "space", None),
        P("image", "space", None),
        P("image", "space", None),
    )
    return jax.shard_map(
        per_device, mesh=mesh, in_specs=placed, out_specs=P("image", None, "space"), check_vma=False
    )
```
